32 devices in a mesh: seq: 4 (over z), batch: 4 (over x, core), mp: 2 (over y).
Axes of the slice: x: 2, y: 2, z: 4, core: 2. Of those that a mesh axis runs over, the one named last changes fastest.
Arguments:
- layer_input: float32 [8, 4096, 1024], P('batch', 'seq'), may hold values from -6 to 6
- lengths: int32 [8, 4], P('batch'), may hold values from 0 to 4096, as said below
- random_blocks: int32 [8, 64, 3], P('batch', 'seq'), may hold values from 0 to 63, as said below
- first_gain: float32 [1024], replicated, may hold values from 0.25 to 1.75
- first_bias: float32 [1024], replicated, may hold values from -1.5 to 1.5
- qkv_weight: bfloat16 [1024, 3, 1024], P(None, None, 'mp'), may hold values from -0.25 to 0.25
- out_weight: bfloat16 [1024, 1024], P('mp'), may hold values from -1.5 to 1.5
- second_gain: float32 [1024], replicated, may hold values from 0.25 to 1.75
- second_bias: float32 [1024], replicated, may hold values from -1.5 to 1.5
- up_weight: bfloat16 [1024, 4096], P(None, 'mp'), may hold values from -0.1875 to 0.1875
- up_bias: float32 [4096], P('mp'), may hold values from -3 to 3
- down_weight: bfloat16 [4096, 1024], P('mp'), may hold values from -0.09375 to 0.09375
- down_bias: float32 [1024], replicated, may hold values from -3 to 3
- cotangent: float32 [8, 4096, 1024], P('batch', 'seq'), may hold values from -6 to 6
Outputs:
- layer_output: float32 [8, 4096, 1024], P('batch', 'seq')
- input_grad: float32 [8, 4096, 1024], P('batch', 'seq')
- first_gain_grad: float32 [1024], replicated
- first_bias_grad: float32 [1024], replicated
- qkv_grad: float32 [1024, 3, 1024], P('seq', None, 'mp')
- out_grad: float32 [1024, 1024], P('mp', 'seq')
- second_gain_grad: float32 [1024], replicated
- second_bias_grad: float32 [1024], replicated
- up_grad: float32 [1024, 4096], P('seq', 'mp')
- up_bias_grad: float32 [4096], P('mp')
- down_grad: float32 [4096, 1024], P('mp', 'seq')
- down_bias_grad: float32 [1024], replicated
The draws below stay inside these ranges and needn't reach their ends.
Inputs may be any that keep to these rules, and one draw needn't show every extreme that they name: Row s holds the lengths of the 4 documents packed in order from the first token of sequence s, some possibly empty; the tokens after them are padding. `random_blocks`: entry [s, i, j] is a block of sequence s that holds some token of the document, or of the padding, that holds the first token of block i.
All inputs are finite; a program needn't handle non-finite values.
Results may differ from the reference program's by a relative error of at most 0.019.
The reference program's roundings to bfloat16 on the way count: a program that leaves them out, or rounds other values in their place, can miss the bound.
Values may be sent and summed in bfloat16 or wider, within the bound.
A program may use at most 384 MiB of HBM per device.

```python
import jax
import jax.numpy as jnp
from jax import lax

D = 1024
H = 16
FF = 4096
BLOCK = 64
RAND = 3
GLOB = 2
WIN = 3
NBLK = 64
NDOC = 4
MB = 2
SEQ_MB = 1
HD = 64
LIST = 8
LEN = 4096
SEQS = 8
N_MP = 2


def packing(key):
    group_size = MB * SEQ_MB
    group_total = SEQS // group_size
    key_pick, key_small, key_tail, key_pad, key_cut = jax.random.split(key, 5)
    chosen = jax.random.randint(key_pick, (group_total,), 0, group_size)
    long_rows = jnp.arange(SEQS, dtype=jnp.int32) % group_size == jnp.repeat(chosen, group_size)
    smalls = jax.random.randint(key_small, (SEQS, NDOC - 1), 1, max(2, BLOCK // 4))
    tail_pads = jax.random.randint(key_tail, (SEQS,), 0, max(1, BLOCK // 2))
    leading = LEN - jnp.sum(smalls, axis=1) - tail_pads
    long_docs = jnp.concatenate([leading[:, None], smalls], axis=1)
    totals = LEN - jax.random.randint(key_pad, (SEQS,), 0, LEN // 4)
    cut_points = jnp.sort(jax.random.randint(key_cut, (SEQS, NDOC - 1), 1, totals[:, None]), axis=1)
    bounds = jnp.concatenate([jnp.zeros((SEQS, 1), jnp.int32), cut_points, totals[:, None]], axis=1)
    short_docs = bounds[:, 1:] - bounds[:, :-1]
    return jnp.where(long_rows[:, None], long_docs, short_docs).astype(jnp.int32)


def draw_lengths(key, part):
    return packing(key)


def draw_random_blocks(key, part):
    doc_lengths = packing(key)
    key = jax.random.fold_in(key, 11)
    doc_ends = jnp.cumsum(doc_lengths, axis=1).astype(jnp.int32)
    doc_starts = doc_ends - doc_lengths
    totals = doc_ends[:, -1:]
    firsts = jnp.arange(NBLK, dtype=jnp.int32) * BLOCK
    segment = jnp.sum((firsts[None, :, None] >= doc_ends[:, None, :]).astype(jnp.int32), axis=-1)
    inner = jnp.clip(segment, 0, NDOC - 1)
    seg_start = jnp.where(segment < NDOC, jnp.take_along_axis(doc_starts, inner, axis=1), totals)
    seg_end = jnp.where(segment < NDOC, jnp.take_along_axis(doc_ends, inner, axis=1), LEN)
    lowest = seg_start // BLOCK
    highest = (seg_end - 1) // BLOCK
    return jax.random.randint(key, (SEQS, NBLK, RAND), lowest[..., None], highest[..., None] + 1).astype(jnp.int32)


def shard_levels(key, extent, cuts, smallest, high):
    level, own = 1.0, jax.random.fold_in(key, 6)
    for dim, shards_of in cuts:
        heights = jnp.exp(jax.random.uniform(jax.random.fold_in(own, dim), (shards_of,), jnp.float32, smallest / len(cuts), high / len(cuts)))
        level = level * jnp.repeat(heights, extent[dim] // shards_of).reshape([-1 if axis == dim else 1 for axis in range(len(extent))])
    return level


def centred(rng, shape, scale, limit, shards=(), kind=jnp.bfloat16):
    values = scale * jax.random.normal(rng, shape, jnp.float32)
    if shards:
        values = values * shard_levels(rng, shape, shards, -0.22, 0.18)
    return jnp.clip(values, -limit, limit).astype(kind)


def setup_inputs(seed: int = 0) -> dict:
    arg_keys = jax.random.split(jax.random.key(seed), 15)
    return {
        "layer_input": centred(arg_keys[0], (SEQS, LEN, D), 1.0, 6.0, ((0, 4), (1, 4)), jnp.float32),
        "lengths": draw_lengths(jax.random.fold_in(arg_keys[14], 71), 0),
        "random_blocks": draw_random_blocks(jax.random.fold_in(arg_keys[14], 71), 0),
        "first_gain": jnp.clip(1.0 + 0.15 * jax.random.normal(arg_keys[3], (D,), jnp.float32), 0.25, 1.75),
        "first_bias": centred(arg_keys[4], (D,), 0.3, 1.5, (), jnp.float32),
        "qkv_weight": centred(arg_keys[5], (D, 3, D), (D // 2) ** -0.5, 0.25, ((2, 2),)),
        "out_weight": centred(arg_keys[6], (D, D), (D // 64) ** -0.5, 1.5, ((0, 2),)),
        "second_gain": jnp.clip(1.0 + 0.15 * jax.random.normal(arg_keys[7], (D,), jnp.float32), 0.25, 1.75),
        "second_bias": centred(arg_keys[8], (D,), 0.3, 1.5, (), jnp.float32),
        "up_weight": centred(arg_keys[9], (D, FF), D ** -0.5, 0.1875, ((1, 2),)),
        "up_bias": centred(arg_keys[10], (FF,), 0.5, 3.0, ((0, 2),), jnp.float32),
        "down_weight": centred(arg_keys[11], (FF, D), FF ** -0.5, 0.09375, ((0, 2),)),
        "down_bias": centred(arg_keys[12], (D,), 0.5, 3.0, (), jnp.float32),
        "cotangent": centred(arg_keys[13], (SEQS, LEN, D), 1.0, 6.0, ((0, 4), (1, 4)), jnp.float32),
    }


NEG = -1e+30
EPS = 1e-05
HIGH = lax.Precision.HIGHEST

@jax.custom_vjp
def low(v):
    return lax.optimization_barrier(v.astype(jnp.bfloat16)).astype(jnp.float32)

@jax.custom_vjp
def low_back(v):
    return v

def low_keep(v):
    return (low(v), None)

def low_pass(kept, grad):
    return (grad,)

def back_keep(v):
    return (v, None)

def back_low(kept, grad):
    return (low(grad),)
low.defvjp(low_keep, low_pass)
low_back.defvjp(back_keep, back_low)

def norm_rows(rows, gain, bias):
    centre = rows - lax.optimization_barrier(jnp.mean(rows, axis=-1, keepdims=True))
    spread = lax.optimization_barrier(jnp.mean(centre * centre, axis=-1, keepdims=True))
    return centre * lax.rsqrt(spread + EPS) * gain + bias

def segment_of(places, doc_ends):
    return lax.optimization_barrier(jnp.sum((places[..., None] >= doc_ends).astype(jnp.int32), axis=-1))

def block_lists(blocks, randoms):
    leading = randoms.shape[:-1]
    globals_part = jnp.broadcast_to(jnp.arange(GLOB, dtype=jnp.int32), leading + (GLOB,))
    window_part = jnp.broadcast_to(blocks[:, None] + jnp.arange(WIN, dtype=jnp.int32) - WIN // 2, leading + (WIN,))
    block_list = jnp.concatenate([globals_part, window_part, randoms], axis=-1)
    inside = (block_list >= 0) & (block_list < NBLK)
    same_entry = block_list[..., :, None] == block_list[..., None, :]
    order_ids = jnp.arange(LIST)
    earlier = order_ids[None, :] < order_ids[:, None]
    repeated = jnp.any(same_entry & earlier, axis=-1)
    return (block_list, inside & jnp.logical_not(repeated))

def sequence_layer(weights_all, seq_rows, doc_ends, randoms):
    first_gain, first_bias, qkv_weight, out_weight, second_gain, second_bias, up_weight, up_bias, down_weight, down_bias = weights_all
    places = jnp.arange(LEN, dtype=jnp.int32)
    segment = segment_of(places, doc_ends)
    valid_rows = (places < doc_ends[-1]).astype(jnp.float32)
    score_scale = HD ** (-0.5)
    normed = low(norm_rows(seq_rows, first_gain, first_bias))
    qkv_rows = jnp.dot(normed, qkv_weight.reshape(D, 3 * D), precision=HIGH)
    qkv_rows = low_back(low(qkv_rows)).reshape(LEN, 3, H, HD)
    queries = qkv_rows[:, 0]
    key_rows = qkv_rows[:, 1]
    values = qkv_rows[:, 2]
    block_list, admitted = block_lists(jnp.arange(NBLK, dtype=jnp.int32), randoms)
    safe_list = jnp.clip(block_list, 0, NBLK - 1)
    key_blocks = key_rows.reshape(NBLK, BLOCK, H, HD)[safe_list]
    value_blocks = values.reshape(NBLK, BLOCK, H, HD)[safe_list]
    seg_blocks = segment.reshape(NBLK, BLOCK)
    key_segs = seg_blocks[safe_list]
    raw_scores = jnp.einsum('bqhd,bjkhd->bhqjk', queries.reshape(NBLK, BLOCK, H, HD), key_blocks, precision=HIGH) * score_scale
    scores = low_back(raw_scores)
    keep_mask = admitted[:, None, None, :, None] & (seg_blocks[:, None, :, None, None] == key_segs[:, None, None, :, :])
    masked = jnp.where(keep_mask, scores, NEG)
    row_top = lax.optimization_barrier(jnp.max(masked, axis=(3, 4), keepdims=True))
    weights = jnp.exp(masked - row_top) * keep_mask.astype(jnp.float32)
    probs_list = weights / lax.optimization_barrier(jnp.sum(weights, axis=(3, 4), keepdims=True))
    listed = jnp.einsum('bhqjk,bjkhd->bqhd', low(probs_list), value_blocks, precision=HIGH).reshape(LEN, H, HD)
    glob_rows = GLOB * BLOCK
    raw_glob = jnp.einsum('qhd,khd->hqk', queries[:glob_rows], key_rows, precision=HIGH) * score_scale
    scores_glob = low_back(raw_glob)
    glob_mask = segment[None, :glob_rows, None] == segment[None, None, :]
    masked_glob = jnp.where(glob_mask, scores_glob, NEG)
    glob_top = lax.optimization_barrier(jnp.max(masked_glob, axis=-1, keepdims=True))
    glob_weights = jnp.exp(masked_glob - glob_top) * glob_mask.astype(jnp.float32)
    glob_probs = glob_weights / lax.optimization_barrier(jnp.sum(glob_weights, axis=-1, keepdims=True))
    glob_out = jnp.einsum('hqk,khd->qhd', glob_probs, values, precision=HIGH)
    attended = jnp.concatenate([glob_out, listed[glob_rows:]], axis=0) * valid_rows[:, None, None]
    attended = low_back(low(attended)).reshape(LEN, D)
    group_cols = D // N_MP
    branch = jnp.zeros((LEN, D), jnp.float32)
    for member in range(N_MP):
        lower_col = member * group_cols
        upper_col = lower_col + group_cols
        branch = branch + low(low_back(jnp.dot(attended[:, lower_col:upper_col], out_weight[lower_col:upper_col], precision=HIGH)))
    hidden = seq_rows + branch
    normed_two = low(norm_rows(hidden, second_gain, second_bias))
    pre_act = low_back(jnp.dot(normed_two, up_weight, precision=HIGH) + up_bias)
    activated = low(jax.nn.gelu(pre_act, approximate=True))
    group_units = FF // N_MP
    ffn_branch = jnp.zeros((LEN, D), jnp.float32)
    for member in range(N_MP):
        lower_unit = member * group_units
        upper_unit = lower_unit + group_units
        ffn_branch = ffn_branch + low(low_back(jnp.dot(activated[:, lower_unit:upper_unit], down_weight[lower_unit:upper_unit], precision=HIGH)))
    return hidden + ffn_branch + down_bias

def reference(layer_input, lengths, random_blocks, first_gain, first_bias, qkv_weight, out_weight, second_gain, second_bias, up_weight, up_bias, down_weight, down_bias, cotangent):
    doc_ends = jnp.cumsum(lengths, axis=1).astype(jnp.int32)
    params = tuple((weight_item.astype(jnp.float32) for weight_item in (first_gain, first_bias, qkv_weight, out_weight, second_gain, second_bias, up_weight, up_bias, down_weight, down_bias)))
    layer_step = jax.checkpoint(sequence_layer)

    def forward(rows_all, *weights_all):

        def step(carried, seq_item):
            return (carried, layer_step(weights_all, seq_item[0], seq_item[1], seq_item[2]))
        _, outputs = lax.scan(step, jnp.zeros((), jnp.float32), (rows_all, doc_ends, random_blocks))
        return outputs
    outputs, pullback = jax.vjp(forward, layer_input.astype(jnp.float32), *params)
    gradients = pullback(cotangent.astype(jnp.float32))
    return (outputs, gradients[0], gradients[1], gradients[2], gradients[3], gradients[4], gradients[5], gradients[6], gradients[7], gradients[8], gradients[9], gradients[10])
```

```python
import functools

import jax
import jax.numpy as jnp
from jax import lax
from jax.experimental import pallas as pl
from jax.experimental.pallas import tpu as pltpu
from jax.sharding import PartitionSpec as P

BLOCK = 64
GLOB = 2
WIN = 3
HD = 64
LIST = 8

NEG = -1e30
EPS = 1e-05
F32 = jnp.float32
BF16 = jnp.bfloat16
VMEM_LIMIT = 60 * 1024 * 1024


def norm_stats(rows):
    centre = rows - jnp.mean(rows, axis=-1, keepdims=True)
    spread = jnp.mean(centre * centre, axis=-1, keepdims=True)
    inverse = lax.rsqrt(spread + EPS)
    return (centre * inverse, inverse)


def norm_back(grad_out, normed, inverse, gain):
    scaled = grad_out * gain
    return inverse * (
        scaled
        - jnp.mean(scaled, axis=-1, keepdims=True)
        - normed * jnp.mean(scaled * normed, axis=-1, keepdims=True)
    )


def block_lists(blocks, randoms, block_count):
    leading = randoms.shape[:-1]
    globals_part = jnp.broadcast_to(jnp.arange(GLOB, dtype=jnp.int32), leading + (GLOB,))
    window_part = jnp.broadcast_to(
        blocks[:, None] + jnp.arange(WIN, dtype=jnp.int32) - WIN // 2, leading + (WIN,)
    )
    block_list = jnp.concatenate([globals_part, window_part, randoms], axis=-1)
    inside = (block_list >= 0) & (block_list < block_count)
    same_entry = block_list[..., :, None] == block_list[..., None, :]
    order_ids = jnp.arange(LIST)
    earlier = order_ids[None, :] < order_ids[:, None]
    repeated = jnp.any(same_entry & earlier, axis=-1)
    admitted = inside & jnp.logical_not(repeated)
    return (jnp.clip(block_list, 0, block_count - 1), admitted.astype(jnp.int32))


def segment_at(places, ends_ref):
    total = jnp.zeros(places.shape, jnp.int32)
    for doc in range(ends_ref.shape[0]):
        total = total + (places >= ends_ref[doc]).astype(jnp.int32)
    return total


def head_spread(rows, heads):
    lane_head = lax.broadcasted_iota(jnp.int32, rows.shape, 1) // HD
    return jnp.concatenate(
        [rows * (lane_head == head).astype(rows.dtype) for head in range(heads)], axis=0
    )


def head_fold(wide, heads):
    rows = wide.shape[0] // heads
    lane_head = lax.broadcasted_iota(jnp.int32, (rows, wide.shape[1]), 1) // HD
    folded = jnp.zeros((rows, wide.shape[1]), wide.dtype)
    for head in range(heads):
        folded = jnp.where(lane_head == head, wide[head * rows : (head + 1) * rows], folded)
    return folded


def fill_segments(key_segs, ends_ref):
    def fill(block, _):
        places = block * BLOCK + lax.broadcasted_iota(jnp.int32, (BLOCK, key_segs.shape[1]), 0)
        key_segs[pl.ds(pl.multiple_of(block * BLOCK, BLOCK), BLOCK), :] = segment_at(places, ends_ref)
        return 0

    lax.fori_loop(0, key_segs.shape[0] // BLOCK, fill, 0)


def query_segments(block, heads, ends_ref):
    lanes = lax.broadcasted_iota(jnp.int32, (8, heads * BLOCK), 1)
    return segment_at(block * BLOCK + lanes % BLOCK, ends_ref)[0:1]


def block_rows(ref, block):
    return ref[pl.ds(pl.multiple_of(block * BLOCK, BLOCK), BLOCK), :]


def dot_nt(left, right):
    return lax.dot_general(left, right, (((1,), (1,)), ((), ())), preferred_element_type=F32)


def dot_tn(left, right):
    return lax.dot_general(left, right, (((0,), (0,)), ((), ())), preferred_element_type=F32)


def dot_nn(left, right):
    return lax.dot_general(left, right, (((1,), (0,)), ((), ())), preferred_element_type=F32)


def listed_scores(block, starts, keeps, query_wide, k_ref, key_segs, seg_row):
    keys = jnp.concatenate([block_rows(k_ref, start) for start in starts], axis=0)
    scores = dot_nt(keys, query_wide)
    pieces = []
    for entry in range(LIST):
        wanted = jnp.where(keeps[entry] > 0, seg_row, -1)
        keep = block_rows(key_segs, starts[entry]) == wanted
        pieces.append(jnp.where(keep, scores[entry * BLOCK : (entry + 1) * BLOCK], NEG))
    return keys, jnp.concatenate(pieces, axis=0)


def forward_kernel(
    heads, ends_ref, lists_ref, admit_ref, q_ref, k_ref, v_ref, o_ref, lse_ref, key_segs, held
):
    scale = HD ** (-0.5)
    rows_total = q_ref.shape[0]
    blocks = rows_total // BLOCK
    chunk = LIST * BLOCK
    fill_segments(key_segs, ends_ref)

    def store(block, wide, top, total):
        out = head_fold(wide, heads)
        places = block * BLOCK + lax.broadcasted_iota(jnp.int32, out.shape, 0)
        out = jnp.where(places < ends_ref[ends_ref.shape[0] - 1], out, 0.0)
        o_ref[pl.ds(pl.multiple_of(block * BLOCK, BLOCK), BLOCK), :] = out.astype(BF16)
        lse_ref[block] = jnp.broadcast_to(top + jnp.log(total), lse_ref.shape[1:])

    def global_block(block, _):
        query_wide = head_spread(block_rows(q_ref, block) * scale, heads)
        seg_row = query_segments(block, heads, ends_ref)

        def score(part, top):
            here = pl.ds(pl.multiple_of(part * chunk, chunk), chunk)
            scores = dot_nt(k_ref[here, :], query_wide)
            scores = jnp.where(key_segs[here, :] == seg_row, scores, NEG)
            held[here, :] = scores
            return jnp.maximum(top, jnp.max(scores, axis=0, keepdims=True))

        top = lax.fori_loop(
            0, rows_total // chunk, score, jnp.full((1, heads * BLOCK), NEG, F32)
        )

        def weigh(part, total):
            here = pl.ds(pl.multiple_of(part * chunk, chunk), chunk)
            weights = jnp.exp(held[here, :] - top)
            held[here, :] = weights
            return total + jnp.sum(weights, axis=0, keepdims=True)

        total = lax.fori_loop(
            0, rows_total // chunk, weigh, jnp.zeros((1, heads * BLOCK), F32)
        )
        inverse = 1.0 / total

        def gather(part, wide):
            here = pl.ds(pl.multiple_of(part * chunk, chunk), chunk)
            probs = (held[here, :] * inverse).astype(BF16)
            return wide + dot_tn(probs, v_ref[here, :])

        wide = lax.fori_loop(
            0,
            rows_total // chunk,
            gather,
            jnp.zeros((heads * BLOCK, q_ref.shape[1]), F32),
        )
        store(block, wide, top, total)
        return 0

    lax.fori_loop(0, GLOB, global_block, 0)

    def listed_block(block):
        query_wide = head_spread(block_rows(q_ref, block) * scale, heads)
        seg_row = query_segments(block, heads, ends_ref)
        starts = [lists_ref[block * LIST + entry] for entry in range(LIST)]
        keeps = [admit_ref[block * LIST + entry] for entry in range(LIST)]
        _, scores = listed_scores(block, starts, keeps, query_wide, k_ref, key_segs, seg_row)
        top = jnp.max(scores, axis=0, keepdims=True)
        weights = jnp.exp(scores - top)
        total = jnp.sum(weights, axis=0, keepdims=True)
        probs = (weights * (1.0 / total)).astype(BF16)
        values = jnp.concatenate([block_rows(v_ref, start) for start in starts], axis=0)
        store(block, dot_tn(probs, values), top, total)

    def listed_pair(pair, _):
        listed_block(GLOB + 2 * pair)
        listed_block(GLOB + 2 * pair + 1)
        return 0

    lax.fori_loop(0, (blocks - GLOB) // 2, listed_pair, 0)


def backward_kernel(
    heads,
    ends_ref,
    lists_ref,
    admit_ref,
    q_ref,
    k_ref,
    v_ref,
    o_ref,
    do_ref,
    lse_ref,
    out_ref,
    key_segs,
    dk_ref,
    dv_ref,
    dq_ref,
):
    scale = HD ** (-0.5)
    rows_total, cols = q_ref.shape
    blocks = rows_total // BLOCK
    chunk = LIST * BLOCK
    fill_segments(key_segs, ends_ref)

    def clear(block, _):
        here = pl.ds(pl.multiple_of(block * BLOCK, BLOCK), BLOCK)
        dk_ref[here, :] = jnp.zeros((BLOCK, cols), F32)
        dv_ref[here, :] = jnp.zeros((BLOCK, cols), F32)
        return 0

    lax.fori_loop(0, blocks, clear, 0)

    def query_side(block):
        query_wide = head_spread(block_rows(q_ref, block) * scale, heads)
        grad_rows = block_rows(do_ref, block)
        grad_wide = head_spread(grad_rows, heads)
        product = grad_rows.astype(F32) * block_rows(o_ref, block).astype(F32)
        spread = head_spread(product, heads).astype(BF16)
        delta = dot_nt(jnp.ones((8, cols), BF16), spread)[0:1]
        return query_wide, grad_wide, delta, lse_ref[block, 0:1]

    def grads(scores, keys, values, query_wide, grad_wide, delta, lse):
        probs = jnp.exp(scores - lse)
        prob_grad = dot_nt(values, grad_wide)
        score_grad = (probs * (prob_grad - delta)).astype(BF16)
        dk = dot_nn(score_grad, query_wide)
        dv = dot_nn(probs.astype(BF16), grad_wide)
        dq = dot_tn(score_grad, keys)
        return dk, dv, dq

    def store_query(block, wide):
        here = pl.ds(pl.multiple_of(block * BLOCK, BLOCK), BLOCK)
        out_ref[here, 0:cols] = (head_fold(wide, heads) * scale).astype(BF16)

    def global_block(block, _):
        query_wide, grad_wide, delta, lse = query_side(block)
        seg_row = query_segments(block, heads, ends_ref)
        dq_ref[...] = jnp.zeros_like(dq_ref)

        def part_of(part, _):
            here = pl.ds(pl.multiple_of(part * chunk, chunk), chunk)
            keys = k_ref[here, :]
            scores = jnp.where(key_segs[here, :] == seg_row, dot_nt(keys, query_wide), NEG)
            dk, dv, dq = grads(scores, keys, v_ref[here, :], query_wide, grad_wide, delta, lse)
            dk_ref[here, :] += dk
            dv_ref[here, :] += dv
            dq_ref[...] += dq
            return 0

        lax.fori_loop(0, rows_total // chunk, part_of, 0)
        store_query(block, dq_ref[...])
        return 0

    lax.fori_loop(0, GLOB, global_block, 0)

    def listed_block(block):
        query_wide, grad_wide, delta, lse = query_side(block)
        seg_row = query_segments(block, heads, ends_ref)
        starts = [lists_ref[block * LIST + entry] for entry in range(LIST)]
        keeps = [admit_ref[block * LIST + entry] for entry in range(LIST)]
        keys, scores = listed_scores(block, starts, keeps, query_wide, k_ref, key_segs, seg_row)
        values = jnp.concatenate([block_rows(v_ref, start) for start in starts], axis=0)
        dk, dv, dq = grads(scores, keys, values, query_wide, grad_wide, delta, lse)
        store_query(block, dq)
        for entry in range(LIST):
            here = pl.ds(pl.multiple_of(starts[entry] * BLOCK, BLOCK), BLOCK)
            dk_ref[here, :] += dk[entry * BLOCK : (entry + 1) * BLOCK]
            dv_ref[here, :] += dv[entry * BLOCK : (entry + 1) * BLOCK]

    def listed_pair(pair, _):
        listed_block(GLOB + 2 * pair)
        listed_block(GLOB + 2 * pair + 1)
        return 0

    lax.fori_loop(0, (blocks - GLOB) // 2, listed_pair, 0)

    def finish(block, _):
        here = pl.ds(pl.multiple_of(block * BLOCK, BLOCK), BLOCK)
        out_ref[here, cols : 2 * cols] = dk_ref[here, :].astype(BF16)
        out_ref[here, 2 * cols : 3 * cols] = dv_ref[here, :].astype(BF16)
        return 0

    lax.fori_loop(0, blocks, finish, 0)


def smem():
    return pl.BlockSpec(memory_space=pltpu.SMEM)


def column(rows, cols, index):
    return pl.BlockSpec((rows, cols), lambda step: (0, index))


def attention_forward(qkv, doc_ends, lists, admits, cols):
    rows = qkv.shape[0]
    heads = cols // HD
    blocks = rows // BLOCK
    return pl.pallas_call(
        functools.partial(forward_kernel, heads),
        grid=(1,),
        in_specs=[smem(), smem(), smem()] + [column(rows, cols, part) for part in range(3)],
        out_specs=[
            column(rows, cols, 0),
            pl.BlockSpec((blocks, 8, heads * BLOCK), lambda step: (0, 0, 0)),
        ],
        out_shape=[
            jax.ShapeDtypeStruct((rows, cols), BF16),
            jax.ShapeDtypeStruct((blocks, 8, heads * BLOCK), F32),
        ],
        scratch_shapes=[
            pltpu.VMEM((rows, heads * BLOCK), jnp.int32),
            pltpu.VMEM((rows, heads * BLOCK), F32),
        ],
        compiler_params=pltpu.CompilerParams(vmem_limit_bytes=VMEM_LIMIT),
        cost_estimate=pl.CostEstimate(
            flops=8 * rows * 10 * LIST * BLOCK * cols * heads,
            bytes_accessed=8 * rows * cols,
            transcendentals=0,
        ),
    )(doc_ends, lists, admits, qkv, qkv, qkv)


def attention_backward(qkv, attended, attended_grad, lse, doc_ends, lists, admits, cols):
    rows = qkv.shape[0]
    heads = cols // HD
    blocks = rows // BLOCK
    return pl.pallas_call(
        functools.partial(backward_kernel, heads),
        grid=(1,),
        in_specs=[smem(), smem(), smem()]
        + [column(rows, cols, part) for part in range(3)]
        + [
            column(rows, cols, 0),
            column(rows, cols, 0),
            pl.BlockSpec((blocks, 8, heads * BLOCK), lambda step: (0, 0, 0)),
        ],
        out_specs=column(rows, 3 * cols, 0),
        out_shape=jax.ShapeDtypeStruct((rows, 3 * cols), BF16),
        scratch_shapes=[
            pltpu.VMEM((rows, heads * BLOCK), jnp.int32),
            pltpu.VMEM((rows, cols), F32),
            pltpu.VMEM((rows, cols), F32),
            pltpu.VMEM((heads * BLOCK, cols), F32),
        ],
        compiler_params=pltpu.CompilerParams(vmem_limit_bytes=VMEM_LIMIT),
        cost_estimate=pl.CostEstimate(
            flops=20 * rows * 10 * LIST * BLOCK * cols * heads,
            bytes_accessed=20 * rows * cols,
            transcendentals=0,
        ),
    )(doc_ends, lists, admits, qkv, qkv, qkv, attended, attended_grad, lse)


def swap(value, axis, distance=1):
    size = lax.axis_size(axis)
    return lax.ppermute(value, axis, [(j, j ^ distance) for j in range(size)])


def all_to_all(value):
    return lax.all_to_all(value, "seq", 0, 0, tiled=True)


def batch_levels():
    return [1 << level for level in range(lax.axis_size("batch").bit_length() - 1)]


def pick(value, index, count):
    size = value.shape[0] // count
    return lax.dynamic_slice_in_dim(value, index * size, size, 0)


def fetch_other(weight):
    parity = lax.axis_index("batch") % 2
    first = swap(pick(weight, parity, 2), "mp")
    return first, swap(first, "batch")


def narrow_add(mine, received):
    return (mine.astype(F32) + received.astype(F32)).astype(BF16)


def halve(value, distance):
    side = (lax.axis_index("batch") // distance) % 2
    return narrow_add(pick(value, side, 2), swap(pick(value, 1 - side, 2), "batch", distance))


def unhalve(value, distance):
    side = (lax.axis_index("batch") // distance) % 2
    other = swap(value, "batch", distance)
    low = jnp.where(side == 0, value, other)
    high = jnp.where(side == 0, other, value)
    return jnp.concatenate([low, high], axis=0)


def reduce_units(own, near, far):
    levels = batch_levels()
    near = narrow_add(near, swap(far, "batch"))
    for distance in levels:
        own = halve(own, distance)
    for distance in levels[1:]:
        near = halve(near, distance)
    own = narrow_add(own, swap(near, "mp"))
    own = lax.psum_scatter(own, "seq", scatter_dimension=1, tiled=True)
    for distance in reversed(levels):
        own = unhalve(own, distance)
    return own.astype(F32)


def both_sequences(own):
    place = lax.axis_index("mp")
    other = swap(own, "mp").astype(F32)
    mine = own.astype(F32)
    return jnp.concatenate(
        [jnp.where(place == 0, mine, other), jnp.where(place == 0, other, mine)], axis=0
    )


def local(
    layer_input,
    lengths,
    random_blocks,
    first_gain,
    first_bias,
    qkv_weight,
    out_weight,
    second_gain,
    second_bias,
    up_weight,
    up_bias,
    down_weight,
    down_bias,
    cotangent,
):
    seq_count = lax.axis_size("seq")
    seq_index = lax.axis_index("seq")
    mp_index = lax.axis_index("mp")
    parity = lax.axis_index("batch") % 2
    _, local_rows, width = layer_input.shape
    rows_total = local_rows * seq_count
    blocks = rows_total // BLOCK
    half_cols = qkv_weight.shape[2]
    cols = width // seq_count
    units = up_weight.shape[1]

    rows_in = lax.dynamic_index_in_dim(layer_input, mp_index, 0, keepdims=False)
    grad_rows = lax.dynamic_index_in_dim(cotangent, mp_index, 0, keepdims=False)
    doc_ends = jnp.cumsum(lax.dynamic_index_in_dim(lengths, mp_index, 0, keepdims=False))
    randoms = lax.dynamic_index_in_dim(random_blocks, mp_index, 0, keepdims=False)
    randoms = lax.all_gather(randoms, "seq", axis=0, tiled=True)
    lists, admits = block_lists(jnp.arange(blocks, dtype=jnp.int32), randoms, blocks)
    lists, admits = lists.reshape(-1), admits.reshape(-1)
    places = seq_index * local_rows + jnp.arange(local_rows, dtype=jnp.int32)
    valid = (places < doc_ends[-1])[:, None]

    own_half = (seq_index * cols) // half_cols
    candidate = lax.dynamic_slice_in_dim(qkv_weight, (seq_index * cols) % half_cols, cols, 2)
    pairs = []
    for place in range(seq_count):
        source = (place * cols) // half_cols
        pairs.append((place * 2 + source, place * 2 + 1 - source))
    fetched = lax.ppermute(candidate, ("seq", "mp"), pairs)
    qkv_own = jnp.where(mp_index == own_half, candidate, fetched).reshape(width, 3 * cols)
    up_own = up_weight.T
    up_near, up_far = fetch_other(up_own)
    down_near, down_far = fetch_other(down_weight)
    out_full = lax.all_gather(out_weight, "mp", axis=0, tiled=True)
    bias_near, bias_far = fetch_other(up_bias)
    up_parts = (up_own, up_near, up_far)
    down_parts = (down_weight, down_near, down_far)
    bias_parts = (up_bias, bias_near, bias_far)

    normed_one, inverse_one = norm_stats(rows_in)
    first_low = (normed_one * first_gain + first_bias).astype(BF16)
    first_all = lax.all_gather(first_low, "seq", axis=0, tiled=True)
    qkv = jnp.dot(first_all, qkv_own, preferred_element_type=F32).astype(BF16)
    attended, lse = attention_forward(qkv, doc_ends, lists, admits, cols)
    attended_low = all_to_all(attended.reshape(seq_count, local_rows, cols))
    attended_low = attended_low.transpose(1, 0, 2).reshape(local_rows, width)
    hidden = rows_in + jnp.dot(attended_low, out_full, preferred_element_type=F32)
    normed_two, inverse_two = norm_stats(hidden)
    second_low = (normed_two * second_gain + second_bias).astype(BF16)
    grad_low = grad_rows.astype(BF16)
    ffn = jnp.zeros((local_rows, width), F32)
    second_grad = jnp.zeros((local_rows, width), F32)
    activations, pre_grads, bias_sums = [], [], []
    for up_part, down_part, bias_part in zip(up_parts, down_parts, bias_parts):
        pre_act = dot_nt(second_low, up_part) + bias_part
        activated = jax.nn.gelu(pre_act, approximate=True).astype(BF16)
        activations.append(activated)
        ffn = ffn + jnp.dot(activated, down_part, preferred_element_type=F32)
        act_grad = dot_nt(grad_low, down_part)
        _, gelu_pull = jax.vjp(lambda inner: jax.nn.gelu(inner, approximate=True), pre_act)
        pre_grad = gelu_pull(act_grad)[0].astype(BF16)
        pre_grads.append(pre_grad)
        bias_sums.append(jnp.sum(pre_grad.astype(F32), axis=0))
        second_grad = second_grad + jnp.dot(pre_grad, up_part, preferred_element_type=F32)
    output_low = lax.optimization_barrier((hidden + ffn + down_bias).astype(BF16))
    layer_output = both_sequences(output_low[None])

    hidden_grad = grad_rows + norm_back(second_grad, normed_two, inverse_two, second_gain)
    hidden_low = hidden_grad.astype(BF16)
    attended_grad = dot_nt(hidden_low, out_full).astype(BF16)
    attended_grad = jnp.where(valid, attended_grad, jnp.zeros_like(attended_grad))
    grad_all = all_to_all(attended_grad.reshape(local_rows, seq_count, cols).transpose(1, 0, 2))
    grad_all = grad_all.reshape(rows_total, cols)
    down_grads = [dot_tn(activated, grad_low).astype(BF16) for activated in activations]
    up_grads = [dot_tn(pre_grad, second_low).astype(BF16) for pre_grad in pre_grads]
    down_grad = reduce_units(*down_grads)
    up_grad = reduce_units(*up_grads)
    out_sum = dot_tn(attended_low, hidden_low).astype(BF16)
    out_other = pick(out_sum, 1 - mp_index, 2)
    out_grad = reduce_units(
        pick(out_sum, mp_index, 2), pick(out_other, parity, 2), pick(out_other, 1 - parity, 2)
    )
    bias_other = jnp.where(
        parity == 0,
        jnp.concatenate([bias_sums[1], bias_sums[2]]),
        jnp.concatenate([bias_sums[2], bias_sums[1]]),
    )
    bias_all = jnp.where(
        mp_index == 0,
        jnp.concatenate([bias_sums[0], bias_other]),
        jnp.concatenate([bias_other, bias_sums[0]]),
    )
    early = lax.psum(
        jnp.concatenate(
            [
                jnp.sum(grad_rows, axis=0),
                jnp.sum(second_grad * normed_two, axis=0),
                jnp.sum(second_grad, axis=0),
                bias_all,
            ]
        ),
        ("seq", "batch", "mp"),
    )

    qkv_low_grad = attention_backward(
        qkv, attended, grad_all, lse, doc_ends, lists, admits, cols
    )
    first_part = dot_nt(qkv_low_grad, qkv_own).astype(BF16)
    first_grad = lax.psum_scatter(first_part, "seq", scatter_dimension=0, tiled=True).astype(F32)
    qkv_sum = dot_tn(first_all, qkv_low_grad).astype(BF16)
    qkv_sum = qkv_sum.reshape(seq_count, -1, 3 * cols).transpose(1, 0, 2)
    levels = batch_levels()
    for distance in levels:
        qkv_sum = halve(qkv_sum, distance)
    qkv_sum = narrow_add(qkv_sum, swap(qkv_sum, "mp"))
    qkv_sum = all_to_all(qkv_sum.transpose(1, 0, 2))
    qkv_sum = pick(qkv_sum, mp_index, 2)
    qkv_sum = qkv_sum.reshape(seq_count // 2, -1, 3, cols).transpose(1, 2, 0, 3)
    qkv_sum = qkv_sum.reshape(-1, 3, half_cols)
    for distance in reversed(levels):
        qkv_sum = unhalve(qkv_sum, distance)
    qkv_grad = qkv_sum.astype(F32)

    late = lax.psum(
        jnp.concatenate([jnp.sum(first_grad * normed_one, axis=0), jnp.sum(first_grad, axis=0)]),
        ("seq", "batch", "mp"),
    )
    input_low = hidden_grad + norm_back(first_grad, normed_one, inverse_one, first_gain)
    input_grad = both_sequences(lax.optimization_barrier(input_low.astype(BF16))[None])
    up_bias_grad = lax.dynamic_slice_in_dim(early, 3 * width + mp_index * units, units)
    return (
        layer_output,
        input_grad,
        late[:width],
        late[width:],
        qkv_grad,
        out_grad,
        early[width : 2 * width],
        early[2 * width : 3 * width],
        up_grad.T,
        up_bias_grad,
        down_grad,
        early[:width],
    )


MB = 2
NBLK = 64
LEN = 4096
HIGH = lax.Precision.HIGHEST


def segment_of(places, doc_ends):
    return jnp.sum((places[..., None] >= doc_ends).astype(jnp.int32), axis=-1)


def block_lists_by_index(blocks, randoms):
    leading = randoms.shape[:-1]
    globals_part = jnp.broadcast_to(jnp.arange(GLOB, dtype=jnp.int32), leading + (GLOB,))
    window_part = jnp.broadcast_to(
        blocks[:, None] + jnp.arange(WIN, dtype=jnp.int32) - WIN // 2, leading + (WIN,)
    )
    block_list = jnp.concatenate([globals_part, window_part, randoms], axis=-1)
    inside = (block_list >= 0) & (block_list < NBLK)
    same_entry = block_list[..., :, None] == block_list[..., None, :]
    order_ids = jnp.arange(LIST)
    earlier = order_ids[None, :] < order_ids[:, None]
    repeated = jnp.any(same_entry & earlier, axis=-1)
    return (block_list, inside & jnp.logical_not(repeated))


def fetch_rows(key_rows, values, wanted):
    batch_seqs, local_rows, head_cols = key_rows.shape
    total_rows = local_rows * lax.axis_size("seq")
    empty_rows = jnp.zeros((batch_seqs, wanted.shape[1], head_cols), jnp.bfloat16)
    initial = (empty_rows, empty_rows)
    empty_whole = jnp.zeros((batch_seqs, total_rows, head_cols), jnp.bfloat16)
    initial = initial + (empty_whole, empty_whole)
    shards_in = (
        lax.all_gather(key_rows, "seq", axis=1, tiled=True),
        lax.all_gather(values, "seq", axis=1, tiled=True),
    )
    piece_rows = shards_in[0].shape[1]
    inside = ((wanted >= 0) & (wanted < piece_rows))[..., None]
    take_index = jnp.clip(wanted, 0, piece_rows - 1)[..., None]
    picked = tuple(
        (
            jnp.where(inside, jnp.take_along_axis(source, take_index, axis=1), previous)
            for source, previous in zip(shards_in, initial[:2])
        )
    )
    placed = tuple((source for source in shards_in))
    return picked + placed


def scatter_rows(kv_source):
    return lax.psum_scatter(
        kv_source.astype(jnp.bfloat16), "seq", scatter_dimension=0, tiled=True
    ).astype(jnp.float32)


def global_partial(seq_item):
    query_rows, key_rows, value_rows, keep_mask = seq_item
    head_count = query_rows.shape[1] // HD
    query_heads = query_rows.reshape(query_rows.shape[0], head_count, HD)
    key_heads = key_rows.reshape(key_rows.shape[0], head_count, HD)
    value_heads = value_rows.astype(jnp.float32).reshape(value_rows.shape[0], head_count, HD)
    raw_scores = jnp.einsum(
        "qhd,khd->hqk", query_heads, key_heads, preferred_element_type=jnp.float32
    ) * HD ** (-0.5)
    masked = jnp.where(keep_mask[None], raw_scores, NEG)
    row_top = jnp.max(masked, axis=-1)
    weights = jnp.exp(masked - row_top[..., None]) * keep_mask[None].astype(jnp.float32)
    numer = jnp.einsum("hqk,khd->hqd", weights, value_heads, precision=HIGH)
    return (row_top, jnp.sum(weights, axis=-1), numer)


def global_back(seq_item):
    query_rows, key_rows, value_rows, keep_mask, row_top, row_total, glob_out, glob_grad = seq_item
    row_count, head_cols = query_rows.shape
    head_count = head_cols // HD
    query_heads = query_rows.reshape(row_count, head_count, HD)
    key_heads = key_rows.reshape(key_rows.shape[0], head_count, HD)
    value_heads = value_rows.astype(jnp.float32).reshape(value_rows.shape[0], head_count, HD)
    raw_scores = jnp.einsum(
        "qhd,khd->hqk", query_heads, key_heads, preferred_element_type=jnp.float32
    ) * HD ** (-0.5)
    masked = jnp.where(keep_mask[None], raw_scores, NEG)
    probs_glob = (
        jnp.exp(masked - row_top[..., None])
        * keep_mask[None].astype(jnp.float32)
        / row_total[..., None]
    )
    grad_heads = glob_grad.astype(jnp.float32).reshape(row_count, head_count, HD)
    prob_grad = jnp.einsum("qhd,khd->hqk", grad_heads, value_heads, precision=HIGH)
    delta = jnp.einsum("qhd,hqd->hq", grad_heads, glob_out, precision=HIGH)
    score_grad = (probs_glob * (prob_grad - delta[..., None])).astype(jnp.bfloat16)
    query_grad = jnp.einsum(
        "hqk,khd->qhd", score_grad, key_heads, preferred_element_type=jnp.float32
    ) * HD ** (-0.5)
    key_grad = jnp.einsum(
        "hqk,qhd->khd", score_grad, query_heads, preferred_element_type=jnp.float32
    ) * HD ** (-0.5)
    value_grad = jnp.einsum("hqk,qhd->khd", probs_glob, grad_heads, precision=HIGH)
    return (
        query_grad.reshape(row_count, head_cols),
        key_grad.reshape(-1, head_cols),
        value_grad.reshape(-1, head_cols),
    )


def local_by_blocks(
    layer_input,
    lengths,
    random_blocks,
    first_gain,
    first_bias,
    qkv_weight,
    out_weight,
    second_gain,
    second_bias,
    up_weight,
    up_bias,
    down_weight,
    down_bias,
    cotangent,
):
    seq_index = lax.axis_index("seq")
    local_seqs, local_rows, model_width = layer_input.shape
    blocks_dev = local_rows // BLOCK
    head_cols = qkv_weight.shape[2]
    head_count = head_cols // HD
    unit_cols = up_weight.shape[1]
    score_scale = HD ** (-0.5)
    glob_rows = GLOB * BLOCK
    batch_seqs = local_seqs // MB
    picked_rows = blocks_dev * LIST * BLOCK
    qkv_flat = qkv_weight.reshape(model_width, 3 * head_cols)
    doc_ends = jnp.cumsum(lengths, axis=1)
    places = seq_index * local_rows + jnp.arange(local_rows, dtype=jnp.int32)
    seg_local = segment_of(places[None, :], doc_ends[:, None, :])
    valid_rows = (places[None, :] < doc_ends[:, -1:]).astype(jnp.float32)
    glob_flag = (places < glob_rows)[None, :, None]
    query_blocks = seq_index * blocks_dev + jnp.arange(blocks_dev, dtype=jnp.int32)
    block_list, admitted = block_lists_by_index(query_blocks, random_blocks)
    key_places = block_list[..., None] * BLOCK + jnp.arange(BLOCK, dtype=jnp.int32)
    key_segs = segment_of(key_places, doc_ends[:, None, None, None, :]).reshape(
        local_seqs, blocks_dev, LIST * BLOCK
    )
    admit_keys = jnp.broadcast_to(admitted[..., None], key_places.shape).reshape(
        local_seqs, blocks_dev, LIST * BLOCK
    )
    query_segs = seg_local.reshape(local_seqs, blocks_dev, BLOCK)
    list_mask = admit_keys[:, :, None, :] & (query_segs[..., None] == key_segs[:, :, None, :])
    wanted_all = jnp.clip(key_places, 0, LEN - 1).reshape(local_seqs, picked_rows)
    glob_segs = segment_of(jnp.arange(glob_rows, dtype=jnp.int32)[None, :], doc_ends[:, None, :])
    qkv_total = jnp.zeros((model_width, 3 * head_cols), jnp.float32)
    out_total = jnp.zeros(out_weight.shape, jnp.float32)
    up_total = jnp.zeros(up_weight.shape, jnp.float32)
    down_total = jnp.zeros(down_weight.shape, jnp.float32)
    gain_one_total = jnp.zeros((model_width,), jnp.float32)
    bias_one_total = jnp.zeros((model_width,), jnp.float32)
    gain_two_total = jnp.zeros((model_width,), jnp.float32)
    bias_two_total = jnp.zeros((model_width,), jnp.float32)
    up_bias_total = jnp.zeros((unit_cols,), jnp.float32)
    down_bias_total = jnp.zeros((model_width,), jnp.float32)
    outputs_all = []
    input_grads = []
    for micro_index in range(MB):
        first_seq = micro_index * batch_seqs
        last_seq = first_seq + batch_seqs
        rows_in = layer_input[first_seq:last_seq]
        ends_now = doc_ends[first_seq:last_seq]
        valid_now = valid_rows[first_seq:last_seq]
        mask_now = list_mask[first_seq:last_seq]
        wanted = wanted_all[first_seq:last_seq]
        glob_segs_now = glob_segs[first_seq:last_seq]
        normed_one, inverse_one = norm_stats(rows_in)
        first_low = (
            (normed_one * first_gain + first_bias).astype(jnp.bfloat16).reshape(-1, model_width)
        )
        qkv_rows = (
            jnp.dot(first_low, qkv_flat, preferred_element_type=jnp.float32)
            .astype(jnp.bfloat16)
            .reshape(batch_seqs, local_rows, 3, head_cols)
        )
        queries = qkv_rows[:, :, 0]
        key_rows = qkv_rows[:, :, 1]
        values = qkv_rows[:, :, 2]
        glob_queries_own = queries[:, :glob_rows]
        picked_keys, picked_values, whole_keys, whole_values = fetch_rows(key_rows, values, wanted)
        glob_queries = glob_queries_own
        seg_whole = segment_of(jnp.arange(LEN, dtype=jnp.int32)[None, :], ends_now[:, None, :])
        glob_mask = glob_segs_now[:, :, None] == seg_whole[:, None, :]

        def global_here():
            return lax.map(global_partial, (glob_queries, whole_keys, whole_values, glob_mask))

        def global_skip():
            return (
                jnp.zeros((batch_seqs, head_count, glob_rows), jnp.float32),
                jnp.ones((batch_seqs, head_count, glob_rows), jnp.float32),
                jnp.zeros((batch_seqs, head_count, glob_rows, HD), jnp.float32),
            )

        glob_top, glob_total, glob_numer = lax.cond(seq_index == 0, global_here, global_skip)
        glob_out = glob_numer / glob_total[..., None]
        query_split = queries.reshape(batch_seqs, blocks_dev, BLOCK, head_count, HD)
        key_split = picked_keys.reshape(batch_seqs, blocks_dev, LIST * BLOCK, head_count, HD)
        value_split = picked_values.reshape(batch_seqs, blocks_dev, LIST * BLOCK, head_count, HD)
        raw_scores = (
            jnp.einsum(
                "sbqhd,sbkhd->sbhqk", query_split, key_split, preferred_element_type=jnp.float32
            )
            * score_scale
        )
        keep_now = mask_now[:, :, None]
        masked = jnp.where(keep_now, raw_scores, NEG)
        row_top = jnp.max(masked, axis=-1, keepdims=True)
        weights = jnp.exp(masked - row_top) * keep_now.astype(jnp.float32)
        row_total = jnp.sum(weights, axis=-1, keepdims=True)
        probs_list = weights / row_total
        probs_low = probs_list.astype(jnp.bfloat16)
        listed = jnp.einsum(
            "sbhqk,sbkhd->sbqhd", probs_low, value_split, preferred_element_type=jnp.float32
        ).reshape(batch_seqs, local_rows, head_cols)
        glob_rows_out = jnp.transpose(glob_out, (0, 2, 1, 3)).reshape(
            batch_seqs, glob_rows, head_cols
        )
        glob_full = jnp.pad(glob_rows_out, ((0, 0), (0, local_rows - glob_rows), (0, 0)))
        attended = jnp.where(glob_flag, glob_full, listed) * valid_now[..., None]
        attended_low = attended.astype(jnp.bfloat16).reshape(-1, head_cols)
        branch = lax.psum(
            jnp.dot(attended_low, out_weight, preferred_element_type=jnp.float32).astype(
                jnp.bfloat16
            ),
            "mp",
        ).astype(jnp.float32)
        hidden = rows_in + branch.reshape(rows_in.shape)
        normed_two, inverse_two = norm_stats(hidden)
        second_low = (
            (normed_two * second_gain + second_bias).astype(jnp.bfloat16).reshape(-1, model_width)
        )
        pre_act = jnp.dot(second_low, up_weight, preferred_element_type=jnp.float32) + up_bias
        activated = jax.nn.gelu(pre_act, approximate=True).astype(jnp.bfloat16)
        ffn_branch = lax.psum(
            jnp.dot(activated, down_weight, preferred_element_type=jnp.float32).astype(
                jnp.bfloat16
            ),
            "mp",
        ).astype(jnp.float32)
        outputs_all.append(hidden + ffn_branch.reshape(rows_in.shape) + down_bias)
        grad_rows = cotangent[first_seq:last_seq].reshape(-1, model_width)
        down_bias_total = down_bias_total + jnp.sum(grad_rows, axis=0)
        grad_low = grad_rows.astype(jnp.bfloat16)
        down_total = down_total + jnp.einsum(
            "rf,rd->fd", activated, grad_low, preferred_element_type=jnp.float32
        )
        act_grad = jnp.einsum(
            "rd,fd->rf", grad_low, down_weight, preferred_element_type=jnp.float32
        )
        _, gelu_pull = jax.vjp(lambda inner: jax.nn.gelu(inner, approximate=True), pre_act)
        pre_grad = gelu_pull(act_grad)[0].astype(jnp.bfloat16)
        up_bias_total = up_bias_total + jnp.sum(pre_grad.astype(jnp.float32), axis=0)
        up_total = up_total + jnp.einsum(
            "rd,rf->df", second_low, pre_grad, preferred_element_type=jnp.float32
        )
        second_grad = (
            lax.psum(
                jnp.einsum(
                    "rf,df->rd", pre_grad, up_weight, preferred_element_type=jnp.float32
                ).astype(jnp.bfloat16),
                "mp",
            )
            .astype(jnp.float32)
            .reshape(rows_in.shape)
        )
        gain_two_total = gain_two_total + jnp.sum(second_grad * normed_two, axis=(0, 1))
        bias_two_total = bias_two_total + jnp.sum(second_grad, axis=(0, 1))
        hidden_grad = grad_rows.reshape(rows_in.shape) + norm_back(
            second_grad, normed_two, inverse_two, second_gain
        )
        hidden_low = hidden_grad.astype(jnp.bfloat16).reshape(-1, model_width)
        out_total = out_total + jnp.einsum(
            "rc,rd->cd", attended_low, hidden_low, preferred_element_type=jnp.float32
        )
        attended_grad = jnp.einsum(
            "rd,cd->rc", hidden_low, out_weight, preferred_element_type=jnp.float32
        ).astype(jnp.bfloat16).reshape(batch_seqs, local_rows, head_cols) * valid_now[
            ..., None
        ].astype(
            jnp.bfloat16
        )
        list_grad = jnp.where(glob_flag, jnp.zeros_like(attended_grad), attended_grad).reshape(
            batch_seqs, blocks_dev, BLOCK, head_count, HD
        )
        prob_grad = jnp.einsum(
            "sbqhd,sbkhd->sbhqk", list_grad, value_split, preferred_element_type=jnp.float32
        )
        delta = jnp.sum(probs_list * prob_grad, axis=-1, keepdims=True)
        score_grad = (probs_list * (prob_grad - delta)).astype(jnp.bfloat16)
        query_grad = (
            jnp.einsum(
                "sbhqk,sbkhd->sbqhd", score_grad, key_split, preferred_element_type=jnp.float32
            )
            * score_scale
        ).reshape(batch_seqs, local_rows, head_cols)
        key_picked_grad = (
            jnp.einsum(
                "sbhqk,sbqhd->sbkhd", score_grad, query_split, preferred_element_type=jnp.float32
            )
            * score_scale
        )
        value_picked_grad = jnp.einsum(
            "sbhqk,sbqhd->sbkhd", probs_low, list_grad, preferred_element_type=jnp.float32
        )
        picked_grads = jnp.concatenate(
            [
                key_picked_grad.reshape(batch_seqs, picked_rows, head_cols),
                value_picked_grad.reshape(batch_seqs, picked_rows, head_cols),
            ],
            axis=-1,
        )
        seg_ids = wanted * batch_seqs + jnp.arange(batch_seqs, dtype=jnp.int32)[:, None]
        kv_term = jax.ops.segment_sum(
            picked_grads.reshape(batch_seqs * picked_rows, 2 * head_cols),
            seg_ids.reshape(-1),
            num_segments=LEN * batch_seqs,
        ).reshape(LEN, batch_seqs, 2 * head_cols)
        glob_grad_own = attended_grad[:, :glob_rows]

        def back_here():
            return lax.map(
                global_back,
                (
                    glob_queries,
                    whole_keys,
                    whole_values,
                    glob_mask,
                    glob_top,
                    glob_total,
                    glob_out,
                    glob_grad_own,
                ),
            )

        def back_skip():
            return (
                jnp.zeros((batch_seqs, glob_rows, head_cols), jnp.float32),
                jnp.zeros((batch_seqs, LEN, head_cols), jnp.float32),
                jnp.zeros((batch_seqs, LEN, head_cols), jnp.float32),
            )

        glob_query_grad, whole_key_grad, whole_value_grad = lax.cond(
            seq_index == 0, back_here, back_skip
        )
        glob_dense = jnp.transpose(
            jnp.concatenate([whole_key_grad, whole_value_grad], axis=-1), (1, 0, 2)
        )
        kv_source = kv_term + glob_dense
        kv_grad = jnp.transpose(scatter_rows(kv_source), (1, 0, 2))
        glob_query_full = jnp.pad(glob_query_grad, ((0, 0), (0, local_rows - glob_rows), (0, 0)))
        query_total = query_grad + jnp.where(glob_flag, glob_query_full, 0.0)
        qkv_low_grad = (
            jnp.stack([query_total, kv_grad[..., :head_cols], kv_grad[..., head_cols:]], axis=2)
            .astype(jnp.bfloat16)
            .reshape(-1, 3 * head_cols)
        )
        qkv_total = qkv_total + jnp.einsum(
            "rd,rc->dc", first_low, qkv_low_grad, preferred_element_type=jnp.float32
        )
        first_grad = (
            lax.psum(
                jnp.einsum(
                    "rc,dc->rd", qkv_low_grad, qkv_flat, preferred_element_type=jnp.float32
                ).astype(jnp.bfloat16),
                "mp",
            )
            .astype(jnp.float32)
            .reshape(rows_in.shape)
        )
        gain_one_total = gain_one_total + jnp.sum(first_grad * normed_one, axis=(0, 1))
        bias_one_total = bias_one_total + jnp.sum(first_grad, axis=(0, 1))
        input_grads.append(hidden_grad + norm_back(first_grad, normed_one, inverse_one, first_gain))
    matrix_grads = (
        lax.psum_scatter(
            qkv_total.reshape(model_width, 3, head_cols).astype(jnp.bfloat16),
            "seq",
            scatter_dimension=0,
            tiled=True,
        ).astype(jnp.float32),
        lax.psum_scatter(
            out_total.astype(jnp.bfloat16), "seq", scatter_dimension=1, tiled=True
        ).astype(jnp.float32),
        lax.psum_scatter(
            up_total.astype(jnp.bfloat16), "seq", scatter_dimension=0, tiled=True
        ).astype(jnp.float32),
        lax.psum_scatter(
            down_total.astype(jnp.bfloat16), "seq", scatter_dimension=1, tiled=True
        ).astype(jnp.float32),
    )
    matrix_grads = (
        lax.psum(matrix_grads[0].astype(jnp.bfloat16), "batch").astype(jnp.float32),
        lax.psum(matrix_grads[1].astype(jnp.bfloat16), "batch").astype(jnp.float32),
        lax.psum(matrix_grads[2].astype(jnp.bfloat16), "batch").astype(jnp.float32),
        lax.psum(matrix_grads[3].astype(jnp.bfloat16), "batch").astype(jnp.float32),
    )
    vector_grads = lax.psum(
        (
            gain_one_total,
            bias_one_total,
            gain_two_total,
            bias_two_total,
            up_bias_total,
            down_bias_total,
        ),
        ("seq", "batch"),
    )
    return (
        jnp.concatenate(outputs_all, axis=0),
        jnp.concatenate(input_grads, axis=0),
        vector_grads[0],
        vector_grads[1],
        matrix_grads[0],
        matrix_grads[1],
        vector_grads[2],
        vector_grads[3],
        matrix_grads[2],
        vector_grads[4],
        matrix_grads[3],
        vector_grads[5],
    )


def solution(mesh):
    placed = (
        P("batch", "seq", None),
        P("batch", None),
        P("batch", "seq", None),
        P(),
        P(),
        P(None, None, "mp"),
        P("mp", None),
        P(),
        P(),
        P(None, "mp"),
        P("mp"),
        P("mp", None),
        P(),
        P("batch", "seq", None),
    )
    by_heads = (1024 // mesh.shape["seq"]) % 128 == 0
    return jax.shard_map(
        local if by_heads else local_by_blocks,
        mesh=mesh,
        in_specs=placed,
        out_specs=(
            P("batch", "seq", None),
            P("batch", "seq", None),
            P(),
            P(),
            P("seq", None, "mp"),
            P("mp", "seq"),
            P(),
            P(),
            P("seq", "mp"),
            P("mp"),
            P("mp", "seq"),
            P(),
        ),
        check_vma=False,
    )
```

```python
import functools

import jax
import jax.numpy as jnp
from jax import lax
from jax.experimental import pallas as pl
from jax.experimental.pallas import tpu as pltpu
from jax.sharding import PartitionSpec as P

BLOCK = 64
GLOB = 2
WIN = 3
HD = 64
LIST = 8

NEG = -1e30
EPS = 1e-05
F32 = jnp.float32
BF16 = jnp.bfloat16
VMEM_LIMIT = 60 * 1024 * 1024


def norm_stats(rows):
    centre = rows - jnp.mean(rows, axis=-1, keepdims=True)
    spread = jnp.mean(centre * centre, axis=-1, keepdims=True)
    inverse = lax.rsqrt(spread + EPS)
    return (centre * inverse, inverse)


def norm_back(grad_out, normed, inverse, gain):
    scaled = grad_out * gain
    return inverse * (
        scaled
        - jnp.mean(scaled, axis=-1, keepdims=True)
        - normed * jnp.mean(scaled * normed, axis=-1, keepdims=True)
    )


def block_lists(blocks, randoms, block_count):
    leading = randoms.shape[:-1]
    globals_part = jnp.broadcast_to(jnp.arange(GLOB, dtype=jnp.int32), leading + (GLOB,))
    window_part = jnp.broadcast_to(
        blocks[:, None] + jnp.arange(WIN, dtype=jnp.int32) - WIN // 2, leading + (WIN,)
    )
    block_list = jnp.concatenate([globals_part, window_part, randoms], axis=-1)
    inside = (block_list >= 0) & (block_list < block_count)
    same_entry = block_list[..., :, None] == block_list[..., None, :]
    order_ids = jnp.arange(LIST)
    earlier = order_ids[None, :] < order_ids[:, None]
    repeated = jnp.any(same_entry & earlier, axis=-1)
    admitted = inside & jnp.logical_not(repeated)
    return (jnp.clip(block_list, 0, block_count - 1), admitted.astype(jnp.int32))


def segment_at(places, ends_ref):
    total = jnp.zeros(places.shape, jnp.int32)
    for doc in range(ends_ref.shape[0]):
        total = total + (places >= ends_ref[doc]).astype(jnp.int32)
    return total


def head_spread(rows, heads):
    lane_head = lax.broadcasted_iota(jnp.int32, (1, rows.shape[1]), 1) // HD
    return jnp.concatenate(
        [rows * (lane_head == head).astype(F32).astype(rows.dtype) for head in range(heads)], axis=0
    )


def head_fold(wide, heads):
    rows = wide.shape[0] // heads
    lane_head = lax.broadcasted_iota(jnp.int32, (rows, wide.shape[1]), 1) // HD
    folded = jnp.zeros((rows, wide.shape[1]), wide.dtype)
    for head in range(heads):
        folded = jnp.where(lane_head == head, wide[head * rows : (head + 1) * rows], folded)
    return folded


def block_at(block):
    return pl.ds(pl.multiple_of(block * BLOCK, BLOCK), BLOCK)


def fill_segments(token_segs, ends_ref):
    def fill(block, _):
        places = block * BLOCK + lax.broadcasted_iota(jnp.int32, (BLOCK, token_segs.shape[1]), 0)
        token_segs[block_at(block), :] = segment_at(places, ends_ref)
        return 0

    lax.fori_loop(0, token_segs.shape[0] // BLOCK, fill, 0)


def query_segments(block, heads, ends_ref):
    lanes = lax.broadcasted_iota(jnp.int32, (8, heads * BLOCK), 1)
    return segment_at(block * BLOCK + lanes % BLOCK, ends_ref)[0:1]


def key_segments(starts, keeps, ends_ref):
    lanes = lax.broadcasted_iota(jnp.int32, (8, 2 * BLOCK), 1)
    first = lanes < BLOCK
    pieces = []
    for entry in range(0, LIST, 2):
        places = lanes + jnp.where(
            first, starts[entry] * BLOCK, (starts[entry + 1] - 1) * BLOCK
        )
        keep = jnp.where(first, keeps[entry], keeps[entry + 1]) > 0
        pieces.append(jnp.where(keep, segment_at(places, ends_ref), -1))
    return jnp.concatenate(pieces, axis=1)[0:1]


def gathered(ref, starts):
    return jnp.concatenate([ref[block_at(start), :] for start in starts], axis=0)


def block_parts(wide):
    return [wide[start : start + BLOCK] for start in range(0, wide.shape[0], BLOCK)]


def dot_nt(left, right):
    return lax.dot_general(left, right, (((1,), (1,)), ((), ())), preferred_element_type=F32)


def dot_tn(left, right):
    return lax.dot_general(left, right, (((0,), (0,)), ((), ())), preferred_element_type=F32)


def dot_nn(left, right):
    return lax.dot_general(left, right, (((1,), (0,)), ((), ())), preferred_element_type=F32)


def as_row(tall):
    count = tall.shape[0]
    row_ids = lax.broadcasted_iota(jnp.int32, (count, count), 0)
    lane_ids = lax.broadcasted_iota(jnp.int32, (count, count), 1)
    return jnp.sum(jnp.where(row_ids == lane_ids, tall, 0.0), axis=0, keepdims=True)


def together(running):
    while running:
        still = []
        for each in running:
            if next(each, 0) is None:
                still.append(each)
        running = still


def forward_kernel(
    heads, ends_ref, lists_ref, admit_ref, q_ref, k_ref, v_ref, o_ref, lse_ref, token_segs, held
):
    scale = HD ** (-0.5)
    rows_total = q_ref.shape[0]
    blocks = rows_total // BLOCK
    chunk = LIST * BLOCK
    fill_segments(token_segs, ends_ref)

    def store(block, wide, top, total):
        out = head_fold(wide, heads)
        places = block * BLOCK + lax.broadcasted_iota(jnp.int32, out.shape, 0)
        out = jnp.where(places < ends_ref[ends_ref.shape[0] - 1], out, 0.0)
        o_ref[block_at(block), :] = out.astype(BF16)
        lse_ref[block] = jnp.broadcast_to(as_row(top + jnp.log(total)), lse_ref.shape[1:])

    def kept(block, key_segs):
        own = token_segs[block_at(block), :]
        return jnp.concatenate([own] * (chunk // own.shape[1]), axis=1) == key_segs

    def global_blocks():
        query_wide = jnp.concatenate(
            [head_spread(q_ref[block_at(block), :] * scale, heads) for block in range(GLOB)], axis=0
        )
        wide_rows = GLOB * heads * BLOCK

        def score(part, top):
            here = pl.ds(pl.multiple_of(part * chunk, chunk), chunk)
            places = part * chunk + lax.broadcasted_iota(jnp.int32, (8, chunk), 1)
            key_segs = segment_at(places, ends_ref)[0:1]
            keeps = [kept(block, key_segs) for block in range(GLOB)]
            scores = dot_nt(query_wide, k_ref[here, :])
            tops = []
            for place, rows in enumerate(block_parts(scores)):
                rows = jnp.where(keeps[place // heads], rows, NEG)
                held[place * BLOCK : (place + 1) * BLOCK, here] = rows
                tops.append(jnp.max(rows, axis=1, keepdims=True))
            return jnp.maximum(top, jnp.concatenate(tops, axis=0))

        top = lax.fori_loop(0, rows_total // chunk, score, jnp.full((wide_rows, 1), NEG, F32))

        def gather(part, carried):
            total, wide = carried
            here = pl.ds(pl.multiple_of(part * chunk, chunk), chunk)
            totals, weights = [], []
            for place, part_top in enumerate(block_parts(top)):
                weight = jnp.exp(held[place * BLOCK : (place + 1) * BLOCK, here] - part_top)
                totals.append(jnp.sum(weight, axis=1, keepdims=True))
                weights.append(weight.astype(BF16))
            wide = wide + dot_nn(jnp.concatenate(weights, axis=0), v_ref[here, :])
            return total + jnp.concatenate(totals, axis=0), wide

        total, wide = lax.fori_loop(
            0,
            rows_total // chunk,
            gather,
            (jnp.zeros((wide_rows, 1), F32), jnp.zeros((wide_rows, q_ref.shape[1]), F32)),
        )
        wide = wide * (1.0 / total)
        for block in range(GLOB):
            own = slice(block * heads * BLOCK, (block + 1) * heads * BLOCK)
            store(block, wide[own], top[own], total[own])

    global_blocks()

    def listed_block(block):
        query_wide = head_spread(q_ref[block_at(block), :] * scale, heads)
        starts = [lists_ref[block * LIST + entry] for entry in range(LIST)]
        keeps = [admit_ref[block * LIST + entry] for entry in range(LIST)]
        keep = kept(block, key_segments(starts, keeps, ends_ref))
        scores = dot_nt(query_wide, gathered(k_ref, starts))
        yield
        tops, totals, probs = [], [], []
        for rows in block_parts(scores):
            rows = jnp.where(keep, rows, NEG)
            top = jnp.max(rows, axis=1, keepdims=True)
            weights = jnp.exp(rows - top)
            total = jnp.sum(weights, axis=1, keepdims=True)
            probs.append((weights * (1.0 / total)).astype(BF16))
            tops.append(top)
            totals.append(total)
            yield
        wide = dot_nn(jnp.concatenate(probs, axis=0), gathered(v_ref, starts))
        store(block, wide, jnp.concatenate(tops, axis=0), jnp.concatenate(totals, axis=0))

    def listed_group(group, _):
        together([listed_block(GLOB + 4 * group + place) for place in range(4)])
        return 0

    lax.fori_loop(0, (blocks - GLOB) // 4, listed_group, 0)
    together([listed_block(blocks - 1 - place) for place in range((blocks - GLOB) % 4)])


def backward_kernel(
    heads,
    ends_ref,
    lists_ref,
    admit_ref,
    q_ref,
    k_ref,
    v_ref,
    o_ref,
    do_ref,
    lse_ref,
    out_ref,
    token_segs,
    dk_ref,
    dv_ref,
    dq_ref,
):
    scale = HD ** (-0.5)
    rows_total, cols = q_ref.shape
    blocks = rows_total // BLOCK
    pair_rows = 2 * BLOCK
    fill_segments(token_segs, ends_ref)

    def prepare(pair, _):
        here = pl.ds(pl.multiple_of(pair * pair_rows, pair_rows), pair_rows)
        dk_ref[here, :] = jnp.zeros((pair_rows, cols), F32)
        dv_ref[here, :] = jnp.zeros((pair_rows, cols), F32)
        return 0

    lax.fori_loop(0, blocks // 2, prepare, 0)

    def query_side(block):
        query_wide = head_spread(q_ref[block_at(block), :] * scale, heads)
        grad_rows = do_ref[block_at(block), :]
        grad_wide = head_spread(grad_rows, heads)
        product = grad_rows.astype(F32) * o_ref[block_at(block), :].astype(F32)
        spread = head_spread(product.astype(BF16), heads)
        delta = dot_nt(jnp.ones((8, cols), BF16), spread)[0:1]
        seg_row = query_segments(block, heads, ends_ref)
        return query_wide, grad_wide, delta, lse_ref[block, 0:1], seg_row

    def unit(starts, keeps, query_wide, grad_wide, delta, lse, seg_row, finish_query):
        keys = gathered(k_ref, starts)
        scores = block_parts(dot_nt(keys, query_wide))
        prob_grads = block_parts(dot_nt(gathered(v_ref, starts), grad_wide))
        yield
        probs, score_grads = [], []
        for entry in range(LIST):
            wanted = seg_row if keeps is None else jnp.where(keeps[entry] > 0, seg_row, -1)
            own = token_segs[block_at(starts[entry]), :]
            keep = jnp.concatenate([own] * (seg_row.shape[1] // own.shape[1]), axis=1) == wanted
            prob = jnp.exp(jnp.where(keep, scores[entry], NEG) - lse)
            probs.append(prob.astype(BF16))
            score_grads.append((prob * (prob_grads[entry] - delta)).astype(BF16))
            if entry % 2:
                yield
        score_grad = jnp.concatenate(score_grads, axis=0)
        finish_query(dot_tn(score_grad, keys))
        dk = dot_nn(score_grad, query_wide)
        dv = dot_nn(jnp.concatenate(probs, axis=0), grad_wide)
        yield
        for entry in range(LIST):
            here = block_at(starts[entry])
            dk_ref[here, :] += dk[entry * BLOCK : (entry + 1) * BLOCK]
            dv_ref[here, :] += dv[entry * BLOCK : (entry + 1) * BLOCK]
        yield

    def store_query(block, wide):
        out_ref[block_at(block), 0:cols] = (head_fold(wide, heads) * scale).astype(BF16)

    def global_blocks():
        sides = [query_side(block) for block in range(GLOB)]
        side = [jnp.concatenate(both, axis=axis) for both, axis in zip(zip(*sides), (0, 0, 1, 1, 1))]
        dq_ref[...] = jnp.zeros_like(dq_ref)

        def part_of(part, _):
            def add_query(wide):
                dq_ref[...] += wide

            together([unit([part * LIST + entry for entry in range(LIST)], None, *side, add_query)])
            return 0

        lax.fori_loop(0, blocks // LIST, part_of, 0)
        for block in range(GLOB):
            store_query(block, dq_ref[block * heads * BLOCK : (block + 1) * heads * BLOCK])

    global_blocks()

    def listed_block(block):
        starts = [lists_ref[block * LIST + entry] for entry in range(LIST)]
        keeps = [admit_ref[block * LIST + entry] for entry in range(LIST)]
        return unit(starts, keeps, *query_side(block), functools.partial(store_query, block))

    def listed_group(group, _):
        together([listed_block(GLOB + 4 * group + place) for place in range(4)])
        return 0

    lax.fori_loop(0, (blocks - GLOB) // 4, listed_group, 0)
    together([listed_block(blocks - 1 - place) for place in range((blocks - GLOB) % 4)])

    def finish(block, _):
        here = block_at(block)
        out_ref[here, cols : 2 * cols] = dk_ref[here, :].astype(BF16)
        out_ref[here, 2 * cols : 3 * cols] = dv_ref[here, :].astype(BF16)
        return 0

    lax.fori_loop(0, blocks, finish, 0)


def smem():
    return pl.BlockSpec(memory_space=pltpu.SMEM)


def column(rows, cols, index):
    return pl.BlockSpec((rows, cols), lambda step: (0, index))


def attention_forward(qkv, doc_ends, lists, admits, cols):
    rows = qkv.shape[0]
    heads = cols // HD
    blocks = rows // BLOCK
    return pl.pallas_call(
        functools.partial(forward_kernel, heads),
        grid=(1,),
        in_specs=[smem(), smem(), smem()] + [column(rows, cols, part) for part in range(3)],
        out_specs=[
            column(rows, cols, 0),
            pl.BlockSpec((blocks, 8, heads * BLOCK), lambda step: (0, 0, 0)),
        ],
        out_shape=[
            jax.ShapeDtypeStruct((rows, cols), BF16),
            jax.ShapeDtypeStruct((blocks, 8, heads * BLOCK), F32),
        ],
        scratch_shapes=[
            pltpu.VMEM((rows, 2 * BLOCK), jnp.int32),
            pltpu.VMEM((GLOB * heads * BLOCK, rows), F32),
        ],
        compiler_params=pltpu.CompilerParams(vmem_limit_bytes=VMEM_LIMIT),
        cost_estimate=pl.CostEstimate(
            flops=rows * LIST * BLOCK * cols * heads * 5,
            bytes_accessed=8 * rows * cols,
            transcendentals=0,
        ),
    )(doc_ends, lists, admits, qkv, qkv, qkv)


def attention_backward(qkv, attended, attended_grad, lse, doc_ends, lists, admits, cols):
    rows = qkv.shape[0]
    heads = cols // HD
    blocks = rows // BLOCK
    return pl.pallas_call(
        functools.partial(backward_kernel, heads),
        grid=(1,),
        in_specs=[smem(), smem(), smem()]
        + [column(rows, cols, part) for part in range(3)]
        + [
            column(rows, cols, 0),
            column(rows, cols, 0),
            pl.BlockSpec((blocks, 8, heads * BLOCK), lambda step: (0, 0, 0)),
        ],
        out_specs=column(rows, 3 * cols, 0),
        out_shape=jax.ShapeDtypeStruct((rows, 3 * cols), BF16),
        scratch_shapes=[
            pltpu.VMEM((rows, 2 * BLOCK), jnp.int32),
            pltpu.VMEM((rows, cols), F32),
            pltpu.VMEM((rows, cols), F32),
            pltpu.VMEM((GLOB * heads * BLOCK, cols), F32),
        ],
        compiler_params=pltpu.CompilerParams(vmem_limit_bytes=VMEM_LIMIT),
        cost_estimate=pl.CostEstimate(
            flops=rows * LIST * BLOCK * cols * heads * 15,
            bytes_accessed=20 * rows * cols,
            transcendentals=0,
        ),
    )(doc_ends, lists, admits, qkv, qkv, qkv, attended, attended_grad, lse)


def row_stats(rows):
    mean = jnp.mean(rows, axis=-1, keepdims=True)
    centre = rows - mean
    spread = jnp.mean(centre * centre, axis=-1, keepdims=True)
    inverse = lax.rsqrt(spread + EPS)
    return centre * inverse, inverse


def gelu_pair(inner):
    root = 0.7978845608028654
    cube = 0.044715
    square = inner * inner
    bent = jnp.tanh(inner * (root + (root * cube) * square))
    half = 0.5 + 0.5 * bent
    value = inner * half
    return value, half + value * (1.0 - bent) * (root + (3.0 * root * cube) * square)


def token_kernel(
    tile,
    where_ref,
    att_ref,
    x_ref,
    grad_ref,
    out_own_ref,
    out_other_ref,
    up_own_ref,
    up_near_ref,
    up_far_ref,
    down_own_ref,
    down_near_ref,
    down_far_ref,
    up_bias_ref,
    gain_ref,
    bias_ref,
    down_bias_ref,
    act_in,
    pre_in,
    second_in,
    hidden_in,
    grad_in,
    output_ref,
    hidden_grad_ref,
    datt_ref,
    act_ref,
    pre_ref,
    second_ref,
    hidden_low_ref,
    grad_low_ref,
    sums_ref,
    unit_sums_ref,
    hidden,
    normed,
    inverse,
    ffn,
    second_grad,
    up_slots,
    down_slots,
    slot_sems,
):
    step = pl.program_id(0)
    steps = pl.num_programs(0)
    rows = hidden.shape[0]
    parts = att_ref.shape[0]
    tiles = [slice(start, start + tile) for start in range(0, rows, tile)]
    chunk = up_slots.shape[2]
    own_steps = up_own_ref.shape[1] // chunk
    near_steps = up_near_ref.shape[1] // chunk

    def copies(up_from, down_from, index, slot):
        here = pl.ds(pl.multiple_of(index * chunk, chunk), chunk)
        return (
            pltpu.make_async_copy(up_from.at[:, here], up_slots.at[slot], slot_sems.at[0, slot]),
            pltpu.make_async_copy(down_from.at[here], down_slots.at[slot], slot_sems.at[1, slot]),
        )

    def fetch(index):
        def begin(up_from, down_from, first):
            for copy in copies(up_from, down_from, index - first, index % 2):
                copy.start()

        @pl.when(index < own_steps)
        def _():
            begin(up_own_ref, down_own_ref, 0)

        @pl.when((index >= own_steps) & (index < own_steps + near_steps))
        def _():
            begin(up_near_ref, down_near_ref, own_steps)

        @pl.when(index >= own_steps + near_steps)
        def _():
            begin(up_far_ref, down_far_ref, own_steps + near_steps)

    half = parts // 2
    own_place = where_ref[0] * half
    other_place = (1 - where_ref[0]) * half
    out_parts = [(own_place + part, out_own_ref, part) for part in range(half)]
    out_parts += [(other_place + part, out_other_ref, part) for part in range(half)]

    @pl.when(step == 0)
    def _():
        fetch(step)

    @pl.when(step + 1 < steps)
    def _():
        fetch(step + 1)

    @pl.when(step == 0)
    def _():
        for here in tiles:
            total = x_ref[0, here, :]
            for part, weight_ref, index in out_parts:
                total = total + dot_nn(att_ref[part, here, :], weight_ref[index])
            hidden[here, :] = total
            unit, scale = row_stats(total)
            normed[here, :] = unit
            inverse[here, :] = jnp.broadcast_to(scale, (tile, inverse.shape[1]))
            second_ref[here, :] = (unit * gain_ref[...] + bias_ref[...]).astype(BF16)
            grad_low_ref[here, :] = grad_ref[0, here, :].astype(BF16)
            ffn[here, :] = jnp.zeros((tile, ffn.shape[1]), F32)
            second_grad[here, :] = jnp.zeros((tile, ffn.shape[1]), F32)

    slot = step % 2
    for copy in copies(up_own_ref, down_own_ref, 0, slot):
        copy.wait()
    up_ref = up_slots.at[slot]
    down_ref = down_slots.at[slot]
    unit_sum = jnp.zeros((1, chunk), F32)
    for here in tiles:
        inner = dot_nn(second_ref[here, :], up_ref[...]) + up_bias_ref[...]
        act_grad = dot_nt(grad_low_ref[here, :], down_ref[...])
        value, slope = gelu_pair(inner)
        value = value.astype(BF16)
        pre_grad = (act_grad * slope).astype(BF16)
        act_ref[here, :] = value
        pre_ref[here, :] = pre_grad
        unit_sum = unit_sum + jnp.sum(pre_grad.astype(F32), axis=0, keepdims=True)
        ffn[here, :] += dot_nn(value, down_ref[...])
        second_grad[here, :] += dot_nt(pre_grad, up_ref[...])
    unit_sums_ref[...] = jnp.broadcast_to(unit_sum, unit_sums_ref.shape)

    @pl.when(step == steps - 1)
    def _():
        width = ffn.shape[1]
        grad_sum = jnp.zeros((1, width), F32)
        gain_sum = jnp.zeros((1, width), F32)
        bias_sum = jnp.zeros((1, width), F32)
        for index, here in enumerate(tiles):
            output_ref[here, :] = (hidden[here, :] + ffn[here, :] + down_bias_ref[...]).astype(BF16)
            grad = grad_ref[0, here, :]
            back = second_grad[here, :]
            unit = normed[here, :]
            scaled = back * gain_ref[...]
            through = (
                scaled
                - jnp.mean(scaled, axis=-1, keepdims=True)
                - unit * jnp.mean(scaled * unit, axis=-1, keepdims=True)
            )
            total = grad + inverse[here, 0:1] * through
            hidden_grad_ref[here, :] = total
            low = total.astype(BF16)
            hidden_low_ref[here, :] = low
            grad_sum = grad_sum + jnp.sum(grad, axis=0, keepdims=True)
            gain_sum = gain_sum + jnp.sum(back * unit, axis=0, keepdims=True)
            bias_sum = bias_sum + jnp.sum(back, axis=0, keepdims=True)
            for part, weight_ref, piece in out_parts:
                spread = dot_nt(low, weight_ref[piece])
                places = where_ref[1] + index * tile + lax.broadcasted_iota(jnp.int32, spread.shape, 0)
                datt_ref[part, here, :] = jnp.where(places < where_ref[2], spread, 0.0).astype(BF16)
        sums_ref[...] = jnp.concatenate(
            [grad_sum, gain_sum, bias_sum, jnp.zeros((5, width), F32)], axis=0
        )


def token_part(
    index, where, att, layer_input, cotangent, outs, ups, downs, up_bias, gain, bias, down_bias, kept
):
    parts, rows, cols = att.shape
    width = layer_input.shape[2]
    units = up_bias.shape[1]
    chunk = min(512, units // 4)
    whole = 2 * rows
    shapes = [(whole, units), (whole, units), (whole, width), (whole, width), (whole, width)]
    if kept is None:
        kept = [jnp.zeros((8, 128), BF16)] * len(shapes)
        aliases = {}
    else:
        aliases = {16 + place: 3 + place for place in range(len(shapes))}
    half = lambda step, where_ref: (index, 0)
    fixed = lambda step, where_ref: (0, 0)
    any_spec = pl.BlockSpec(memory_space=pl.ANY)
    rows_spec = pl.BlockSpec((1, rows, width), lambda step, where_ref: (where_ref[0], index, 0))
    cube = lambda step, where_ref: (0, 0, 0)
    vector = pl.BlockSpec((1, width), fixed)
    return pl.pallas_call(
        functools.partial(token_kernel, min(256, rows)),
        grid_spec=pltpu.PrefetchScalarGridSpec(
            num_scalar_prefetch=1,
            grid=(units // chunk,),
            in_specs=[
                pl.BlockSpec((parts, rows, cols), cube),
                rows_spec,
                rows_spec,
                pl.BlockSpec((parts // 2, cols, width), cube),
                pl.BlockSpec((parts // 2, cols, width), cube),
            ]
            + [any_spec] * 6
            + [
                pl.BlockSpec((1, chunk), lambda step, where_ref: (0, step)),
                vector,
                vector,
                vector,
            ]
            + [any_spec] * len(shapes),
            out_specs=[
                pl.BlockSpec((rows, width), fixed),
                pl.BlockSpec((rows, width), fixed),
                pl.BlockSpec((parts, rows, cols), cube),
                pl.BlockSpec((rows, chunk), lambda step, where_ref: (index, step)),
                pl.BlockSpec((rows, chunk), lambda step, where_ref: (index, step)),
                pl.BlockSpec((rows, width), half),
                pl.BlockSpec((rows, width), half),
                pl.BlockSpec((rows, width), half),
                pl.BlockSpec((8, width), fixed),
                pl.BlockSpec((8, chunk), lambda step, where_ref: (0, step)),
            ],
            scratch_shapes=[
                pltpu.VMEM((rows, width), F32),
                pltpu.VMEM((rows, width), F32),
                pltpu.VMEM((rows, 128), F32),
                pltpu.VMEM((rows, width), F32),
                pltpu.VMEM((rows, width), F32),
                pltpu.VMEM((2, width, chunk), BF16),
                pltpu.VMEM((2, chunk, width), BF16),
                pltpu.SemaphoreType.DMA((2, 2)),
            ],
        ),
        out_shape=[
            jax.ShapeDtypeStruct((rows, width), BF16),
            jax.ShapeDtypeStruct((rows, width), F32),
            jax.ShapeDtypeStruct((parts, rows, cols), BF16),
        ]
        + [jax.ShapeDtypeStruct(shape, BF16) for shape in shapes]
        + [jax.ShapeDtypeStruct((8, width), F32), jax.ShapeDtypeStruct((8, units), F32)],
        input_output_aliases=aliases,
        compiler_params=pltpu.CompilerParams(vmem_limit_bytes=VMEM_LIMIT),
        cost_estimate=pl.CostEstimate(
            flops=rows * width * (8 * units + 4 * width),
            bytes_accessed=8 * units * width,
            transcendentals=0,
        ),
    )(where, att, layer_input, cotangent, *outs, *ups, *downs, up_bias, gain, bias, down_bias, *kept)


MESH = pl.DeviceIdType.MESH


def greet(me, count, partner=None):
    barrier = pltpu.get_barrier_semaphore()

    @pl.when(me > 0)
    def _():
        pl.semaphore_signal(barrier, inc=1, device_id={"seq": me - 1}, device_id_type=MESH)

    @pl.when(me < count - 1)
    def _():
        pl.semaphore_signal(barrier, inc=1, device_id={"seq": me + 1}, device_id_type=MESH)

    peers = jnp.minimum(me, 1) + jnp.minimum(count - 1 - me, 1)
    if partner is not None:
        pl.semaphore_signal(barrier, inc=1, device_id={"mp": partner}, device_id_type=MESH)
        peers = peers + 1
    pl.semaphore_wait(barrier, peers)


def gather_kernel(
    count,
    chunks,
    half_cols,
    x_ref,
    gain_ref,
    bias_ref,
    weight_ref,
    all_ref,
    qkv_ref,
    own_ref,
    rows_in,
    shards,
    results,
    weight,
    weight_sems,
    load_sems,
    send_sems,
    recv_sems,
    all_sems,
    qkv_sems,
):
    me = lax.axis_index("seq")
    place = lax.axis_index("mp")
    step = rows_in.shape[0] // chunks
    cols = weight.shape[1] // 3

    def at(chunk):
        return pl.ds(pl.multiple_of(chunk * step, step), step)

    def load(chunk):
        return pltpu.make_async_copy(
            x_ref.at[place, at(chunk)], rows_in.at[at(chunk)], load_sems.at[chunk]
        )

    def send(side, hop, chunk):
        shard = me - hop if side == 0 else me + hop
        target = me + 1 if side == 0 else me - 1
        return pltpu.make_async_remote_copy(
            src_ref=shards.at[shard, at(chunk)],
            dst_ref=shards.at[shard, at(chunk)],
            send_sem=send_sems.at[side, hop, chunk],
            recv_sem=recv_sems.at[side, hop, chunk],
            device_id={"seq": target},
            device_id_type=MESH,
        )

    def keep_all(shard, chunk):
        return pltpu.make_async_copy(
            shards.at[shard, at(chunk)], all_ref.at[shard, at(chunk)], all_sems.at[shard, chunk]
        )

    def keep_qkv(shard, chunk):
        return pltpu.make_async_copy(
            results.at[shard, at(chunk)], qkv_ref.at[shard, at(chunk)], qkv_sems.at[shard, chunk]
        )

    def over_chunks(body):
        def run(chunk, _):
            body(chunk)
            return 0

        lax.fori_loop(0, chunks, run, 0)

    over_chunks(lambda chunk: load(chunk).start())
    greet(me, count, 1 - place)

    here = (me * cols) // half_cols == place
    fetch = pltpu.make_async_remote_copy(
        src_ref=weight_ref,
        dst_ref=weight,
        send_sem=weight_sems.at[0],
        recv_sem=weight_sems.at[1],
        device_id={"mp": 1 - place},
        device_id_type=MESH,
    )
    copy = pltpu.make_async_copy(weight_ref, weight, weight_sems.at[2])

    @pl.when(here)
    def _():
        fetch.start()
        copy.start()

    def norm(chunk):
        load(chunk).wait()
        unit, _ = row_stats(rows_in[at(chunk), :])
        shards[me, at(chunk), :] = (unit * gain_ref[...] + bias_ref[...]).astype(BF16)
        keep_all(me, chunk).start()

        @pl.when(me < count - 1)
        def _():
            send(0, 0, chunk).start()

        @pl.when(me > 0)
        def _():
            send(1, 0, chunk).start()

    over_chunks(norm)

    def project(shard, chunk):
        rows = dot_nn(shards[shard, at(chunk), :], weight[...])
        results[shard, at(chunk), :] = rows.astype(BF16)
        keep_qkv(shard, chunk).start()

    def receive(hop, chunk):
        @pl.when(me >= hop + 1)
        def _():
            send(0, hop, chunk).wait_recv()
            if hop + 1 < count - 1:

                @pl.when(me < count - 1)
                def _():
                    send(0, hop + 1, chunk).start()

            keep_all(me - hop - 1, chunk).start()

        @pl.when(me + hop + 1 < count)
        def _():
            send(1, hop, chunk).wait_recv()
            if hop + 1 < count - 1:

                @pl.when(me > 0)
                def _():
                    send(1, hop + 1, chunk).start()

            keep_all(me + hop + 1, chunk).start()

    for hop in range(count - 2):
        over_chunks(functools.partial(receive, hop))

    @pl.when(here)
    def _():
        copy.wait()

    @pl.when(jnp.logical_not(here))
    def _():
        fetch.wait_recv()

    keep_weight = pltpu.make_async_copy(weight, own_ref, weight_sems.at[3])
    keep_weight.start()

    def last(chunk):
        project(me, chunk)
        for hop in range(count - 1):
            if hop == count - 2:
                receive(hop, chunk)

            @pl.when(me >= hop + 1)
            def _():
                project(me - hop - 1, chunk)

            @pl.when(me + hop + 1 < count)
            def _():
                project(me + hop + 1, chunk)

    over_chunks(last)

    def finish(chunk):
        for hop in range(count - 1):

            @pl.when((me >= hop) & (me < count - 1))
            def _():
                send(0, hop, chunk).wait_send()

            @pl.when((me + hop < count) & (me > 0))
            def _():
                send(1, hop, chunk).wait_send()

        for shard in range(count):
            keep_all(shard, chunk).wait()
            keep_qkv(shard, chunk).wait()

    over_chunks(finish)
    keep_weight.wait()

    @pl.when(here)
    def _():
        fetch.wait_send()


def gather_project(layer_input, gain, bias, weight, half_cols):
    count = lax.axis_size("seq")
    _, rows, width = layer_input.shape
    cols = weight.shape[1]
    chunks = max(1, rows // 128)
    any_spec = pl.BlockSpec(memory_space=pl.ANY)
    vmem = pl.BlockSpec(memory_space=pltpu.VMEM)
    dma = pltpu.SemaphoreType.DMA
    return pl.pallas_call(
        functools.partial(gather_kernel, count, chunks, half_cols),
        in_specs=[any_spec, vmem, vmem, vmem],
        out_specs=[any_spec, any_spec, any_spec],
        out_shape=[
            jax.ShapeDtypeStruct((count, rows, width), BF16),
            jax.ShapeDtypeStruct((count, rows, cols), BF16),
            jax.ShapeDtypeStruct((width, cols), BF16),
        ],
        scratch_shapes=[
            pltpu.VMEM((rows, width), F32),
            pltpu.VMEM((count, rows, width), BF16),
            pltpu.VMEM((count, rows, cols), BF16),
            pltpu.VMEM((width, cols), BF16),
            dma((4,)),
            dma((chunks,)),
            dma((2, count - 1, chunks)),
            dma((2, count - 1, chunks)),
            dma((count, chunks)),
            dma((count, chunks)),
        ],
        compiler_params=pltpu.CompilerParams(
            collective_id=0, has_side_effects=True, vmem_limit_bytes=VMEM_LIMIT
        ),
        cost_estimate=pl.CostEstimate(
            flops=150_000_000_000, bytes_accessed=1, transcendentals=0
        ),
    )(layer_input, gain, bias, weight)


def return_kernel(
    count,
    chunks,
    lag,
    offset,
    parts_ref,
    weight_ref,
    x_ref,
    hidden_grad_ref,
    gain_ref,
    input_ref,
    sums_ref,
    rows_in,
    sending,
    received,
    load_sem,
    send_sems,
    recv_sems,
):
    me = lax.axis_index("seq")
    place = lax.axis_index("mp")
    rows = hidden_grad_ref.shape[0]
    step = rows // chunks
    width = gain_ref.shape[1]
    steps = (count - 1) * chunks

    def at(chunk):
        return pl.ds(pl.multiple_of(chunk * step, step), step)

    load = pltpu.make_async_copy(x_ref.at[place, pl.ds(offset, rows)], rows_in, load_sem.at[0])
    load.start()
    greet(me, count)

    def send(side, message, chunk):
        return pltpu.make_async_remote_copy(
            src_ref=sending.at[side, message, at(chunk)],
            dst_ref=received.at[side, message, at(chunk)],
            send_sem=send_sems.at[side, message, chunk],
            recv_sem=recv_sems.at[side, message, chunk],
            device_id={"seq": me + 1 - 2 * side},
            device_id_type=MESH,
        )

    def flow(side, index):
        message = index // chunks
        chunk = index % chunks
        target = (1 - side) * (count - 1 - message) + side * message

        @pl.when((target - me) * (1 - 2 * side) > 0)
        def _():
            total = dot_nt(parts_ref[target, at(chunk), :], weight_ref[...])
            first = (1 - side) * me + side * (count - 1 - me)

            @pl.when(first == 0)
            def _():
                sending[side, message, at(chunk), :] = total.astype(BF16)

            @pl.when(first > 0)
            def _():
                send(side, message, chunk).wait_recv()
                come = received[side, message, at(chunk), :].astype(F32)
                sending[side, message, at(chunk), :] = (total + come).astype(BF16)

            send(side, message, chunk).start()

    near = me // (count // 2)

    def advance(index, _):
        @pl.when(index < steps)
        def _():
            flow(near, index)

        @pl.when(index >= lag)
        def _():
            flow(1 - near, index - lag)

        return 0

    lax.fori_loop(0, steps + lag, advance, 0)
    load.wait()

    def own(chunk, carried):
        here = at(chunk)
        rows_in_now = rows_in[here, :]
        total = dot_nt(parts_ref[me, here, :], weight_ref[...])

        @pl.when(me > 0)
        def _():
            send(0, count - 1 - me, chunk).wait_recv()

        @pl.when(me < count - 1)
        def _():
            send(1, me, chunk).wait_recv()

        left = received[0, jnp.minimum(count - 1 - me, count - 2), here, :].astype(F32)
        right = received[1, jnp.minimum(me, count - 2), here, :].astype(F32)
        total = total + jnp.where(me > 0, left, 0.0) + jnp.where(me < count - 1, right, 0.0)
        unit, inverse = row_stats(rows_in_now)
        scaled = total * gain_ref[...]
        through = (
            scaled
            - jnp.mean(scaled, axis=-1, keepdims=True)
            - unit * jnp.mean(scaled * unit, axis=-1, keepdims=True)
        )
        input_ref[here, :] = (hidden_grad_ref[here, :] + inverse * through).astype(BF16)
        gain_sum, bias_sum = carried
        return (
            gain_sum + jnp.sum(total * unit, axis=0, keepdims=True),
            bias_sum + jnp.sum(total, axis=0, keepdims=True),
        )

    zero = jnp.zeros((1, width), F32)
    gain_sum, bias_sum = lax.fori_loop(0, chunks, own, (zero, zero))
    sums_ref[...] = jnp.concatenate([gain_sum, bias_sum, jnp.zeros((6, width), F32)], axis=0)

    def finish(index, _):
        message = index // chunks
        chunk = index % chunks

        @pl.when(count - 1 - message > me)
        def _():
            send(0, message, chunk).wait_send()

        @pl.when(message < me)
        def _():
            send(1, message, chunk).wait_send()

        return 0

    lax.fori_loop(0, steps, finish, 0)


def return_part(index, parts, weight, layer_input, hidden_grad, gain):
    count, rows, cols = parts.shape
    rows = rows // 2
    width = weight.shape[0]
    chunks = max(1, rows // 128)
    any_spec = pl.BlockSpec(memory_space=pl.ANY)
    dma = pltpu.SemaphoreType.DMA
    fixed = lambda step: (0, 0)
    return pl.pallas_call(
        functools.partial(return_kernel, count, chunks, 2, index * rows),
        grid=(1,),
        in_specs=[
            pl.BlockSpec((count, rows, cols), lambda step: (0, index, 0)),
            pl.BlockSpec((width, cols), fixed),
            any_spec,
            pl.BlockSpec((rows, width), fixed),
            pl.BlockSpec((1, width), fixed),
        ],
        out_specs=[pl.BlockSpec((rows, width), fixed), pl.BlockSpec((8, width), fixed)],
        out_shape=[
            jax.ShapeDtypeStruct((rows, width), BF16),
            jax.ShapeDtypeStruct((8, width), F32),
        ],
        scratch_shapes=[
            pltpu.VMEM((rows, width), F32),
            pltpu.VMEM((2, count - 1, rows, width), BF16),
            pltpu.VMEM((2, count - 1, rows, width), BF16),
            dma((1,)),
            dma((2, count - 1, chunks)),
            dma((2, count - 1, chunks)),
        ],
        compiler_params=pltpu.CompilerParams(
            collective_id=1 + index, has_side_effects=True, vmem_limit_bytes=VMEM_LIMIT
        ),
        cost_estimate=pl.CostEstimate(flops=80_000_000_000, bytes_accessed=1, transcendentals=0),
    )(parts, weight, layer_input, hidden_grad, gain)


def swap(value, axis, distance=1):
    size = lax.axis_size(axis)
    return lax.ppermute(value, axis, [(j, j ^ distance) for j in range(size)])


def after(value, *earlier):
    return lax.optimization_barrier((value,) + earlier)[0]


def all_to_all(value):
    return lax.all_to_all(value, "seq", 0, 0, tiled=True)


def halves(value):
    return jnp.split(value, 2, axis=1)


def levels_of(axis):
    return [1 << level for level in range(lax.axis_size(axis).bit_length() - 1)]


def sum_everywhere(value):
    for axis in ("batch", "seq", "mp"):
        for distance in levels_of(axis):
            value = value + swap(value, axis, distance)
    return value


def gather_small(value):
    place = lax.axis_index("seq")
    count = lax.axis_size("seq")
    parts = [value] + [swap(value, "seq", distance) for distance in range(1, count)]
    stacked = jnp.stack(parts)
    order = jnp.arange(count, dtype=jnp.int32) ^ place
    return jnp.take(stacked, order, axis=0).reshape((-1,) + value.shape[1:])


def pick(value, index, count, axis=0):
    size = value.shape[axis] // count
    return lax.dynamic_slice_in_dim(value, index * size, size, axis)


def fetch_near(weight, axis):
    return swap(pick(weight, lax.axis_index("batch") % 2, 2, axis), "mp")


def narrow_add(mine, received):
    return (mine.astype(F32) + received.astype(F32)).astype(BF16)


def halve(value, distance, axis):
    side = (lax.axis_index("batch") // distance) % 2
    return narrow_add(
        pick(value, side, 2, axis), swap(pick(value, 1 - side, 2, axis), "batch", distance)
    )


def unhalve(value, distance, axis):
    side = (lax.axis_index("batch") // distance) % 2
    other = swap(value, "batch", distance)
    low = jnp.where(side == 0, value, other)
    high = jnp.where(side == 0, other, value)
    return jnp.concatenate([low, high], axis=axis)


def sum_cores(own, near, far, axis):
    return halve(own, 1, axis), narrow_add(near, swap(far, "batch"))


def sum_chips(own, near, axis):
    for distance in levels_of("batch")[1:]:
        own = halve(own, distance, axis)
        near = halve(near, distance, axis)
    return own, near


def scatter_rows_of(own, axis):
    return lax.psum_scatter(own, "seq", scatter_dimension=1 - axis, tiled=True)


def spread_batch(value, axis):
    for distance in reversed(levels_of("batch")):
        value = unhalve(value, distance, axis)
    return value.astype(F32)


def place_kernel(place_ref, own_first, own_second, other_first, other_second, out_ref):
    place = place_ref[0]

    @pl.when(pl.program_id(0) == 0)
    def _():
        out_ref[place] = own_first[...].astype(F32)
        out_ref[1 - place] = other_first[...].astype(F32)

    @pl.when(pl.program_id(0) == 1)
    def _():
        out_ref[place] = own_second[...].astype(F32)
        out_ref[1 - place] = other_second[...].astype(F32)


def both_sequences(own):
    other = [swap(part, "mp") for part in own]
    rows, width = own[0].shape
    step = min(256, rows)
    steps = rows // step
    first = pl.BlockSpec(
        (step, width), lambda half, index, place_ref: (index * (1 - half) + (steps - 1) * half, 0)
    )
    second = pl.BlockSpec((step, width), lambda half, index, place_ref: (index * half, 0))
    return pl.pallas_call(
        place_kernel,
        grid_spec=pltpu.PrefetchScalarGridSpec(
            num_scalar_prefetch=1,
            grid=(2, steps),
            in_specs=[first, second, first, second],
            out_specs=pl.BlockSpec(
                (2, step, width), lambda half, index, place_ref: (0, half * steps + index, 0)
            ),
        ),
        out_shape=jax.ShapeDtypeStruct((2, 2 * rows, width), F32),
    )(lax.axis_index("mp").astype(jnp.int32)[None], *own, *other)


def local(
    layer_input,
    lengths,
    random_blocks,
    first_gain,
    first_bias,
    qkv_weight,
    out_weight,
    second_gain,
    second_bias,
    up_weight,
    up_bias,
    down_weight,
    down_bias,
    cotangent,
):
    seq_count = lax.axis_size("seq")
    seq_index = lax.axis_index("seq")
    mp_index = lax.axis_index("mp")
    parity = lax.axis_index("batch") % 2
    _, local_rows, width = layer_input.shape
    rows_total = local_rows * seq_count
    blocks = rows_total // BLOCK
    half_cols = qkv_weight.shape[2]
    cols = width // seq_count
    units = up_weight.shape[1]

    doc_ends = jnp.cumsum(lax.dynamic_index_in_dim(lengths, mp_index, 0, keepdims=False))
    randoms = lax.dynamic_index_in_dim(random_blocks, mp_index, 0, keepdims=False)
    randoms = gather_small(randoms)
    lists, admits = block_lists(jnp.arange(blocks, dtype=jnp.int32), randoms, blocks)
    lists, admits = lists.reshape(-1), admits.reshape(-1)

    qkv_near = lax.dynamic_slice_in_dim(qkv_weight, (seq_index * cols) % half_cols, cols, 2)
    qkv_near = qkv_near.reshape(width, 3 * cols)
    up_near = fetch_near(up_weight, 1)
    bias_near = fetch_near(up_bias, 0)
    out_other = swap(out_weight, "mp")

    first_all, qkv, qkv_own = gather_project(
        layer_input, first_gain[None], first_bias[None], qkv_near, half_cols
    )
    first_all = first_all.reshape(rows_total, width)
    qkv, up_near, out_other, bias_near, lists, down_cut = lax.optimization_barrier(
        (qkv.reshape(rows_total, 3 * cols), up_near, out_other, bias_near, lists, down_weight)
    )
    up_far, bias_far = swap(up_near, "batch"), swap(bias_near, "batch")
    down_near = fetch_near(down_cut, 0)
    attended, lse = attention_forward(qkv, doc_ends, lists, admits, cols)
    attended, up_far, down_near, bias_far = lax.optimization_barrier(
        (attended, up_far, down_near, bias_far)
    )
    down_far = swap(down_near, "batch")
    bias_full = jnp.concatenate([up_bias, bias_near, bias_far])[None]
    half_rows = local_rows // 2
    attended_halves = [
        all_to_all(part) for part in halves(attended.reshape(seq_count, local_rows, cols))
    ]
    outs = [part.reshape(seq_count // 2, cols, width) for part in (out_weight, out_other)]
    kept, results = None, []
    for index, att in enumerate(attended_halves):
        where = jnp.stack(
            [mp_index, seq_index * local_rows + index * half_rows, doc_ends[-1]]
        ).astype(jnp.int32)
        result = token_part(
            index,
            where,
            att,
            layer_input,
            cotangent,
            outs,
            (up_weight, up_near, up_far),
            (down_weight, down_near, down_far),
            bias_full,
            second_gain[None],
            second_bias[None],
            down_bias[None],
            kept,
        )
        kept = result[3:8]
        results.append(result[:3] + result[8:])
    activated, pre_grad, second_low, hidden_low, grad_low = kept
    sums = results[0][3][:3] + results[1][3][:3]
    unit_sums = results[0][4][0] + results[1][4][0]
    bias_sums = [unit_sums[:units], unit_sums[units : units * 3 // 2], unit_sums[units * 3 // 2 :]]
    layer_output = both_sequences([result[0] for result in results])
    grad_all = jnp.concatenate([all_to_all(result[2]) for result in results], axis=1)
    grad_all = grad_all.reshape(rows_total, cols)

    down_sum = dot_tn(activated, grad_low).astype(BF16)
    up_sum = dot_tn(second_low, pre_grad).astype(BF16)
    attended_low = jnp.concatenate(attended_halves, axis=1)
    out_sum = jnp.einsum(
        "zrc,rd->zcd", attended_low, hidden_low, preferred_element_type=F32
    ).astype(BF16).reshape(width, width)
    cuts = [units, units * 3 // 2]
    down_sum = sum_cores(*jnp.split(down_sum, cuts, axis=0), 0)
    up_sum = sum_cores(*jnp.split(up_sum, cuts, axis=1), 1)
    out_theirs = pick(out_sum, 1 - mp_index, 2)
    out_sum = sum_cores(
        pick(out_sum, mp_index, 2), pick(out_theirs, parity, 2), pick(out_theirs, 1 - parity, 2), 0
    )
    bias_other = jnp.where(
        parity == 0,
        jnp.concatenate([bias_sums[1], bias_sums[2]]),
        jnp.concatenate([bias_sums[2], bias_sums[1]]),
    )
    bias_all = jnp.where(
        mp_index == 0,
        jnp.concatenate([bias_sums[0], bias_other]),
        jnp.concatenate([bias_other, bias_sums[0]]),
    )
    early = sum_everywhere(jnp.concatenate([sums.reshape(-1), bias_all]))
    grad_all, down_sum, up_sum, out_sum = lax.optimization_barrier(
        (grad_all, down_sum, up_sum, out_sum)
    )
    down_sum, up_sum, out_sum = sum_chips(*down_sum, 0), sum_chips(*up_sum, 1), sum_chips(*out_sum, 0)
    qkv_low_grad = attention_backward(
        qkv, attended, grad_all, lse, doc_ends, lists, admits, cols
    )
    qkv_sum = dot_tn(first_all, qkv_low_grad).astype(BF16)
    qkv_sum = qkv_sum.reshape(seq_count, -1, 3 * cols).transpose(1, 0, 2)
    levels = levels_of("batch")
    sums_now = [down_sum, up_sum, out_sum]
    qkv_low_grad, qkv_sum, sums_now = lax.optimization_barrier((qkv_low_grad, qkv_sum, sums_now))
    near_sums = [swap(near, "mp") for _, near in sums_now]
    qkv_part = halve(qkv_sum, levels[0], 0)
    parts = qkv_low_grad.reshape(seq_count, local_rows, 3 * cols)
    input_first, first_sums = return_part(
        0, parts, qkv_own, layer_input, results[0][1], first_gain[None]
    )
    input_first, near_sums, qkv_part = lax.optimization_barrier((input_first, near_sums, qkv_part))
    own_sums = [narrow_add(own, near) for (own, _), near in zip(sums_now, near_sums)]
    second_grad, input_first, own_sums = lax.optimization_barrier(
        (results[1][1], input_first, own_sums)
    )
    down_grad, up_grad, out_grad = [
        scatter_rows_of(own, axis) for own, axis in zip(own_sums, (0, 1, 0))
    ]
    for distance in levels[1:]:
        qkv_part = halve(qkv_part, distance, 0)
    input_second, second_sums = return_part(
        1, parts, qkv_own, layer_input, second_grad, first_gain[None]
    )
    input_second, qkv_part, down_grad, up_grad, out_grad = lax.optimization_barrier(
        (input_second, qkv_part, down_grad, up_grad, out_grad)
    )
    late = sum_everywhere((first_sums + second_sums)[:2])
    qkv_part = narrow_add(qkv_part, swap(qkv_part, "mp"))
    qkv_part = all_to_all(qkv_part.transpose(1, 0, 2))
    qkv_part = pick(qkv_part, mp_index, 2)
    qkv_part = qkv_part.reshape(seq_count // 2, -1, 3, cols).transpose(1, 2, 0, 3)
    qkv_grad = spread_batch(qkv_part.reshape(-1, 3, half_cols), 0)
    down_grad = spread_batch(down_grad, 0)
    up_grad = spread_batch(up_grad, 1)
    out_grad = spread_batch(out_grad, 0)
    input_grad = both_sequences([input_first, input_second])
    up_bias_grad = lax.dynamic_slice_in_dim(early, 3 * width + mp_index * units, units)
    return (
        layer_output,
        input_grad,
        late[0],
        late[1],
        qkv_grad,
        out_grad,
        early[width : 2 * width],
        early[2 * width : 3 * width],
        up_grad,
        up_bias_grad,
        down_grad,
        early[:width],
    )


MB = 2
NBLK = 64
LEN = 4096
HIGH = lax.Precision.HIGHEST


def segment_of(places, doc_ends):
    return jnp.sum((places[..., None] >= doc_ends).astype(jnp.int32), axis=-1)


def block_lists_by_index(blocks, randoms):
    leading = randoms.shape[:-1]
    globals_part = jnp.broadcast_to(jnp.arange(GLOB, dtype=jnp.int32), leading + (GLOB,))
    window_part = jnp.broadcast_to(
        blocks[:, None] + jnp.arange(WIN, dtype=jnp.int32) - WIN // 2, leading + (WIN,)
    )
    block_list = jnp.concatenate([globals_part, window_part, randoms], axis=-1)
    inside = (block_list >= 0) & (block_list < NBLK)
    same_entry = block_list[..., :, None] == block_list[..., None, :]
    order_ids = jnp.arange(LIST)
    earlier = order_ids[None, :] < order_ids[:, None]
    repeated = jnp.any(same_entry & earlier, axis=-1)
    return (block_list, inside & jnp.logical_not(repeated))


def fetch_rows(key_rows, values, wanted):
    batch_seqs, local_rows, head_cols = key_rows.shape
    total_rows = local_rows * lax.axis_size("seq")
    empty_rows = jnp.zeros((batch_seqs, wanted.shape[1], head_cols), jnp.bfloat16)
    initial = (empty_rows, empty_rows)
    empty_whole = jnp.zeros((batch_seqs, total_rows, head_cols), jnp.bfloat16)
    initial = initial + (empty_whole, empty_whole)
    shards_in = (
        lax.all_gather(key_rows, "seq", axis=1, tiled=True),
        lax.all_gather(values, "seq", axis=1, tiled=True),
    )
    piece_rows = shards_in[0].shape[1]
    inside = ((wanted >= 0) & (wanted < piece_rows))[..., None]
    take_index = jnp.clip(wanted, 0, piece_rows - 1)[..., None]
    picked = tuple(
        (
            jnp.where(inside, jnp.take_along_axis(source, take_index, axis=1), previous)
            for source, previous in zip(shards_in, initial[:2])
        )
    )
    placed = tuple((source for source in shards_in))
    return picked + placed


def scatter_rows(kv_source):
    return lax.psum_scatter(
        kv_source.astype(jnp.bfloat16), "seq", scatter_dimension=0, tiled=True
    ).astype(jnp.float32)


def global_partial(seq_item):
    query_rows, key_rows, value_rows, keep_mask = seq_item
    head_count = query_rows.shape[1] // HD
    query_heads = query_rows.reshape(query_rows.shape[0], head_count, HD)
    key_heads = key_rows.reshape(key_rows.shape[0], head_count, HD)
    value_heads = value_rows.astype(jnp.float32).reshape(value_rows.shape[0], head_count, HD)
    raw_scores = jnp.einsum(
        "qhd,khd->hqk", query_heads, key_heads, preferred_element_type=jnp.float32
    ) * HD ** (-0.5)
    masked = jnp.where(keep_mask[None], raw_scores, NEG)
    row_top = jnp.max(masked, axis=-1)
    weights = jnp.exp(masked - row_top[..., None]) * keep_mask[None].astype(jnp.float32)
    numer = jnp.einsum("hqk,khd->hqd", weights, value_heads, precision=HIGH)
    return (row_top, jnp.sum(weights, axis=-1), numer)


def global_back(seq_item):
    query_rows, key_rows, value_rows, keep_mask, row_top, row_total, glob_out, glob_grad = seq_item
    row_count, head_cols = query_rows.shape
    head_count = head_cols // HD
    query_heads = query_rows.reshape(row_count, head_count, HD)
    key_heads = key_rows.reshape(key_rows.shape[0], head_count, HD)
    value_heads = value_rows.astype(jnp.float32).reshape(value_rows.shape[0], head_count, HD)
    raw_scores = jnp.einsum(
        "qhd,khd->hqk", query_heads, key_heads, preferred_element_type=jnp.float32
    ) * HD ** (-0.5)
    masked = jnp.where(keep_mask[None], raw_scores, NEG)
    probs_glob = (
        jnp.exp(masked - row_top[..., None])
        * keep_mask[None].astype(jnp.float32)
        / row_total[..., None]
    )
    grad_heads = glob_grad.astype(jnp.float32).reshape(row_count, head_count, HD)
    prob_grad = jnp.einsum("qhd,khd->hqk", grad_heads, value_heads, precision=HIGH)
    delta = jnp.einsum("qhd,hqd->hq", grad_heads, glob_out, precision=HIGH)
    score_grad = (probs_glob * (prob_grad - delta[..., None])).astype(jnp.bfloat16)
    query_grad = jnp.einsum(
        "hqk,khd->qhd", score_grad, key_heads, preferred_element_type=jnp.float32
    ) * HD ** (-0.5)
    key_grad = jnp.einsum(
        "hqk,qhd->khd", score_grad, query_heads, preferred_element_type=jnp.float32
    ) * HD ** (-0.5)
    value_grad = jnp.einsum("hqk,qhd->khd", probs_glob, grad_heads, precision=HIGH)
    return (
        query_grad.reshape(row_count, head_cols),
        key_grad.reshape(-1, head_cols),
        value_grad.reshape(-1, head_cols),
    )


def local_by_blocks(
    layer_input,
    lengths,
    random_blocks,
    first_gain,
    first_bias,
    qkv_weight,
    out_weight,
    second_gain,
    second_bias,
    up_weight,
    up_bias,
    down_weight,
    down_bias,
    cotangent,
):
    seq_index = lax.axis_index("seq")
    local_seqs, local_rows, model_width = layer_input.shape
    blocks_dev = local_rows // BLOCK
    head_cols = qkv_weight.shape[2]
    head_count = head_cols // HD
    unit_cols = up_weight.shape[1]
    score_scale = HD ** (-0.5)
    glob_rows = GLOB * BLOCK
    batch_seqs = local_seqs // MB
    picked_rows = blocks_dev * LIST * BLOCK
    qkv_flat = qkv_weight.reshape(model_width, 3 * head_cols)
    doc_ends = jnp.cumsum(lengths, axis=1)
    places = seq_index * local_rows + jnp.arange(local_rows, dtype=jnp.int32)
    seg_local = segment_of(places[None, :], doc_ends[:, None, :])
    valid_rows = (places[None, :] < doc_ends[:, -1:]).astype(jnp.float32)
    glob_flag = (places < glob_rows)[None, :, None]
    query_blocks = seq_index * blocks_dev + jnp.arange(blocks_dev, dtype=jnp.int32)
    block_list, admitted = block_lists_by_index(query_blocks, random_blocks)
    key_places = block_list[..., None] * BLOCK + jnp.arange(BLOCK, dtype=jnp.int32)
    key_segs = segment_of(key_places, doc_ends[:, None, None, None, :]).reshape(
        local_seqs, blocks_dev, LIST * BLOCK
    )
    admit_keys = jnp.broadcast_to(admitted[..., None], key_places.shape).reshape(
        local_seqs, blocks_dev, LIST * BLOCK
    )
    query_segs = seg_local.reshape(local_seqs, blocks_dev, BLOCK)
    list_mask = admit_keys[:, :, None, :] & (query_segs[..., None] == key_segs[:, :, None, :])
    wanted_all = jnp.clip(key_places, 0, LEN - 1).reshape(local_seqs, picked_rows)
    glob_segs = segment_of(jnp.arange(glob_rows, dtype=jnp.int32)[None, :], doc_ends[:, None, :])
    qkv_total = jnp.zeros((model_width, 3 * head_cols), jnp.float32)
    out_total = jnp.zeros(out_weight.shape, jnp.float32)
    up_total = jnp.zeros(up_weight.shape, jnp.float32)
    down_total = jnp.zeros(down_weight.shape, jnp.float32)
    gain_one_total = jnp.zeros((model_width,), jnp.float32)
    bias_one_total = jnp.zeros((model_width,), jnp.float32)
    gain_two_total = jnp.zeros((model_width,), jnp.float32)
    bias_two_total = jnp.zeros((model_width,), jnp.float32)
    up_bias_total = jnp.zeros((unit_cols,), jnp.float32)
    down_bias_total = jnp.zeros((model_width,), jnp.float32)
    outputs_all = []
    input_grads = []
    for micro_index in range(MB):
        first_seq = micro_index * batch_seqs
        last_seq = first_seq + batch_seqs
        rows_in = layer_input[first_seq:last_seq]
        ends_now = doc_ends[first_seq:last_seq]
        valid_now = valid_rows[first_seq:last_seq]
        mask_now = list_mask[first_seq:last_seq]
        wanted = wanted_all[first_seq:last_seq]
        glob_segs_now = glob_segs[first_seq:last_seq]
        normed_one, inverse_one = norm_stats(rows_in)
        first_low = (
            (normed_one * first_gain + first_bias).astype(jnp.bfloat16).reshape(-1, model_width)
        )
        qkv_rows = (
            jnp.dot(first_low, qkv_flat, preferred_element_type=jnp.float32)
            .astype(jnp.bfloat16)
            .reshape(batch_seqs, local_rows, 3, head_cols)
        )
        queries = qkv_rows[:, :, 0]
        key_rows = qkv_rows[:, :, 1]
        values = qkv_rows[:, :, 2]
        glob_queries_own = queries[:, :glob_rows]
        picked_keys, picked_values, whole_keys, whole_values = fetch_rows(key_rows, values, wanted)
        glob_queries = glob_queries_own
        seg_whole = segment_of(jnp.arange(LEN, dtype=jnp.int32)[None, :], ends_now[:, None, :])
        glob_mask = glob_segs_now[:, :, None] == seg_whole[:, None, :]

        def global_here():
            return lax.map(global_partial, (glob_queries, whole_keys, whole_values, glob_mask))

        def global_skip():
            return (
                jnp.zeros((batch_seqs, head_count, glob_rows), jnp.float32),
                jnp.ones((batch_seqs, head_count, glob_rows), jnp.float32),
                jnp.zeros((batch_seqs, head_count, glob_rows, HD), jnp.float32),
            )

        glob_top, glob_total, glob_numer = lax.cond(seq_index == 0, global_here, global_skip)
        glob_out = glob_numer / glob_total[..., None]
        query_split = queries.reshape(batch_seqs, blocks_dev, BLOCK, head_count, HD)
        key_split = picked_keys.reshape(batch_seqs, blocks_dev, LIST * BLOCK, head_count, HD)
        value_split = picked_values.reshape(batch_seqs, blocks_dev, LIST * BLOCK, head_count, HD)
        raw_scores = (
            jnp.einsum(
                "sbqhd,sbkhd->sbhqk", query_split, key_split, preferred_element_type=jnp.float32
            )
            * score_scale
        )
        keep_now = mask_now[:, :, None]
        masked = jnp.where(keep_now, raw_scores, NEG)
        row_top = jnp.max(masked, axis=-1, keepdims=True)
        weights = jnp.exp(masked - row_top) * keep_now.astype(jnp.float32)
        row_total = jnp.sum(weights, axis=-1, keepdims=True)
        probs_list = weights / row_total
        probs_low = probs_list.astype(jnp.bfloat16)
        listed = jnp.einsum(
            "sbhqk,sbkhd->sbqhd", probs_low, value_split, preferred_element_type=jnp.float32
        ).reshape(batch_seqs, local_rows, head_cols)
        glob_rows_out = jnp.transpose(glob_out, (0, 2, 1, 3)).reshape(
            batch_seqs, glob_rows, head_cols
        )
        glob_full = jnp.pad(glob_rows_out, ((0, 0), (0, local_rows - glob_rows), (0, 0)))
        attended = jnp.where(glob_flag, glob_full, listed) * valid_now[..., None]
        attended_low = attended.astype(jnp.bfloat16).reshape(-1, head_cols)
        branch = lax.psum(
            jnp.dot(attended_low, out_weight, preferred_element_type=jnp.float32).astype(
                jnp.bfloat16
            ),
            "mp",
        ).astype(jnp.float32)
        hidden = rows_in + branch.reshape(rows_in.shape)
        normed_two, inverse_two = norm_stats(hidden)
        second_low = (
            (normed_two * second_gain + second_bias).astype(jnp.bfloat16).reshape(-1, model_width)
        )
        pre_act = jnp.dot(second_low, up_weight, preferred_element_type=jnp.float32) + up_bias
        activated = jax.nn.gelu(pre_act, approximate=True).astype(jnp.bfloat16)
        ffn_branch = lax.psum(
            jnp.dot(activated, down_weight, preferred_element_type=jnp.float32).astype(
                jnp.bfloat16
            ),
            "mp",
        ).astype(jnp.float32)
        outputs_all.append(hidden + ffn_branch.reshape(rows_in.shape) + down_bias)
        grad_rows = cotangent[first_seq:last_seq].reshape(-1, model_width)
        down_bias_total = down_bias_total + jnp.sum(grad_rows, axis=0)
        grad_low = grad_rows.astype(jnp.bfloat16)
        down_total = down_total + jnp.einsum(
            "rf,rd->fd", activated, grad_low, preferred_element_type=jnp.float32
        )
        act_grad = jnp.einsum(
            "rd,fd->rf", grad_low, down_weight, preferred_element_type=jnp.float32
        )
        _, gelu_pull = jax.vjp(lambda inner: jax.nn.gelu(inner, approximate=True), pre_act)
        pre_grad = gelu_pull(act_grad)[0].astype(jnp.bfloat16)
        up_bias_total = up_bias_total + jnp.sum(pre_grad.astype(jnp.float32), axis=0)
        up_total = up_total + jnp.einsum(
            "rd,rf->df", second_low, pre_grad, preferred_element_type=jnp.float32
        )
        second_grad = (
            lax.psum(
                jnp.einsum(
                    "rf,df->rd", pre_grad, up_weight, preferred_element_type=jnp.float32
                ).astype(jnp.bfloat16),
                "mp",
            )
            .astype(jnp.float32)
            .reshape(rows_in.shape)
        )
        gain_two_total = gain_two_total + jnp.sum(second_grad * normed_two, axis=(0, 1))
        bias_two_total = bias_two_total + jnp.sum(second_grad, axis=(0, 1))
        hidden_grad = grad_rows.reshape(rows_in.shape) + norm_back(
            second_grad, normed_two, inverse_two, second_gain
        )
        hidden_low = hidden_grad.astype(jnp.bfloat16).reshape(-1, model_width)
        out_total = out_total + jnp.einsum(
            "rc,rd->cd", attended_low, hidden_low, preferred_element_type=jnp.float32
        )
        attended_grad = jnp.einsum(
            "rd,cd->rc", hidden_low, out_weight, preferred_element_type=jnp.float32
        ).astype(jnp.bfloat16).reshape(batch_seqs, local_rows, head_cols) * valid_now[
            ..., None
        ].astype(
            jnp.bfloat16
        )
        list_grad = jnp.where(glob_flag, jnp.zeros_like(attended_grad), attended_grad).reshape(
            batch_seqs, blocks_dev, BLOCK, head_count, HD
        )
        prob_grad = jnp.einsum(
            "sbqhd,sbkhd->sbhqk", list_grad, value_split, preferred_element_type=jnp.float32
        )
        delta = jnp.sum(probs_list * prob_grad, axis=-1, keepdims=True)
        score_grad = (probs_list * (prob_grad - delta)).astype(jnp.bfloat16)
        query_grad = (
            jnp.einsum(
                "sbhqk,sbkhd->sbqhd", score_grad, key_split, preferred_element_type=jnp.float32
            )
            * score_scale
        ).reshape(batch_seqs, local_rows, head_cols)
        key_picked_grad = (
            jnp.einsum(
                "sbhqk,sbqhd->sbkhd", score_grad, query_split, preferred_element_type=jnp.float32
            )
            * score_scale
        )
        value_picked_grad = jnp.einsum(
            "sbhqk,sbqhd->sbkhd", probs_low, list_grad, preferred_element_type=jnp.float32
        )
        picked_grads = jnp.concatenate(
            [
                key_picked_grad.reshape(batch_seqs, picked_rows, head_cols),
                value_picked_grad.reshape(batch_seqs, picked_rows, head_cols),
            ],
            axis=-1,
        )
        seg_ids = wanted * batch_seqs + jnp.arange(batch_seqs, dtype=jnp.int32)[:, None]
        kv_term = jax.ops.segment_sum(
            picked_grads.reshape(batch_seqs * picked_rows, 2 * head_cols),
            seg_ids.reshape(-1),
            num_segments=LEN * batch_seqs,
        ).reshape(LEN, batch_seqs, 2 * head_cols)
        glob_grad_own = attended_grad[:, :glob_rows]

        def back_here():
            return lax.map(
                global_back,
                (
                    glob_queries,
                    whole_keys,
                    whole_values,
                    glob_mask,
                    glob_top,
                    glob_total,
                    glob_out,
                    glob_grad_own,
                ),
            )

        def back_skip():
            return (
                jnp.zeros((batch_seqs, glob_rows, head_cols), jnp.float32),
                jnp.zeros((batch_seqs, LEN, head_cols), jnp.float32),
                jnp.zeros((batch_seqs, LEN, head_cols), jnp.float32),
            )

        glob_query_grad, whole_key_grad, whole_value_grad = lax.cond(
            seq_index == 0, back_here, back_skip
        )
        glob_dense = jnp.transpose(
            jnp.concatenate([whole_key_grad, whole_value_grad], axis=-1), (1, 0, 2)
        )
        kv_source = kv_term + glob_dense
        kv_grad = jnp.transpose(scatter_rows(kv_source), (1, 0, 2))
        glob_query_full = jnp.pad(glob_query_grad, ((0, 0), (0, local_rows - glob_rows), (0, 0)))
        query_total = query_grad + jnp.where(glob_flag, glob_query_full, 0.0)
        qkv_low_grad = (
            jnp.stack([query_total, kv_grad[..., :head_cols], kv_grad[..., head_cols:]], axis=2)
            .astype(jnp.bfloat16)
            .reshape(-1, 3 * head_cols)
        )
        qkv_total = qkv_total + jnp.einsum(
            "rd,rc->dc", first_low, qkv_low_grad, preferred_element_type=jnp.float32
        )
        first_grad = (
            lax.psum(
                jnp.einsum(
                    "rc,dc->rd", qkv_low_grad, qkv_flat, preferred_element_type=jnp.float32
                ).astype(jnp.bfloat16),
                "mp",
            )
            .astype(jnp.float32)
            .reshape(rows_in.shape)
        )
        gain_one_total = gain_one_total + jnp.sum(first_grad * normed_one, axis=(0, 1))
        bias_one_total = bias_one_total + jnp.sum(first_grad, axis=(0, 1))
        input_grads.append(hidden_grad + norm_back(first_grad, normed_one, inverse_one, first_gain))
    matrix_grads = (
        lax.psum_scatter(
            qkv_total.reshape(model_width, 3, head_cols).astype(jnp.bfloat16),
            "seq",
            scatter_dimension=0,
            tiled=True,
        ).astype(jnp.float32),
        lax.psum_scatter(
            out_total.astype(jnp.bfloat16), "seq", scatter_dimension=1, tiled=True
        ).astype(jnp.float32),
        lax.psum_scatter(
            up_total.astype(jnp.bfloat16), "seq", scatter_dimension=0, tiled=True
        ).astype(jnp.float32),
        lax.psum_scatter(
            down_total.astype(jnp.bfloat16), "seq", scatter_dimension=1, tiled=True
        ).astype(jnp.float32),
    )
    matrix_grads = (
        lax.psum(matrix_grads[0].astype(jnp.bfloat16), "batch").astype(jnp.float32),
        lax.psum(matrix_grads[1].astype(jnp.bfloat16), "batch").astype(jnp.float32),
        lax.psum(matrix_grads[2].astype(jnp.bfloat16), "batch").astype(jnp.float32),
        lax.psum(matrix_grads[3].astype(jnp.bfloat16), "batch").astype(jnp.float32),
    )
    vector_grads = lax.psum(
        (
            gain_one_total,
            bias_one_total,
            gain_two_total,
            bias_two_total,
            up_bias_total,
            down_bias_total,
        ),
        ("seq", "batch"),
    )
    return (
        jnp.concatenate(outputs_all, axis=0),
        jnp.concatenate(input_grads, axis=0),
        vector_grads[0],
        vector_grads[1],
        matrix_grads[0],
        matrix_grads[1],
        vector_grads[2],
        vector_grads[3],
        matrix_grads[2],
        vector_grads[4],
        matrix_grads[3],
        vector_grads[5],
    )


def solution(mesh):
    placed = (
        P("batch", "seq", None),
        P("batch", None),
        P("batch", "seq", None),
        P(),
        P(),
        P(None, None, "mp"),
        P("mp", None),
        P(),
        P(),
        P(None, "mp"),
        P("mp"),
        P("mp", None),
        P(),
        P("batch", "seq", None),
    )
    by_heads = (1024 // mesh.shape["seq"]) % 128 == 0
    return jax.shard_map(
        local if by_heads else local_by_blocks,
        mesh=mesh,
        in_specs=placed,
        out_specs=(
            P("batch", "seq", None),
            P("batch", "seq", None),
            P(),
            P(),
            P("seq", None, "mp"),
            P("mp", "seq"),
            P(),
            P(),
            P("seq", "mp"),
            P("mp"),
            P("mp", "seq"),
            P(),
        ),
        check_vma=False,
    )
```

```python
import functools

import jax
import jax.numpy as jnp
from jax import lax
from jax.experimental import pallas as pl
from jax.experimental.pallas import tpu as pltpu
from jax.sharding import PartitionSpec as P

BLOCK = 64
GLOB = 2
WIN = 3
HD = 64
LIST = 8

NEG = -1e30
EPS = 1e-05
F32 = jnp.float32
BF16 = jnp.bfloat16
VMEM_LIMIT = 60 * 1024 * 1024


def norm_stats(rows):
    centre = rows - jnp.mean(rows, axis=-1, keepdims=True)
    spread = jnp.mean(centre * centre, axis=-1, keepdims=True)
    inverse = lax.rsqrt(spread + EPS)
    return (centre * inverse, inverse)


def norm_back(grad_out, normed, inverse, gain):
    scaled = grad_out * gain
    return inverse * (
        scaled
        - jnp.mean(scaled, axis=-1, keepdims=True)
        - normed * jnp.mean(scaled * normed, axis=-1, keepdims=True)
    )


def block_lists(blocks, randoms, block_count):
    leading = randoms.shape[:-1]
    globals_part = jnp.broadcast_to(jnp.arange(GLOB, dtype=jnp.int32), leading + (GLOB,))
    window_part = jnp.broadcast_to(
        blocks[:, None] + jnp.arange(WIN, dtype=jnp.int32) - WIN // 2, leading + (WIN,)
    )
    block_list = jnp.concatenate([globals_part, window_part, randoms], axis=-1)
    inside = (block_list >= 0) & (block_list < block_count)
    same_entry = block_list[..., :, None] == block_list[..., None, :]
    order_ids = jnp.arange(LIST)
    earlier = order_ids[None, :] < order_ids[:, None]
    repeated = jnp.any(same_entry & earlier, axis=-1)
    admitted = inside & jnp.logical_not(repeated)
    return (jnp.clip(block_list, 0, block_count - 1), admitted.astype(jnp.int32))


MESH = pl.DeviceIdType.MESH


class Trade:
    def __init__(self, source, target, send_sems, recv_sems, own_sem):
        self.source, self.target = source, target
        self.send_sems, self.recv_sems, self.own_sem = send_sems, recv_sems, own_sem
        self.count = source.shape[0]
        self.me = lax.axis_index("seq")

    def greet(self, others):
        barrier = pltpu.get_barrier_semaphore()
        for distance in range(1, self.count):
            other = lax.rem(self.me + distance, self.count)
            pl.semaphore_signal(barrier, inc=1, device_id={"seq": other}, device_id_type=MESH)
        pl.semaphore_wait(barrier, self.count - 1 + others)

    def copy(self, distance):
        other = lax.rem(self.me + distance, self.count)
        return pltpu.make_async_remote_copy(
            src_ref=self.source.at[other],
            dst_ref=self.target.at[self.me],
            send_sem=self.send_sems.at[distance - 1],
            recv_sem=self.recv_sems.at[distance - 1],
            device_id={"seq": other},
            device_id_type=MESH,
        )

    def own(self):
        return pltpu.make_async_copy(
            self.source.at[self.me], self.target.at[self.me], self.own_sem.at[0]
        )

    def start(self, others=0):
        self.greet(others)
        for distance in range(1, self.count):
            self.copy(distance).start()
        self.own().start()

    def finish(self):
        for distance in range(1, self.count):
            self.copy(distance).wait()
        self.own().wait()


def trade_scratch(count):
    dma = pltpu.SemaphoreType.DMA
    return [dma((count - 1,)), dma((count - 1,)), dma((1,))]


def segment_at(places, ends_ref):
    total = jnp.zeros(places.shape, jnp.int32)
    for doc in range(ends_ref.shape[0]):
        total = total + (places >= ends_ref[doc]).astype(jnp.int32)
    return total


def head_spread(rows, heads):
    lane_head = lax.broadcasted_iota(jnp.int32, (1, rows.shape[1]), 1) // HD
    return jnp.concatenate(
        [rows * (lane_head == head).astype(F32).astype(rows.dtype) for head in range(heads)], axis=0
    )


def head_fold(wide, heads):
    rows = wide.shape[0] // heads
    lane_head = lax.broadcasted_iota(jnp.int32, (rows, wide.shape[1]), 1) // HD
    folded = jnp.zeros((rows, wide.shape[1]), wide.dtype)
    for head in range(heads):
        folded = jnp.where(lane_head == head, wide[head * rows : (head + 1) * rows], folded)
    return folded


def block_at(block):
    return pl.ds(pl.multiple_of(block * BLOCK, BLOCK), BLOCK)


def fill_segments(token_segs, ends_ref):
    def fill(block, _):
        places = block * BLOCK + lax.broadcasted_iota(jnp.int32, (BLOCK, token_segs.shape[1]), 0)
        token_segs[block_at(block), :] = segment_at(places, ends_ref)
        return 0

    lax.fori_loop(0, token_segs.shape[0] // BLOCK, fill, 0)


def query_segments(block, heads, ends_ref):
    lanes = lax.broadcasted_iota(jnp.int32, (8, heads * BLOCK), 1)
    return segment_at(block * BLOCK + lanes % BLOCK, ends_ref)[0:1]


def key_segments(starts, keeps, ends_ref):
    lanes = lax.broadcasted_iota(jnp.int32, (8, 2 * BLOCK), 1)
    first = lanes < BLOCK
    pieces = []
    for entry in range(0, LIST, 2):
        places = lanes + jnp.where(
            first, starts[entry] * BLOCK, (starts[entry + 1] - 1) * BLOCK
        )
        keep = jnp.where(first, keeps[entry], keeps[entry + 1]) > 0
        pieces.append(jnp.where(keep, segment_at(places, ends_ref), -1))
    return jnp.concatenate(pieces, axis=1)[0:1]


def gathered(ref, starts):
    return jnp.concatenate([ref[block_at(start), :] for start in starts], axis=0)


def block_parts(wide):
    return [wide[start : start + BLOCK] for start in range(0, wide.shape[0], BLOCK)]


def dot_nt(left, right):
    return lax.dot_general(left, right, (((1,), (1,)), ((), ())), preferred_element_type=F32)


def dot_tn(left, right):
    return lax.dot_general(left, right, (((0,), (0,)), ((), ())), preferred_element_type=F32)


def dot_nn(left, right):
    return lax.dot_general(left, right, (((1,), (0,)), ((), ())), preferred_element_type=F32)


def as_row(tall):
    count = tall.shape[0]
    row_ids = lax.broadcasted_iota(jnp.int32, (count, count), 0)
    lane_ids = lax.broadcasted_iota(jnp.int32, (count, count), 1)
    return jnp.sum(jnp.where(row_ids == lane_ids, tall, 0.0), axis=0, keepdims=True)


def together(running):
    while running:
        still = []
        for each in running:
            if next(each, 0) is None:
                still.append(each)
        running = still


def unit_block(unit, half, parts, rows_total):
    per = rows_total // parts // BLOCK // 2
    part = unit // per
    inside = unit - part * per
    return part, inside, part * 2 * per + half * per + inside


def forward_kernel(heads, half, ends_ref, lists_ref, admit_ref, q_ref, k_ref, v_ref, *rest):
    o_ref, lse_ref, token_segs, *held = rest
    held = held[0] if held else None
    scale = HD ** (-0.5)
    rows_total = q_ref.shape[0]
    units = o_ref.shape[0] * o_ref.shape[1] // BLOCK
    first_unit = GLOB if half == 0 else 0
    chunk = LIST * BLOCK
    fill_segments(token_segs, ends_ref)

    def store(unit, wide, top, total):
        part, inside, block = unit_block(unit, half, o_ref.shape[0], rows_total)
        out = head_fold(wide, heads)
        places = block * BLOCK + lax.broadcasted_iota(jnp.int32, out.shape, 0)
        out = jnp.where(places < ends_ref[ends_ref.shape[0] - 1], out, 0.0)
        o_ref[part, block_at(inside), :] = out.astype(BF16)
        lse_ref[unit] = jnp.broadcast_to(as_row(top + jnp.log(total)), lse_ref.shape[1:])

    def kept(block, key_segs):
        own = token_segs[block_at(block), :]
        return jnp.concatenate([own] * (chunk // own.shape[1]), axis=1) == key_segs

    def global_blocks():
        query_wide = jnp.concatenate(
            [head_spread(q_ref[block_at(block), :] * scale, heads) for block in range(GLOB)], axis=0
        )
        wide_rows = GLOB * heads * BLOCK

        def score(part, top):
            here = pl.ds(pl.multiple_of(part * chunk, chunk), chunk)
            places = part * chunk + lax.broadcasted_iota(jnp.int32, (8, chunk), 1)
            key_segs = segment_at(places, ends_ref)[0:1]
            keeps = [kept(block, key_segs) for block in range(GLOB)]
            scores = dot_nt(query_wide, k_ref[here, :])
            tops = []
            for place, rows in enumerate(block_parts(scores)):
                rows = jnp.where(keeps[place // heads], rows, NEG)
                held[place * BLOCK : (place + 1) * BLOCK, here] = rows
                tops.append(jnp.max(rows, axis=1, keepdims=True))
            return jnp.maximum(top, jnp.concatenate(tops, axis=0))

        top = lax.fori_loop(0, rows_total // chunk, score, jnp.full((wide_rows, 1), NEG, F32))

        def gather(part, carried):
            total, wide = carried
            here = pl.ds(pl.multiple_of(part * chunk, chunk), chunk)
            totals, weights = [], []
            for place, part_top in enumerate(block_parts(top)):
                weight = jnp.exp(held[place * BLOCK : (place + 1) * BLOCK, here] - part_top)
                totals.append(jnp.sum(weight, axis=1, keepdims=True))
                weights.append(weight.astype(BF16))
            wide = wide + dot_nn(jnp.concatenate(weights, axis=0), v_ref[here, :])
            return total + jnp.concatenate(totals, axis=0), wide

        total, wide = lax.fori_loop(
            0,
            rows_total // chunk,
            gather,
            (jnp.zeros((wide_rows, 1), F32), jnp.zeros((wide_rows, q_ref.shape[1]), F32)),
        )
        wide = wide * (1.0 / total)
        for block in range(GLOB):
            own = slice(block * heads * BLOCK, (block + 1) * heads * BLOCK)
            store(block, wide[own], top[own], total[own])

    if half == 0:
        global_blocks()

    def listed_block(unit):
        _, _, block = unit_block(unit, half, o_ref.shape[0], rows_total)
        query_wide = head_spread(q_ref[block_at(block), :] * scale, heads)
        starts = [lists_ref[block * LIST + entry] for entry in range(LIST)]
        keeps = [admit_ref[block * LIST + entry] for entry in range(LIST)]
        keep = kept(block, key_segments(starts, keeps, ends_ref))
        scores = dot_nt(query_wide, gathered(k_ref, starts))
        yield
        tops, totals, probs = [], [], []
        for rows in block_parts(scores):
            rows = jnp.where(keep, rows, NEG)
            top = jnp.max(rows, axis=1, keepdims=True)
            weights = jnp.exp(rows - top)
            total = jnp.sum(weights, axis=1, keepdims=True)
            probs.append((weights * (1.0 / total)).astype(BF16))
            tops.append(top)
            totals.append(total)
            yield
        wide = dot_nn(jnp.concatenate(probs, axis=0), gathered(v_ref, starts))
        store(unit, wide, jnp.concatenate(tops, axis=0), jnp.concatenate(totals, axis=0))

    def listed_group(group, _):
        together([listed_block(first_unit + 4 * group + place) for place in range(4)])
        return 0

    lax.fori_loop(0, (units - first_unit) // 4, listed_group, 0)
    together([listed_block(units - 1 - place) for place in range((units - first_unit) % 4)])


def backward_kernel(
    heads,
    ends_ref,
    lists_ref,
    admit_ref,
    q_ref,
    k_ref,
    v_ref,
    o_first,
    o_second,
    do_first,
    do_second,
    lse_first,
    lse_second,
    out_ref,
    token_segs,
    dk_ref,
    dv_ref,
    dq_ref,
):
    scale = HD ** (-0.5)
    rows_total, cols = q_ref.shape
    blocks = rows_total // BLOCK
    pair_rows = 2 * BLOCK
    fill_segments(token_segs, ends_ref)

    def prepare(pair, _):
        here = pl.ds(pl.multiple_of(pair * pair_rows, pair_rows), pair_rows)
        dk_ref[here, :] = jnp.zeros((pair_rows, cols), F32)
        dv_ref[here, :] = jnp.zeros((pair_rows, cols), F32)
        return 0

    lax.fori_loop(0, blocks // 2, prepare, 0)

    parts = o_first.shape[0]
    halves_of = ((o_first, do_first, lse_first), (o_second, do_second, lse_second))

    def query_side(unit, half):
        o_ref, do_ref, lse_ref = halves_of[half]
        part, inside, block = unit_block(unit, half, parts, rows_total)
        query_wide = head_spread(q_ref[block_at(block), :] * scale, heads)
        grad_rows = do_ref[part, block_at(inside), :]
        grad_wide = head_spread(grad_rows, heads)
        product = grad_rows.astype(F32) * o_ref[part, block_at(inside), :].astype(F32)
        spread = head_spread(product.astype(BF16), heads)
        delta = dot_nt(jnp.ones((8, cols), BF16), spread)[0:1]
        seg_row = query_segments(block, heads, ends_ref)
        return query_wide, grad_wide, delta, lse_ref[unit, 0:1], seg_row

    def unit(starts, keeps, query_wide, grad_wide, delta, lse, seg_row, finish_query):
        keys = gathered(k_ref, starts)
        scores = block_parts(dot_nt(keys, query_wide))
        prob_grads = block_parts(dot_nt(gathered(v_ref, starts), grad_wide))
        yield
        probs, score_grads = [], []
        for entry in range(LIST):
            wanted = seg_row if keeps is None else jnp.where(keeps[entry] > 0, seg_row, -1)
            own = token_segs[block_at(starts[entry]), :]
            keep = jnp.concatenate([own] * (seg_row.shape[1] // own.shape[1]), axis=1) == wanted
            prob = jnp.exp(jnp.where(keep, scores[entry], NEG) - lse)
            probs.append(prob.astype(BF16))
            score_grads.append((prob * (prob_grads[entry] - delta)).astype(BF16))
            if entry % 2:
                yield
        score_grad = jnp.concatenate(score_grads, axis=0)
        finish_query(dot_tn(score_grad, keys))
        dk = dot_nn(score_grad, query_wide)
        dv = dot_nn(jnp.concatenate(probs, axis=0), grad_wide)
        yield
        for entry in range(LIST):
            here = block_at(starts[entry])
            dk_ref[here, :] += dk[entry * BLOCK : (entry + 1) * BLOCK]
            dv_ref[here, :] += dv[entry * BLOCK : (entry + 1) * BLOCK]
        yield

    def store_query(block, wide):
        out_ref[block_at(block), 0:cols] = (head_fold(wide, heads) * scale).astype(BF16)

    def global_blocks():
        sides = [query_side(block, 0) for block in range(GLOB)]
        side = [jnp.concatenate(both, axis=axis) for both, axis in zip(zip(*sides), (0, 0, 1, 1, 1))]
        dq_ref[...] = jnp.zeros_like(dq_ref)

        def part_of(part, _):
            def add_query(wide):
                dq_ref[...] += wide

            together([unit([part * LIST + entry for entry in range(LIST)], None, *side, add_query)])
            return 0

        lax.fori_loop(0, blocks // LIST, part_of, 0)
        for block in range(GLOB):
            store_query(block, dq_ref[block * heads * BLOCK : (block + 1) * heads * BLOCK])

    global_blocks()

    def listed_block(place, half):
        _, _, block = unit_block(place, half, parts, rows_total)
        starts = [lists_ref[block * LIST + entry] for entry in range(LIST)]
        keeps = [admit_ref[block * LIST + entry] for entry in range(LIST)]
        return unit(
            starts, keeps, *query_side(place, half), functools.partial(store_query, block)
        )

    for half, first_unit in ((0, GLOB), (1, 0)):
        units = blocks // 2

        def listed_group(group, _):
            together([listed_block(first_unit + 4 * group + place, half) for place in range(4)])
            return 0

        lax.fori_loop(0, (units - first_unit) // 4, listed_group, 0)
        together([listed_block(units - 1 - place, half) for place in range((units - first_unit) % 4)])

    def finish(block, _):
        here = block_at(block)
        out_ref[here, cols : 2 * cols] = dk_ref[here, :].astype(BF16)
        out_ref[here, 2 * cols : 3 * cols] = dv_ref[here, :].astype(BF16)
        return 0

    lax.fori_loop(0, blocks, finish, 0)


def smem():
    return pl.BlockSpec(memory_space=pltpu.SMEM)


def column(rows, cols, index):
    return pl.BlockSpec((rows, cols), lambda step: (0, index))


def attention_forward(half, qkv, doc_ends, lists, admits, parts):
    rows = qkv.shape[0]
    cols = qkv.shape[1] // 3
    heads = cols // HD
    blocks = rows // BLOCK
    out = jax.ShapeDtypeStruct((parts, rows // parts // 2, cols), BF16)
    lse = jax.ShapeDtypeStruct((blocks // 2, 8, heads * BLOCK), F32)
    cube = lambda step: (0, 0, 0)
    return pl.pallas_call(
        functools.partial(forward_kernel, heads, half),
        grid=(1,),
        in_specs=[smem(), smem(), smem()] + [column(rows, cols, part) for part in range(3)],
        out_specs=[pl.BlockSpec(out.shape, cube), pl.BlockSpec(lse.shape, cube)],
        out_shape=[out, lse],
        scratch_shapes=[pltpu.VMEM((rows, 2 * BLOCK), jnp.int32)]
        + ([] if half else [pltpu.VMEM((GLOB * heads * BLOCK, rows), F32)]),
        compiler_params=pltpu.CompilerParams(vmem_limit_bytes=VMEM_LIMIT),
        cost_estimate=pl.CostEstimate(
            flops=rows * LIST * BLOCK * cols * heads * 5,
            bytes_accessed=8 * rows * cols,
            transcendentals=0,
        ),
    )(doc_ends, lists, admits, qkv, qkv, qkv)


def attention_backward(qkv, attended, attended_grad, lse, doc_ends, lists, admits):
    rows = qkv.shape[0]
    cols = qkv.shape[1] // 3
    heads = cols // HD
    cube = lambda step: (0, 0, 0)
    return pl.pallas_call(
        functools.partial(backward_kernel, heads),
        grid=(1,),
        in_specs=[smem(), smem(), smem()]
        + [column(rows, cols, part) for part in range(3)]
        + [pl.BlockSpec(part.shape, cube) for part in (*attended, *attended_grad, *lse)],
        out_specs=column(rows, 3 * cols, 0),
        out_shape=jax.ShapeDtypeStruct((rows, 3 * cols), BF16),
        scratch_shapes=[
            pltpu.VMEM((rows, 2 * BLOCK), jnp.int32),
            pltpu.VMEM((rows, cols), F32),
            pltpu.VMEM((rows, cols), F32),
            pltpu.VMEM((GLOB * heads * BLOCK, cols), F32),
        ],
        compiler_params=pltpu.CompilerParams(vmem_limit_bytes=VMEM_LIMIT),
        cost_estimate=pl.CostEstimate(
            flops=rows * LIST * BLOCK * cols * heads * 15,
            bytes_accessed=20 * rows * cols,
            transcendentals=0,
        ),
    )(doc_ends, lists, admits, qkv, qkv, qkv, *attended, *attended_grad, *lse)


def row_stats(rows):
    mean = jnp.mean(rows, axis=-1, keepdims=True)
    centre = rows - mean
    spread = jnp.mean(centre * centre, axis=-1, keepdims=True)
    inverse = lax.rsqrt(spread + EPS)
    return centre * inverse, inverse


def gelu_pair(inner):
    root = 0.7978845608028654
    cube = 0.044715
    square = inner * inner
    bent = jnp.tanh(inner * (root + (root * cube) * square))
    half = 0.5 + 0.5 * bent
    value = inner * half
    return value, half + value * (1.0 - bent) * (root + (3.0 * root * cube) * square)


def token_kernel(
    tile,
    index,
    ends_ref,
    att_ref,
    x_ref,
    cotangent_ref,
    out_own_ref,
    out_other_ref,
    up_own_ref,
    up_near_ref,
    up_far_ref,
    down_own_ref,
    down_near_ref,
    down_far_ref,
    up_bias_ref,
    gain_ref,
    bias_ref,
    down_bias_ref,
    trade_source,
    act_in,
    pre_in,
    second_in,
    hidden_in,
    grad_in,
    att_in,
    output_ref,
    hidden_grad_ref,
    datt_ref,
    act_ref,
    pre_ref,
    second_ref,
    hidden_low_ref,
    grad_low_ref,
    att_rows_ref,
    sums_ref,
    unit_sums_ref,
    trade_target,
    hidden,
    normed,
    inverse,
    ffn,
    second_grad,
    grad_rows,
    up_slots,
    down_slots,
    slot_sems,
    row_sems,
    *trade_sems,
):
    step = pl.program_id(0)
    steps = pl.num_programs(0)
    rows = hidden.shape[0]
    parts = att_ref.shape[0]
    tiles = [slice(start, start + tile) for start in range(0, rows, tile)]
    chunk = up_slots.shape[2]
    own_steps = up_own_ref.shape[1] // chunk
    near_steps = up_near_ref.shape[1] // chunk

    def copies(up_from, down_from, index, slot):
        here = pl.ds(pl.multiple_of(index * chunk, chunk), chunk)
        return (
            pltpu.make_async_copy(up_from.at[:, here], up_slots.at[slot], slot_sems.at[0, slot]),
            pltpu.make_async_copy(down_from.at[here], down_slots.at[slot], slot_sems.at[1, slot]),
        )

    def fetch(index):
        def begin(up_from, down_from, first):
            for copy in copies(up_from, down_from, index - first, index % 2):
                copy.start()

        @pl.when(index < own_steps)
        def _():
            begin(up_own_ref, down_own_ref, 0)

        @pl.when((index >= own_steps) & (index < own_steps + near_steps))
        def _():
            begin(up_near_ref, down_near_ref, own_steps)

        @pl.when(index >= own_steps + near_steps)
        def _():
            begin(up_far_ref, down_far_ref, own_steps + near_steps)

    half = parts // 2
    me = lax.axis_index("seq")
    place = lax.axis_index("mp")
    own_place = place * half
    other_place = (1 - place) * half
    first_row = index * rows
    row_copies = [
        pltpu.make_async_copy(source.at[place, pl.ds(first_row, rows)], target, row_sems.at[which])
        for which, (source, target) in enumerate(((x_ref, hidden), (cotangent_ref, grad_rows)))
    ]
    trade = Trade(trade_source, trade_target, *trade_sems)
    out_parts = [(own_place + part, out_own_ref, part) for part in range(half)]
    out_parts += [(other_place + part, out_other_ref, part) for part in range(half)]

    @pl.when(step == 0)
    def _():
        for copy in row_copies:
            copy.start()
        fetch(step)
        trade.start()

    @pl.when(step + 1 < steps)
    def _():
        fetch(step + 1)

    @pl.when(step == 0)
    def _():
        for copy in row_copies:
            copy.wait()
        for here in tiles:
            total = hidden[here, :]
            for part, weight_ref, index in out_parts:
                total = total + dot_nn(att_ref[part, here, :], weight_ref[index])
            for part in range(parts):
                cols = att_ref.shape[2]
                att_rows_ref[here, part * cols : (part + 1) * cols] = att_ref[part, here, :]
            hidden[here, :] = total
            unit, scale = row_stats(total)
            normed[here, :] = unit
            inverse[here, :] = jnp.broadcast_to(scale, (tile, inverse.shape[1]))
            second_ref[here, :] = (unit * gain_ref[...] + bias_ref[...]).astype(BF16)
            grad_low_ref[here, :] = grad_rows[here, :].astype(BF16)
            ffn[here, :] = jnp.zeros((tile, ffn.shape[1]), F32)
            second_grad[here, :] = jnp.zeros((tile, ffn.shape[1]), F32)

    slot = step % 2
    for copy in copies(up_own_ref, down_own_ref, 0, slot):
        copy.wait()
    up_ref = up_slots.at[slot]
    down_ref = down_slots.at[slot]
    unit_sum = jnp.zeros((1, chunk), F32)
    for here in tiles:
        inner = dot_nn(second_ref[here, :], up_ref[...]) + up_bias_ref[...]
        act_grad = dot_nt(grad_low_ref[here, :], down_ref[...])
        value, slope = gelu_pair(inner)
        value = value.astype(BF16)
        pre_grad = (act_grad * slope).astype(BF16)
        act_ref[here, :] = value
        pre_ref[here, :] = pre_grad
        unit_sum = unit_sum + jnp.sum(pre_grad.astype(F32), axis=0, keepdims=True)
        ffn[here, :] += dot_nn(value, down_ref[...])
        second_grad[here, :] += dot_nt(pre_grad, up_ref[...])
    unit_sums_ref[...] = jnp.broadcast_to(unit_sum, unit_sums_ref.shape)

    @pl.when(step == steps - 1)
    def _():
        width = ffn.shape[1]
        grad_sum = jnp.zeros((1, width), F32)
        gain_sum = jnp.zeros((1, width), F32)
        bias_sum = jnp.zeros((1, width), F32)
        for number, here in enumerate(tiles):
            output_ref[here, :] = (hidden[here, :] + ffn[here, :] + down_bias_ref[...]).astype(BF16)
            grad = grad_rows[here, :]
            back = second_grad[here, :]
            unit = normed[here, :]
            scaled = back * gain_ref[...]
            through = (
                scaled
                - jnp.mean(scaled, axis=-1, keepdims=True)
                - unit * jnp.mean(scaled * unit, axis=-1, keepdims=True)
            )
            total = grad + inverse[here, 0:1] * through
            hidden_grad_ref[here, :] = total
            low = total.astype(BF16)
            hidden_low_ref[here, :] = low
            grad_sum = grad_sum + jnp.sum(grad, axis=0, keepdims=True)
            gain_sum = gain_sum + jnp.sum(back * unit, axis=0, keepdims=True)
            bias_sum = bias_sum + jnp.sum(back, axis=0, keepdims=True)
            for part, weight_ref, piece in out_parts:
                spread = dot_nt(low, weight_ref[piece])
                places = me * 2 * rows + first_row + number * tile
                places = places + lax.broadcasted_iota(jnp.int32, spread.shape, 0)
                inside = places < ends_ref[ends_ref.shape[0] - 1]
                datt_ref[part, here, :] = jnp.where(inside, spread, 0.0).astype(BF16)
        sums_ref[...] = jnp.concatenate(
            [grad_sum, gain_sum, bias_sum, jnp.zeros((5, width), F32)], axis=0
        )
        trade.finish()


def token_part(
    index, doc_ends, att, layer_input, cotangent, outs, ups, downs, up_bias, gain, bias, down_bias, source, kept
):
    parts, rows, cols = att.shape
    width = layer_input.shape[2]
    units = up_bias.shape[1]
    chunk = min(512, units // 4)
    whole = 2 * rows
    shapes = [(whole, units)] * 2 + [(whole, width)] * 4
    if kept is None:
        kept = [jnp.zeros((8, 128), BF16)] * len(shapes)
        aliases = {}
    else:
        aliases = {17 + place: 3 + place for place in range(len(shapes))}
    half = lambda step: (index, 0)
    fixed = lambda step: (0, 0)
    any_spec = pl.BlockSpec(memory_space=pl.ANY)
    cube = lambda step: (0, 0, 0)
    vector = pl.BlockSpec((1, width), fixed)
    return pl.pallas_call(
        functools.partial(token_kernel, min(256, rows), index),
        grid=(units // chunk,),
        in_specs=[
            smem(),
            pl.BlockSpec((parts, rows, cols), cube),
            any_spec,
            any_spec,
            pl.BlockSpec((parts // 2, cols, width), cube),
            pl.BlockSpec((parts // 2, cols, width), cube),
        ]
        + [any_spec] * 6
        + [pl.BlockSpec((1, chunk), lambda step: (0, step)), vector, vector, vector]
        + [any_spec] * (1 + len(shapes)),
        out_specs=[
            pl.BlockSpec((rows, width), fixed),
            pl.BlockSpec((rows, width), fixed),
            pl.BlockSpec((parts, rows, cols), cube),
            pl.BlockSpec((rows, chunk), lambda step: (index, step)),
            pl.BlockSpec((rows, chunk), lambda step: (index, step)),
            pl.BlockSpec((rows, width), half),
            pl.BlockSpec((rows, width), half),
            pl.BlockSpec((rows, width), half),
            pl.BlockSpec((rows, width), half),
            pl.BlockSpec((8, width), fixed),
            pl.BlockSpec((8, chunk), lambda step: (0, step)),
            any_spec,
        ],
        scratch_shapes=[
            pltpu.VMEM((rows, width), F32),
            pltpu.VMEM((rows, width), F32),
            pltpu.VMEM((rows, 128), F32),
            pltpu.VMEM((rows, width), F32),
            pltpu.VMEM((rows, width), F32),
            pltpu.VMEM((rows, width), F32),
            pltpu.VMEM((2, width, chunk), BF16),
            pltpu.VMEM((2, chunk, width), BF16),
            pltpu.SemaphoreType.DMA((2, 2)),
            pltpu.SemaphoreType.DMA((2,)),
        ]
        + trade_scratch(parts),
        out_shape=[
            jax.ShapeDtypeStruct((rows, width), BF16),
            jax.ShapeDtypeStruct((rows, width), F32),
            jax.ShapeDtypeStruct((parts, rows, cols), BF16),
        ]
        + [jax.ShapeDtypeStruct(shape, BF16) for shape in shapes]
        + [
            jax.ShapeDtypeStruct((8, width), F32),
            jax.ShapeDtypeStruct((8, units), F32),
            jax.ShapeDtypeStruct((parts, rows, cols), BF16),
        ],
        input_output_aliases=aliases,
        compiler_params=pltpu.CompilerParams(
            collective_id=5 + index, has_side_effects=True, vmem_limit_bytes=VMEM_LIMIT
        ),
        cost_estimate=pl.CostEstimate(
            flops=rows * width * (8 * units + 4 * width),
            bytes_accessed=8 * units * width,
            transcendentals=0,
        ),
    )(
        doc_ends,
        att,
        layer_input,
        cotangent,
        *outs,
        *ups,
        *downs,
        up_bias,
        gain,
        bias,
        down_bias,
        source,
        *kept,
    )


def greet(me, count, partner=None):
    barrier = pltpu.get_barrier_semaphore()

    @pl.when(me > 0)
    def _():
        pl.semaphore_signal(barrier, inc=1, device_id={"seq": me - 1}, device_id_type=MESH)

    @pl.when(me < count - 1)
    def _():
        pl.semaphore_signal(barrier, inc=1, device_id={"seq": me + 1}, device_id_type=MESH)

    peers = jnp.minimum(me, 1) + jnp.minimum(count - 1 - me, 1)
    if partner is not None:
        pl.semaphore_signal(barrier, inc=1, device_id={"mp": partner}, device_id_type=MESH)
        peers = peers + 1
    pl.semaphore_wait(barrier, peers)


def gather_kernel(
    count,
    chunks,
    half_cols,
    x_ref,
    gain_ref,
    bias_ref,
    weight_ref,
    all_ref,
    qkv_ref,
    own_ref,
    rows_in,
    shards,
    results,
    weight,
    weight_sems,
    load_sems,
    send_sems,
    recv_sems,
    all_sems,
    qkv_sems,
):
    me = lax.axis_index("seq")
    place = lax.axis_index("mp")
    step = rows_in.shape[0] // chunks
    cols = weight.shape[1] // 3

    def at(chunk):
        return pl.ds(pl.multiple_of(chunk * step, step), step)

    def load(chunk):
        return pltpu.make_async_copy(
            x_ref.at[place, at(chunk)], rows_in.at[at(chunk)], load_sems.at[chunk]
        )

    def send(side, hop, chunk):
        shard = me - hop if side == 0 else me + hop
        target = me + 1 if side == 0 else me - 1
        return pltpu.make_async_remote_copy(
            src_ref=shards.at[shard, at(chunk)],
            dst_ref=shards.at[shard, at(chunk)],
            send_sem=send_sems.at[side, hop, chunk],
            recv_sem=recv_sems.at[side, hop, chunk],
            device_id={"seq": target},
            device_id_type=MESH,
        )

    def keep_all(shard, chunk):
        return pltpu.make_async_copy(
            shards.at[shard, at(chunk)], all_ref.at[shard, at(chunk)], all_sems.at[shard, chunk]
        )

    def keep_qkv(shard, chunk):
        return pltpu.make_async_copy(
            results.at[shard, at(chunk)], qkv_ref.at[shard, at(chunk)], qkv_sems.at[shard, chunk]
        )

    def over_chunks(body):
        def run(chunk, _):
            body(chunk)
            return 0

        lax.fori_loop(0, chunks, run, 0)

    over_chunks(lambda chunk: load(chunk).start())
    greet(me, count, 1 - place)

    here = (me * cols) // half_cols == place
    fetch = pltpu.make_async_remote_copy(
        src_ref=weight_ref,
        dst_ref=weight,
        send_sem=weight_sems.at[0],
        recv_sem=weight_sems.at[1],
        device_id={"mp": 1 - place},
        device_id_type=MESH,
    )
    copy = pltpu.make_async_copy(weight_ref, weight, weight_sems.at[2])

    @pl.when(here)
    def _():
        fetch.start()
        copy.start()

    def norm(chunk):
        load(chunk).wait()
        unit, _ = row_stats(rows_in[at(chunk), :])
        shards[me, at(chunk), :] = (unit * gain_ref[...] + bias_ref[...]).astype(BF16)
        keep_all(me, chunk).start()

        @pl.when(me < count - 1)
        def _():
            send(0, 0, chunk).start()

        @pl.when(me > 0)
        def _():
            send(1, 0, chunk).start()

    over_chunks(norm)

    def project(shard, chunk):
        rows = dot_nn(shards[shard, at(chunk), :], weight[...])
        results[shard, at(chunk), :] = rows.astype(BF16)
        keep_qkv(shard, chunk).start()

    def receive(hop, chunk):
        @pl.when(me >= hop + 1)
        def _():
            send(0, hop, chunk).wait_recv()
            if hop + 1 < count - 1:

                @pl.when(me < count - 1)
                def _():
                    send(0, hop + 1, chunk).start()

            keep_all(me - hop - 1, chunk).start()

        @pl.when(me + hop + 1 < count)
        def _():
            send(1, hop, chunk).wait_recv()
            if hop + 1 < count - 1:

                @pl.when(me > 0)
                def _():
                    send(1, hop + 1, chunk).start()

            keep_all(me + hop + 1, chunk).start()

    for hop in range(count - 2):
        over_chunks(functools.partial(receive, hop))

    @pl.when(here)
    def _():
        copy.wait()

    @pl.when(jnp.logical_not(here))
    def _():
        fetch.wait_recv()

    keep_weight = pltpu.make_async_copy(weight, own_ref, weight_sems.at[3])
    keep_weight.start()

    def last(chunk):
        project(me, chunk)
        for hop in range(count - 1):
            if hop == count - 2:
                receive(hop, chunk)

            @pl.when(me >= hop + 1)
            def _():
                project(me - hop - 1, chunk)

            @pl.when(me + hop + 1 < count)
            def _():
                project(me + hop + 1, chunk)

    over_chunks(last)

    def finish(chunk):
        for hop in range(count - 1):

            @pl.when((me >= hop) & (me < count - 1))
            def _():
                send(0, hop, chunk).wait_send()

            @pl.when((me + hop < count) & (me > 0))
            def _():
                send(1, hop, chunk).wait_send()

        for shard in range(count):
            keep_all(shard, chunk).wait()
            keep_qkv(shard, chunk).wait()

    over_chunks(finish)
    keep_weight.wait()

    @pl.when(here)
    def _():
        fetch.wait_send()


def gather_project(layer_input, gain, bias, weight, half_cols):
    count = lax.axis_size("seq")
    _, rows, width = layer_input.shape
    cols = weight.shape[1]
    chunks = max(1, rows // 128)
    any_spec = pl.BlockSpec(memory_space=pl.ANY)
    vmem = pl.BlockSpec(memory_space=pltpu.VMEM)
    dma = pltpu.SemaphoreType.DMA
    return pl.pallas_call(
        functools.partial(gather_kernel, count, chunks, half_cols),
        in_specs=[any_spec, vmem, vmem, vmem],
        out_specs=[any_spec, any_spec, any_spec],
        out_shape=[
            jax.ShapeDtypeStruct((count, rows, width), BF16),
            jax.ShapeDtypeStruct((count, rows, cols), BF16),
            jax.ShapeDtypeStruct((width, cols), BF16),
        ],
        scratch_shapes=[
            pltpu.VMEM((rows, width), F32),
            pltpu.VMEM((count, rows, width), BF16),
            pltpu.VMEM((count, rows, cols), BF16),
            pltpu.VMEM((width, cols), BF16),
            dma((4,)),
            dma((chunks,)),
            dma((2, count - 1, chunks)),
            dma((2, count - 1, chunks)),
            dma((count, chunks)),
            dma((count, chunks)),
        ],
        compiler_params=pltpu.CompilerParams(
            collective_id=0, has_side_effects=True, vmem_limit_bytes=VMEM_LIMIT
        ),
        cost_estimate=pl.CostEstimate(
            flops=150_000_000_000, bytes_accessed=1, transcendentals=0
        ),
    )(layer_input, gain, bias, weight)


def return_kernel(
    count,
    chunks,
    lag,
    offset,
    parts_ref,
    weight_ref,
    x_ref,
    hidden_grad_ref,
    gain_ref,
    input_ref,
    sums_ref,
    rows_in,
    sending,
    received,
    load_sem,
    send_sems,
    recv_sems,
):
    me = lax.axis_index("seq")
    place = lax.axis_index("mp")
    rows = hidden_grad_ref.shape[0]
    step = rows // chunks
    width = gain_ref.shape[1]
    steps = (count - 1) * chunks

    def at(chunk):
        return pl.ds(pl.multiple_of(chunk * step, step), step)

    load = pltpu.make_async_copy(x_ref.at[place, pl.ds(offset, rows)], rows_in, load_sem.at[0])
    load.start()
    greet(me, count)

    def send(side, message, chunk):
        return pltpu.make_async_remote_copy(
            src_ref=sending.at[side, message, at(chunk)],
            dst_ref=received.at[side, message, at(chunk)],
            send_sem=send_sems.at[side, message, chunk],
            recv_sem=recv_sems.at[side, message, chunk],
            device_id={"seq": me + 1 - 2 * side},
            device_id_type=MESH,
        )

    def flow(side, index):
        message = index // chunks
        chunk = index % chunks
        target = (1 - side) * (count - 1 - message) + side * message

        @pl.when((target - me) * (1 - 2 * side) > 0)
        def _():
            total = dot_nt(parts_ref[target, at(chunk), :], weight_ref[...])
            first = (1 - side) * me + side * (count - 1 - me)

            @pl.when(first == 0)
            def _():
                sending[side, message, at(chunk), :] = total.astype(BF16)

            @pl.when(first > 0)
            def _():
                send(side, message, chunk).wait_recv()
                come = received[side, message, at(chunk), :].astype(F32)
                sending[side, message, at(chunk), :] = (total + come).astype(BF16)

            send(side, message, chunk).start()

    near = me // (count // 2)

    def advance(index, _):
        @pl.when(index < steps)
        def _():
            flow(near, index)

        @pl.when(index >= lag)
        def _():
            flow(1 - near, index - lag)

        return 0

    lax.fori_loop(0, steps + lag, advance, 0)
    load.wait()

    def own(chunk, carried):
        here = at(chunk)
        rows_in_now = rows_in[here, :]
        total = dot_nt(parts_ref[me, here, :], weight_ref[...])

        @pl.when(me > 0)
        def _():
            send(0, count - 1 - me, chunk).wait_recv()

        @pl.when(me < count - 1)
        def _():
            send(1, me, chunk).wait_recv()

        left = received[0, jnp.minimum(count - 1 - me, count - 2), here, :].astype(F32)
        right = received[1, jnp.minimum(me, count - 2), here, :].astype(F32)
        total = total + jnp.where(me > 0, left, 0.0) + jnp.where(me < count - 1, right, 0.0)
        unit, inverse = row_stats(rows_in_now)
        scaled = total * gain_ref[...]
        through = (
            scaled
            - jnp.mean(scaled, axis=-1, keepdims=True)
            - unit * jnp.mean(scaled * unit, axis=-1, keepdims=True)
        )
        input_ref[here, :] = (hidden_grad_ref[here, :] + inverse * through).astype(BF16)
        gain_sum, bias_sum = carried
        return (
            gain_sum + jnp.sum(total * unit, axis=0, keepdims=True),
            bias_sum + jnp.sum(total, axis=0, keepdims=True),
        )

    zero = jnp.zeros((1, width), F32)
    gain_sum, bias_sum = lax.fori_loop(0, chunks, own, (zero, zero))
    sums_ref[...] = jnp.concatenate([gain_sum, bias_sum, jnp.zeros((6, width), F32)], axis=0)

    def finish(index, _):
        message = index // chunks
        chunk = index % chunks

        @pl.when(count - 1 - message > me)
        def _():
            send(0, message, chunk).wait_send()

        @pl.when(message < me)
        def _():
            send(1, message, chunk).wait_send()

        return 0

    lax.fori_loop(0, steps, finish, 0)


def return_part(index, parts, weight, layer_input, hidden_grad, gain):
    count, rows, cols = parts.shape
    rows = rows // 2
    width = weight.shape[0]
    chunks = max(1, rows // 128)
    any_spec = pl.BlockSpec(memory_space=pl.ANY)
    dma = pltpu.SemaphoreType.DMA
    fixed = lambda step: (0, 0)
    return pl.pallas_call(
        functools.partial(return_kernel, count, chunks, 2, index * rows),
        grid=(1,),
        in_specs=[
            pl.BlockSpec((count, rows, cols), lambda step: (0, index, 0)),
            pl.BlockSpec((width, cols), fixed),
            any_spec,
            pl.BlockSpec((rows, width), fixed),
            pl.BlockSpec((1, width), fixed),
        ],
        out_specs=[pl.BlockSpec((rows, width), fixed), pl.BlockSpec((8, width), fixed)],
        out_shape=[
            jax.ShapeDtypeStruct((rows, width), BF16),
            jax.ShapeDtypeStruct((8, width), F32),
        ],
        scratch_shapes=[
            pltpu.VMEM((rows, width), F32),
            pltpu.VMEM((2, count - 1, rows, width), BF16),
            pltpu.VMEM((2, count - 1, rows, width), BF16),
            dma((1,)),
            dma((2, count - 1, chunks)),
            dma((2, count - 1, chunks)),
        ],
        compiler_params=pltpu.CompilerParams(
            collective_id=1 + index, has_side_effects=True, vmem_limit_bytes=VMEM_LIMIT
        ),
        cost_estimate=pl.CostEstimate(flops=80_000_000_000, bytes_accessed=1, transcendentals=0),
    )(parts, weight, layer_input, hidden_grad, gain)


def weight_grad_kernel(
    tile,
    second_ref,
    grad_ref,
    hidden_ref,
    pre_ref,
    act_ref,
    att_ref,
    trade_source,
    up_own,
    up_near,
    down_own,
    down_near,
    out_own,
    out_near,
    trade_target,
    turned,
    slots,
    sending,
    received,
    slot_sems,
    send_sems,
    recv_sems,
    out_sems,
    *trade_sems,
):
    rows, width = second_ref.shape
    units = pre_ref.shape[1]
    me = lax.axis_index("batch")
    place = lax.axis_index("mp")
    parity = me % 2
    mate = me + 1 - 2 * parity
    barrier = pltpu.get_barrier_semaphore()
    pl.semaphore_signal(barrier, inc=1, device_id={"batch": mate}, device_id_type=MESH)
    trade = Trade(trade_source, trade_target, *trade_sems)
    trade.start(1)

    piece = units // 4
    head_piece = width // 4
    jobs = []
    for matrix, source, own, near in ((0, pre_ref, up_own, up_near), (1, act_ref, down_own, down_near)):
        for start in range(0, piece, tile):
            jobs.append(
                (matrix, source, tile, (1 - parity) * piece + start, parity * piece + start, own, start)
            )
        for start in range(0, piece, tile):
            jobs.append((matrix, source, tile, 3 * piece + start, 2 * piece + start, near, start))
    for side, target in ((place, out_own), (1 - place, out_near)):
        first = 2 * side * head_piece
        jobs.append(
            (
                2,
                att_ref,
                head_piece,
                first + (1 - parity) * head_piece,
                first + parity * head_piece,
                target,
                0,
            )
        )
    count = len(jobs)
    order = [(job, 3) for job in range(count)] + [(job, 4) for job in range(count)]

    def fetch(index):
        job, which = order[index]
        _, source, size, *_ = jobs[job]
        start = jobs[job][which]
        return pltpu.make_async_copy(
            source.at[:, pl.ds(pl.multiple_of(start, 128), size)],
            slots.at[index % 2, :, pl.ds(0, size)],
            slot_sems.at[index % 2],
        )

    def exchange(job):
        size = jobs[job][2]
        return pltpu.make_async_remote_copy(
            src_ref=sending.at[job, :, pl.ds(0, size)],
            dst_ref=received.at[job, :, pl.ds(0, size)],
            send_sem=send_sems.at[job],
            recv_sem=recv_sems.at[job],
            device_id={"batch": mate},
            device_id_type=MESH,
        )

    def put(job):
        size, target, start = jobs[job][2], jobs[job][5], jobs[job][6]
        return pltpu.make_async_copy(
            received.at[job, :, pl.ds(0, size)], target.at[:, pl.ds(start, size)], out_sems.at[job]
        )

    fetch(0).start()
    block = min(256, width)
    for matrix, source in enumerate((second_ref, grad_ref, hidden_ref)):

        def turn(index, _):
            here = pl.ds(pl.multiple_of(index * 128, 128), 128)
            turned[matrix, :, here] = source[here, :].T
            return 0

        lax.fori_loop(0, rows // 128, turn, 0)

    for index, (job, which) in enumerate(order):
        matrix, _, size, *_ = jobs[job]
        fetch(index).wait()
        if index + 1 < len(order):
            fetch(index + 1).start()
        if which == 4:
            exchange(job).wait_recv()

        def multiply(part, _):
            here = pl.ds(pl.multiple_of(part * block, block), block)
            total = dot_nn(turned[matrix, here, :], slots[index % 2, :, 0:size])
            if which == 3:
                sending[job, here, 0:size] = total.astype(BF16)
            else:
                total = total + received[job, here, 0:size].astype(F32)
                received[job, here, 0:size] = total.astype(BF16)
            return 0

        lax.fori_loop(0, width // block, multiply, 0)
        if which == 3:
            exchange(job).start()
        else:
            put(job).start()
    for job in range(count):
        exchange(job).wait_send()
        put(job).wait()
    trade.finish()


def weight_grads(second_low, grad_low, hidden_low, pre_grad, activated, attended, source):
    rows, width = second_low.shape
    units = pre_grad.shape[1]
    piece = units // 4
    tile = min(512, piece)
    jobs = 4 * (piece // tile) + 2
    any_spec = pl.BlockSpec(memory_space=pl.ANY)
    vmem = pl.BlockSpec(memory_space=pltpu.VMEM)
    dma = pltpu.SemaphoreType.DMA
    shapes = [(width, piece)] * 4 + [(width, width // 4)] * 2
    return pl.pallas_call(
        functools.partial(weight_grad_kernel, tile),
        in_specs=[vmem] * 3 + [any_spec] * 4,
        out_specs=[any_spec] * 7,
        out_shape=[jax.ShapeDtypeStruct(shape, BF16) for shape in shapes + [source.shape]],
        scratch_shapes=[
            pltpu.VMEM((3, width, rows), BF16),
            pltpu.VMEM((2, rows, tile), BF16),
            pltpu.VMEM((jobs, width, tile), BF16),
            pltpu.VMEM((jobs, width, tile), BF16),
            dma((2,)),
            dma((jobs,)),
            dma((jobs,)),
            dma((jobs,)),
        ]
        + trade_scratch(source.shape[0]),
        compiler_params=pltpu.CompilerParams(
            collective_id=3, has_side_effects=True, vmem_limit_bytes=VMEM_LIMIT
        ),
        cost_estimate=pl.CostEstimate(
            flops=2 * rows * width * (2 * units + width),
            bytes_accessed=4 * rows * units,
            transcendentals=0,
        ),
    )(second_low, grad_low, hidden_low, pre_grad, activated, attended, source)


def swap(value, axis, distance=1):
    size = lax.axis_size(axis)
    return lax.ppermute(value, axis, [(j, j ^ distance) for j in range(size)])


def after(value, *earlier):
    return lax.optimization_barrier((value,) + earlier)[0]


def all_to_all(value):
    return lax.all_to_all(value, "seq", 0, 0, tiled=True)


def halves(value):
    return jnp.split(value, 2, axis=1)


def trade_pieces(value):
    place, count = lax.axis_index("seq"), lax.axis_size("seq")
    pieces = [pick(value, place, count)]
    for distance in range(1, count):
        pairs = [(j, (j + distance) % count) for j in range(count)]
        pieces.append(
            lax.ppermute(pick(value, (place + distance) % count, count), "seq", pairs)
        )
    return pieces


def place_pieces(pieces):
    place, count = lax.axis_index("seq"), len(pieces)
    whole = jnp.concatenate(pieces, axis=0)
    return jnp.roll(whole[::-1], place + 1, axis=0)


def levels_of(axis):
    return [1 << level for level in range(lax.axis_size(axis).bit_length() - 1)]


def sum_everywhere(value):
    for axis in ("batch", "seq", "mp"):
        for distance in levels_of(axis):
            value = value + swap(value, axis, distance)
    return value


def gather_small(value):
    place = lax.axis_index("seq")
    count = lax.axis_size("seq")
    parts = [value] + [swap(value, "seq", distance) for distance in range(1, count)]
    stacked = jnp.stack(parts)
    order = jnp.arange(count, dtype=jnp.int32) ^ place
    return jnp.take(stacked, order, axis=0).reshape((-1,) + value.shape[1:])


def pick(value, index, count, axis=0):
    size = value.shape[axis] // count
    return lax.dynamic_slice_in_dim(value, index * size, size, axis)


def fetch_near(weight, axis):
    return swap(pick(weight, lax.axis_index("batch") % 2, 2, axis), "mp")


def narrow_add(mine, received):
    return (mine.astype(F32) + received.astype(F32)).astype(BF16)


def halve(value, distance, axis):
    side = (lax.axis_index("batch") // distance) % 2
    return narrow_add(
        pick(value, side, 2, axis), swap(pick(value, 1 - side, 2, axis), "batch", distance)
    )


def unhalve(value, distance, axis):
    side = (lax.axis_index("batch") // distance) % 2
    other = swap(value, "batch", distance)
    low = jnp.where(side == 0, value, other)
    high = jnp.where(side == 0, other, value)
    return jnp.concatenate([low, high], axis=axis)


def spread_batch(value, axis):
    for distance in reversed(levels_of("batch")):
        value = unhalve(value, distance, axis)
    return value.astype(F32)


def place_kernel(place_ref, own_first, own_second, other_first, other_second, out_ref):
    place = place_ref[0]

    @pl.when(pl.program_id(0) == 0)
    def _():
        out_ref[place] = own_first[...].astype(F32)
        out_ref[1 - place] = other_first[...].astype(F32)

    @pl.when(pl.program_id(0) == 1)
    def _():
        out_ref[place] = own_second[...].astype(F32)
        out_ref[1 - place] = other_second[...].astype(F32)


def both_sequences(own):
    other = [swap(part, "mp") for part in own]
    rows, width = own[0].shape
    step = min(256, rows)
    steps = rows // step
    first = pl.BlockSpec(
        (step, width), lambda half, index, place_ref: (index * (1 - half) + (steps - 1) * half, 0)
    )
    second = pl.BlockSpec((step, width), lambda half, index, place_ref: (index * half, 0))
    return pl.pallas_call(
        place_kernel,
        grid_spec=pltpu.PrefetchScalarGridSpec(
            num_scalar_prefetch=1,
            grid=(2, steps),
            in_specs=[first, second, first, second],
            out_specs=pl.BlockSpec(
                (2, step, width), lambda half, index, place_ref: (0, half * steps + index, 0)
            ),
        ),
        out_shape=jax.ShapeDtypeStruct((2, 2 * rows, width), F32),
    )(lax.axis_index("mp").astype(jnp.int32)[None], *own, *other)


def local(
    layer_input,
    lengths,
    random_blocks,
    first_gain,
    first_bias,
    qkv_weight,
    out_weight,
    second_gain,
    second_bias,
    up_weight,
    up_bias,
    down_weight,
    down_bias,
    cotangent,
):
    seq_count = lax.axis_size("seq")
    seq_index = lax.axis_index("seq")
    mp_index = lax.axis_index("mp")
    parity = lax.axis_index("batch") % 2
    _, local_rows, width = layer_input.shape
    rows_total = local_rows * seq_count
    blocks = rows_total // BLOCK
    half_cols = qkv_weight.shape[2]
    cols = width // seq_count
    units = up_weight.shape[1]

    doc_ends = jnp.cumsum(lax.dynamic_index_in_dim(lengths, mp_index, 0, keepdims=False))
    randoms = lax.dynamic_index_in_dim(random_blocks, mp_index, 0, keepdims=False)
    randoms = gather_small(randoms)
    lists, admits = block_lists(jnp.arange(blocks, dtype=jnp.int32), randoms, blocks)
    lists, admits = lists.reshape(-1), admits.reshape(-1)

    qkv_near = lax.dynamic_slice_in_dim(qkv_weight, (seq_index * cols) % half_cols, cols, 2)
    qkv_near = qkv_near.reshape(width, 3 * cols)
    up_near = fetch_near(up_weight, 1)
    bias_near = fetch_near(up_bias, 0)
    out_other = swap(out_weight, "mp")

    first_all, qkv, qkv_own = gather_project(
        layer_input, first_gain[None], first_bias[None], qkv_near, half_cols
    )
    first_all = first_all.reshape(rows_total, width)
    qkv, up_near, out_other, bias_near, lists, down_cut = lax.optimization_barrier(
        (qkv.reshape(rows_total, 3 * cols), up_near, out_other, bias_near, lists, down_weight)
    )
    up_far, bias_far = swap(up_near, "batch"), swap(bias_near, "batch")
    down_near = fetch_near(down_cut, 0)
    attended_first, lse_first = attention_forward(0, qkv, doc_ends, lists, admits, seq_count)
    att_pieces = trade_pieces(attended_first)
    attended_second, lse_second = attention_forward(1, qkv, doc_ends, lists, admits, seq_count)
    *att_pieces, attended_second = lax.optimization_barrier((*att_pieces, attended_second))
    att_first = place_pieces(att_pieces)
    att_first, up_far, down_near, bias_far = lax.optimization_barrier(
        (att_first, up_far, down_near, bias_far)
    )
    down_far = swap(down_near, "batch")
    bias_full = jnp.concatenate([up_bias, bias_near, bias_far])[None]
    outs = [part.reshape(seq_count // 2, cols, width) for part in (out_weight, out_other)]
    kept, results = None, []
    att, source = att_first, attended_second
    for index in range(2):
        result = token_part(
            index,
            doc_ends,
            att,
            layer_input,
            cotangent,
            outs,
            (up_weight, up_near, up_far),
            (down_weight, down_near, down_far),
            bias_full,
            second_gain[None],
            second_bias[None],
            down_bias[None],
            source,
            kept,
        )
        kept = result[3:9]
        results.append(result[:3] + result[9:])
        att, source = result[11], result[2]
    grad_first = att
    activated, pre_grad, second_low, hidden_low, grad_low, attended_low = kept
    sums = results[0][3][:3] + results[1][3][:3]
    unit_sums = results[0][4][0] + results[1][4][0]
    bias_sums = [unit_sums[:units], unit_sums[units : units * 3 // 2], unit_sums[units * 3 // 2 :]]
    layer_output = both_sequences([result[0] for result in results])
    up_own, up_near, down_own, down_near, out_own, out_near, grad_second = weight_grads(
        second_low, grad_low, hidden_low, pre_grad, activated, attended_low, source
    )
    bias_other = jnp.where(
        parity == 0,
        jnp.concatenate([bias_sums[1], bias_sums[2]]),
        jnp.concatenate([bias_sums[2], bias_sums[1]]),
    )
    bias_all = jnp.where(
        mp_index == 0,
        jnp.concatenate([bias_sums[0], bias_other]),
        jnp.concatenate([bias_other, bias_sums[0]]),
    )
    early = sum_everywhere(jnp.concatenate([sums.reshape(-1), bias_all]))
    levels = levels_of("batch")
    for distance in levels[1:]:
        up_own, up_near = halve(up_own, distance, 1), halve(up_near, distance, 1)
        out_own, out_near = halve(out_own, distance, 1), halve(out_near, distance, 1)
    down_own = narrow_add(down_own, swap(down_near, "mp"))
    qkv_low_grad = attention_backward(
        qkv,
        (attended_first, attended_second),
        (grad_first, grad_second),
        (lse_first, lse_second),
        doc_ends,
        lists,
        admits,
    )
    qkv_sum = dot_tn(first_all, qkv_low_grad).astype(BF16)
    qkv_sum = qkv_sum.reshape(seq_count, -1, 3 * cols).transpose(1, 0, 2)
    qkv_low_grad, qkv_sum, up_own, up_near, down_own, out_own, out_near = lax.optimization_barrier(
        (qkv_low_grad, qkv_sum, up_own, up_near, down_own, out_own, out_near)
    )
    up_own = narrow_add(up_own, swap(up_near, "mp"))
    out_own = narrow_add(out_own, swap(out_near, "mp"))
    for distance in levels[1:]:
        down_own = halve(down_own, distance, 1)
    qkv_part = halve(qkv_sum, levels[0], 0)
    parts = qkv_low_grad.reshape(seq_count, local_rows, 3 * cols)
    input_first, first_sums = return_part(
        0, parts, qkv_own, layer_input, results[0][1], first_gain[None]
    )
    second_grad, input_first, up_own, down_own, out_own, qkv_part = lax.optimization_barrier(
        (results[1][1], input_first, up_own, down_own, out_own, qkv_part)
    )
    up_grad, down_grad, out_grad = [
        lax.psum_scatter(own, "seq", scatter_dimension=0, tiled=True)
        for own in (up_own, down_own, out_own)
    ]
    for distance in levels[1:]:
        qkv_part = halve(qkv_part, distance, 0)
    input_second, second_sums = return_part(
        1, parts, qkv_own, layer_input, second_grad, first_gain[None]
    )
    input_second, qkv_part, down_grad, up_grad, out_grad = lax.optimization_barrier(
        (input_second, qkv_part, down_grad, up_grad, out_grad)
    )
    late = sum_everywhere((first_sums + second_sums)[:2])
    qkv_part = narrow_add(qkv_part, swap(qkv_part, "mp"))
    qkv_part = all_to_all(qkv_part.transpose(1, 0, 2))
    qkv_part = pick(qkv_part, mp_index, 2)
    qkv_part = qkv_part.reshape(seq_count // 2, -1, 3, cols).transpose(1, 2, 0, 3)
    qkv_grad = spread_batch(qkv_part.reshape(-1, 3, half_cols), 0)
    up_grad, down_grad, out_grad = [
        spread_batch(grad, 1) for grad in (up_grad, down_grad, out_grad)
    ]
    input_grad = both_sequences([input_first, input_second])
    up_bias_grad = lax.dynamic_slice_in_dim(early, 3 * width + mp_index * units, units)
    return (
        layer_output,
        input_grad,
        late[0],
        late[1],
        qkv_grad,
        out_grad.T,
        early[width : 2 * width],
        early[2 * width : 3 * width],
        up_grad,
        up_bias_grad,
        down_grad.T,
        early[:width],
    )


MB = 2
NBLK = 64
LEN = 4096
HIGH = lax.Precision.HIGHEST


def segment_of(places, doc_ends):
    return jnp.sum((places[..., None] >= doc_ends).astype(jnp.int32), axis=-1)


def block_lists_by_index(blocks, randoms):
    leading = randoms.shape[:-1]
    globals_part = jnp.broadcast_to(jnp.arange(GLOB, dtype=jnp.int32), leading + (GLOB,))
    window_part = jnp.broadcast_to(
        blocks[:, None] + jnp.arange(WIN, dtype=jnp.int32) - WIN // 2, leading + (WIN,)
    )
    block_list = jnp.concatenate([globals_part, window_part, randoms], axis=-1)
    inside = (block_list >= 0) & (block_list < NBLK)
    same_entry = block_list[..., :, None] == block_list[..., None, :]
    order_ids = jnp.arange(LIST)
    earlier = order_ids[None, :] < order_ids[:, None]
    repeated = jnp.any(same_entry & earlier, axis=-1)
    return (block_list, inside & jnp.logical_not(repeated))


def fetch_rows(key_rows, values, wanted):
    batch_seqs, local_rows, head_cols = key_rows.shape
    total_rows = local_rows * lax.axis_size("seq")
    empty_rows = jnp.zeros((batch_seqs, wanted.shape[1], head_cols), jnp.bfloat16)
    initial = (empty_rows, empty_rows)
    empty_whole = jnp.zeros((batch_seqs, total_rows, head_cols), jnp.bfloat16)
    initial = initial + (empty_whole, empty_whole)
    shards_in = (
        lax.all_gather(key_rows, "seq", axis=1, tiled=True),
        lax.all_gather(values, "seq", axis=1, tiled=True),
    )
    piece_rows = shards_in[0].shape[1]
    inside = ((wanted >= 0) & (wanted < piece_rows))[..., None]
    take_index = jnp.clip(wanted, 0, piece_rows - 1)[..., None]
    picked = tuple(
        (
            jnp.where(inside, jnp.take_along_axis(source, take_index, axis=1), previous)
            for source, previous in zip(shards_in, initial[:2])
        )
    )
    placed = tuple((source for source in shards_in))
    return picked + placed


def scatter_rows(kv_source):
    return lax.psum_scatter(
        kv_source.astype(jnp.bfloat16), "seq", scatter_dimension=0, tiled=True
    ).astype(jnp.float32)


def global_partial(seq_item):
    query_rows, key_rows, value_rows, keep_mask = seq_item
    head_count = query_rows.shape[1] // HD
    query_heads = query_rows.reshape(query_rows.shape[0], head_count, HD)
    key_heads = key_rows.reshape(key_rows.shape[0], head_count, HD)
    value_heads = value_rows.astype(jnp.float32).reshape(value_rows.shape[0], head_count, HD)
    raw_scores = jnp.einsum(
        "qhd,khd->hqk", query_heads, key_heads, preferred_element_type=jnp.float32
    ) * HD ** (-0.5)
    masked = jnp.where(keep_mask[None], raw_scores, NEG)
    row_top = jnp.max(masked, axis=-1)
    weights = jnp.exp(masked - row_top[..., None]) * keep_mask[None].astype(jnp.float32)
    numer = jnp.einsum("hqk,khd->hqd", weights, value_heads, precision=HIGH)
    return (row_top, jnp.sum(weights, axis=-1), numer)


def global_back(seq_item):
    query_rows, key_rows, value_rows, keep_mask, row_top, row_total, glob_out, glob_grad = seq_item
    row_count, head_cols = query_rows.shape
    head_count = head_cols // HD
    query_heads = query_rows.reshape(row_count, head_count, HD)
    key_heads = key_rows.reshape(key_rows.shape[0], head_count, HD)
    value_heads = value_rows.astype(jnp.float32).reshape(value_rows.shape[0], head_count, HD)
    raw_scores = jnp.einsum(
        "qhd,khd->hqk", query_heads, key_heads, preferred_element_type=jnp.float32
    ) * HD ** (-0.5)
    masked = jnp.where(keep_mask[None], raw_scores, NEG)
    probs_glob = (
        jnp.exp(masked - row_top[..., None])
        * keep_mask[None].astype(jnp.float32)
        / row_total[..., None]
    )
    grad_heads = glob_grad.astype(jnp.float32).reshape(row_count, head_count, HD)
    prob_grad = jnp.einsum("qhd,khd->hqk", grad_heads, value_heads, precision=HIGH)
    delta = jnp.einsum("qhd,hqd->hq", grad_heads, glob_out, precision=HIGH)
    score_grad = (probs_glob * (prob_grad - delta[..., None])).astype(jnp.bfloat16)
    query_grad = jnp.einsum(
        "hqk,khd->qhd", score_grad, key_heads, preferred_element_type=jnp.float32
    ) * HD ** (-0.5)
    key_grad = jnp.einsum(
        "hqk,qhd->khd", score_grad, query_heads, preferred_element_type=jnp.float32
    ) * HD ** (-0.5)
    value_grad = jnp.einsum("hqk,qhd->khd", probs_glob, grad_heads, precision=HIGH)
    return (
        query_grad.reshape(row_count, head_cols),
        key_grad.reshape(-1, head_cols),
        value_grad.reshape(-1, head_cols),
    )


def local_by_blocks(
    layer_input,
    lengths,
    random_blocks,
    first_gain,
    first_bias,
    qkv_weight,
    out_weight,
    second_gain,
    second_bias,
    up_weight,
    up_bias,
    down_weight,
    down_bias,
    cotangent,
):
    seq_index = lax.axis_index("seq")
    local_seqs, local_rows, model_width = layer_input.shape
    blocks_dev = local_rows // BLOCK
    head_cols = qkv_weight.shape[2]
    head_count = head_cols // HD
    unit_cols = up_weight.shape[1]
    score_scale = HD ** (-0.5)
    glob_rows = GLOB * BLOCK
    batch_seqs = local_seqs // MB
    picked_rows = blocks_dev * LIST * BLOCK
    qkv_flat = qkv_weight.reshape(model_width, 3 * head_cols)
    doc_ends = jnp.cumsum(lengths, axis=1)
    places = seq_index * local_rows + jnp.arange(local_rows, dtype=jnp.int32)
    seg_local = segment_of(places[None, :], doc_ends[:, None, :])
    valid_rows = (places[None, :] < doc_ends[:, -1:]).astype(jnp.float32)
    glob_flag = (places < glob_rows)[None, :, None]
    query_blocks = seq_index * blocks_dev + jnp.arange(blocks_dev, dtype=jnp.int32)
    block_list, admitted = block_lists_by_index(query_blocks, random_blocks)
    key_places = block_list[..., None] * BLOCK + jnp.arange(BLOCK, dtype=jnp.int32)
    key_segs = segment_of(key_places, doc_ends[:, None, None, None, :]).reshape(
        local_seqs, blocks_dev, LIST * BLOCK
    )
    admit_keys = jnp.broadcast_to(admitted[..., None], key_places.shape).reshape(
        local_seqs, blocks_dev, LIST * BLOCK
    )
    query_segs = seg_local.reshape(local_seqs, blocks_dev, BLOCK)
    list_mask = admit_keys[:, :, None, :] & (query_segs[..., None] == key_segs[:, :, None, :])
    wanted_all = jnp.clip(key_places, 0, LEN - 1).reshape(local_seqs, picked_rows)
    glob_segs = segment_of(jnp.arange(glob_rows, dtype=jnp.int32)[None, :], doc_ends[:, None, :])
    qkv_total = jnp.zeros((model_width, 3 * head_cols), jnp.float32)
    out_total = jnp.zeros(out_weight.shape, jnp.float32)
    up_total = jnp.zeros(up_weight.shape, jnp.float32)
    down_total = jnp.zeros(down_weight.shape, jnp.float32)
    gain_one_total = jnp.zeros((model_width,), jnp.float32)
    bias_one_total = jnp.zeros((model_width,), jnp.float32)
    gain_two_total = jnp.zeros((model_width,), jnp.float32)
    bias_two_total = jnp.zeros((model_width,), jnp.float32)
    up_bias_total = jnp.zeros((unit_cols,), jnp.float32)
    down_bias_total = jnp.zeros((model_width,), jnp.float32)
    outputs_all = []
    input_grads = []
    for micro_index in range(MB):
        first_seq = micro_index * batch_seqs
        last_seq = first_seq + batch_seqs
        rows_in = layer_input[first_seq:last_seq]
        ends_now = doc_ends[first_seq:last_seq]
        valid_now = valid_rows[first_seq:last_seq]
        mask_now = list_mask[first_seq:last_seq]
        wanted = wanted_all[first_seq:last_seq]
        glob_segs_now = glob_segs[first_seq:last_seq]
        normed_one, inverse_one = norm_stats(rows_in)
        first_low = (
            (normed_one * first_gain + first_bias).astype(jnp.bfloat16).reshape(-1, model_width)
        )
        qkv_rows = (
            jnp.dot(first_low, qkv_flat, preferred_element_type=jnp.float32)
            .astype(jnp.bfloat16)
            .reshape(batch_seqs, local_rows, 3, head_cols)
        )
        queries = qkv_rows[:, :, 0]
        key_rows = qkv_rows[:, :, 1]
        values = qkv_rows[:, :, 2]
        glob_queries_own = queries[:, :glob_rows]
        picked_keys, picked_values, whole_keys, whole_values = fetch_rows(key_rows, values, wanted)
        glob_queries = glob_queries_own
        seg_whole = segment_of(jnp.arange(LEN, dtype=jnp.int32)[None, :], ends_now[:, None, :])
        glob_mask = glob_segs_now[:, :, None] == seg_whole[:, None, :]

        def global_here():
            return lax.map(global_partial, (glob_queries, whole_keys, whole_values, glob_mask))

        def global_skip():
            return (
                jnp.zeros((batch_seqs, head_count, glob_rows), jnp.float32),
                jnp.ones((batch_seqs, head_count, glob_rows), jnp.float32),
                jnp.zeros((batch_seqs, head_count, glob_rows, HD), jnp.float32),
            )

        glob_top, glob_total, glob_numer = lax.cond(seq_index == 0, global_here, global_skip)
        glob_out = glob_numer / glob_total[..., None]
        query_split = queries.reshape(batch_seqs, blocks_dev, BLOCK, head_count, HD)
        key_split = picked_keys.reshape(batch_seqs, blocks_dev, LIST * BLOCK, head_count, HD)
        value_split = picked_values.reshape(batch_seqs, blocks_dev, LIST * BLOCK, head_count, HD)
        raw_scores = (
            jnp.einsum(
                "sbqhd,sbkhd->sbhqk", query_split, key_split, preferred_element_type=jnp.float32
            )
            * score_scale
        )
        keep_now = mask_now[:, :, None]
        masked = jnp.where(keep_now, raw_scores, NEG)
        row_top = jnp.max(masked, axis=-1, keepdims=True)
        weights = jnp.exp(masked - row_top) * keep_now.astype(jnp.float32)
        row_total = jnp.sum(weights, axis=-1, keepdims=True)
        probs_list = weights / row_total
        probs_low = probs_list.astype(jnp.bfloat16)
        listed = jnp.einsum(
            "sbhqk,sbkhd->sbqhd", probs_low, value_split, preferred_element_type=jnp.float32
        ).reshape(batch_seqs, local_rows, head_cols)
        glob_rows_out = jnp.transpose(glob_out, (0, 2, 1, 3)).reshape(
            batch_seqs, glob_rows, head_cols
        )
        glob_full = jnp.pad(glob_rows_out, ((0, 0), (0, local_rows - glob_rows), (0, 0)))
        attended = jnp.where(glob_flag, glob_full, listed) * valid_now[..., None]
        attended_low = attended.astype(jnp.bfloat16).reshape(-1, head_cols)
        branch = lax.psum(
            jnp.dot(attended_low, out_weight, preferred_element_type=jnp.float32).astype(
                jnp.bfloat16
            ),
            "mp",
        ).astype(jnp.float32)
        hidden = rows_in + branch.reshape(rows_in.shape)
        normed_two, inverse_two = norm_stats(hidden)
        second_low = (
            (normed_two * second_gain + second_bias).astype(jnp.bfloat16).reshape(-1, model_width)
        )
        pre_act = jnp.dot(second_low, up_weight, preferred_element_type=jnp.float32) + up_bias
        activated = jax.nn.gelu(pre_act, approximate=True).astype(jnp.bfloat16)
        ffn_branch = lax.psum(
            jnp.dot(activated, down_weight, preferred_element_type=jnp.float32).astype(
                jnp.bfloat16
            ),
            "mp",
        ).astype(jnp.float32)
        outputs_all.append(hidden + ffn_branch.reshape(rows_in.shape) + down_bias)
        grad_rows = cotangent[first_seq:last_seq].reshape(-1, model_width)
        down_bias_total = down_bias_total + jnp.sum(grad_rows, axis=0)
        grad_low = grad_rows.astype(jnp.bfloat16)
        down_total = down_total + jnp.einsum(
            "rf,rd->fd", activated, grad_low, preferred_element_type=jnp.float32
        )
        act_grad = jnp.einsum(
            "rd,fd->rf", grad_low, down_weight, preferred_element_type=jnp.float32
        )
        _, gelu_pull = jax.vjp(lambda inner: jax.nn.gelu(inner, approximate=True), pre_act)
        pre_grad = gelu_pull(act_grad)[0].astype(jnp.bfloat16)
        up_bias_total = up_bias_total + jnp.sum(pre_grad.astype(jnp.float32), axis=0)
        up_total = up_total + jnp.einsum(
            "rd,rf->df", second_low, pre_grad, preferred_element_type=jnp.float32
        )
        second_grad = (
            lax.psum(
                jnp.einsum(
                    "rf,df->rd", pre_grad, up_weight, preferred_element_type=jnp.float32
                ).astype(jnp.bfloat16),
                "mp",
            )
            .astype(jnp.float32)
            .reshape(rows_in.shape)
        )
        gain_two_total = gain_two_total + jnp.sum(second_grad * normed_two, axis=(0, 1))
        bias_two_total = bias_two_total + jnp.sum(second_grad, axis=(0, 1))
        hidden_grad = grad_rows.reshape(rows_in.shape) + norm_back(
            second_grad, normed_two, inverse_two, second_gain
        )
        hidden_low = hidden_grad.astype(jnp.bfloat16).reshape(-1, model_width)
        out_total = out_total + jnp.einsum(
            "rc,rd->cd", attended_low, hidden_low, preferred_element_type=jnp.float32
        )
        attended_grad = jnp.einsum(
            "rd,cd->rc", hidden_low, out_weight, preferred_element_type=jnp.float32
        ).astype(jnp.bfloat16).reshape(batch_seqs, local_rows, head_cols) * valid_now[
            ..., None
        ].astype(
            jnp.bfloat16
        )
        list_grad = jnp.where(glob_flag, jnp.zeros_like(attended_grad), attended_grad).reshape(
            batch_seqs, blocks_dev, BLOCK, head_count, HD
        )
        prob_grad = jnp.einsum(
            "sbqhd,sbkhd->sbhqk", list_grad, value_split, preferred_element_type=jnp.float32
        )
        delta = jnp.sum(probs_list * prob_grad, axis=-1, keepdims=True)
        score_grad = (probs_list * (prob_grad - delta)).astype(jnp.bfloat16)
        query_grad = (
            jnp.einsum(
                "sbhqk,sbkhd->sbqhd", score_grad, key_split, preferred_element_type=jnp.float32
            )
            * score_scale
        ).reshape(batch_seqs, local_rows, head_cols)
        key_picked_grad = (
            jnp.einsum(
                "sbhqk,sbqhd->sbkhd", score_grad, query_split, preferred_element_type=jnp.float32
            )
            * score_scale
        )
        value_picked_grad = jnp.einsum(
            "sbhqk,sbqhd->sbkhd", probs_low, list_grad, preferred_element_type=jnp.float32
        )
        picked_grads = jnp.concatenate(
            [
                key_picked_grad.reshape(batch_seqs, picked_rows, head_cols),
                value_picked_grad.reshape(batch_seqs, picked_rows, head_cols),
            ],
            axis=-1,
        )
        seg_ids = wanted * batch_seqs + jnp.arange(batch_seqs, dtype=jnp.int32)[:, None]
        kv_term = jax.ops.segment_sum(
            picked_grads.reshape(batch_seqs * picked_rows, 2 * head_cols),
            seg_ids.reshape(-1),
            num_segments=LEN * batch_seqs,
        ).reshape(LEN, batch_seqs, 2 * head_cols)
        glob_grad_own = attended_grad[:, :glob_rows]

        def back_here():
            return lax.map(
                global_back,
                (
                    glob_queries,
                    whole_keys,
                    whole_values,
                    glob_mask,
                    glob_top,
                    glob_total,
                    glob_out,
                    glob_grad_own,
                ),
            )

        def back_skip():
            return (
                jnp.zeros((batch_seqs, glob_rows, head_cols), jnp.float32),
                jnp.zeros((batch_seqs, LEN, head_cols), jnp.float32),
                jnp.zeros((batch_seqs, LEN, head_cols), jnp.float32),
            )

        glob_query_grad, whole_key_grad, whole_value_grad = lax.cond(
            seq_index == 0, back_here, back_skip
        )
        glob_dense = jnp.transpose(
            jnp.concatenate([whole_key_grad, whole_value_grad], axis=-1), (1, 0, 2)
        )
        kv_source = kv_term + glob_dense
        kv_grad = jnp.transpose(scatter_rows(kv_source), (1, 0, 2))
        glob_query_full = jnp.pad(glob_query_grad, ((0, 0), (0, local_rows - glob_rows), (0, 0)))
        query_total = query_grad + jnp.where(glob_flag, glob_query_full, 0.0)
        qkv_low_grad = (
            jnp.stack([query_total, kv_grad[..., :head_cols], kv_grad[..., head_cols:]], axis=2)
            .astype(jnp.bfloat16)
            .reshape(-1, 3 * head_cols)
        )
        qkv_total = qkv_total + jnp.einsum(
            "rd,rc->dc", first_low, qkv_low_grad, preferred_element_type=jnp.float32
        )
        first_grad = (
            lax.psum(
                jnp.einsum(
                    "rc,dc->rd", qkv_low_grad, qkv_flat, preferred_element_type=jnp.float32
                ).astype(jnp.bfloat16),
                "mp",
            )
            .astype(jnp.float32)
            .reshape(rows_in.shape)
        )
        gain_one_total = gain_one_total + jnp.sum(first_grad * normed_one, axis=(0, 1))
        bias_one_total = bias_one_total + jnp.sum(first_grad, axis=(0, 1))
        input_grads.append(hidden_grad + norm_back(first_grad, normed_one, inverse_one, first_gain))
    matrix_grads = (
        lax.psum_scatter(
            qkv_total.reshape(model_width, 3, head_cols).astype(jnp.bfloat16),
            "seq",
            scatter_dimension=0,
            tiled=True,
        ).astype(jnp.float32),
        lax.psum_scatter(
            out_total.astype(jnp.bfloat16), "seq", scatter_dimension=1, tiled=True
        ).astype(jnp.float32),
        lax.psum_scatter(
            up_total.astype(jnp.bfloat16), "seq", scatter_dimension=0, tiled=True
        ).astype(jnp.float32),
        lax.psum_scatter(
            down_total.astype(jnp.bfloat16), "seq", scatter_dimension=1, tiled=True
        ).astype(jnp.float32),
    )
    matrix_grads = (
        lax.psum(matrix_grads[0].astype(jnp.bfloat16), "batch").astype(jnp.float32),
        lax.psum(matrix_grads[1].astype(jnp.bfloat16), "batch").astype(jnp.float32),
        lax.psum(matrix_grads[2].astype(jnp.bfloat16), "batch").astype(jnp.float32),
        lax.psum(matrix_grads[3].astype(jnp.bfloat16), "batch").astype(jnp.float32),
    )
    vector_grads = lax.psum(
        (
            gain_one_total,
            bias_one_total,
            gain_two_total,
            bias_two_total,
            up_bias_total,
            down_bias_total,
        ),
        ("seq", "batch"),
    )
    return (
        jnp.concatenate(outputs_all, axis=0),
        jnp.concatenate(input_grads, axis=0),
        vector_grads[0],
        vector_grads[1],
        matrix_grads[0],
        matrix_grads[1],
        vector_grads[2],
        vector_grads[3],
        matrix_grads[2],
        vector_grads[4],
        matrix_grads[3],
        vector_grads[5],
    )


def solution(mesh):
    placed = (
        P("batch", "seq", None),
        P("batch", None),
        P("batch", "seq", None),
        P(),
        P(),
        P(None, None, "mp"),
        P("mp", None),
        P(),
        P(),
        P(None, "mp"),
        P("mp"),
        P("mp", None),
        P(),
        P("batch", "seq", None),
    )
    by_heads = (1024 // mesh.shape["seq"]) % 128 == 0
    return jax.shard_map(
        local if by_heads else local_by_blocks,
        mesh=mesh,
        in_specs=placed,
        out_specs=(
            P("batch", "seq", None),
            P("batch", "seq", None),
            P(),
            P(),
            P("seq", None, "mp"),
            P("mp", "seq"),
            P(),
            P(),
            P("seq", "mp"),
            P("mp"),
            P("mp", "seq"),
            P(),
        ),
        check_vma=False,
    )
```

```python
import functools

import jax
import jax.numpy as jnp
from jax import lax
from jax.experimental import pallas as pl
from jax.experimental.pallas import tpu as pltpu
from jax.sharding import PartitionSpec as P

BLOCK = 64
GLOB = 2
WIN = 3
HD = 64
LIST = 8

NEG = -1e30
EPS = 1e-05
F32 = jnp.float32
BF16 = jnp.bfloat16
VMEM_LIMIT = 60 * 1024 * 1024


def norm_stats(rows):
    centre = rows - jnp.mean(rows, axis=-1, keepdims=True)
    spread = jnp.mean(centre * centre, axis=-1, keepdims=True)
    inverse = lax.rsqrt(spread + EPS)
    return (centre * inverse, inverse)


def norm_back(grad_out, normed, inverse, gain):
    scaled = grad_out * gain
    return inverse * (
        scaled
        - jnp.mean(scaled, axis=-1, keepdims=True)
        - normed * jnp.mean(scaled * normed, axis=-1, keepdims=True)
    )


def block_lists(blocks, randoms, block_count):
    leading = randoms.shape[:-1]
    globals_part = jnp.broadcast_to(jnp.arange(GLOB, dtype=jnp.int32), leading + (GLOB,))
    window_part = jnp.broadcast_to(
        blocks[:, None] + jnp.arange(WIN, dtype=jnp.int32) - WIN // 2, leading + (WIN,)
    )
    block_list = jnp.concatenate([globals_part, window_part, randoms], axis=-1)
    inside = (block_list >= 0) & (block_list < block_count)
    same_entry = block_list[..., :, None] == block_list[..., None, :]
    order_ids = jnp.arange(LIST)
    earlier = order_ids[None, :] < order_ids[:, None]
    repeated = jnp.any(same_entry & earlier, axis=-1)
    admitted = inside & jnp.logical_not(repeated)
    return (jnp.clip(block_list, 0, block_count - 1), admitted.astype(jnp.int32))


MESH = pl.DeviceIdType.MESH


class Trade:
    def __init__(self, source, target, send_sems, recv_sems, own_sem, pair=None):
        self.source, self.target, self.pair = source, target, pair
        self.send_sems, self.recv_sems, self.own_sem = send_sems, recv_sems, own_sem
        self.count = source.shape[0]
        self.me = lax.axis_index("seq")

    def greet(self, others):
        barrier = pltpu.get_barrier_semaphore()
        for distance in range(1, self.count):
            other = lax.rem(self.me + distance, self.count)
            pl.semaphore_signal(barrier, inc=1, device_id={"seq": other}, device_id_type=MESH)
        if self.pair is not None:
            partner = 1 - lax.axis_index("mp")
            pl.semaphore_signal(barrier, inc=1, device_id={"mp": partner}, device_id_type=MESH)
            others = others + 1
        pl.semaphore_wait(barrier, self.count - 1 + others)

    def copy(self, distance):
        other = lax.rem(self.me + distance, self.count)
        return pltpu.make_async_remote_copy(
            src_ref=self.source.at[other],
            dst_ref=self.target.at[self.me],
            send_sem=self.send_sems.at[distance - 1],
            recv_sem=self.recv_sems.at[distance - 1],
            device_id={"seq": other},
            device_id_type=MESH,
        )

    def pair_copy(self):
        source, target, sems = self.pair
        return pltpu.make_async_remote_copy(
            src_ref=source,
            dst_ref=target,
            send_sem=sems.at[0],
            recv_sem=sems.at[1],
            device_id={"mp": 1 - lax.axis_index("mp")},
            device_id_type=MESH,
        )

    def own(self):
        return pltpu.make_async_copy(
            self.source.at[self.me], self.target.at[self.me], self.own_sem.at[0]
        )

    def start(self, others=0):
        self.greet(others)
        for distance in range(1, self.count):
            self.copy(distance).start()
        if self.pair is not None:
            self.pair_copy().start()
        self.own().start()

    def finish(self):
        for distance in range(1, self.count):
            self.copy(distance).wait()
        if self.pair is not None:
            self.pair_copy().wait()
        self.own().wait()


def trade_scratch(count):
    dma = pltpu.SemaphoreType.DMA
    return [dma((count - 1,)), dma((count - 1,)), dma((1,))]


def segment_at(places, ends_ref):
    total = jnp.zeros(places.shape, jnp.int32)
    for doc in range(ends_ref.shape[0]):
        total = total + (places >= ends_ref[doc]).astype(jnp.int32)
    return total


def head_spread(rows, heads):
    lane_head = lax.broadcasted_iota(jnp.int32, (1, rows.shape[1]), 1) // HD
    return jnp.concatenate(
        [rows * (lane_head == head).astype(F32).astype(rows.dtype) for head in range(heads)], axis=0
    )


def head_fold(wide, heads):
    rows = wide.shape[0] // heads
    lane_head = lax.broadcasted_iota(jnp.int32, (rows, wide.shape[1]), 1) // HD
    folded = jnp.zeros((rows, wide.shape[1]), wide.dtype)
    for head in range(heads):
        folded = jnp.where(lane_head == head, wide[head * rows : (head + 1) * rows], folded)
    return folded


def block_at(block):
    return pl.ds(pl.multiple_of(block * BLOCK, BLOCK), BLOCK)


def fill_segments(token_segs, ends_ref):
    def fill(block, _):
        places = block * BLOCK + lax.broadcasted_iota(jnp.int32, (BLOCK, token_segs.shape[1]), 0)
        token_segs[block_at(block), :] = segment_at(places, ends_ref)
        return 0

    lax.fori_loop(0, token_segs.shape[0] // BLOCK, fill, 0)


def query_segments(block, heads, ends_ref):
    lanes = lax.broadcasted_iota(jnp.int32, (8, heads * BLOCK), 1)
    return segment_at(block * BLOCK + lanes % BLOCK, ends_ref)[0:1]


def key_segments(starts, keeps, ends_ref):
    lanes = lax.broadcasted_iota(jnp.int32, (8, 2 * BLOCK), 1)
    first = lanes < BLOCK
    pieces = []
    for entry in range(0, LIST, 2):
        places = lanes + jnp.where(
            first, starts[entry] * BLOCK, (starts[entry + 1] - 1) * BLOCK
        )
        keep = jnp.where(first, keeps[entry], keeps[entry + 1]) > 0
        pieces.append(jnp.where(keep, segment_at(places, ends_ref), -1))
    return jnp.concatenate(pieces, axis=1)[0:1]


def gathered(ref, starts):
    return jnp.concatenate([ref[block_at(start), :] for start in starts], axis=0)


def block_parts(wide):
    return [wide[start : start + BLOCK] for start in range(0, wide.shape[0], BLOCK)]


def dot_nt(left, right):
    return lax.dot_general(left, right, (((1,), (1,)), ((), ())), preferred_element_type=F32)


def dot_tn(left, right):
    return lax.dot_general(left, right, (((0,), (0,)), ((), ())), preferred_element_type=F32)


def dot_nn(left, right):
    return lax.dot_general(left, right, (((1,), (0,)), ((), ())), preferred_element_type=F32)


def as_row(tall):
    count = tall.shape[0]
    row_ids = lax.broadcasted_iota(jnp.int32, (count, count), 0)
    lane_ids = lax.broadcasted_iota(jnp.int32, (count, count), 1)
    return jnp.sum(jnp.where(row_ids == lane_ids, tall, 0.0), axis=0, keepdims=True)


def together(running):
    while running:
        still = []
        for each in running:
            if next(each, 0) is None:
                still.append(each)
        running = still


def unit_block(unit, half, parts, rows_total):
    per = rows_total // parts // BLOCK // 2
    part = unit // per
    inside = unit - part * per
    return part, inside, part * 2 * per + half * per + inside


def forward_kernel(heads, half, ends_ref, lists_ref, admit_ref, q_ref, k_ref, v_ref, *rest):
    o_ref, lse_ref, token_segs, *held = rest
    held = held[0] if held else None
    scale = HD ** (-0.5)
    rows_total = q_ref.shape[0]
    units = o_ref.shape[0] * o_ref.shape[1] // BLOCK
    first_unit = GLOB if half == 0 else 0
    chunk = LIST * BLOCK
    fill_segments(token_segs, ends_ref)

    def store(unit, wide, top, total):
        part, inside, block = unit_block(unit, half, o_ref.shape[0], rows_total)
        out = head_fold(wide, heads)
        places = block * BLOCK + lax.broadcasted_iota(jnp.int32, out.shape, 0)
        out = jnp.where(places < ends_ref[ends_ref.shape[0] - 1], out, 0.0)
        o_ref[part, block_at(inside), :] = out.astype(BF16)
        lse_ref[unit] = jnp.broadcast_to(as_row(top + jnp.log(total)), lse_ref.shape[1:])

    def kept(block, key_segs):
        own = token_segs[block_at(block), :]
        return jnp.concatenate([own] * (chunk // own.shape[1]), axis=1) == key_segs

    def global_blocks():
        query_wide = jnp.concatenate(
            [head_spread(q_ref[block_at(block), :] * scale, heads) for block in range(GLOB)], axis=0
        )
        wide_rows = GLOB * heads * BLOCK

        def score(part, top):
            here = pl.ds(pl.multiple_of(part * chunk, chunk), chunk)
            places = part * chunk + lax.broadcasted_iota(jnp.int32, (8, chunk), 1)
            key_segs = segment_at(places, ends_ref)[0:1]
            keeps = [kept(block, key_segs) for block in range(GLOB)]
            scores = dot_nt(query_wide, k_ref[here, :])
            tops = []
            for place, rows in enumerate(block_parts(scores)):
                rows = jnp.where(keeps[place // heads], rows, NEG)
                held[place * BLOCK : (place + 1) * BLOCK, here] = rows
                tops.append(jnp.max(rows, axis=1, keepdims=True))
            return jnp.maximum(top, jnp.concatenate(tops, axis=0))

        top = lax.fori_loop(0, rows_total // chunk, score, jnp.full((wide_rows, 1), NEG, F32))

        def gather(part, carried):
            total, wide = carried
            here = pl.ds(pl.multiple_of(part * chunk, chunk), chunk)
            totals, weights = [], []
            for place, part_top in enumerate(block_parts(top)):
                weight = jnp.exp(held[place * BLOCK : (place + 1) * BLOCK, here] - part_top)
                totals.append(jnp.sum(weight, axis=1, keepdims=True))
                weights.append(weight.astype(BF16))
            wide = wide + dot_nn(jnp.concatenate(weights, axis=0), v_ref[here, :])
            return total + jnp.concatenate(totals, axis=0), wide

        total, wide = lax.fori_loop(
            0,
            rows_total // chunk,
            gather,
            (jnp.zeros((wide_rows, 1), F32), jnp.zeros((wide_rows, q_ref.shape[1]), F32)),
        )
        wide = wide * (1.0 / total)
        for block in range(GLOB):
            own = slice(block * heads * BLOCK, (block + 1) * heads * BLOCK)
            store(block, wide[own], top[own], total[own])

    if half == 0:
        global_blocks()

    def listed_block(unit):
        _, _, block = unit_block(unit, half, o_ref.shape[0], rows_total)
        query_wide = head_spread(q_ref[block_at(block), :] * scale, heads)
        starts = [lists_ref[block * LIST + entry] for entry in range(LIST)]
        keeps = [admit_ref[block * LIST + entry] for entry in range(LIST)]
        keep = kept(block, key_segments(starts, keeps, ends_ref))
        scores = dot_nt(query_wide, gathered(k_ref, starts))
        yield
        tops, totals, probs = [], [], []
        for rows in block_parts(scores):
            rows = jnp.where(keep, rows, NEG)
            top = jnp.max(rows, axis=1, keepdims=True)
            weights = jnp.exp(rows - top)
            total = jnp.sum(weights, axis=1, keepdims=True)
            probs.append((weights * (1.0 / total)).astype(BF16))
            tops.append(top)
            totals.append(total)
            yield
        wide = dot_nn(jnp.concatenate(probs, axis=0), gathered(v_ref, starts))
        store(unit, wide, jnp.concatenate(tops, axis=0), jnp.concatenate(totals, axis=0))

    def listed_group(group, _):
        together([listed_block(first_unit + 4 * group + place) for place in range(4)])
        return 0

    lax.fori_loop(0, (units - first_unit) // 4, listed_group, 0)
    together([listed_block(units - 1 - place) for place in range((units - first_unit) % 4)])


def backward_kernel(
    heads,
    ends_ref,
    lists_ref,
    admit_ref,
    q_ref,
    k_ref,
    v_ref,
    o_first,
    o_second,
    do_first,
    do_second,
    lse_first,
    lse_second,
    out_ref,
    token_segs,
    dk_ref,
    dv_ref,
    dq_ref,
):
    scale = HD ** (-0.5)
    rows_total, cols = q_ref.shape
    blocks = rows_total // BLOCK
    pair_rows = 2 * BLOCK
    fill_segments(token_segs, ends_ref)

    def prepare(pair, _):
        here = pl.ds(pl.multiple_of(pair * pair_rows, pair_rows), pair_rows)
        dk_ref[here, :] = jnp.zeros((pair_rows, cols), F32)
        dv_ref[here, :] = jnp.zeros((pair_rows, cols), F32)
        return 0

    lax.fori_loop(0, blocks // 2, prepare, 0)

    parts = o_first.shape[0]
    halves_of = ((o_first, do_first, lse_first), (o_second, do_second, lse_second))

    def query_side(unit, half):
        o_ref, do_ref, lse_ref = halves_of[half]
        part, inside, block = unit_block(unit, half, parts, rows_total)
        query_wide = head_spread(q_ref[block_at(block), :] * scale, heads)
        grad_rows = do_ref[part, block_at(inside), :]
        grad_wide = head_spread(grad_rows, heads)
        product = grad_rows.astype(F32) * o_ref[part, block_at(inside), :].astype(F32)
        spread = head_spread(product.astype(BF16), heads)
        delta = dot_nt(jnp.ones((8, cols), BF16), spread)[0:1]
        seg_row = query_segments(block, heads, ends_ref)
        return query_wide, grad_wide, delta, lse_ref[unit, 0:1], seg_row

    def unit(starts, keeps, query_wide, grad_wide, delta, lse, seg_row, finish_query):
        keys = gathered(k_ref, starts)
        scores = block_parts(dot_nt(keys, query_wide))
        prob_grads = block_parts(dot_nt(gathered(v_ref, starts), grad_wide))
        yield
        probs, score_grads = [], []
        for entry in range(LIST):
            wanted = seg_row if keeps is None else jnp.where(keeps[entry] > 0, seg_row, -1)
            own = token_segs[block_at(starts[entry]), :]
            keep = jnp.concatenate([own] * (seg_row.shape[1] // own.shape[1]), axis=1) == wanted
            prob = jnp.exp(jnp.where(keep, scores[entry], NEG) - lse)
            probs.append(prob.astype(BF16))
            score_grads.append((prob * (prob_grads[entry] - delta)).astype(BF16))
            if entry % 2:
                yield
        score_grad = jnp.concatenate(score_grads, axis=0)
        finish_query(dot_tn(score_grad, keys))
        dk = dot_nn(score_grad, query_wide)
        dv = dot_nn(jnp.concatenate(probs, axis=0), grad_wide)
        yield
        for entry in range(LIST):
            here = block_at(starts[entry])
            dk_ref[here, :] += dk[entry * BLOCK : (entry + 1) * BLOCK]
            dv_ref[here, :] += dv[entry * BLOCK : (entry + 1) * BLOCK]
        yield

    def store_query(block, wide):
        out_ref[block_at(block), 0:cols] = (head_fold(wide, heads) * scale).astype(BF16)

    def global_blocks():
        sides = [query_side(block, 0) for block in range(GLOB)]
        side = [jnp.concatenate(both, axis=axis) for both, axis in zip(zip(*sides), (0, 0, 1, 1, 1))]
        dq_ref[...] = jnp.zeros_like(dq_ref)

        def part_of(part, _):
            def add_query(wide):
                dq_ref[...] += wide

            together([unit([part * LIST + entry for entry in range(LIST)], None, *side, add_query)])
            return 0

        lax.fori_loop(0, blocks // LIST, part_of, 0)
        for block in range(GLOB):
            store_query(block, dq_ref[block * heads * BLOCK : (block + 1) * heads * BLOCK])

    global_blocks()

    def listed_block(place, half):
        _, _, block = unit_block(place, half, parts, rows_total)
        starts = [lists_ref[block * LIST + entry] for entry in range(LIST)]
        keeps = [admit_ref[block * LIST + entry] for entry in range(LIST)]
        return unit(
            starts, keeps, *query_side(place, half), functools.partial(store_query, block)
        )

    for half, first_unit in ((0, GLOB), (1, 0)):
        units = blocks // 2

        def listed_group(group, _):
            together([listed_block(first_unit + 4 * group + place, half) for place in range(4)])
            return 0

        lax.fori_loop(0, (units - first_unit) // 4, listed_group, 0)
        together([listed_block(units - 1 - place, half) for place in range((units - first_unit) % 4)])

    def finish(block, _):
        here = block_at(block)
        out_ref[here, cols : 2 * cols] = dk_ref[here, :].astype(BF16)
        out_ref[here, 2 * cols : 3 * cols] = dv_ref[here, :].astype(BF16)
        return 0

    lax.fori_loop(0, blocks, finish, 0)


def smem():
    return pl.BlockSpec(memory_space=pltpu.SMEM)


def column(rows, cols, index):
    return pl.BlockSpec((rows, cols), lambda step: (0, index))


def attention_forward(half, qkv, doc_ends, lists, admits, parts):
    rows = qkv.shape[0]
    cols = qkv.shape[1] // 3
    heads = cols // HD
    blocks = rows // BLOCK
    out = jax.ShapeDtypeStruct((parts, rows // parts // 2, cols), BF16)
    lse = jax.ShapeDtypeStruct((blocks // 2, 8, heads * BLOCK), F32)
    cube = lambda step: (0, 0, 0)
    return pl.pallas_call(
        functools.partial(forward_kernel, heads, half),
        grid=(1,),
        in_specs=[smem(), smem(), smem()] + [column(rows, cols, part) for part in range(3)],
        out_specs=[pl.BlockSpec(out.shape, cube), pl.BlockSpec(lse.shape, cube)],
        out_shape=[out, lse],
        scratch_shapes=[pltpu.VMEM((rows, 2 * BLOCK), jnp.int32)]
        + ([] if half else [pltpu.VMEM((GLOB * heads * BLOCK, rows), F32)]),
        compiler_params=pltpu.CompilerParams(vmem_limit_bytes=VMEM_LIMIT),
        cost_estimate=pl.CostEstimate(
            flops=rows * LIST * BLOCK * cols * heads * 5,
            bytes_accessed=8 * rows * cols,
            transcendentals=0,
        ),
    )(doc_ends, lists, admits, qkv, qkv, qkv)


def attention_backward(qkv, attended, attended_grad, lse, doc_ends, lists, admits):
    rows = qkv.shape[0]
    cols = qkv.shape[1] // 3
    heads = cols // HD
    cube = lambda step: (0, 0, 0)
    return pl.pallas_call(
        functools.partial(backward_kernel, heads),
        grid=(1,),
        in_specs=[smem(), smem(), smem()]
        + [column(rows, cols, part) for part in range(3)]
        + [pl.BlockSpec(part.shape, cube) for part in (*attended, *attended_grad, *lse)],
        out_specs=column(rows, 3 * cols, 0),
        out_shape=jax.ShapeDtypeStruct((rows, 3 * cols), BF16),
        scratch_shapes=[
            pltpu.VMEM((rows, 2 * BLOCK), jnp.int32),
            pltpu.VMEM((rows, cols), F32),
            pltpu.VMEM((rows, cols), F32),
            pltpu.VMEM((GLOB * heads * BLOCK, cols), F32),
        ],
        compiler_params=pltpu.CompilerParams(vmem_limit_bytes=VMEM_LIMIT),
        cost_estimate=pl.CostEstimate(
            flops=rows * LIST * BLOCK * cols * heads * 15,
            bytes_accessed=20 * rows * cols,
            transcendentals=0,
        ),
    )(doc_ends, lists, admits, qkv, qkv, qkv, *attended, *attended_grad, *lse)


def row_stats(rows):
    mean = jnp.mean(rows, axis=-1, keepdims=True)
    centre = rows - mean
    spread = jnp.mean(centre * centre, axis=-1, keepdims=True)
    inverse = lax.rsqrt(spread + EPS)
    return centre * inverse, inverse


def gelu_pair(inner):
    root = 0.7978845608028654
    cube = 0.044715
    square = inner * inner
    bent = jnp.tanh(inner * (root + (root * cube) * square))
    half = 0.5 + 0.5 * bent
    value = inner * half
    return value, half + value * (1.0 - bent) * (root + (3.0 * root * cube) * square)


def token_kernel(
    tile,
    index,
    ends_ref,
    att_ref,
    x_ref,
    cotangent_ref,
    out_own_ref,
    out_other_ref,
    up_own_ref,
    up_near_ref,
    up_far_ref,
    down_own_ref,
    down_near_ref,
    down_far_ref,
    up_bias_ref,
    gain_ref,
    bias_ref,
    down_bias_ref,
    trade_source,
    pair_source,
    act_in,
    pre_in,
    second_in,
    hidden_in,
    grad_in,
    att_in,
    output_ref,
    hidden_grad_ref,
    datt_ref,
    act_ref,
    pre_ref,
    second_ref,
    hidden_low_ref,
    grad_low_ref,
    att_rows_ref,
    sums_ref,
    unit_sums_ref,
    trade_target,
    pair_target,
    hidden,
    normed,
    inverse,
    ffn,
    second_grad,
    grad_rows,
    up_slots,
    down_slots,
    slot_sems,
    row_sems,
    pair_sems,
    *trade_sems,
):
    step = pl.program_id(0)
    steps = pl.num_programs(0)
    rows = hidden.shape[0]
    parts = att_ref.shape[0]
    tiles = [slice(start, start + tile) for start in range(0, rows, tile)]
    chunk = up_slots.shape[2]
    own_steps = up_own_ref.shape[1] // chunk
    near_steps = up_near_ref.shape[1] // chunk

    def copies(up_from, down_from, index, slot):
        here = pl.ds(pl.multiple_of(index * chunk, chunk), chunk)
        return (
            pltpu.make_async_copy(up_from.at[:, here], up_slots.at[slot], slot_sems.at[0, slot]),
            pltpu.make_async_copy(down_from.at[here], down_slots.at[slot], slot_sems.at[1, slot]),
        )

    def fetch(index):
        def begin(up_from, down_from, first):
            for copy in copies(up_from, down_from, index - first, index % 2):
                copy.start()

        @pl.when(index < own_steps)
        def _():
            begin(up_own_ref, down_own_ref, 0)

        @pl.when((index >= own_steps) & (index < own_steps + near_steps))
        def _():
            begin(up_near_ref, down_near_ref, own_steps)

        @pl.when(index >= own_steps + near_steps)
        def _():
            begin(up_far_ref, down_far_ref, own_steps + near_steps)

    half = parts // 2
    me = lax.axis_index("seq")
    place = lax.axis_index("mp")
    own_place = place * half
    other_place = (1 - place) * half
    first_row = index * rows
    row_copies = [
        pltpu.make_async_copy(source.at[place, pl.ds(first_row, rows)], target, row_sems.at[which])
        for which, (source, target) in enumerate(((x_ref, hidden), (cotangent_ref, grad_rows)))
    ]
    pair = (pair_source, pair_target, pair_sems) if index else None
    trade = Trade(trade_source, trade_target, *trade_sems, pair)
    out_parts = [(own_place + part, out_own_ref, part) for part in range(half)]
    out_parts += [(other_place + part, out_other_ref, part) for part in range(half)]

    @pl.when(step == 0)
    def _():
        for copy in row_copies:
            copy.start()
        fetch(step)
        trade.start()

    @pl.when(step + 1 < steps)
    def _():
        fetch(step + 1)

    @pl.when(step == 0)
    def _():
        for copy in row_copies:
            copy.wait()
        for here in tiles:
            total = hidden[here, :]
            for part, weight_ref, index in out_parts:
                total = total + dot_nn(att_ref[part, here, :], weight_ref[index])
            for part in range(parts):
                cols = att_ref.shape[2]
                att_rows_ref[here, part * cols : (part + 1) * cols] = att_ref[part, here, :]
            hidden[here, :] = total
            unit, scale = row_stats(total)
            normed[here, :] = unit
            inverse[here, :] = jnp.broadcast_to(scale, (tile, inverse.shape[1]))
            second_ref[here, :] = (unit * gain_ref[...] + bias_ref[...]).astype(BF16)
            grad_low_ref[here, :] = grad_rows[here, :].astype(BF16)
            ffn[here, :] = jnp.zeros((tile, ffn.shape[1]), F32)
            second_grad[here, :] = jnp.zeros((tile, ffn.shape[1]), F32)

    slot = step % 2
    for copy in copies(up_own_ref, down_own_ref, 0, slot):
        copy.wait()
    up_ref = up_slots.at[slot]
    down_ref = down_slots.at[slot]
    unit_sum = jnp.zeros((1, chunk), F32)
    for here in tiles:
        inner = dot_nn(second_ref[here, :], up_ref[...]) + up_bias_ref[...]
        act_grad = dot_nt(grad_low_ref[here, :], down_ref[...])
        value, slope = gelu_pair(inner)
        value = value.astype(BF16)
        pre_grad = (act_grad * slope).astype(BF16)
        act_ref[here, :] = value
        pre_ref[here, :] = pre_grad
        unit_sum = unit_sum + jnp.sum(pre_grad.astype(F32), axis=0, keepdims=True)
        ffn[here, :] += dot_nn(value, down_ref[...])
        second_grad[here, :] += dot_nt(pre_grad, up_ref[...])
    unit_sums_ref[...] = jnp.broadcast_to(unit_sum, unit_sums_ref.shape)

    @pl.when(step == steps - 1)
    def _():
        width = ffn.shape[1]
        grad_sum = jnp.zeros((1, width), F32)
        gain_sum = jnp.zeros((1, width), F32)
        bias_sum = jnp.zeros((1, width), F32)
        for number, here in enumerate(tiles):
            output_ref[here, :] = (hidden[here, :] + ffn[here, :] + down_bias_ref[...]).astype(BF16)
            grad = grad_rows[here, :]
            back = second_grad[here, :]
            unit = normed[here, :]
            scaled = back * gain_ref[...]
            through = (
                scaled
                - jnp.mean(scaled, axis=-1, keepdims=True)
                - unit * jnp.mean(scaled * unit, axis=-1, keepdims=True)
            )
            total = grad + inverse[here, 0:1] * through
            hidden_grad_ref[here, :] = total
            low = total.astype(BF16)
            hidden_low_ref[here, :] = low
            grad_sum = grad_sum + jnp.sum(grad, axis=0, keepdims=True)
            gain_sum = gain_sum + jnp.sum(back * unit, axis=0, keepdims=True)
            bias_sum = bias_sum + jnp.sum(back, axis=0, keepdims=True)
            for part, weight_ref, piece in out_parts:
                spread = dot_nt(low, weight_ref[piece])
                places = me * 2 * rows + first_row + number * tile
                places = places + lax.broadcasted_iota(jnp.int32, spread.shape, 0)
                inside = places < ends_ref[ends_ref.shape[0] - 1]
                datt_ref[part, here, :] = jnp.where(inside, spread, 0.0).astype(BF16)
        sums_ref[...] = jnp.concatenate(
            [grad_sum, gain_sum, bias_sum, jnp.zeros((5, width), F32)], axis=0
        )
        trade.finish()


def token_part(
    index, doc_ends, att, layer_input, cotangent, outs, ups, downs, up_bias, gain, bias, down_bias, source, pair, kept
):
    parts, rows, cols = att.shape
    width = layer_input.shape[2]
    units = up_bias.shape[1]
    chunk = min(512, units // 4)
    whole = 2 * rows
    shapes = [(whole, units)] * 2 + [(whole, width)] * 4
    if kept is None:
        kept = [jnp.zeros((8, 128), BF16)] * len(shapes)
        aliases = {}
    else:
        aliases = {18 + place: 3 + place for place in range(len(shapes))}
    half = lambda step: (index, 0)
    fixed = lambda step: (0, 0)
    any_spec = pl.BlockSpec(memory_space=pl.ANY)
    cube = lambda step: (0, 0, 0)
    vector = pl.BlockSpec((1, width), fixed)
    return pl.pallas_call(
        functools.partial(token_kernel, min(256, rows), index),
        grid=(units // chunk,),
        in_specs=[
            smem(),
            pl.BlockSpec((parts, rows, cols), cube),
            any_spec,
            any_spec,
            pl.BlockSpec((parts // 2, cols, width), cube),
            pl.BlockSpec((parts // 2, cols, width), cube),
        ]
        + [any_spec] * 6
        + [pl.BlockSpec((1, chunk), lambda step: (0, step)), vector, vector, vector]
        + [any_spec] * (2 + len(shapes)),
        out_specs=[
            pl.BlockSpec((rows, width), fixed),
            pl.BlockSpec((rows, width), fixed),
            pl.BlockSpec((parts, rows, cols), cube),
            pl.BlockSpec((rows, chunk), lambda step: (index, step)),
            pl.BlockSpec((rows, chunk), lambda step: (index, step)),
            pl.BlockSpec((rows, width), half),
            pl.BlockSpec((rows, width), half),
            pl.BlockSpec((rows, width), half),
            pl.BlockSpec((rows, width), half),
            pl.BlockSpec((8, width), fixed),
            pl.BlockSpec((8, chunk), lambda step: (0, step)),
            any_spec,
            any_spec,
        ],
        scratch_shapes=[
            pltpu.VMEM((rows, width), F32),
            pltpu.VMEM((rows, width), F32),
            pltpu.VMEM((rows, 128), F32),
            pltpu.VMEM((rows, width), F32),
            pltpu.VMEM((rows, width), F32),
            pltpu.VMEM((rows, width), F32),
            pltpu.VMEM((2, width, chunk), BF16),
            pltpu.VMEM((2, chunk, width), BF16),
            pltpu.SemaphoreType.DMA((2, 2)),
            pltpu.SemaphoreType.DMA((2,)),
            pltpu.SemaphoreType.DMA((2,)),
        ]
        + trade_scratch(parts),
        out_shape=[
            jax.ShapeDtypeStruct((rows, width), BF16),
            jax.ShapeDtypeStruct((rows, width), F32),
            jax.ShapeDtypeStruct((parts, rows, cols), BF16),
        ]
        + [jax.ShapeDtypeStruct(shape, BF16) for shape in shapes]
        + [
            jax.ShapeDtypeStruct((8, width), F32),
            jax.ShapeDtypeStruct((8, units), F32),
            jax.ShapeDtypeStruct((parts, rows, cols), BF16),
            jax.ShapeDtypeStruct(pair.shape, BF16),
        ],
        input_output_aliases=aliases,
        compiler_params=pltpu.CompilerParams(
            collective_id=5 + index, has_side_effects=True, vmem_limit_bytes=VMEM_LIMIT
        ),
        cost_estimate=pl.CostEstimate(
            flops=rows * width * (8 * units + 4 * width),
            bytes_accessed=8 * units * width,
            transcendentals=0,
        ),
    )(
        doc_ends,
        att,
        layer_input,
        cotangent,
        *outs,
        *ups,
        *downs,
        up_bias,
        gain,
        bias,
        down_bias,
        source,
        pair,
        *kept,
    )


def greet(me, count, partner=None):
    barrier = pltpu.get_barrier_semaphore()

    @pl.when(me > 0)
    def _():
        pl.semaphore_signal(barrier, inc=1, device_id={"seq": me - 1}, device_id_type=MESH)

    @pl.when(me < count - 1)
    def _():
        pl.semaphore_signal(barrier, inc=1, device_id={"seq": me + 1}, device_id_type=MESH)

    peers = jnp.minimum(me, 1) + jnp.minimum(count - 1 - me, 1)
    if partner is not None:
        pl.semaphore_signal(barrier, inc=1, device_id={"mp": partner}, device_id_type=MESH)
        peers = peers + 1
    pl.semaphore_wait(barrier, peers)


def gather_kernel(
    count,
    chunks,
    half_cols,
    x_ref,
    gain_ref,
    bias_ref,
    weight_ref,
    all_ref,
    qkv_ref,
    own_ref,
    rows_in,
    shards,
    results,
    weight,
    weight_sems,
    load_sems,
    send_sems,
    recv_sems,
    all_sems,
    qkv_sems,
):
    me = lax.axis_index("seq")
    place = lax.axis_index("mp")
    step = rows_in.shape[0] // chunks
    cols = weight.shape[1] // 3

    def at(chunk):
        return pl.ds(pl.multiple_of(chunk * step, step), step)

    def load(chunk):
        return pltpu.make_async_copy(
            x_ref.at[place, at(chunk)], rows_in.at[at(chunk)], load_sems.at[chunk]
        )

    def send(side, hop, chunk):
        shard = me - hop if side == 0 else me + hop
        target = me + 1 if side == 0 else me - 1
        return pltpu.make_async_remote_copy(
            src_ref=shards.at[shard, at(chunk)],
            dst_ref=shards.at[shard, at(chunk)],
            send_sem=send_sems.at[side, hop, chunk],
            recv_sem=recv_sems.at[side, hop, chunk],
            device_id={"seq": target},
            device_id_type=MESH,
        )

    def keep_all(shard, chunk):
        return pltpu.make_async_copy(
            shards.at[shard, at(chunk)], all_ref.at[shard, at(chunk)], all_sems.at[shard, chunk]
        )

    def keep_qkv(shard, chunk):
        return pltpu.make_async_copy(
            results.at[shard, at(chunk)], qkv_ref.at[shard, at(chunk)], qkv_sems.at[shard, chunk]
        )

    def over_chunks(body):
        def run(chunk, _):
            body(chunk)
            return 0

        lax.fori_loop(0, chunks, run, 0)

    over_chunks(lambda chunk: load(chunk).start())
    greet(me, count, 1 - place)

    here = (me * cols) // half_cols == place
    fetch = pltpu.make_async_remote_copy(
        src_ref=weight_ref,
        dst_ref=weight,
        send_sem=weight_sems.at[0],
        recv_sem=weight_sems.at[1],
        device_id={"mp": 1 - place},
        device_id_type=MESH,
    )
    copy = pltpu.make_async_copy(weight_ref, weight, weight_sems.at[2])

    @pl.when(here)
    def _():
        fetch.start()
        copy.start()

    def norm(chunk):
        load(chunk).wait()
        unit, _ = row_stats(rows_in[at(chunk), :])
        shards[me, at(chunk), :] = (unit * gain_ref[...] + bias_ref[...]).astype(BF16)
        keep_all(me, chunk).start()

        @pl.when(me < count - 1)
        def _():
            send(0, 0, chunk).start()

        @pl.when(me > 0)
        def _():
            send(1, 0, chunk).start()

    over_chunks(norm)

    def project(shard, chunk):
        rows = dot_nn(shards[shard, at(chunk), :], weight[...])
        results[shard, at(chunk), :] = rows.astype(BF16)
        keep_qkv(shard, chunk).start()

    def receive(hop, chunk):
        @pl.when(me >= hop + 1)
        def _():
            send(0, hop, chunk).wait_recv()
            if hop + 1 < count - 1:

                @pl.when(me < count - 1)
                def _():
                    send(0, hop + 1, chunk).start()

            keep_all(me - hop - 1, chunk).start()

        @pl.when(me + hop + 1 < count)
        def _():
            send(1, hop, chunk).wait_recv()
            if hop + 1 < count - 1:

                @pl.when(me > 0)
                def _():
                    send(1, hop + 1, chunk).start()

            keep_all(me + hop + 1, chunk).start()

    for hop in range(count - 2):
        over_chunks(functools.partial(receive, hop))

    @pl.when(here)
    def _():
        copy.wait()

    @pl.when(jnp.logical_not(here))
    def _():
        fetch.wait_recv()

    keep_weight = pltpu.make_async_copy(weight, own_ref, weight_sems.at[3])
    keep_weight.start()

    def last(chunk):
        project(me, chunk)
        for hop in range(count - 1):
            if hop == count - 2:
                receive(hop, chunk)

            @pl.when(me >= hop + 1)
            def _():
                project(me - hop - 1, chunk)

            @pl.when(me + hop + 1 < count)
            def _():
                project(me + hop + 1, chunk)

    over_chunks(last)

    def finish(chunk):
        for hop in range(count - 1):

            @pl.when((me >= hop) & (me < count - 1))
            def _():
                send(0, hop, chunk).wait_send()

            @pl.when((me + hop < count) & (me > 0))
            def _():
                send(1, hop, chunk).wait_send()

        for shard in range(count):
            keep_all(shard, chunk).wait()
            keep_qkv(shard, chunk).wait()

    over_chunks(finish)
    keep_weight.wait()

    @pl.when(here)
    def _():
        fetch.wait_send()


def gather_project(layer_input, gain, bias, weight, half_cols):
    count = lax.axis_size("seq")
    _, rows, width = layer_input.shape
    cols = weight.shape[1]
    chunks = max(1, rows // 128)
    any_spec = pl.BlockSpec(memory_space=pl.ANY)
    vmem = pl.BlockSpec(memory_space=pltpu.VMEM)
    dma = pltpu.SemaphoreType.DMA
    return pl.pallas_call(
        functools.partial(gather_kernel, count, chunks, half_cols),
        in_specs=[any_spec, vmem, vmem, vmem],
        out_specs=[any_spec, any_spec, any_spec],
        out_shape=[
            jax.ShapeDtypeStruct((count, rows, width), BF16),
            jax.ShapeDtypeStruct((count, rows, cols), BF16),
            jax.ShapeDtypeStruct((width, cols), BF16),
        ],
        scratch_shapes=[
            pltpu.VMEM((rows, width), F32),
            pltpu.VMEM((count, rows, width), BF16),
            pltpu.VMEM((count, rows, cols), BF16),
            pltpu.VMEM((width, cols), BF16),
            dma((4,)),
            dma((chunks,)),
            dma((2, count - 1, chunks)),
            dma((2, count - 1, chunks)),
            dma((count, chunks)),
            dma((count, chunks)),
        ],
        compiler_params=pltpu.CompilerParams(
            collective_id=0, has_side_effects=True, vmem_limit_bytes=VMEM_LIMIT
        ),
        cost_estimate=pl.CostEstimate(
            flops=150_000_000_000, bytes_accessed=1, transcendentals=0
        ),
    )(layer_input, gain, bias, weight)


class VectorSum:
    def __init__(self, group, line, sems):
        self.group, self.line, self.sems = group, line, sems
        self.me, self.count = lax.axis_index("seq"), lax.axis_size("seq")
        self.pairs = lax.axis_size("mp")
        self.members = lax.axis_size("batch") * self.pairs
        self.mine = lax.axis_index("batch") * self.pairs + lax.axis_index("mp")

    def member(self, distance):
        other = lax.rem(self.mine + distance, self.members)
        return {"batch": other // self.pairs, "mp": lax.rem(other, self.pairs)}

    def along(self, distance):
        return {"seq": lax.rem(self.me + distance, self.count)}

    def greet(self):
        barrier = pltpu.get_barrier_semaphore()
        for distance in range(1, self.members):
            pl.semaphore_signal(
                barrier, inc=1, device_id=self.member(distance), device_id_type=MESH
            )
        for distance in range(1, self.count):
            pl.semaphore_signal(barrier, inc=1, device_id=self.along(distance), device_id_type=MESH)
        pl.semaphore_wait(barrier, self.members + self.count - 2)

    def share(self, distance, along):
        buffer, place = (self.line, self.me) if along else (self.group, self.mine)
        which = distance - 1 + (self.members - 1 if along else 0)
        return pltpu.make_async_remote_copy(
            src_ref=buffer.at[place],
            dst_ref=buffer.at[place],
            send_sem=self.sems.at[0, which],
            recv_sem=self.sems.at[1, which],
            device_id=self.along(distance) if along else self.member(distance),
            device_id_type=MESH,
        )

    def start(self, value):
        self.group[self.mine] = value
        for distance in range(1, self.members):
            self.share(distance, False).start()

    def middle(self):
        for distance in range(1, self.members):
            self.share(distance, False).wait()
        total = self.group[0]
        for place in range(1, self.members):
            total = total + self.group[place]
        self.line[self.me] = total
        for distance in range(1, self.count):
            self.share(distance, True).start()

    def finish(self):
        for distance in range(1, self.count):
            self.share(distance, True).wait()
        total = self.line[0]
        for place in range(1, self.count):
            total = total + self.line[place]
        return total


class Extra:
    def __init__(self, kind, source, target, sems):
        self.source, self.target, self.sems = source, target, sems
        batch, place, me = lax.axis_index("batch"), lax.axis_index("mp"), lax.axis_index("seq")
        self.local = None
        if kind == "mp":
            self.moves = [(source, target, {"mp": 1 - place})]
        elif kind == "chip":
            side = (batch // 2) % 2
            size = source.shape[1] // 2
            there = pl.ds(pl.multiple_of((1 - side) * size, 128), size)
            self.moves = [(source.at[:, there], target, {"batch": batch + 2 - 4 * side})]
        else:
            count = source.shape[0]
            pairs = lax.axis_size("mp")
            mine = me if kind == "line" else batch * pairs + place
            self.moves = []
            for distance in range(1, count):
                other = lax.rem(mine + distance, count)
                device = {"batch": other // pairs, "mp": lax.rem(other, pairs)}
                if kind == "line":
                    device = {"seq": other}
                self.moves.append((source.at[other], target.at[mine], device))
            self.local = (source.at[mine], target.at[mine])

    def copies(self):
        for index, (source, target, device) in enumerate(self.moves):
            yield pltpu.make_async_remote_copy(
                src_ref=source,
                dst_ref=target,
                send_sem=self.sems.at[0, index],
                recv_sem=self.sems.at[1, index],
                device_id=device,
                device_id_type=MESH,
            )
        if self.local is not None:
            yield pltpu.make_async_copy(*self.local, self.sems.at[0, len(self.moves)])

    def start(self):
        for copy in self.copies():
            copy.start()

    def finish(self):
        for copy in self.copies():
            copy.wait()


def extra_target(kind, source):
    rows, *rest = source.shape
    return (rows, rest[0] // 2) if kind == "chip" else source.shape


def extra_moves(kind, source):
    return 1 if kind in ("mp", "chip") else source.shape[0]


def in_rows(vectors, width):
    pieces = []
    for row in range(vectors.shape[0]):
        for start in range(0, vectors.shape[1], width):
            pieces.append(vectors[row : row + 1, start : start + width])
    return jnp.concatenate(pieces, axis=0)


class WeightChain:
    def __init__(self, terms, qkv_terms, gathered, heads_ref, sending, received, result, head_sum, heads_in, sems):
        self.up, self.up_come, self.out, self.out_come, self.down, self.down_come = terms
        self.qkv_terms, self.gathered, self.heads_ref = qkv_terms, gathered, heads_ref
        self.sending, self.received, self.result = sending, received, result
        self.head_sum, self.heads_in, self.sems = head_sum, heads_in, sems
        self.me, self.count = lax.axis_index("seq"), lax.axis_size("seq")
        self.batch, self.place = lax.axis_index("batch"), lax.axis_index("mp")
        self.rows = result.shape[1]
        self.chunks = 2
        self.step = self.rows // self.chunks
        self.steps = (self.count - 1) * self.chunks
        self.members = qkv_terms.shape[0]
        self.mine = self.batch * 2 + self.place
        self.used = 2 * self.steps

    def at(self, chunk):
        return pl.ds(pl.multiple_of(chunk * self.step, self.step), self.step)

    def term(self, target, chunk):
        here = pl.ds(pl.multiple_of(target * self.rows + chunk * self.step, self.step), self.step)
        size = self.down.shape[1] // 2
        kept = pl.ds(pl.multiple_of((self.batch // 2) % 2 * size, 128), size)
        pairs = (
            (self.up[here, :], self.up_come[here, :]),
            (self.down[here, kept], self.down_come[here, :]),
            (self.out[here, :], self.out_come[here, :]),
        )
        return jnp.concatenate([own.astype(F32) + come.astype(F32) for own, come in pairs], axis=1)

    def send(self, side, message, chunk):
        which = (side * (self.count - 1) + message) * self.chunks + chunk
        return pltpu.make_async_remote_copy(
            src_ref=self.sending.at[side, message, self.at(chunk)],
            dst_ref=self.received.at[side, message, self.at(chunk)],
            send_sem=self.sems.at[0, which],
            recv_sem=self.sems.at[1, which],
            device_id={"seq": self.me + 1 - 2 * side},
            device_id_type=MESH,
        )

    def flow(self, side, index):
        message, chunk = index // self.chunks, index % self.chunks
        target = (1 - side) * (self.count - 1 - message) + side * message

        @pl.when((target - self.me) * (1 - 2 * side) > 0)
        def _():
            total = self.term(target, chunk)
            first = (1 - side) * self.me + side * (self.count - 1 - self.me)

            @pl.when(first == 0)
            def _():
                self.sending[side, message, self.at(chunk), :] = total.astype(BF16)

            @pl.when(first > 0)
            def _():
                self.send(side, message, chunk).wait_recv()
                come = self.received[side, message, self.at(chunk), :].astype(F32)
                self.sending[side, message, self.at(chunk), :] = (total + come).astype(BF16)

            self.send(side, message, chunk).start()

    def heads_line(self, distance):
        other = lax.rem(self.me + distance, self.count)
        which = self.used + distance - 1
        return pltpu.make_async_remote_copy(
            src_ref=self.head_sum.at[other],
            dst_ref=self.heads_in.at[self.me],
            send_sem=self.sems.at[0, which],
            recv_sem=self.sems.at[1, which],
            device_id={"seq": other},
            device_id_type=MESH,
        )

    def heads_member(self, distance):
        other = lax.rem(self.mine + distance, self.members)
        which = self.used + self.count - 1 + distance - 1
        parts = self.count // 2
        return pltpu.make_async_remote_copy(
            src_ref=self.heads_in.at[pl.ds(lax.rem(other, 2) * parts, parts)],
            dst_ref=self.heads_ref.at[self.mine],
            send_sem=self.sems.at[0, which],
            recv_sem=self.sems.at[1, which],
            device_id={"batch": other // 2, "mp": lax.rem(other, 2)},
            device_id_type=MESH,
        )

    def heads_own(self):
        parts = self.count // 2
        return pltpu.make_async_copy(
            self.heads_in.at[pl.ds(self.place * parts, parts)],
            self.heads_ref.at[self.mine],
            self.sems.at[0, self.used + self.count + self.members - 2],
        )

    def piece(self, index):
        which = self.used + self.count + self.members - 1 + index
        side = (self.batch // 2) % 2
        parity = self.batch % 2
        other = self.batch + 1 - 2 * parity if index else self.batch + 2 - 4 * side
        source = max(index - 1, 0)
        return pltpu.make_async_remote_copy(
            src_ref=self.result.at[source],
            dst_ref=self.result.at[source + (2 if index else 1)],
            send_sem=self.sems.at[0, which],
            recv_sem=self.sems.at[1, which],
            device_id={"batch": other},
            device_id_type=MESH,
        )

    def start(self):
        total = self.qkv_terms[0].astype(F32)
        for member in range(1, self.members):
            total = total + self.qkv_terms[member].astype(F32)
        self.head_sum[...] = total.astype(BF16)
        self.heads_in[self.me] = self.head_sum[self.me]
        for distance in range(1, self.count):
            self.heads_line(distance).start()

    def own(self):
        for chunk in range(self.chunks):
            here = self.at(chunk)
            total = self.term(self.me, chunk)

            @pl.when(self.me > 0)
            def _():
                self.send(0, self.count - 1 - self.me, chunk).wait_recv()

            @pl.when(self.me < self.count - 1)
            def _():
                self.send(1, self.me, chunk).wait_recv()

            left = self.received[0, jnp.minimum(self.count - 1 - self.me, self.count - 2), here, :]
            right = self.received[1, jnp.minimum(self.me, self.count - 2), here, :]
            total = total + jnp.where(self.me > 0, left.astype(F32), 0.0)
            total = total + jnp.where(self.me < self.count - 1, right.astype(F32), 0.0)
            self.result[0, here, :] = total.astype(BF16)
        self.piece(0).start()
        for distance in range(1, self.count):
            self.heads_line(distance).wait()
        for distance in range(1, self.members):
            self.heads_member(distance).start()
        self.heads_own().start()

    def spread(self):
        self.piece(0).wait()
        self.piece(1).start()
        self.piece(2).start()

    def finish(self):
        for index in range(self.steps):
            message, chunk = index // self.chunks, index % self.chunks

            @pl.when(self.count - 1 - message > self.me)
            def _():
                self.send(0, message, chunk).wait_send()

            @pl.when(message < self.me)
            def _():
                self.send(1, message, chunk).wait_send()

        self.piece(1).wait()
        self.piece(2).wait()
        self.heads_own().wait()
        for distance in range(1, self.members):
            self.heads_member(distance).wait()
        copy = pltpu.make_async_copy(
            self.result, self.gathered, self.sems.at[0, self.used + self.count + self.members + 2]
        )
        copy.start()
        copy.wait()


def return_kernel(
    count,
    chunks,
    lag,
    index_of,
    kinds,
    parts_ref,
    weight_ref,
    x_ref,
    hidden_grad_ref,
    gain_ref,
    vectors_ref,
    *rest,
):
    extras = len(kinds)
    sources, rest = rest[:extras], rest[extras:]
    if index_of:
        *weight_terms, qkv_terms = rest[:7]
        rest = rest[7:]
    input_ref, sums_ref, total_ref, other_ref, *rest = rest
    targets, rest = rest[:extras], rest[extras:]
    if index_of:
        gathered, heads_ref, *rest = rest
    rows_in, sending, received, group, line, load_sem, *rest = rest
    send_sems, recv_sems, pair_send_sems, pair_recv_sems, vector_sems, *extra_sems = rest
    late = extra_sems[extras:]
    extras = [Extra(*each) for each in zip(kinds, sources, targets, extra_sems)]
    me = lax.axis_index("seq")
    place = lax.axis_index("mp")
    rows = hidden_grad_ref.shape[0]
    step = rows // chunks
    width = gain_ref.shape[1]
    steps = (count - 1) * chunks

    def at(chunk):
        return pl.ds(pl.multiple_of(chunk * step, step), step)

    load = pltpu.make_async_copy(x_ref.at[place, pl.ds(index_of * rows, rows)], rows_in, load_sem.at[0])
    load.start()
    vector_sum = VectorSum(group, line, vector_sems)
    vector_sum.greet()
    if index_of == 0:
        vector_sum.start(vectors_ref[...])
    for extra in extras:
        extra.start()

    def send(side, message, chunk):
        return pltpu.make_async_remote_copy(
            src_ref=sending.at[side, message, at(chunk)],
            dst_ref=received.at[side, message, at(chunk)],
            send_sem=send_sems.at[side, message, chunk],
            recv_sem=recv_sems.at[side, message, chunk],
            device_id={"seq": me + 1 - 2 * side},
            device_id_type=MESH,
        )

    def flow(side, index):
        message = index // chunks
        chunk = index % chunks
        target = (1 - side) * (count - 1 - message) + side * message

        @pl.when((target - me) * (1 - 2 * side) > 0)
        def _():
            total = dot_nt(parts_ref[target, at(chunk), :], weight_ref[...])
            first = (1 - side) * me + side * (count - 1 - me)

            @pl.when(first == 0)
            def _():
                sending[side, message, at(chunk), :] = total.astype(BF16)

            @pl.when(first > 0)
            def _():
                send(side, message, chunk).wait_recv()
                come = received[side, message, at(chunk), :].astype(F32)
                sending[side, message, at(chunk), :] = (total + come).astype(BF16)

            send(side, message, chunk).start()

    if index_of:
        chain = WeightChain(weight_terms, qkv_terms, gathered, heads_ref, *late)
        chain.start()
    else:
        chain = None
    ahead = chain.steps if chain else 0
    near = me // (count // 2)

    def pair(chunk):
        return pltpu.make_async_remote_copy(
            src_ref=input_ref.at[at(chunk)],
            dst_ref=other_ref.at[at(chunk)],
            send_sem=pair_send_sems.at[chunk],
            recv_sem=pair_recv_sems.at[chunk],
            device_id={"mp": 1 - place},
            device_id_type=MESH,
        )

    def own(chunk):
        here = at(chunk)
        total = dot_nt(parts_ref[me, here, :], weight_ref[...])

        @pl.when(me > 0)
        def _():
            send(0, count - 1 - me, chunk).wait_recv()

        @pl.when(me < count - 1)
        def _():
            send(1, me, chunk).wait_recv()

        left = received[0, jnp.minimum(count - 1 - me, count - 2), here, :].astype(F32)
        right = received[1, jnp.minimum(me, count - 2), here, :].astype(F32)
        total = total + jnp.where(me > 0, left, 0.0) + jnp.where(me < count - 1, right, 0.0)
        unit, inverse = row_stats(rows_in[here, :])
        scaled = total * gain_ref[...]
        through = (
            scaled
            - jnp.mean(scaled, axis=-1, keepdims=True)
            - unit * jnp.mean(scaled * unit, axis=-1, keepdims=True)
        )
        input_ref[here, :] = (hidden_grad_ref[here, :] + inverse * through).astype(BF16)
        if index_of:
            pair(chunk).start()
        sums_ref[0:1, :] += jnp.sum(total * unit, axis=0, keepdims=True)
        sums_ref[1:2, :] += jnp.sum(total, axis=0, keepdims=True)

    sums_ref[...] = jnp.zeros_like(sums_ref)
    load.wait()
    wait_for = ahead + ((count - 2) * chunks + lag + 1 if index_of else steps + lag)
    steps_all = ahead + steps

    def flow_of(side, index):
        if chain is not None:

            @pl.when(index < ahead)
            def _():
                chain.flow(side, index)

        @pl.when(index >= ahead)
        def _():
            flow(side, index - ahead)

    def advance(index, _):
        @pl.when(index < steps_all)
        def _():
            flow_of(near, index)

        @pl.when((index >= lag) & (index < steps_all + lag))
        def _():
            flow_of(1 - near, index - lag)

        if chain is not None:

            @pl.when(index == ahead + lag + 2)
            def _():
                chain.own()

            @pl.when(index == ahead + lag + 6)
            def _():
                chain.spread()

        @pl.when(index >= wait_for)
        def _():
            own(index - wait_for)

        return 0

    lax.fori_loop(0, wait_for + chunks, advance, 0)
    if index_of:
        vector_sum.start(in_rows(sums_ref[0:2, :] + vectors_ref[0:2, :], group.shape[2]))
    vector_sum.middle()

    def finish(index, _):
        message = index // chunks
        chunk = index % chunks

        @pl.when(count - 1 - message > me)
        def _():
            send(0, message, chunk).wait_send()

        @pl.when(message < me)
        def _():
            send(1, message, chunk).wait_send()

        return 0

    lax.fori_loop(0, steps, finish, 0)

    def finish_pair(chunk, _):
        pair(chunk).wait()
        return 0

    if index_of:
        lax.fori_loop(0, chunks, finish_pair, 0)
    total_ref[...] = vector_sum.finish()
    if chain is not None:
        chain.finish()
    for extra in extras:
        extra.finish()


def return_part(
    index, parts, weight, layer_input, hidden_grad, gain, vectors, extras, weight_terms=(), qkv_terms=None
):
    count, rows, cols = parts.shape
    rows = rows // 2
    width = weight.shape[0]
    chunks = max(1, rows // 128)
    members = lax.axis_size("batch") * lax.axis_size("mp")
    small = (8, 2 * width // 8) if index else vectors.shape
    kinds, sources = [kind for kind, _ in extras], [source for _, source in extras]
    late_in, late_out, late_scratch = [], [], []
    if index:
        late_in = [*weight_terms, qkv_terms]
        up, _, out, *_ = weight_terms
        part = (width // count, 2 * up.shape[1] + out.shape[1])
        batches = lax.axis_size("batch")
        head = qkv_terms.shape[2:]
        late_out = [(batches,) + part, (members, count // 2) + head]
        messages = (2, count - 1) + part
        late_scratch = [
            pltpu.VMEM(messages, BF16),
            pltpu.VMEM(messages, BF16),
            pltpu.VMEM((batches,) + part, BF16),
            pltpu.VMEM((count,) + head, BF16),
            pltpu.VMEM((count,) + head, BF16),
            pltpu.SemaphoreType.DMA((2, 4 * (count - 1) + count + members + 3)),
        ]
    any_spec = pl.BlockSpec(memory_space=pl.ANY)
    dma = pltpu.SemaphoreType.DMA
    fixed = lambda step: (0, 0)
    return pl.pallas_call(
        functools.partial(return_kernel, count, chunks, 2, index, kinds),
        grid=(1,),
        in_specs=[
            pl.BlockSpec((count, rows, cols), lambda step: (0, index, 0)),
            pl.BlockSpec((width, cols), fixed),
            any_spec,
            pl.BlockSpec((rows, width), fixed),
            pl.BlockSpec((1, width), fixed),
            pl.BlockSpec(vectors.shape, fixed),
        ]
        + [any_spec] * len(extras)
        + [pl.BlockSpec(memory_space=pltpu.VMEM)] * len(late_in),
        out_specs=[
            pl.BlockSpec((rows, width), fixed),
            pl.BlockSpec((8, width), fixed),
            pl.BlockSpec(small, fixed),
            any_spec,
        ]
        + [any_spec] * (len(extras) + len(late_out)),
        out_shape=[
            jax.ShapeDtypeStruct((rows, width), BF16),
            jax.ShapeDtypeStruct((8, width), F32),
            jax.ShapeDtypeStruct(small, F32),
            jax.ShapeDtypeStruct((rows, width), BF16),
        ]
        + [jax.ShapeDtypeStruct(extra_target(*extra), BF16) for extra in extras]
        + [jax.ShapeDtypeStruct(shape, BF16) for shape in late_out],
        scratch_shapes=[
            pltpu.VMEM((rows, width), F32),
            pltpu.VMEM((2, count - 1, rows, width), BF16),
            pltpu.VMEM((2, count - 1, rows, width), BF16),
            pltpu.VMEM((members,) + small, F32),
            pltpu.VMEM((count,) + small, F32),
            dma((1,)),
            dma((2, count - 1, chunks)),
            dma((2, count - 1, chunks)),
            dma((chunks,)),
            dma((chunks,)),
            dma((2, members + count - 2)),
        ]
        + [dma((2, extra_moves(*extra))) for extra in extras]
        + late_scratch,
        compiler_params=pltpu.CompilerParams(
            collective_id=1 + index, has_side_effects=True, vmem_limit_bytes=VMEM_LIMIT
        ),
        cost_estimate=pl.CostEstimate(flops=80_000_000_000, bytes_accessed=1, transcendentals=0),
    )(parts, weight, layer_input, hidden_grad, gain, vectors, *sources, *late_in)


def weight_grad_kernel(
    tile,
    second_ref,
    grad_ref,
    hidden_ref,
    pre_ref,
    act_ref,
    att_ref,
    trade_source,
    pair_source,
    up_own,
    up_near,
    down_own,
    down_near,
    out_own,
    out_near,
    trade_target,
    pair_target,
    turned,
    slots,
    sending,
    received,
    slot_sems,
    send_sems,
    recv_sems,
    out_sems,
    pair_sems,
    *trade_sems,
):
    rows, width = second_ref.shape
    units = pre_ref.shape[1]
    me = lax.axis_index("batch")
    place = lax.axis_index("mp")
    parity = me % 2
    mate = me + 1 - 2 * parity
    barrier = pltpu.get_barrier_semaphore()
    pl.semaphore_signal(barrier, inc=1, device_id={"batch": mate}, device_id_type=MESH)
    trade = Trade(trade_source, trade_target, *trade_sems, (pair_source, pair_target, pair_sems))
    trade.start(1)

    piece = units // 4
    head_piece = width // 4
    jobs = []
    for matrix, source, own, near in ((0, pre_ref, up_own, up_near), (1, act_ref, down_own, down_near)):
        for start in range(0, piece, tile):
            jobs.append(
                (matrix, source, tile, (1 - parity) * piece + start, parity * piece + start, own, start)
            )
        for start in range(0, piece, tile):
            jobs.append((matrix, source, tile, 3 * piece + start, 2 * piece + start, near, start))
    for side, target in ((place, out_own), (1 - place, out_near)):
        first = 2 * side * head_piece
        jobs.append(
            (
                2,
                att_ref,
                head_piece,
                first + (1 - parity) * head_piece,
                first + parity * head_piece,
                target,
                0,
            )
        )
    count = len(jobs)
    order = [(job, 3) for job in range(count)] + [(job, 4) for job in range(count)]

    def fetch(index):
        job, which = order[index]
        _, source, size, *_ = jobs[job]
        start = jobs[job][which]
        return pltpu.make_async_copy(
            source.at[:, pl.ds(pl.multiple_of(start, 128), size)],
            slots.at[index % 2, :, pl.ds(0, size)],
            slot_sems.at[index % 2],
        )

    def exchange(job):
        size = jobs[job][2]
        return pltpu.make_async_remote_copy(
            src_ref=sending.at[job, :, pl.ds(0, size)],
            dst_ref=received.at[job, :, pl.ds(0, size)],
            send_sem=send_sems.at[job],
            recv_sem=recv_sems.at[job],
            device_id={"batch": mate},
            device_id_type=MESH,
        )

    def put(job):
        size, target, start = jobs[job][2], jobs[job][5], jobs[job][6]
        return pltpu.make_async_copy(
            received.at[job, :, pl.ds(0, size)], target.at[:, pl.ds(start, size)], out_sems.at[job]
        )

    fetch(0).start()
    block = min(256, width)
    for matrix, source in enumerate((second_ref, grad_ref, hidden_ref)):

        def turn(index, _):
            here = pl.ds(pl.multiple_of(index * 128, 128), 128)
            turned[matrix, :, here] = source[here, :].T
            return 0

        lax.fori_loop(0, rows // 128, turn, 0)

    for index, (job, which) in enumerate(order):
        matrix, _, size, *_ = jobs[job]
        fetch(index).wait()
        if index + 1 < len(order):
            fetch(index + 1).start()
        if which == 4:
            exchange(job).wait_recv()

        def multiply(part, _):
            here = pl.ds(pl.multiple_of(part * block, block), block)
            total = dot_nn(turned[matrix, here, :], slots[index % 2, :, 0:size])
            if which == 3:
                sending[job, here, 0:size] = total.astype(BF16)
            else:
                total = total + received[job, here, 0:size].astype(F32)
                received[job, here, 0:size] = total.astype(BF16)
            return 0

        lax.fori_loop(0, width // block, multiply, 0)
        if which == 3:
            exchange(job).start()
        else:
            put(job).start()
    for job in range(count):
        exchange(job).wait_send()
        put(job).wait()
    trade.finish()


def weight_grads(second_low, grad_low, hidden_low, pre_grad, activated, attended, source, pair):
    rows, width = second_low.shape
    units = pre_grad.shape[1]
    piece = units // 4
    tile = min(512, piece)
    jobs = 4 * (piece // tile) + 2
    any_spec = pl.BlockSpec(memory_space=pl.ANY)
    vmem = pl.BlockSpec(memory_space=pltpu.VMEM)
    dma = pltpu.SemaphoreType.DMA
    shapes = [(width, piece)] * 4 + [(width, width // 4)] * 2
    return pl.pallas_call(
        functools.partial(weight_grad_kernel, tile),
        in_specs=[vmem] * 3 + [any_spec] * 5,
        out_specs=[any_spec] * 8,
        out_shape=[
            jax.ShapeDtypeStruct(shape, BF16) for shape in shapes + [source.shape, pair.shape]
        ],
        scratch_shapes=[
            pltpu.VMEM((3, width, rows), BF16),
            pltpu.VMEM((2, rows, tile), BF16),
            pltpu.VMEM((jobs, width, tile), BF16),
            pltpu.VMEM((jobs, width, tile), BF16),
            dma((2,)),
            dma((jobs,)),
            dma((jobs,)),
            dma((jobs,)),
            dma((2,)),
        ]
        + trade_scratch(source.shape[0]),
        compiler_params=pltpu.CompilerParams(
            collective_id=3, has_side_effects=True, vmem_limit_bytes=VMEM_LIMIT
        ),
        cost_estimate=pl.CostEstimate(
            flops=2 * rows * width * (2 * units + width),
            bytes_accessed=4 * rows * units,
            transcendentals=0,
        ),
    )(second_low, grad_low, hidden_low, pre_grad, activated, attended, source, pair)


def swap(value, axis, distance=1):
    size = lax.axis_size(axis)
    return lax.ppermute(value, axis, [(j, j ^ distance) for j in range(size)])


def after(value, *earlier):
    return lax.optimization_barrier((value,) + earlier)[0]


def all_to_all(value):
    return lax.all_to_all(value, "seq", 0, 0, tiled=True)


def halves(value):
    return jnp.split(value, 2, axis=1)


def trade_pieces(value):
    place, count = lax.axis_index("seq"), lax.axis_size("seq")
    pieces = [pick(value, place, count)]
    for distance in range(1, count):
        pairs = [(j, (j + distance) % count) for j in range(count)]
        pieces.append(
            lax.ppermute(pick(value, (place + distance) % count, count), "seq", pairs)
        )
    return pieces


def place_pieces(pieces):
    place, count = lax.axis_index("seq"), len(pieces)
    whole = jnp.concatenate(pieces, axis=0)
    return jnp.roll(whole[::-1], place + 1, axis=0)


def levels_of(axis):
    return [1 << level for level in range(lax.axis_size(axis).bit_length() - 1)]


def gather_small(value):
    place = lax.axis_index("seq")
    count = lax.axis_size("seq")
    parts = [value] + [swap(value, "seq", distance) for distance in range(1, count)]
    stacked = jnp.stack(parts)
    order = jnp.arange(count, dtype=jnp.int32) ^ place
    return jnp.take(stacked, order, axis=0).reshape((-1,) + value.shape[1:])


def pick(value, index, count, axis=0):
    size = value.shape[axis] // count
    return lax.dynamic_slice_in_dim(value, index * size, size, axis)


def fetch_near(weight, axis):
    return swap(pick(weight, lax.axis_index("batch") % 2, 2, axis), "mp")


def narrow_add(mine, received):
    return (mine.astype(F32) + received.astype(F32)).astype(BF16)


def halve(value, distance, axis):
    side = (lax.axis_index("batch") // distance) % 2
    return narrow_add(
        pick(value, side, 2, axis), swap(pick(value, 1 - side, 2, axis), "batch", distance)
    )


def assemble_kernel(unit_cols, pieces, heads, up_ref, down_ref, out_ref, qkv_ref):
    batch = lax.axis_index("batch")
    batches = pieces.shape[0]
    levels = batches.bit_length() - 1
    for index in range(batches):
        source = jnp.bitwise_xor(batch, index // 2 + 2 * (index % 2))
        slot = 0
        for level in range(levels):
            slot = slot + ((source >> level) % 2) * (batches >> (level + 1))
        start = 0
        for size, target, turn in (
            (unit_cols, up_ref, False),
            (unit_cols, down_ref, True),
            (pieces.shape[2] - 2 * unit_cols, out_ref, True),
        ):
            value = pieces[index, :, start : start + size].astype(F32)
            here = pl.ds(pl.multiple_of(slot * size, 128), size)
            if turn:
                target[here, :] = value.T
            else:
                target[:, here] = value
            start = start + size
    members, parts, rows, cols = heads.shape
    cols = cols // 3
    for member in range(members):
        for matrix in range(3):
            for part in range(parts):
                start = (matrix * parts + part) * cols
                qkv_ref[member * rows : (member + 1) * rows, start : start + cols] = heads[
                    member, part, :, matrix * cols : (matrix + 1) * cols
                ].astype(F32)


def assemble(unit_cols, pieces, heads):
    batches, rows, all_cols = pieces.shape
    out_cols = all_cols - 2 * unit_cols
    shapes = [
        (rows, batches * unit_cols),
        (batches * unit_cols, rows),
        (batches * out_cols, rows),
        (heads.shape[0] * heads.shape[2], heads.shape[1] * heads.shape[3]),
    ]
    vmem = pl.BlockSpec(memory_space=pltpu.VMEM)
    return pl.pallas_call(
        functools.partial(assemble_kernel, unit_cols),
        in_specs=[vmem] * 2,
        out_specs=[vmem] * 4,
        out_shape=[jax.ShapeDtypeStruct(shape, F32) for shape in shapes],
        compiler_params=pltpu.CompilerParams(vmem_limit_bytes=VMEM_LIMIT),
    )(pieces, heads)


def place_kernel(place_ref, own_first, own_second, other_first, other_second, out_ref):
    place = place_ref[0]

    @pl.when(pl.program_id(0) == 0)
    def _():
        out_ref[place] = own_first[...].astype(F32)
        out_ref[1 - place] = other_first[...].astype(F32)

    @pl.when(pl.program_id(0) == 1)
    def _():
        out_ref[place] = own_second[...].astype(F32)
        out_ref[1 - place] = other_second[...].astype(F32)


def both_sequences(own, other):
    rows, width = own[0].shape
    step = min(256, rows)
    steps = rows // step
    first = pl.BlockSpec(
        (step, width), lambda half, index, place_ref: (index * (1 - half) + (steps - 1) * half, 0)
    )
    second = pl.BlockSpec((step, width), lambda half, index, place_ref: (index * half, 0))
    return pl.pallas_call(
        place_kernel,
        grid_spec=pltpu.PrefetchScalarGridSpec(
            num_scalar_prefetch=1,
            grid=(2, steps),
            in_specs=[first, second, first, second],
            out_specs=pl.BlockSpec(
                (2, step, width), lambda half, index, place_ref: (0, half * steps + index, 0)
            ),
        ),
        out_shape=jax.ShapeDtypeStruct((2, 2 * rows, width), F32),
    )(lax.axis_index("mp").astype(jnp.int32)[None], *own, *other)


def local(
    layer_input,
    lengths,
    random_blocks,
    first_gain,
    first_bias,
    qkv_weight,
    out_weight,
    second_gain,
    second_bias,
    up_weight,
    up_bias,
    down_weight,
    down_bias,
    cotangent,
):
    seq_count = lax.axis_size("seq")
    seq_index = lax.axis_index("seq")
    mp_index = lax.axis_index("mp")
    parity = lax.axis_index("batch") % 2
    _, local_rows, width = layer_input.shape
    rows_total = local_rows * seq_count
    blocks = rows_total // BLOCK
    half_cols = qkv_weight.shape[2]
    cols = width // seq_count
    units = up_weight.shape[1]

    doc_ends = jnp.cumsum(lax.dynamic_index_in_dim(lengths, mp_index, 0, keepdims=False))
    randoms = lax.dynamic_index_in_dim(random_blocks, mp_index, 0, keepdims=False)
    randoms = gather_small(randoms)
    lists, admits = block_lists(jnp.arange(blocks, dtype=jnp.int32), randoms, blocks)
    lists, admits = lists.reshape(-1), admits.reshape(-1)

    qkv_near = lax.dynamic_slice_in_dim(qkv_weight, (seq_index * cols) % half_cols, cols, 2)
    qkv_near = qkv_near.reshape(width, 3 * cols)
    up_near = fetch_near(up_weight, 1)
    bias_near = fetch_near(up_bias, 0)
    out_other = swap(out_weight, "mp")

    first_all, qkv, qkv_own = gather_project(
        layer_input, first_gain[None], first_bias[None], qkv_near, half_cols
    )
    first_all = first_all.reshape(rows_total, width)
    qkv, up_near, out_other, bias_near, lists, down_cut = lax.optimization_barrier(
        (qkv.reshape(rows_total, 3 * cols), up_near, out_other, bias_near, lists, down_weight)
    )
    up_far, bias_far = swap(up_near, "batch"), swap(bias_near, "batch")
    down_near = fetch_near(down_cut, 0)
    attended_first, lse_first = attention_forward(0, qkv, doc_ends, lists, admits, seq_count)
    att_pieces = trade_pieces(attended_first)
    attended_second, lse_second = attention_forward(1, qkv, doc_ends, lists, admits, seq_count)
    *att_pieces, attended_second = lax.optimization_barrier((*att_pieces, attended_second))
    att_first = place_pieces(att_pieces)
    att_first, up_far, down_near, bias_far = lax.optimization_barrier(
        (att_first, up_far, down_near, bias_far)
    )
    down_far = swap(down_near, "batch")
    bias_full = jnp.concatenate([up_bias, bias_near, bias_far])[None]
    outs = [part.reshape(seq_count // 2, cols, width) for part in (out_weight, out_other)]
    kept, results = None, []
    att, source, pair = att_first, attended_second, jnp.zeros((8, 128), BF16)
    for index in range(2):
        result = token_part(
            index,
            doc_ends,
            att,
            layer_input,
            cotangent,
            outs,
            (up_weight, up_near, up_far),
            (down_weight, down_near, down_far),
            bias_full,
            second_gain[None],
            second_bias[None],
            down_bias[None],
            source,
            pair,
            kept,
        )
        kept = result[3:9]
        results.append(result[:3] + result[9:])
        att, source, pair = result[11], result[2], result[0]
        other_output = result[12]
    grad_first = att
    activated, pre_grad, second_low, hidden_low, grad_low, attended_low = kept
    sums = results[0][3][:3] + results[1][3][:3]
    unit_sums = results[0][4][0] + results[1][4][0]
    bias_sums = [unit_sums[:units], unit_sums[units : units * 3 // 2], unit_sums[units * 3 // 2 :]]
    up_own, up_near, down_own, down_near, out_own, out_near, grad_second, other_second = weight_grads(
        second_low, grad_low, hidden_low, pre_grad, activated, attended_low, source, pair
    )
    outputs, other_outputs = [result[0] for result in results], [other_output, other_second]
    bias_other = jnp.where(
        parity == 0,
        jnp.concatenate([bias_sums[1], bias_sums[2]]),
        jnp.concatenate([bias_sums[2], bias_sums[1]]),
    )
    bias_all = jnp.where(
        mp_index == 0,
        jnp.concatenate([bias_sums[0], bias_other]),
        jnp.concatenate([bias_other, bias_sums[0]]),
    )
    levels = levels_of("batch")
    for distance in levels[1:]:
        up_own, up_near = halve(up_own, distance, 1), halve(up_near, distance, 1)
        out_own, out_near = halve(out_own, distance, 1), halve(out_near, distance, 1)
    down_own = narrow_add(down_own, swap(down_near, "mp"))
    qkv_low_grad = attention_backward(
        qkv,
        (attended_first, attended_second),
        (grad_first, grad_second),
        (lse_first, lse_second),
        doc_ends,
        lists,
        admits,
    )
    qkv_sum = dot_tn(first_all, qkv_low_grad).astype(BF16)
    members = lax.axis_size("batch") * 2
    mine = lax.axis_index("batch") * 2 + mp_index
    qkv_sum = qkv_sum.reshape(seq_count, members, -1, 3 * cols).transpose(1, 0, 2, 3)
    qkv_low_grad, qkv_sum, up_own, up_near, down_own, out_own, out_near = lax.optimization_barrier(
        (qkv_low_grad, qkv_sum, up_own, up_near, down_own, out_own, out_near)
    )
    parts = qkv_low_grad.reshape(seq_count, local_rows, 3 * cols)
    early = jnp.concatenate([sums, bias_all.reshape(-1, width)], axis=0)
    input_first, first_sums, early, _, up_come, out_come, down_come, qkv_terms = return_part(
        0,
        parts,
        qkv_own,
        layer_input,
        results[0][1],
        first_gain[None],
        early.reshape(8, -1),
        [("mp", up_near), ("mp", out_near), ("chip", down_own), ("group", qkv_sum)],
    )
    input_second, _, late, other_second, other_first, weights_back, qkv_back = return_part(
        1,
        parts,
        qkv_own,
        layer_input,
        results[1][1],
        first_gain[None],
        first_sums,
        [("mp", input_first)],
        (up_own, up_come, out_own, out_come, down_own, down_come),
        qkv_terms,
    )
    layer_output = both_sequences(outputs, other_outputs)
    input_grad = both_sequences([input_first, input_second], [other_first, other_second])
    up_grad, down_grad, out_grad, qkv_grad = assemble(up_own.shape[1], weights_back, qkv_back)
    early, late = early.reshape(-1), late.reshape(-1)
    up_bias_grad = lax.dynamic_slice_in_dim(early, 3 * width + mp_index * units, units)
    return (
        layer_output,
        input_grad,
        late[:width],
        late[width:],
        qkv_grad.reshape(-1, 3, half_cols),
        out_grad,
        early[width : 2 * width],
        early[2 * width : 3 * width],
        up_grad,
        up_bias_grad,
        down_grad,
        early[:width],
    )


MB = 2
NBLK = 64
LEN = 4096
HIGH = lax.Precision.HIGHEST


def segment_of(places, doc_ends):
    return jnp.sum((places[..., None] >= doc_ends).astype(jnp.int32), axis=-1)


def block_lists_by_index(blocks, randoms):
    leading = randoms.shape[:-1]
    globals_part = jnp.broadcast_to(jnp.arange(GLOB, dtype=jnp.int32), leading + (GLOB,))
    window_part = jnp.broadcast_to(
        blocks[:, None] + jnp.arange(WIN, dtype=jnp.int32) - WIN // 2, leading + (WIN,)
    )
    block_list = jnp.concatenate([globals_part, window_part, randoms], axis=-1)
    inside = (block_list >= 0) & (block_list < NBLK)
    same_entry = block_list[..., :, None] == block_list[..., None, :]
    order_ids = jnp.arange(LIST)
    earlier = order_ids[None, :] < order_ids[:, None]
    repeated = jnp.any(same_entry & earlier, axis=-1)
    return (block_list, inside & jnp.logical_not(repeated))


def fetch_rows(key_rows, values, wanted):
    batch_seqs, local_rows, head_cols = key_rows.shape
    total_rows = local_rows * lax.axis_size("seq")
    empty_rows = jnp.zeros((batch_seqs, wanted.shape[1], head_cols), jnp.bfloat16)
    initial = (empty_rows, empty_rows)
    empty_whole = jnp.zeros((batch_seqs, total_rows, head_cols), jnp.bfloat16)
    initial = initial + (empty_whole, empty_whole)
    shards_in = (
        lax.all_gather(key_rows, "seq", axis=1, tiled=True),
        lax.all_gather(values, "seq", axis=1, tiled=True),
    )
    piece_rows = shards_in[0].shape[1]
    inside = ((wanted >= 0) & (wanted < piece_rows))[..., None]
    take_index = jnp.clip(wanted, 0, piece_rows - 1)[..., None]
    picked = tuple(
        (
            jnp.where(inside, jnp.take_along_axis(source, take_index, axis=1), previous)
            for source, previous in zip(shards_in, initial[:2])
        )
    )
    placed = tuple((source for source in shards_in))
    return picked + placed


def scatter_rows(kv_source):
    return lax.psum_scatter(
        kv_source.astype(jnp.bfloat16), "seq", scatter_dimension=0, tiled=True
    ).astype(jnp.float32)


def global_partial(seq_item):
    query_rows, key_rows, value_rows, keep_mask = seq_item
    head_count = query_rows.shape[1] // HD
    query_heads = query_rows.reshape(query_rows.shape[0], head_count, HD)
    key_heads = key_rows.reshape(key_rows.shape[0], head_count, HD)
    value_heads = value_rows.astype(jnp.float32).reshape(value_rows.shape[0], head_count, HD)
    raw_scores = jnp.einsum(
        "qhd,khd->hqk", query_heads, key_heads, preferred_element_type=jnp.float32
    ) * HD ** (-0.5)
    masked = jnp.where(keep_mask[None], raw_scores, NEG)
    row_top = jnp.max(masked, axis=-1)
    weights = jnp.exp(masked - row_top[..., None]) * keep_mask[None].astype(jnp.float32)
    numer = jnp.einsum("hqk,khd->hqd", weights, value_heads, precision=HIGH)
    return (row_top, jnp.sum(weights, axis=-1), numer)


def global_back(seq_item):
    query_rows, key_rows, value_rows, keep_mask, row_top, row_total, glob_out, glob_grad = seq_item
    row_count, head_cols = query_rows.shape
    head_count = head_cols // HD
    query_heads = query_rows.reshape(row_count, head_count, HD)
    key_heads = key_rows.reshape(key_rows.shape[0], head_count, HD)
    value_heads = value_rows.astype(jnp.float32).reshape(value_rows.shape[0], head_count, HD)
    raw_scores = jnp.einsum(
        "qhd,khd->hqk", query_heads, key_heads, preferred_element_type=jnp.float32
    ) * HD ** (-0.5)
    masked = jnp.where(keep_mask[None], raw_scores, NEG)
    probs_glob = (
        jnp.exp(masked - row_top[..., None])
        * keep_mask[None].astype(jnp.float32)
        / row_total[..., None]
    )
    grad_heads = glob_grad.astype(jnp.float32).reshape(row_count, head_count, HD)
    prob_grad = jnp.einsum("qhd,khd->hqk", grad_heads, value_heads, precision=HIGH)
    delta = jnp.einsum("qhd,hqd->hq", grad_heads, glob_out, precision=HIGH)
    score_grad = (probs_glob * (prob_grad - delta[..., None])).astype(jnp.bfloat16)
    query_grad = jnp.einsum(
        "hqk,khd->qhd", score_grad, key_heads, preferred_element_type=jnp.float32
    ) * HD ** (-0.5)
    key_grad = jnp.einsum(
        "hqk,qhd->khd", score_grad, query_heads, preferred_element_type=jnp.float32
    ) * HD ** (-0.5)
    value_grad = jnp.einsum("hqk,qhd->khd", probs_glob, grad_heads, precision=HIGH)
    return (
        query_grad.reshape(row_count, head_cols),
        key_grad.reshape(-1, head_cols),
        value_grad.reshape(-1, head_cols),
    )


def local_by_blocks(
    layer_input,
    lengths,
    random_blocks,
    first_gain,
    first_bias,
    qkv_weight,
    out_weight,
    second_gain,
    second_bias,
    up_weight,
    up_bias,
    down_weight,
    down_bias,
    cotangent,
):
    seq_index = lax.axis_index("seq")
    local_seqs, local_rows, model_width = layer_input.shape
    blocks_dev = local_rows // BLOCK
    head_cols = qkv_weight.shape[2]
    head_count = head_cols // HD
    unit_cols = up_weight.shape[1]
    score_scale = HD ** (-0.5)
    glob_rows = GLOB * BLOCK
    batch_seqs = local_seqs // MB
    picked_rows = blocks_dev * LIST * BLOCK
    qkv_flat = qkv_weight.reshape(model_width, 3 * head_cols)
    doc_ends = jnp.cumsum(lengths, axis=1)
    places = seq_index * local_rows + jnp.arange(local_rows, dtype=jnp.int32)
    seg_local = segment_of(places[None, :], doc_ends[:, None, :])
    valid_rows = (places[None, :] < doc_ends[:, -1:]).astype(jnp.float32)
    glob_flag = (places < glob_rows)[None, :, None]
    query_blocks = seq_index * blocks_dev + jnp.arange(blocks_dev, dtype=jnp.int32)
    block_list, admitted = block_lists_by_index(query_blocks, random_blocks)
    key_places = block_list[..., None] * BLOCK + jnp.arange(BLOCK, dtype=jnp.int32)
    key_segs = segment_of(key_places, doc_ends[:, None, None, None, :]).reshape(
        local_seqs, blocks_dev, LIST * BLOCK
    )
    admit_keys = jnp.broadcast_to(admitted[..., None], key_places.shape).reshape(
        local_seqs, blocks_dev, LIST * BLOCK
    )
    query_segs = seg_local.reshape(local_seqs, blocks_dev, BLOCK)
    list_mask = admit_keys[:, :, None, :] & (query_segs[..., None] == key_segs[:, :, None, :])
    wanted_all = jnp.clip(key_places, 0, LEN - 1).reshape(local_seqs, picked_rows)
    glob_segs = segment_of(jnp.arange(glob_rows, dtype=jnp.int32)[None, :], doc_ends[:, None, :])
    qkv_total = jnp.zeros((model_width, 3 * head_cols), jnp.float32)
    out_total = jnp.zeros(out_weight.shape, jnp.float32)
    up_total = jnp.zeros(up_weight.shape, jnp.float32)
    down_total = jnp.zeros(down_weight.shape, jnp.float32)
    gain_one_total = jnp.zeros((model_width,), jnp.float32)
    bias_one_total = jnp.zeros((model_width,), jnp.float32)
    gain_two_total = jnp.zeros((model_width,), jnp.float32)
    bias_two_total = jnp.zeros((model_width,), jnp.float32)
    up_bias_total = jnp.zeros((unit_cols,), jnp.float32)
    down_bias_total = jnp.zeros((model_width,), jnp.float32)
    outputs_all = []
    input_grads = []
    for micro_index in range(MB):
        first_seq = micro_index * batch_seqs
        last_seq = first_seq + batch_seqs
        rows_in = layer_input[first_seq:last_seq]
        ends_now = doc_ends[first_seq:last_seq]
        valid_now = valid_rows[first_seq:last_seq]
        mask_now = list_mask[first_seq:last_seq]
        wanted = wanted_all[first_seq:last_seq]
        glob_segs_now = glob_segs[first_seq:last_seq]
        normed_one, inverse_one = norm_stats(rows_in)
        first_low = (
            (normed_one * first_gain + first_bias).astype(jnp.bfloat16).reshape(-1, model_width)
        )
        qkv_rows = (
            jnp.dot(first_low, qkv_flat, preferred_element_type=jnp.float32)
            .astype(jnp.bfloat16)
            .reshape(batch_seqs, local_rows, 3, head_cols)
        )
        queries = qkv_rows[:, :, 0]
        key_rows = qkv_rows[:, :, 1]
        values = qkv_rows[:, :, 2]
        glob_queries_own = queries[:, :glob_rows]
        picked_keys, picked_values, whole_keys, whole_values = fetch_rows(key_rows, values, wanted)
        glob_queries = glob_queries_own
        seg_whole = segment_of(jnp.arange(LEN, dtype=jnp.int32)[None, :], ends_now[:, None, :])
        glob_mask = glob_segs_now[:, :, None] == seg_whole[:, None, :]

        def global_here():
            return lax.map(global_partial, (glob_queries, whole_keys, whole_values, glob_mask))

        def global_skip():
            return (
                jnp.zeros((batch_seqs, head_count, glob_rows), jnp.float32),
                jnp.ones((batch_seqs, head_count, glob_rows), jnp.float32),
                jnp.zeros((batch_seqs, head_count, glob_rows, HD), jnp.float32),
            )

        glob_top, glob_total, glob_numer = lax.cond(seq_index == 0, global_here, global_skip)
        glob_out = glob_numer / glob_total[..., None]
        query_split = queries.reshape(batch_seqs, blocks_dev, BLOCK, head_count, HD)
        key_split = picked_keys.reshape(batch_seqs, blocks_dev, LIST * BLOCK, head_count, HD)
        value_split = picked_values.reshape(batch_seqs, blocks_dev, LIST * BLOCK, head_count, HD)
        raw_scores = (
            jnp.einsum(
                "sbqhd,sbkhd->sbhqk", query_split, key_split, preferred_element_type=jnp.float32
            )
            * score_scale
        )
        keep_now = mask_now[:, :, None]
        masked = jnp.where(keep_now, raw_scores, NEG)
        row_top = jnp.max(masked, axis=-1, keepdims=True)
        weights = jnp.exp(masked - row_top) * keep_now.astype(jnp.float32)
        row_total = jnp.sum(weights, axis=-1, keepdims=True)
        probs_list = weights / row_total
        probs_low = probs_list.astype(jnp.bfloat16)
        listed = jnp.einsum(
            "sbhqk,sbkhd->sbqhd", probs_low, value_split, preferred_element_type=jnp.float32
        ).reshape(batch_seqs, local_rows, head_cols)
        glob_rows_out = jnp.transpose(glob_out, (0, 2, 1, 3)).reshape(
            batch_seqs, glob_rows, head_cols
        )
        glob_full = jnp.pad(glob_rows_out, ((0, 0), (0, local_rows - glob_rows), (0, 0)))
        attended = jnp.where(glob_flag, glob_full, listed) * valid_now[..., None]
        attended_low = attended.astype(jnp.bfloat16).reshape(-1, head_cols)
        branch = lax.psum(
            jnp.dot(attended_low, out_weight, preferred_element_type=jnp.float32).astype(
                jnp.bfloat16
            ),
            "mp",
        ).astype(jnp.float32)
        hidden = rows_in + branch.reshape(rows_in.shape)
        normed_two, inverse_two = norm_stats(hidden)
        second_low = (
            (normed_two * second_gain + second_bias).astype(jnp.bfloat16).reshape(-1, model_width)
        )
        pre_act = jnp.dot(second_low, up_weight, preferred_element_type=jnp.float32) + up_bias
        activated = jax.nn.gelu(pre_act, approximate=True).astype(jnp.bfloat16)
        ffn_branch = lax.psum(
            jnp.dot(activated, down_weight, preferred_element_type=jnp.float32).astype(
                jnp.bfloat16
            ),
            "mp",
        ).astype(jnp.float32)
        outputs_all.append(hidden + ffn_branch.reshape(rows_in.shape) + down_bias)
        grad_rows = cotangent[first_seq:last_seq].reshape(-1, model_width)
        down_bias_total = down_bias_total + jnp.sum(grad_rows, axis=0)
        grad_low = grad_rows.astype(jnp.bfloat16)
        down_total = down_total + jnp.einsum(
            "rf,rd->fd", activated, grad_low, preferred_element_type=jnp.float32
        )
        act_grad = jnp.einsum(
            "rd,fd->rf", grad_low, down_weight, preferred_element_type=jnp.float32
        )
        _, gelu_pull = jax.vjp(lambda inner: jax.nn.gelu(inner, approximate=True), pre_act)
        pre_grad = gelu_pull(act_grad)[0].astype(jnp.bfloat16)
        up_bias_total = up_bias_total + jnp.sum(pre_grad.astype(jnp.float32), axis=0)
        up_total = up_total + jnp.einsum(
            "rd,rf->df", second_low, pre_grad, preferred_element_type=jnp.float32
        )
        second_grad = (
            lax.psum(
                jnp.einsum(
                    "rf,df->rd", pre_grad, up_weight, preferred_element_type=jnp.float32
                ).astype(jnp.bfloat16),
                "mp",
            )
            .astype(jnp.float32)
            .reshape(rows_in.shape)
        )
        gain_two_total = gain_two_total + jnp.sum(second_grad * normed_two, axis=(0, 1))
        bias_two_total = bias_two_total + jnp.sum(second_grad, axis=(0, 1))
        hidden_grad = grad_rows.reshape(rows_in.shape) + norm_back(
            second_grad, normed_two, inverse_two, second_gain
        )
        hidden_low = hidden_grad.astype(jnp.bfloat16).reshape(-1, model_width)
        out_total = out_total + jnp.einsum(
            "rc,rd->cd", attended_low, hidden_low, preferred_element_type=jnp.float32
        )
        attended_grad = jnp.einsum(
            "rd,cd->rc", hidden_low, out_weight, preferred_element_type=jnp.float32
        ).astype(jnp.bfloat16).reshape(batch_seqs, local_rows, head_cols) * valid_now[
            ..., None
        ].astype(
            jnp.bfloat16
        )
        list_grad = jnp.where(glob_flag, jnp.zeros_like(attended_grad), attended_grad).reshape(
            batch_seqs, blocks_dev, BLOCK, head_count, HD
        )
        prob_grad = jnp.einsum(
            "sbqhd,sbkhd->sbhqk", list_grad, value_split, preferred_element_type=jnp.float32
        )
        delta = jnp.sum(probs_list * prob_grad, axis=-1, keepdims=True)
        score_grad = (probs_list * (prob_grad - delta)).astype(jnp.bfloat16)
        query_grad = (
            jnp.einsum(
                "sbhqk,sbkhd->sbqhd", score_grad, key_split, preferred_element_type=jnp.float32
            )
            * score_scale
        ).reshape(batch_seqs, local_rows, head_cols)
        key_picked_grad = (
            jnp.einsum(
                "sbhqk,sbqhd->sbkhd", score_grad, query_split, preferred_element_type=jnp.float32
            )
            * score_scale
        )
        value_picked_grad = jnp.einsum(
            "sbhqk,sbqhd->sbkhd", probs_low, list_grad, preferred_element_type=jnp.float32
        )
        picked_grads = jnp.concatenate(
            [
                key_picked_grad.reshape(batch_seqs, picked_rows, head_cols),
                value_picked_grad.reshape(batch_seqs, picked_rows, head_cols),
            ],
            axis=-1,
        )
        seg_ids = wanted * batch_seqs + jnp.arange(batch_seqs, dtype=jnp.int32)[:, None]
        kv_term = jax.ops.segment_sum(
            picked_grads.reshape(batch_seqs * picked_rows, 2 * head_cols),
            seg_ids.reshape(-1),
            num_segments=LEN * batch_seqs,
        ).reshape(LEN, batch_seqs, 2 * head_cols)
        glob_grad_own = attended_grad[:, :glob_rows]

        def back_here():
            return lax.map(
                global_back,
                (
                    glob_queries,
                    whole_keys,
                    whole_values,
                    glob_mask,
                    glob_top,
                    glob_total,
                    glob_out,
                    glob_grad_own,
                ),
            )

        def back_skip():
            return (
                jnp.zeros((batch_seqs, glob_rows, head_cols), jnp.float32),
                jnp.zeros((batch_seqs, LEN, head_cols), jnp.float32),
                jnp.zeros((batch_seqs, LEN, head_cols), jnp.float32),
            )

        glob_query_grad, whole_key_grad, whole_value_grad = lax.cond(
            seq_index == 0, back_here, back_skip
        )
        glob_dense = jnp.transpose(
            jnp.concatenate([whole_key_grad, whole_value_grad], axis=-1), (1, 0, 2)
        )
        kv_source = kv_term + glob_dense
        kv_grad = jnp.transpose(scatter_rows(kv_source), (1, 0, 2))
        glob_query_full = jnp.pad(glob_query_grad, ((0, 0), (0, local_rows - glob_rows), (0, 0)))
        query_total = query_grad + jnp.where(glob_flag, glob_query_full, 0.0)
        qkv_low_grad = (
            jnp.stack([query_total, kv_grad[..., :head_cols], kv_grad[..., head_cols:]], axis=2)
            .astype(jnp.bfloat16)
            .reshape(-1, 3 * head_cols)
        )
        qkv_total = qkv_total + jnp.einsum(
            "rd,rc->dc", first_low, qkv_low_grad, preferred_element_type=jnp.float32
        )
        first_grad = (
            lax.psum(
                jnp.einsum(
                    "rc,dc->rd", qkv_low_grad, qkv_flat, preferred_element_type=jnp.float32
                ).astype(jnp.bfloat16),
                "mp",
            )
            .astype(jnp.float32)
            .reshape(rows_in.shape)
        )
        gain_one_total = gain_one_total + jnp.sum(first_grad * normed_one, axis=(0, 1))
        bias_one_total = bias_one_total + jnp.sum(first_grad, axis=(0, 1))
        input_grads.append(hidden_grad + norm_back(first_grad, normed_one, inverse_one, first_gain))
    matrix_grads = (
        lax.psum_scatter(
            qkv_total.reshape(model_width, 3, head_cols).astype(jnp.bfloat16),
            "seq",
            scatter_dimension=0,
            tiled=True,
        ).astype(jnp.float32),
        lax.psum_scatter(
            out_total.astype(jnp.bfloat16), "seq", scatter_dimension=1, tiled=True
        ).astype(jnp.float32),
        lax.psum_scatter(
            up_total.astype(jnp.bfloat16), "seq", scatter_dimension=0, tiled=True
        ).astype(jnp.float32),
        lax.psum_scatter(
            down_total.astype(jnp.bfloat16), "seq", scatter_dimension=1, tiled=True
        ).astype(jnp.float32),
    )
    matrix_grads = (
        lax.psum(matrix_grads[0].astype(jnp.bfloat16), "batch").astype(jnp.float32),
        lax.psum(matrix_grads[1].astype(jnp.bfloat16), "batch").astype(jnp.float32),
        lax.psum(matrix_grads[2].astype(jnp.bfloat16), "batch").astype(jnp.float32),
        lax.psum(matrix_grads[3].astype(jnp.bfloat16), "batch").astype(jnp.float32),
    )
    vector_grads = lax.psum(
        (
            gain_one_total,
            bias_one_total,
            gain_two_total,
            bias_two_total,
            up_bias_total,
            down_bias_total,
        ),
        ("seq", "batch"),
    )
    return (
        jnp.concatenate(outputs_all, axis=0),
        jnp.concatenate(input_grads, axis=0),
        vector_grads[0],
        vector_grads[1],
        matrix_grads[0],
        matrix_grads[1],
        vector_grads[2],
        vector_grads[3],
        matrix_grads[2],
        vector_grads[4],
        matrix_grads[3],
        vector_grads[5],
    )


def solution(mesh):
    placed = (
        P("batch", "seq", None),
        P("batch", None),
        P("batch", "seq", None),
        P(),
        P(),
        P(None, None, "mp"),
        P("mp", None),
        P(),
        P(),
        P(None, "mp"),
        P("mp"),
        P("mp", None),
        P(),
        P("batch", "seq", None),
    )
    sizes = mesh.shape
    by_heads = (1024 // sizes["seq"]) % 128 == 0 and sizes["batch"] == 4 and sizes["mp"] == 2
    return jax.shard_map(
        local if by_heads else local_by_blocks,
        mesh=mesh,
        in_specs=placed,
        out_specs=(
            P("batch", "seq", None),
            P("batch", "seq", None),
            P(),
            P(),
            P("seq", None, "mp"),
            P("mp", "seq"),
            P(),
            P(),
            P("seq", "mp"),
            P("mp"),
            P("mp", "seq"),
            P(),
        ),
        check_vma=False,
    )
```

```python
import functools

import jax
import jax.numpy as jnp
from jax import lax
from jax.experimental import pallas as pl
from jax.experimental.pallas import tpu as pltpu
from jax.sharding import PartitionSpec as P

BLOCK = 64
GLOB = 2
WIN = 3
HD = 64
LIST = 8

NEG = -1e30
EPS = 1e-05
F32 = jnp.float32
BF16 = jnp.bfloat16
VMEM_LIMIT = 60 * 1024 * 1024


def norm_stats(rows):
    centre = rows - jnp.mean(rows, axis=-1, keepdims=True)
    spread = jnp.mean(centre * centre, axis=-1, keepdims=True)
    inverse = lax.rsqrt(spread + EPS)
    return (centre * inverse, inverse)


def norm_back(grad_out, normed, inverse, gain):
    scaled = grad_out * gain
    return inverse * (
        scaled
        - jnp.mean(scaled, axis=-1, keepdims=True)
        - normed * jnp.mean(scaled * normed, axis=-1, keepdims=True)
    )


def block_lists(blocks, randoms, block_count):
    leading = randoms.shape[:-1]
    globals_part = jnp.broadcast_to(jnp.arange(GLOB, dtype=jnp.int32), leading + (GLOB,))
    window_part = jnp.broadcast_to(
        blocks[:, None] + jnp.arange(WIN, dtype=jnp.int32) - WIN // 2, leading + (WIN,)
    )
    block_list = jnp.concatenate([globals_part, window_part, randoms], axis=-1)
    inside = (block_list >= 0) & (block_list < block_count)
    same_entry = block_list[..., :, None] == block_list[..., None, :]
    order_ids = jnp.arange(LIST)
    earlier = order_ids[None, :] < order_ids[:, None]
    repeated = jnp.any(same_entry & earlier, axis=-1)
    admitted = inside & jnp.logical_not(repeated)
    return (jnp.clip(block_list, 0, block_count - 1), admitted.astype(jnp.int32))


MESH = pl.DeviceIdType.MESH


class Trade:
    def __init__(self, source, target, send_sems, recv_sems, own_sem, pair=None):
        self.source, self.target, self.pair = source, target, pair
        self.send_sems, self.recv_sems, self.own_sem = send_sems, recv_sems, own_sem
        self.count = source.shape[0]
        self.me = lax.axis_index("seq")

    def greet(self, others):
        barrier = pltpu.get_barrier_semaphore()
        for distance in range(1, self.count):
            other = lax.rem(self.me + distance, self.count)
            pl.semaphore_signal(barrier, inc=1, device_id={"seq": other}, device_id_type=MESH)
        if self.pair is not None:
            partner = 1 - lax.axis_index("mp")
            pl.semaphore_signal(barrier, inc=1, device_id={"mp": partner}, device_id_type=MESH)
            others = others + 1
        pl.semaphore_wait(barrier, self.count - 1 + others)

    def copy(self, distance):
        other = lax.rem(self.me + distance, self.count)
        return pltpu.make_async_remote_copy(
            src_ref=self.source.at[other],
            dst_ref=self.target.at[self.me],
            send_sem=self.send_sems.at[distance - 1],
            recv_sem=self.recv_sems.at[distance - 1],
            device_id={"seq": other},
            device_id_type=MESH,
        )

    def pair_copy(self):
        source, target, sems = self.pair
        return pltpu.make_async_remote_copy(
            src_ref=source,
            dst_ref=target,
            send_sem=sems.at[0],
            recv_sem=sems.at[1],
            device_id={"mp": 1 - lax.axis_index("mp")},
            device_id_type=MESH,
        )

    def own(self):
        return pltpu.make_async_copy(
            self.source.at[self.me], self.target.at[self.me], self.own_sem.at[0]
        )

    def start(self, others=0):
        self.greet(others)
        for distance in range(1, self.count):
            self.copy(distance).start()
        if self.pair is not None:
            self.pair_copy().start()
        self.own().start()

    def finish(self):
        for distance in range(1, self.count):
            self.copy(distance).wait()
        if self.pair is not None:
            self.pair_copy().wait()
        self.own().wait()


def trade_scratch(count):
    dma = pltpu.SemaphoreType.DMA
    return [dma((count - 1,)), dma((count - 1,)), dma((1,))]


def segment_at(places, ends_ref):
    total = jnp.zeros(places.shape, jnp.int32)
    for doc in range(ends_ref.shape[0]):
        total = total + (places >= ends_ref[doc]).astype(jnp.int32)
    return total


def head_spread(rows, heads):
    lane_head = lax.broadcasted_iota(jnp.int32, (1, rows.shape[1]), 1) // HD
    return jnp.concatenate(
        [rows * (lane_head == head).astype(F32).astype(rows.dtype) for head in range(heads)], axis=0
    )


def head_fold(wide, heads):
    rows = wide.shape[0] // heads
    lane_head = lax.broadcasted_iota(jnp.int32, (rows, wide.shape[1]), 1) // HD
    folded = jnp.zeros((rows, wide.shape[1]), wide.dtype)
    for head in range(heads):
        folded = jnp.where(lane_head == head, wide[head * rows : (head + 1) * rows], folded)
    return folded


def block_at(block):
    return pl.ds(pl.multiple_of(block * BLOCK, BLOCK), BLOCK)


def fill_segments(token_segs, ends_ref):
    def fill(block, _):
        places = block * BLOCK + lax.broadcasted_iota(jnp.int32, (BLOCK, token_segs.shape[1]), 0)
        token_segs[block_at(block), :] = segment_at(places, ends_ref)
        return 0

    lax.fori_loop(0, token_segs.shape[0] // BLOCK, fill, 0)


def query_segments(block, heads, ends_ref):
    lanes = lax.broadcasted_iota(jnp.int32, (8, heads * BLOCK), 1)
    return segment_at(block * BLOCK + lanes % BLOCK, ends_ref)[0:1]


def key_segments(starts, keeps, ends_ref):
    lanes = lax.broadcasted_iota(jnp.int32, (8, 2 * BLOCK), 1)
    first = lanes < BLOCK
    pieces = []
    for entry in range(0, LIST, 2):
        places = lanes + jnp.where(
            first, starts[entry] * BLOCK, (starts[entry + 1] - 1) * BLOCK
        )
        keep = jnp.where(first, keeps[entry], keeps[entry + 1]) > 0
        pieces.append(jnp.where(keep, segment_at(places, ends_ref), -1))
    return jnp.concatenate(pieces, axis=1)[0:1]


def gathered(ref, starts):
    return jnp.concatenate([ref[block_at(start), :] for start in starts], axis=0)


def block_parts(wide):
    return [wide[start : start + BLOCK] for start in range(0, wide.shape[0], BLOCK)]


def dot_nt(left, right):
    return lax.dot_general(left, right, (((1,), (1,)), ((), ())), preferred_element_type=F32)


def dot_tn(left, right):
    return lax.dot_general(left, right, (((0,), (0,)), ((), ())), preferred_element_type=F32)


def dot_nn(left, right):
    return lax.dot_general(left, right, (((1,), (0,)), ((), ())), preferred_element_type=F32)


def as_row(tall):
    count = tall.shape[0]
    row_ids = lax.broadcasted_iota(jnp.int32, (count, count), 0)
    lane_ids = lax.broadcasted_iota(jnp.int32, (count, count), 1)
    return jnp.sum(jnp.where(row_ids == lane_ids, tall, 0.0), axis=0, keepdims=True)


def together(running):
    while running:
        still = []
        for each in running:
            if next(each, 0) is None:
                still.append(each)
        running = still


def unit_block(unit, half, parts, rows_total):
    per = rows_total // parts // BLOCK // 2
    part = unit // per
    inside = unit - part * per
    return part, inside, part * 2 * per + half * per + inside


def forward_kernel(heads, half, ends_ref, lists_ref, admit_ref, q_ref, k_ref, v_ref, *rest):
    o_ref, lse_ref, token_segs, *held = rest
    held = held[0] if held else None
    scale = HD ** (-0.5)
    rows_total = q_ref.shape[0]
    units = o_ref.shape[0] * o_ref.shape[1] // BLOCK
    first_unit = GLOB if half == 0 else 0
    chunk = LIST * BLOCK
    fill_segments(token_segs, ends_ref)

    def store(unit, wide, top, total):
        part, inside, block = unit_block(unit, half, o_ref.shape[0], rows_total)
        out = head_fold(wide, heads)
        places = block * BLOCK + lax.broadcasted_iota(jnp.int32, out.shape, 0)
        out = jnp.where(places < ends_ref[ends_ref.shape[0] - 1], out, 0.0)
        o_ref[part, block_at(inside), :] = out.astype(BF16)
        lse_ref[unit] = jnp.broadcast_to(as_row(top + jnp.log(total)), lse_ref.shape[1:])

    def kept(block, key_segs):
        own = token_segs[block_at(block), :]
        return jnp.concatenate([own] * (chunk // own.shape[1]), axis=1) == key_segs

    def global_blocks():
        query_wide = jnp.concatenate(
            [head_spread(q_ref[block_at(block), :] * scale, heads) for block in range(GLOB)], axis=0
        )
        wide_rows = GLOB * heads * BLOCK

        def score(part, top):
            here = pl.ds(pl.multiple_of(part * chunk, chunk), chunk)
            places = part * chunk + lax.broadcasted_iota(jnp.int32, (8, chunk), 1)
            key_segs = segment_at(places, ends_ref)[0:1]
            keeps = [kept(block, key_segs) for block in range(GLOB)]
            scores = dot_nt(query_wide, k_ref[here, :])
            tops = []
            for place, rows in enumerate(block_parts(scores)):
                rows = jnp.where(keeps[place // heads], rows, NEG)
                held[place * BLOCK : (place + 1) * BLOCK, here] = rows
                tops.append(jnp.max(rows, axis=1, keepdims=True))
            return jnp.maximum(top, jnp.concatenate(tops, axis=0))

        top = lax.fori_loop(0, rows_total // chunk, score, jnp.full((wide_rows, 1), NEG, F32))

        def gather(part, carried):
            total, wide = carried
            here = pl.ds(pl.multiple_of(part * chunk, chunk), chunk)
            totals, weights = [], []
            for place, part_top in enumerate(block_parts(top)):
                weight = jnp.exp(held[place * BLOCK : (place + 1) * BLOCK, here] - part_top)
                totals.append(jnp.sum(weight, axis=1, keepdims=True))
                weights.append(weight.astype(BF16))
            wide = wide + dot_nn(jnp.concatenate(weights, axis=0), v_ref[here, :])
            return total + jnp.concatenate(totals, axis=0), wide

        total, wide = lax.fori_loop(
            0,
            rows_total // chunk,
            gather,
            (jnp.zeros((wide_rows, 1), F32), jnp.zeros((wide_rows, q_ref.shape[1]), F32)),
        )
        wide = wide * (1.0 / total)
        for block in range(GLOB):
            own = slice(block * heads * BLOCK, (block + 1) * heads * BLOCK)
            store(block, wide[own], top[own], total[own])

    if half == 0:
        global_blocks()

    def listed_block(unit):
        _, _, block = unit_block(unit, half, o_ref.shape[0], rows_total)
        query_wide = head_spread(q_ref[block_at(block), :] * scale, heads)
        starts = [lists_ref[block * LIST + entry] for entry in range(LIST)]
        keeps = [admit_ref[block * LIST + entry] for entry in range(LIST)]
        keep = kept(block, key_segments(starts, keeps, ends_ref))
        scores = dot_nt(query_wide, gathered(k_ref, starts))
        yield
        tops, totals, probs = [], [], []
        for rows in block_parts(scores):
            rows = jnp.where(keep, rows, NEG)
            top = jnp.max(rows, axis=1, keepdims=True)
            weights = jnp.exp(rows - top)
            total = jnp.sum(weights, axis=1, keepdims=True)
            probs.append((weights * (1.0 / total)).astype(BF16))
            tops.append(top)
            totals.append(total)
            yield
        wide = dot_nn(jnp.concatenate(probs, axis=0), gathered(v_ref, starts))
        store(unit, wide, jnp.concatenate(tops, axis=0), jnp.concatenate(totals, axis=0))

    def listed_group(group, _):
        together([listed_block(first_unit + 4 * group + place) for place in range(4)])
        return 0

    lax.fori_loop(0, (units - first_unit) // 4, listed_group, 0)
    together([listed_block(units - 1 - place) for place in range((units - first_unit) % 4)])


def backward_kernel(
    heads,
    ends_ref,
    lists_ref,
    admit_ref,
    q_ref,
    k_ref,
    v_ref,
    o_first,
    o_second,
    do_first,
    do_second,
    lse_first,
    lse_second,
    out_ref,
    token_segs,
    dk_ref,
    dv_ref,
    dq_ref,
):
    scale = HD ** (-0.5)
    rows_total, cols = q_ref.shape
    blocks = rows_total // BLOCK
    pair_rows = 2 * BLOCK
    fill_segments(token_segs, ends_ref)

    def prepare(pair, _):
        here = pl.ds(pl.multiple_of(pair * pair_rows, pair_rows), pair_rows)
        dk_ref[here, :] = jnp.zeros((pair_rows, cols), F32)
        dv_ref[here, :] = jnp.zeros((pair_rows, cols), F32)
        return 0

    lax.fori_loop(0, blocks // 2, prepare, 0)

    parts = o_first.shape[0]
    halves_of = ((o_first, do_first, lse_first), (o_second, do_second, lse_second))

    def query_side(unit, half):
        o_ref, do_ref, lse_ref = halves_of[half]
        part, inside, block = unit_block(unit, half, parts, rows_total)
        query_wide = head_spread(q_ref[block_at(block), :] * scale, heads)
        grad_rows = do_ref[part, block_at(inside), :]
        grad_wide = head_spread(grad_rows, heads)
        product = grad_rows.astype(F32) * o_ref[part, block_at(inside), :].astype(F32)
        spread = head_spread(product.astype(BF16), heads)
        delta = dot_nt(jnp.ones((8, cols), BF16), spread)[0:1]
        seg_row = query_segments(block, heads, ends_ref)
        return query_wide, grad_wide, delta, lse_ref[unit, 0:1], seg_row

    def unit(starts, keeps, query_wide, grad_wide, delta, lse, seg_row, finish_query):
        keys = gathered(k_ref, starts)
        scores = block_parts(dot_nt(keys, query_wide))
        prob_grads = block_parts(dot_nt(gathered(v_ref, starts), grad_wide))
        yield
        probs, score_grads = [], []
        for entry in range(LIST):
            wanted = seg_row if keeps is None else jnp.where(keeps[entry] > 0, seg_row, -1)
            own = token_segs[block_at(starts[entry]), :]
            keep = jnp.concatenate([own] * (seg_row.shape[1] // own.shape[1]), axis=1) == wanted
            prob = jnp.exp(jnp.where(keep, scores[entry], NEG) - lse)
            probs.append(prob.astype(BF16))
            score_grads.append((prob * (prob_grads[entry] - delta)).astype(BF16))
            if entry % 2:
                yield
        score_grad = jnp.concatenate(score_grads, axis=0)
        finish_query(dot_tn(score_grad, keys))
        dk = dot_nn(score_grad, query_wide)
        dv = dot_nn(jnp.concatenate(probs, axis=0), grad_wide)
        yield
        for entry in range(LIST):
            here = block_at(starts[entry])
            dk_ref[here, :] += dk[entry * BLOCK : (entry + 1) * BLOCK]
            dv_ref[here, :] += dv[entry * BLOCK : (entry + 1) * BLOCK]
        yield

    def store_query(block, wide):
        out_ref[block_at(block), 0:cols] = (head_fold(wide, heads) * scale).astype(BF16)

    def global_blocks():
        sides = [query_side(block, 0) for block in range(GLOB)]
        side = [jnp.concatenate(both, axis=axis) for both, axis in zip(zip(*sides), (0, 0, 1, 1, 1))]
        dq_ref[...] = jnp.zeros_like(dq_ref)

        def part_of(part, _):
            def add_query(wide):
                dq_ref[...] += wide

            together([unit([part * LIST + entry for entry in range(LIST)], None, *side, add_query)])
            return 0

        lax.fori_loop(0, blocks // LIST, part_of, 0)
        for block in range(GLOB):
            store_query(block, dq_ref[block * heads * BLOCK : (block + 1) * heads * BLOCK])

    global_blocks()

    def listed_block(place, half):
        _, _, block = unit_block(place, half, parts, rows_total)
        starts = [lists_ref[block * LIST + entry] for entry in range(LIST)]
        keeps = [admit_ref[block * LIST + entry] for entry in range(LIST)]
        return unit(
            starts, keeps, *query_side(place, half), functools.partial(store_query, block)
        )

    for half, first_unit in ((0, GLOB), (1, 0)):
        units = blocks // 2

        def listed_group(group, _):
            together([listed_block(first_unit + 4 * group + place, half) for place in range(4)])
            return 0

        lax.fori_loop(0, (units - first_unit) // 4, listed_group, 0)
        together([listed_block(units - 1 - place, half) for place in range((units - first_unit) % 4)])

    def finish(block, _):
        here = block_at(block)
        out_ref[here, cols : 2 * cols] = dk_ref[here, :].astype(BF16)
        out_ref[here, 2 * cols : 3 * cols] = dv_ref[here, :].astype(BF16)
        return 0

    lax.fori_loop(0, blocks, finish, 0)


def smem():
    return pl.BlockSpec(memory_space=pltpu.SMEM)


def column(rows, cols, index):
    return pl.BlockSpec((rows, cols), lambda step: (0, index))


def attention_forward(half, qkv, doc_ends, lists, admits, parts):
    rows = qkv.shape[0]
    cols = qkv.shape[1] // 3
    heads = cols // HD
    blocks = rows // BLOCK
    out = jax.ShapeDtypeStruct((parts, rows // parts // 2, cols), BF16)
    lse = jax.ShapeDtypeStruct((blocks // 2, 8, heads * BLOCK), F32)
    cube = lambda step: (0, 0, 0)
    return pl.pallas_call(
        functools.partial(forward_kernel, heads, half),
        grid=(1,),
        in_specs=[smem(), smem(), smem()] + [column(rows, cols, part) for part in range(3)],
        out_specs=[pl.BlockSpec(out.shape, cube), pl.BlockSpec(lse.shape, cube)],
        out_shape=[out, lse],
        scratch_shapes=[pltpu.VMEM((rows, 2 * BLOCK), jnp.int32)]
        + ([] if half else [pltpu.VMEM((GLOB * heads * BLOCK, rows), F32)]),
        compiler_params=pltpu.CompilerParams(vmem_limit_bytes=VMEM_LIMIT),
        cost_estimate=pl.CostEstimate(
            flops=rows * LIST * BLOCK * cols * heads * 5,
            bytes_accessed=8 * rows * cols,
            transcendentals=0,
        ),
    )(doc_ends, lists, admits, qkv, qkv, qkv)


def attention_backward(qkv, attended, attended_grad, lse, doc_ends, lists, admits):
    rows = qkv.shape[0]
    cols = qkv.shape[1] // 3
    heads = cols // HD
    cube = lambda step: (0, 0, 0)
    return pl.pallas_call(
        functools.partial(backward_kernel, heads),
        grid=(1,),
        in_specs=[smem(), smem(), smem()]
        + [column(rows, cols, part) for part in range(3)]
        + [pl.BlockSpec(part.shape, cube) for part in (*attended, *attended_grad, *lse)],
        out_specs=column(rows, 3 * cols, 0),
        out_shape=jax.ShapeDtypeStruct((rows, 3 * cols), BF16),
        scratch_shapes=[
            pltpu.VMEM((rows, 2 * BLOCK), jnp.int32),
            pltpu.VMEM((rows, cols), F32),
            pltpu.VMEM((rows, cols), F32),
            pltpu.VMEM((GLOB * heads * BLOCK, cols), F32),
        ],
        compiler_params=pltpu.CompilerParams(vmem_limit_bytes=VMEM_LIMIT),
        cost_estimate=pl.CostEstimate(
            flops=rows * LIST * BLOCK * cols * heads * 15,
            bytes_accessed=20 * rows * cols,
            transcendentals=0,
        ),
    )(doc_ends, lists, admits, qkv, qkv, qkv, *attended, *attended_grad, *lse)


def row_stats(rows):
    mean = jnp.mean(rows, axis=-1, keepdims=True)
    centre = rows - mean
    spread = jnp.mean(centre * centre, axis=-1, keepdims=True)
    inverse = lax.rsqrt(spread + EPS)
    return centre * inverse, inverse


def gelu_pair(inner):
    root = 0.7978845608028654
    cube = 0.044715
    square = inner * inner
    bent = jnp.tanh(inner * (root + (root * cube) * square))
    half = 0.5 + 0.5 * bent
    value = inner * half
    return value, half + value * (1.0 - bent) * (root + (3.0 * root * cube) * square)


def token_kernel(
    tile,
    index,
    ends_ref,
    att_ref,
    x_ref,
    cotangent_ref,
    out_own_ref,
    out_other_ref,
    up_own_ref,
    up_near_ref,
    up_far_ref,
    down_own_ref,
    down_near_ref,
    down_far_ref,
    up_bias_ref,
    gain_ref,
    bias_ref,
    down_bias_ref,
    trade_source,
    pair_source,
    act_in,
    pre_in,
    second_in,
    hidden_in,
    grad_in,
    att_in,
    output_ref,
    hidden_grad_ref,
    datt_ref,
    act_ref,
    pre_ref,
    second_ref,
    hidden_low_ref,
    grad_low_ref,
    att_rows_ref,
    sums_ref,
    unit_sums_ref,
    trade_target,
    pair_target,
    hidden,
    normed,
    inverse,
    ffn,
    second_grad,
    grad_rows,
    up_slots,
    down_slots,
    slot_sems,
    row_sems,
    pair_sems,
    *trade_sems,
):
    step = pl.program_id(0)
    steps = pl.num_programs(0)
    rows = hidden.shape[0]
    parts = att_ref.shape[0]
    tiles = [slice(start, start + tile) for start in range(0, rows, tile)]
    chunk = up_slots.shape[2]
    own_steps = up_own_ref.shape[1] // chunk
    near_steps = up_near_ref.shape[1] // chunk

    def copies(up_from, down_from, index, slot):
        here = pl.ds(pl.multiple_of(index * chunk, chunk), chunk)
        return (
            pltpu.make_async_copy(up_from.at[:, here], up_slots.at[slot], slot_sems.at[0, slot]),
            pltpu.make_async_copy(down_from.at[here], down_slots.at[slot], slot_sems.at[1, slot]),
        )

    def fetch(index):
        def begin(up_from, down_from, first):
            for copy in copies(up_from, down_from, index - first, index % 2):
                copy.start()

        @pl.when(index < own_steps)
        def _():
            begin(up_own_ref, down_own_ref, 0)

        @pl.when((index >= own_steps) & (index < own_steps + near_steps))
        def _():
            begin(up_near_ref, down_near_ref, own_steps)

        @pl.when(index >= own_steps + near_steps)
        def _():
            begin(up_far_ref, down_far_ref, own_steps + near_steps)

    half = parts // 2
    me = lax.axis_index("seq")
    place = lax.axis_index("mp")
    own_place = place * half
    other_place = (1 - place) * half
    first_row = index * rows
    row_copies = [
        pltpu.make_async_copy(source.at[place, pl.ds(first_row, rows)], target, row_sems.at[which])
        for which, (source, target) in enumerate(((x_ref, hidden), (cotangent_ref, grad_rows)))
    ]
    pair = (pair_source, pair_target, pair_sems) if index else None
    trade = Trade(trade_source, trade_target, *trade_sems, pair)
    out_parts = [(own_place + part, out_own_ref, part) for part in range(half)]
    out_parts += [(other_place + part, out_other_ref, part) for part in range(half)]

    @pl.when(step == 0)
    def _():
        for copy in row_copies:
            copy.start()
        fetch(step)
        trade.start()

    @pl.when(step + 1 < steps)
    def _():
        fetch(step + 1)

    @pl.when(step == 0)
    def _():
        for copy in row_copies:
            copy.wait()
        for here in tiles:
            total = hidden[here, :]
            for part, weight_ref, index in out_parts:
                total = total + dot_nn(att_ref[part, here, :], weight_ref[index])
            for part in range(parts):
                cols = att_ref.shape[2]
                att_rows_ref[here, part * cols : (part + 1) * cols] = att_ref[part, here, :]
            hidden[here, :] = total
            unit, scale = row_stats(total)
            normed[here, :] = unit
            inverse[here, :] = jnp.broadcast_to(scale, (tile, inverse.shape[1]))
            second_ref[here, :] = (unit * gain_ref[...] + bias_ref[...]).astype(BF16)
            grad_low_ref[here, :] = grad_rows[here, :].astype(BF16)
            ffn[here, :] = jnp.zeros((tile, ffn.shape[1]), F32)
            second_grad[here, :] = jnp.zeros((tile, ffn.shape[1]), F32)

    slot = step % 2
    for copy in copies(up_own_ref, down_own_ref, 0, slot):
        copy.wait()
    up_ref = up_slots.at[slot]
    down_ref = down_slots.at[slot]
    unit_sum = jnp.zeros((1, chunk), F32)
    for here in tiles:
        inner = dot_nn(second_ref[here, :], up_ref[...]) + up_bias_ref[...]
        act_grad = dot_nt(grad_low_ref[here, :], down_ref[...])
        value, slope = gelu_pair(inner)
        value = value.astype(BF16)
        pre_grad = (act_grad * slope).astype(BF16)
        act_ref[here, :] = value
        pre_ref[here, :] = pre_grad
        unit_sum = unit_sum + jnp.sum(pre_grad.astype(F32), axis=0, keepdims=True)
        ffn[here, :] += dot_nn(value, down_ref[...])
        second_grad[here, :] += dot_nt(pre_grad, up_ref[...])
    unit_sums_ref[...] = jnp.broadcast_to(unit_sum, unit_sums_ref.shape)

    @pl.when(step == steps - 1)
    def _():
        width = ffn.shape[1]
        grad_sum = jnp.zeros((1, width), F32)
        gain_sum = jnp.zeros((1, width), F32)
        bias_sum = jnp.zeros((1, width), F32)
        for number, here in enumerate(tiles):
            output_ref[here, :] = (hidden[here, :] + ffn[here, :] + down_bias_ref[...]).astype(BF16)
            grad = grad_rows[here, :]
            back = second_grad[here, :]
            unit = normed[here, :]
            scaled = back * gain_ref[...]
            through = (
                scaled
                - jnp.mean(scaled, axis=-1, keepdims=True)
                - unit * jnp.mean(scaled * unit, axis=-1, keepdims=True)
            )
            total = grad + inverse[here, 0:1] * through
            hidden_grad_ref[here, :] = total
            low = total.astype(BF16)
            hidden_low_ref[here, :] = low
            grad_sum = grad_sum + jnp.sum(grad, axis=0, keepdims=True)
            gain_sum = gain_sum + jnp.sum(back * unit, axis=0, keepdims=True)
            bias_sum = bias_sum + jnp.sum(back, axis=0, keepdims=True)
            for part, weight_ref, piece in out_parts:
                spread = dot_nt(low, weight_ref[piece])
                places = me * 2 * rows + first_row + number * tile
                places = places + lax.broadcasted_iota(jnp.int32, spread.shape, 0)
                inside = places < ends_ref[ends_ref.shape[0] - 1]
                datt_ref[part, here, :] = jnp.where(inside, spread, 0.0).astype(BF16)
        sums_ref[...] = jnp.concatenate(
            [grad_sum, gain_sum, bias_sum, jnp.zeros((5, width), F32)], axis=0
        )
        trade.finish()


def token_part(
    index, doc_ends, att, layer_input, cotangent, outs, ups, downs, up_bias, gain, bias, down_bias, source, pair, kept
):
    parts, rows, cols = att.shape
    width = layer_input.shape[2]
    units = up_bias.shape[1]
    chunk = min(512, units // 4)
    whole = 2 * rows
    shapes = [(whole, units)] * 2 + [(whole, width)] * 4
    if kept is None:
        kept = [jnp.zeros((8, 128), BF16)] * len(shapes)
        aliases = {}
    else:
        aliases = {18 + place: 3 + place for place in range(len(shapes))}
    half = lambda step: (index, 0)
    fixed = lambda step: (0, 0)
    any_spec = pl.BlockSpec(memory_space=pl.ANY)
    cube = lambda step: (0, 0, 0)
    vector = pl.BlockSpec((1, width), fixed)
    return pl.pallas_call(
        functools.partial(token_kernel, min(256, rows), index),
        grid=(units // chunk,),
        in_specs=[
            smem(),
            pl.BlockSpec((parts, rows, cols), cube),
            any_spec,
            any_spec,
            pl.BlockSpec((parts // 2, cols, width), cube),
            pl.BlockSpec((parts // 2, cols, width), cube),
        ]
        + [any_spec] * 6
        + [pl.BlockSpec((1, chunk), lambda step: (0, step)), vector, vector, vector]
        + [any_spec] * (2 + len(shapes)),
        out_specs=[
            pl.BlockSpec((rows, width), fixed),
            pl.BlockSpec((rows, width), fixed),
            pl.BlockSpec((parts, rows, cols), cube),
            pl.BlockSpec((rows, chunk), lambda step: (index, step)),
            pl.BlockSpec((rows, chunk), lambda step: (index, step)),
            pl.BlockSpec((rows, width), half),
            pl.BlockSpec((rows, width), half),
            pl.BlockSpec((rows, width), half),
            pl.BlockSpec((rows, width), half),
            pl.BlockSpec((8, width), fixed),
            pl.BlockSpec((8, chunk), lambda step: (0, step)),
            any_spec,
            any_spec,
        ],
        scratch_shapes=[
            pltpu.VMEM((rows, width), F32),
            pltpu.VMEM((rows, width), F32),
            pltpu.VMEM((rows, 128), F32),
            pltpu.VMEM((rows, width), F32),
            pltpu.VMEM((rows, width), F32),
            pltpu.VMEM((rows, width), F32),
            pltpu.VMEM((2, width, chunk), BF16),
            pltpu.VMEM((2, chunk, width), BF16),
            pltpu.SemaphoreType.DMA((2, 2)),
            pltpu.SemaphoreType.DMA((2,)),
            pltpu.SemaphoreType.DMA((2,)),
        ]
        + trade_scratch(parts),
        out_shape=[
            jax.ShapeDtypeStruct((rows, width), BF16),
            jax.ShapeDtypeStruct((rows, width), F32),
            jax.ShapeDtypeStruct((parts, rows, cols), BF16),
        ]
        + [jax.ShapeDtypeStruct(shape, BF16) for shape in shapes]
        + [
            jax.ShapeDtypeStruct((8, width), F32),
            jax.ShapeDtypeStruct((8, units), F32),
            jax.ShapeDtypeStruct((parts, rows, cols), BF16),
            jax.ShapeDtypeStruct(pair.shape, BF16),
        ],
        input_output_aliases=aliases,
        compiler_params=pltpu.CompilerParams(
            collective_id=5 + index, has_side_effects=True, vmem_limit_bytes=VMEM_LIMIT
        ),
        cost_estimate=pl.CostEstimate(
            flops=rows * width * (8 * units + 4 * width),
            bytes_accessed=8 * units * width,
            transcendentals=0,
        ),
    )(
        doc_ends,
        att,
        layer_input,
        cotangent,
        *outs,
        *ups,
        *downs,
        up_bias,
        gain,
        bias,
        down_bias,
        source,
        pair,
        *kept,
    )


def greet(me, count, partner=None):
    barrier = pltpu.get_barrier_semaphore()

    @pl.when(me > 0)
    def _():
        pl.semaphore_signal(barrier, inc=1, device_id={"seq": me - 1}, device_id_type=MESH)

    @pl.when(me < count - 1)
    def _():
        pl.semaphore_signal(barrier, inc=1, device_id={"seq": me + 1}, device_id_type=MESH)

    peers = jnp.minimum(me, 1) + jnp.minimum(count - 1 - me, 1)
    if partner is not None:
        pl.semaphore_signal(barrier, inc=1, device_id={"mp": partner}, device_id_type=MESH)
        peers = peers + 1
    pl.semaphore_wait(barrier, peers)


def gather_kernel(
    count,
    chunks,
    half_cols,
    x_ref,
    gain_ref,
    bias_ref,
    weight_ref,
    all_ref,
    qkv_ref,
    own_ref,
    rows_in,
    shards,
    results,
    weight,
    weight_sems,
    load_sems,
    send_sems,
    recv_sems,
    all_sems,
    qkv_sems,
):
    me = lax.axis_index("seq")
    place = lax.axis_index("mp")
    step = rows_in.shape[0] // chunks
    cols = weight.shape[1] // 3

    def at(chunk):
        return pl.ds(pl.multiple_of(chunk * step, step), step)

    def load(chunk):
        return pltpu.make_async_copy(
            x_ref.at[place, at(chunk)], rows_in.at[at(chunk)], load_sems.at[chunk]
        )

    def send(side, hop, chunk):
        shard = me - hop if side == 0 else me + hop
        target = me + 1 if side == 0 else me - 1
        return pltpu.make_async_remote_copy(
            src_ref=shards.at[shard, at(chunk)],
            dst_ref=shards.at[shard, at(chunk)],
            send_sem=send_sems.at[side, hop, chunk],
            recv_sem=recv_sems.at[side, hop, chunk],
            device_id={"seq": target},
            device_id_type=MESH,
        )

    def keep_all(shard, chunk):
        return pltpu.make_async_copy(
            shards.at[shard, at(chunk)], all_ref.at[shard, at(chunk)], all_sems.at[shard, chunk]
        )

    def keep_qkv(shard, chunk):
        return pltpu.make_async_copy(
            results.at[shard, at(chunk)], qkv_ref.at[shard, at(chunk)], qkv_sems.at[shard, chunk]
        )

    def over_chunks(body):
        def run(chunk, _):
            body(chunk)
            return 0

        lax.fori_loop(0, chunks, run, 0)

    over_chunks(lambda chunk: load(chunk).start())
    greet(me, count, 1 - place)

    here = (me * cols) // half_cols == place
    fetch = pltpu.make_async_remote_copy(
        src_ref=weight_ref,
        dst_ref=weight,
        send_sem=weight_sems.at[0],
        recv_sem=weight_sems.at[1],
        device_id={"mp": 1 - place},
        device_id_type=MESH,
    )
    copy = pltpu.make_async_copy(weight_ref, weight, weight_sems.at[2])

    @pl.when(here)
    def _():
        fetch.start()
        copy.start()

    def norm(chunk):
        load(chunk).wait()
        unit, _ = row_stats(rows_in[at(chunk), :])
        shards[me, at(chunk), :] = (unit * gain_ref[...] + bias_ref[...]).astype(BF16)
        keep_all(me, chunk).start()

        @pl.when(me < count - 1)
        def _():
            send(0, 0, chunk).start()

        @pl.when(me > 0)
        def _():
            send(1, 0, chunk).start()

    over_chunks(norm)

    def project(shard, chunk):
        rows = dot_nn(shards[shard, at(chunk), :], weight[...])
        results[shard, at(chunk), :] = rows.astype(BF16)
        keep_qkv(shard, chunk).start()

    def receive(hop, chunk):
        @pl.when(me >= hop + 1)
        def _():
            send(0, hop, chunk).wait_recv()
            if hop + 1 < count - 1:

                @pl.when(me < count - 1)
                def _():
                    send(0, hop + 1, chunk).start()

            keep_all(me - hop - 1, chunk).start()

        @pl.when(me + hop + 1 < count)
        def _():
            send(1, hop, chunk).wait_recv()
            if hop + 1 < count - 1:

                @pl.when(me > 0)
                def _():
                    send(1, hop + 1, chunk).start()

            keep_all(me + hop + 1, chunk).start()

    for hop in range(count - 2):
        over_chunks(functools.partial(receive, hop))

    @pl.when(here)
    def _():
        copy.wait()

    @pl.when(jnp.logical_not(here))
    def _():
        fetch.wait_recv()

    keep_weight = pltpu.make_async_copy(weight, own_ref, weight_sems.at[3])
    keep_weight.start()

    def last(chunk):
        project(me, chunk)
        for hop in range(count - 1):
            if hop == count - 2:
                receive(hop, chunk)

            @pl.when(me >= hop + 1)
            def _():
                project(me - hop - 1, chunk)

            @pl.when(me + hop + 1 < count)
            def _():
                project(me + hop + 1, chunk)

    over_chunks(last)

    def finish(chunk):
        for hop in range(count - 1):

            @pl.when((me >= hop) & (me < count - 1))
            def _():
                send(0, hop, chunk).wait_send()

            @pl.when((me + hop < count) & (me > 0))
            def _():
                send(1, hop, chunk).wait_send()

        for shard in range(count):
            keep_all(shard, chunk).wait()
            keep_qkv(shard, chunk).wait()

    over_chunks(finish)
    keep_weight.wait()

    @pl.when(here)
    def _():
        fetch.wait_send()


def gather_project(layer_input, gain, bias, weight, half_cols):
    count = lax.axis_size("seq")
    _, rows, width = layer_input.shape
    cols = weight.shape[1]
    chunks = max(1, rows // 128)
    any_spec = pl.BlockSpec(memory_space=pl.ANY)
    vmem = pl.BlockSpec(memory_space=pltpu.VMEM)
    dma = pltpu.SemaphoreType.DMA
    return pl.pallas_call(
        functools.partial(gather_kernel, count, chunks, half_cols),
        in_specs=[any_spec, vmem, vmem, vmem],
        out_specs=[any_spec, any_spec, any_spec],
        out_shape=[
            jax.ShapeDtypeStruct((count, rows, width), BF16),
            jax.ShapeDtypeStruct((count, rows, cols), BF16),
            jax.ShapeDtypeStruct((width, cols), BF16),
        ],
        scratch_shapes=[
            pltpu.VMEM((rows, width), F32),
            pltpu.VMEM((count, rows, width), BF16),
            pltpu.VMEM((count, rows, cols), BF16),
            pltpu.VMEM((width, cols), BF16),
            dma((4,)),
            dma((chunks,)),
            dma((2, count - 1, chunks)),
            dma((2, count - 1, chunks)),
            dma((count, chunks)),
            dma((count, chunks)),
        ],
        compiler_params=pltpu.CompilerParams(
            collective_id=0, has_side_effects=True, vmem_limit_bytes=VMEM_LIMIT
        ),
        cost_estimate=pl.CostEstimate(
            flops=150_000_000_000, bytes_accessed=1, transcendentals=0
        ),
    )(layer_input, gain, bias, weight)


class VectorSum:
    def __init__(self, group, line, sems):
        self.group, self.line, self.sems = group, line, sems
        self.me, self.count = lax.axis_index("seq"), lax.axis_size("seq")
        self.pairs = lax.axis_size("mp")
        self.members = lax.axis_size("batch") * self.pairs
        self.mine = lax.axis_index("batch") * self.pairs + lax.axis_index("mp")

    def member(self, distance):
        other = lax.rem(self.mine + distance, self.members)
        return {"batch": other // self.pairs, "mp": lax.rem(other, self.pairs)}

    def along(self, distance):
        return {"seq": lax.rem(self.me + distance, self.count)}

    def greet(self):
        barrier = pltpu.get_barrier_semaphore()
        for distance in range(1, self.members):
            pl.semaphore_signal(
                barrier, inc=1, device_id=self.member(distance), device_id_type=MESH
            )
        for distance in range(1, self.count):
            pl.semaphore_signal(barrier, inc=1, device_id=self.along(distance), device_id_type=MESH)
        pl.semaphore_wait(barrier, self.members + self.count - 2)

    def share(self, distance, along):
        buffer, place = (self.line, self.me) if along else (self.group, self.mine)
        which = distance - 1 + (self.members - 1 if along else 0)
        return pltpu.make_async_remote_copy(
            src_ref=buffer.at[place],
            dst_ref=buffer.at[place],
            send_sem=self.sems.at[0, which],
            recv_sem=self.sems.at[1, which],
            device_id=self.along(distance) if along else self.member(distance),
            device_id_type=MESH,
        )

    def start(self, value):
        self.group[self.mine] = value
        for distance in range(1, self.members):
            self.share(distance, False).start()

    def middle(self):
        for distance in range(1, self.members):
            self.share(distance, False).wait()
        total = self.group[0]
        for place in range(1, self.members):
            total = total + self.group[place]
        self.line[self.me] = total
        for distance in range(1, self.count):
            self.share(distance, True).start()

    def finish(self):
        for distance in range(1, self.count):
            self.share(distance, True).wait()
        total = self.line[0]
        for place in range(1, self.count):
            total = total + self.line[place]
        return total


class Extra:
    def __init__(self, kind, source, target, sems):
        self.source, self.target, self.sems = source, target, sems
        batch, place = lax.axis_index("batch"), lax.axis_index("mp")
        self.local = None
        if kind == "mp":
            self.moves = [(source, target, {"mp": 1 - place})]
        else:
            count = source.shape[0]
            pairs = lax.axis_size("mp")
            mine = batch * pairs + place
            self.moves = []
            for distance in range(1, count):
                other = lax.rem(mine + distance, count)
                device = {"batch": other // pairs, "mp": lax.rem(other, pairs)}
                self.moves.append((source.at[other], target.at[mine], device))
            self.local = (source.at[mine], target.at[mine])

    def copies(self):
        for index, (source, target, device) in enumerate(self.moves):
            yield pltpu.make_async_remote_copy(
                src_ref=source,
                dst_ref=target,
                send_sem=self.sems.at[0, index],
                recv_sem=self.sems.at[1, index],
                device_id=device,
                device_id_type=MESH,
            )
        if self.local is not None:
            yield pltpu.make_async_copy(*self.local, self.sems.at[0, len(self.moves)])

    def start(self):
        for copy in self.copies():
            copy.start()

    def finish(self):
        for copy in self.copies():
            copy.wait()


def extra_moves(kind, source):
    return 1 if kind == "mp" else source.shape[0]


def in_rows(vectors, width):
    pieces = []
    for row in range(vectors.shape[0]):
        for start in range(0, vectors.shape[1], width):
            pieces.append(vectors[row : row + 1, start : start + width])
    return jnp.concatenate(pieces, axis=0)


class WeightBegin:
    def __init__(self, terms, targets, near_sum, own_sum, down_sum, sems):
        self.terms, self.targets, self.sems = terms, targets, sems
        self.near_sum, self.own_sum, self.down_sum = near_sum, own_sum, down_sum

    def copies(self):
        own_out, near_target, down_out, down_target = self.targets
        batch, place = lax.axis_index("batch"), lax.axis_index("mp")
        side = (batch // 2) % 2
        size = self.down_sum.shape[1] // 2
        kept = pl.ds(pl.multiple_of(side * size, 128), size)
        there = pl.ds(pl.multiple_of((1 - side) * size, 128), size)
        return [
            pltpu.make_async_remote_copy(
                src_ref=self.near_sum,
                dst_ref=near_target,
                send_sem=self.sems.at[0],
                recv_sem=self.sems.at[1],
                device_id={"mp": 1 - place},
                device_id_type=MESH,
            ),
            pltpu.make_async_remote_copy(
                src_ref=self.down_sum.at[:, there],
                dst_ref=down_target,
                send_sem=self.sems.at[2],
                recv_sem=self.sems.at[3],
                device_id={"batch": batch + 2 - 4 * side},
                device_id_type=MESH,
            ),
            pltpu.make_async_copy(self.own_sum, own_out, self.sems.at[4]),
            pltpu.make_async_copy(self.down_sum.at[:, kept], down_out, self.sems.at[5]),
        ]

    def start(self):
        keep, come, down, down_come = self.terms
        rows = keep.shape[1]
        step = min(128, rows)

        def add(index, _):
            here = pl.ds(pl.multiple_of(index * step, step), step)
            near = keep[1, here, :].astype(F32) + come[1, here, :].astype(F32)
            own = keep[0, here, :].astype(F32) + come[0, here, :].astype(F32)
            low = down[here, :].astype(F32) + down_come[here, :].astype(F32)
            self.near_sum[here, :] = near.astype(BF16)
            self.own_sum[here, :] = own.astype(BF16)
            self.down_sum[here, :] = low.astype(BF16)
            return 0

        lax.fori_loop(0, rows // step, add, 0)
        for copy in self.copies():
            copy.start()

    def finish(self):
        for copy in self.copies():
            copy.wait()


class WeightChain:
    def __init__(self, terms, qkv_terms, gathered, heads_ref, sending, received, result, head_sum, heads_in, sems):
        self.terms = terms
        self.qkv_terms, self.gathered, self.heads_ref = qkv_terms, gathered, heads_ref
        self.sending, self.received, self.result = sending, received, result
        self.head_sum, self.heads_in, self.sems = head_sum, heads_in, sems
        self.me, self.count = lax.axis_index("seq"), lax.axis_size("seq")
        self.batch, self.place = lax.axis_index("batch"), lax.axis_index("mp")
        self.rows = result.shape[1]
        self.chunks = 2
        self.step = self.rows // self.chunks
        self.steps = (self.count - 1) * self.chunks
        self.members = qkv_terms.shape[0]
        self.mine = self.batch * 2 + self.place
        self.used = 2 * self.steps

    def at(self, chunk):
        return pl.ds(pl.multiple_of(chunk * self.step, self.step), self.step)

    def term(self, target, chunk):
        here = pl.ds(pl.multiple_of(target * self.rows + chunk * self.step, self.step), self.step)
        own, own_come, down, down_come = (term[here, :].astype(F32) for term in self.terms)
        return jnp.concatenate([own + own_come, down + down_come], axis=1)

    def send(self, side, message, chunk):
        which = (side * (self.count - 1) + message) * self.chunks + chunk
        return pltpu.make_async_remote_copy(
            src_ref=self.sending.at[side, message, self.at(chunk)],
            dst_ref=self.received.at[side, message, self.at(chunk)],
            send_sem=self.sems.at[0, which],
            recv_sem=self.sems.at[1, which],
            device_id={"seq": self.me + 1 - 2 * side},
            device_id_type=MESH,
        )

    def flow(self, side, index):
        message, chunk = index // self.chunks, index % self.chunks
        target = (1 - side) * (self.count - 1 - message) + side * message

        @pl.when((target - self.me) * (1 - 2 * side) > 0)
        def _():
            total = self.term(target, chunk)
            first = (1 - side) * self.me + side * (self.count - 1 - self.me)

            @pl.when(first == 0)
            def _():
                self.sending[side, message, self.at(chunk), :] = total.astype(BF16)

            @pl.when(first > 0)
            def _():
                self.send(side, message, chunk).wait_recv()
                come = self.received[side, message, self.at(chunk), :].astype(F32)
                self.sending[side, message, self.at(chunk), :] = (total + come).astype(BF16)

            self.send(side, message, chunk).start()

    def heads_line(self, distance):
        other = lax.rem(self.me + distance, self.count)
        which = self.used + distance - 1
        return pltpu.make_async_remote_copy(
            src_ref=self.head_sum.at[other],
            dst_ref=self.heads_in.at[self.me],
            send_sem=self.sems.at[0, which],
            recv_sem=self.sems.at[1, which],
            device_id={"seq": other},
            device_id_type=MESH,
        )

    def heads_member(self, distance):
        other = lax.rem(self.mine + distance, self.members)
        which = self.used + self.count - 1 + distance - 1
        parts = self.count // 2
        return pltpu.make_async_remote_copy(
            src_ref=self.heads_in.at[pl.ds(lax.rem(other, 2) * parts, parts)],
            dst_ref=self.heads_ref.at[self.mine],
            send_sem=self.sems.at[0, which],
            recv_sem=self.sems.at[1, which],
            device_id={"batch": other // 2, "mp": lax.rem(other, 2)},
            device_id_type=MESH,
        )

    def heads_own(self):
        parts = self.count // 2
        return pltpu.make_async_copy(
            self.heads_in.at[pl.ds(self.place * parts, parts)],
            self.heads_ref.at[self.mine],
            self.sems.at[0, self.used + self.count + self.members - 2],
        )

    def piece(self, index):
        which = self.used + self.count + self.members - 1 + index
        side = (self.batch // 2) % 2
        parity = self.batch % 2
        other = self.batch + 1 - 2 * parity if index else self.batch + 2 - 4 * side
        source = max(index - 1, 0)
        return pltpu.make_async_remote_copy(
            src_ref=self.result.at[source],
            dst_ref=self.result.at[source + (2 if index else 1)],
            send_sem=self.sems.at[0, which],
            recv_sem=self.sems.at[1, which],
            device_id={"batch": other},
            device_id_type=MESH,
        )

    def start(self):
        total = self.qkv_terms[0].astype(F32)
        for member in range(1, self.members):
            total = total + self.qkv_terms[member].astype(F32)
        self.head_sum[...] = total.astype(BF16)
        self.heads_in[self.me] = self.head_sum[self.me]
        for distance in range(1, self.count):
            self.heads_line(distance).start()

    def own(self):
        for chunk in range(self.chunks):
            here = self.at(chunk)
            total = self.term(self.me, chunk)

            @pl.when(self.me > 0)
            def _():
                self.send(0, self.count - 1 - self.me, chunk).wait_recv()

            @pl.when(self.me < self.count - 1)
            def _():
                self.send(1, self.me, chunk).wait_recv()

            left = self.received[0, jnp.minimum(self.count - 1 - self.me, self.count - 2), here, :]
            right = self.received[1, jnp.minimum(self.me, self.count - 2), here, :]
            total = total + jnp.where(self.me > 0, left.astype(F32), 0.0)
            total = total + jnp.where(self.me < self.count - 1, right.astype(F32), 0.0)
            self.result[0, here, :] = total.astype(BF16)
        self.piece(0).start()
        for distance in range(1, self.count):
            self.heads_line(distance).wait()
        for distance in range(1, self.members):
            self.heads_member(distance).start()
        self.heads_own().start()

    def spread(self):
        self.piece(0).wait()
        self.piece(1).start()
        self.piece(2).start()

    def finish(self):
        for index in range(self.steps):
            message, chunk = index // self.chunks, index % self.chunks

            @pl.when(self.count - 1 - message > self.me)
            def _():
                self.send(0, message, chunk).wait_send()

            @pl.when(message < self.me)
            def _():
                self.send(1, message, chunk).wait_send()

        self.piece(1).wait()
        self.piece(2).wait()
        self.heads_own().wait()
        for distance in range(1, self.members):
            self.heads_member(distance).wait()
        copy = pltpu.make_async_copy(
            self.result, self.gathered, self.sems.at[0, self.used + self.count + self.members + 2]
        )
        copy.start()
        copy.wait()


def return_kernel(
    count,
    chunks,
    lag,
    index_of,
    kinds,
    parts_ref,
    weight_ref,
    edge_weight_ref,
    x_ref,
    hidden_grad_ref,
    gain_ref,
    vectors_ref,
    *rest,
):
    extras = len(kinds)
    sources, rest = rest[:extras], rest[extras:]
    weight_terms, rest = rest[:4], rest[4:]
    if index_of:
        qkv_terms, *rest = rest
    input_ref, sums_ref, total_ref, other_ref, *rest = rest
    targets, rest = rest[:extras], rest[extras:]
    late_out, rest = (rest[:2], rest[2:]) if index_of else (rest[:4], rest[4:])
    rows_in, sending, received, edge_in, summed, group, line, load_sem, *rest = rest
    send_sems, recv_sems, pair_send_sems, pair_recv_sems, vector_sems, *extra_sems = rest
    late = extra_sems[extras:]
    extras = [Extra(*each) for each in zip(kinds, sources, targets, extra_sems)]
    me = lax.axis_index("seq")
    place = lax.axis_index("mp")
    rows = hidden_grad_ref.shape[0]
    step = rows // chunks
    width = gain_ref.shape[1]
    steps = (count - 1) * chunks

    def at(chunk):
        return pl.ds(pl.multiple_of(chunk * step, step), step)

    load = pltpu.make_async_copy(x_ref.at[place, pl.ds(index_of * rows, rows)], rows_in, load_sem.at[0])
    load.start()
    vector_sum = VectorSum(group, line, vector_sems)
    vector_sum.greet()
    if index_of == 0:
        vector_sum.start(vectors_ref[...])
    for extra in extras:
        extra.start()

    def send(side, message, chunk):
        return pltpu.make_async_remote_copy(
            src_ref=sending.at[side, message, at(chunk)],
            dst_ref=received.at[side, message, at(chunk)],
            send_sem=send_sems.at[side, message, chunk],
            recv_sem=recv_sems.at[side, message, chunk],
            device_id={"seq": me + 1 - 2 * side},
            device_id_type=MESH,
        )

    def send_edge(side, message, chunk):
        target = (1 - side) * (count - 1 - message) + side * message
        return pltpu.make_async_remote_copy(
            src_ref=parts_ref.at[target, at(chunk)],
            dst_ref=edge_in.at[message, at(chunk)],
            send_sem=send_sems.at[side, message, chunk],
            recv_sem=recv_sems.at[side, message, chunk],
            device_id={"seq": me + 1 - 2 * side},
            device_id_type=MESH,
        )

    def flow(side, index):
        message = index // chunks
        chunk = index % chunks
        target = (1 - side) * (count - 1 - message) + side * message

        @pl.when((target - me) * (1 - 2 * side) > 0)
        def _():
            first = (1 - side) * me + side * (count - 1 - me)

            @pl.when(first == 0)
            def _():
                send_edge(side, message, chunk).start()

            @pl.when(first == 1)
            def _():
                send_edge(side, message, chunk).wait_recv()
                total = dot_nt(parts_ref[target, at(chunk), :], weight_ref[...])
                total = total + dot_nt(edge_in[message, at(chunk), :], edge_weight_ref[...])
                sending[side, message, at(chunk), :] = total.astype(BF16)
                send(side, message, chunk).start()

            @pl.when(first > 1)
            def _():
                total = dot_nt(parts_ref[target, at(chunk), :], weight_ref[...])
                send(side, message, chunk).wait_recv()
                come = received[side, message, at(chunk), :].astype(F32)
                sending[side, message, at(chunk), :] = (total + come).astype(BF16)
                send(side, message, chunk).start()

    if index_of:
        chain = WeightChain(weight_terms, qkv_terms, *late_out, *late)
        chain.start()
        begin = None
    else:
        chain = None
        begin = WeightBegin(weight_terms, late_out, *late)
    ahead = chain.steps if chain else 0
    near = me // (count // 2)

    def pair(chunk):
        return pltpu.make_async_remote_copy(
            src_ref=input_ref.at[at(chunk)],
            dst_ref=other_ref.at[at(chunk)],
            send_sem=pair_send_sems.at[chunk],
            recv_sem=pair_recv_sems.at[chunk],
            device_id={"mp": 1 - place},
            device_id_type=MESH,
        )

    def own(chunk):
        here = at(chunk)
        summed[...] = dot_nt(parts_ref[me, here, :], weight_ref[...])
        for side in range(2):
            first = me if side == 0 else count - 1 - me
            message = count - 1 - me if side == 0 else me

            @pl.when(first == 1)
            def _():
                send_edge(side, message, chunk).wait_recv()
                summed[...] += dot_nt(edge_in[message, here, :], edge_weight_ref[...])

            @pl.when(first > 1)
            def _():
                send(side, message, chunk).wait_recv()
                summed[...] += received[side, message, here, :].astype(F32)

        total = summed[...]
        unit, inverse = row_stats(rows_in[here, :])
        scaled = total * gain_ref[...]
        through = (
            scaled
            - jnp.mean(scaled, axis=-1, keepdims=True)
            - unit * jnp.mean(scaled * unit, axis=-1, keepdims=True)
        )
        input_ref[here, :] = (hidden_grad_ref[here, :] + inverse * through).astype(BF16)
        if index_of:
            pair(chunk).start()
        sums_ref[0:1, :] += jnp.sum(total * unit, axis=0, keepdims=True)
        sums_ref[1:2, :] += jnp.sum(total, axis=0, keepdims=True)

    sums_ref[...] = jnp.zeros_like(sums_ref)
    load.wait()
    wait_for = ahead + ((count - 2) * chunks + lag + 1 if index_of else steps + lag)
    steps_all = ahead + steps

    def flow_of(side, index):
        if chain is not None:

            @pl.when(index < ahead)
            def _():
                chain.flow(side, index)

        @pl.when(index >= ahead)
        def _():
            flow(side, index - ahead)

    def advance(index, _):
        @pl.when(index < steps_all)
        def _():
            flow_of(near, index)

        @pl.when((index >= lag) & (index < steps_all + lag))
        def _():
            flow_of(1 - near, index - lag)

        if begin is not None:
            @pl.when(index == 2)
            def _():
                begin.start()

        if chain is not None:

            @pl.when(index == ahead + lag + 2)
            def _():
                chain.own()

            @pl.when(index == ahead + lag + 6)
            def _():
                chain.spread()

        @pl.when(index >= wait_for)
        def _():
            own(index - wait_for)

        return 0

    lax.fori_loop(0, wait_for + chunks, advance, 0)
    if index_of:
        vector_sum.start(in_rows(sums_ref[0:2, :] + vectors_ref[0:2, :], group.shape[2]))
    vector_sum.middle()

    def finish(index, _):
        message = index // chunks
        chunk = index % chunks

        @pl.when((count - 1 - message > me) & (me > 0))
        def _():
            send(0, message, chunk).wait_send()

        @pl.when((count - 1 - message > me) & (me == 0))
        def _():
            send_edge(0, message, chunk).wait_send()

        @pl.when((message < me) & (me < count - 1))
        def _():
            send(1, message, chunk).wait_send()

        @pl.when((message < me) & (me == count - 1))
        def _():
            send_edge(1, message, chunk).wait_send()

        return 0

    lax.fori_loop(0, steps, finish, 0)

    def finish_pair(chunk, _):
        pair(chunk).wait()
        return 0

    if index_of:
        lax.fori_loop(0, chunks, finish_pair, 0)
    total_ref[...] = vector_sum.finish()
    if chain is not None:
        chain.finish()
    else:
        begin.finish()
    for extra in extras:
        extra.finish()


def return_part(
    index, parts, weight, edge_weight, layer_input, hidden_grad, gain, vectors, extras, weight_terms, qkv_terms=None
):
    count, rows, cols = parts.shape
    rows = rows // 2
    width = weight.shape[0]
    chunks = max(1, rows // 128)
    members = lax.axis_size("batch") * lax.axis_size("mp")
    small = (8, 2 * width // 8) if index else vectors.shape
    kinds, sources = [kind for kind, _ in extras], [source for _, source in extras]
    late_in = [*weight_terms]
    if not index:
        keep, _, down, _ = weight_terms
        half = (width, down.shape[1] // 2)
        late_out = [keep.shape[1:], keep.shape[1:], half, half]
        late_scratch = [
            pltpu.VMEM(keep.shape[1:], BF16),
            pltpu.VMEM(keep.shape[1:], BF16),
            pltpu.VMEM(down.shape, BF16),
            pltpu.SemaphoreType.DMA((6,)),
        ]
    else:
        late_in = late_in + [qkv_terms]
        part = (width // count, weight_terms[0].shape[1] + weight_terms[2].shape[1])
        batches = lax.axis_size("batch")
        head = qkv_terms.shape[2:]
        late_out = [(batches,) + part, (members, count // 2) + head]
        messages = (2, count - 1) + part
        late_scratch = [
            pltpu.VMEM(messages, BF16),
            pltpu.VMEM(messages, BF16),
            pltpu.VMEM((batches,) + part, BF16),
            pltpu.VMEM((count,) + head, BF16),
            pltpu.VMEM((count,) + head, BF16),
            pltpu.SemaphoreType.DMA((2, 4 * (count - 1) + count + members + 3)),
        ]
    any_spec = pl.BlockSpec(memory_space=pl.ANY)
    dma = pltpu.SemaphoreType.DMA
    fixed = lambda step: (0, 0)
    return pl.pallas_call(
        functools.partial(return_kernel, count, chunks, 2, index, kinds),
        grid=(1,),
        in_specs=[
            pl.BlockSpec((count, rows, cols), lambda step: (0, index, 0)),
            pl.BlockSpec((width, cols), fixed),
            pl.BlockSpec((width, cols), fixed),
            any_spec,
            pl.BlockSpec((rows, width), fixed),
            pl.BlockSpec((1, width), fixed),
            pl.BlockSpec(vectors.shape, fixed),
        ]
        + [any_spec] * len(extras)
        + [pl.BlockSpec(memory_space=pltpu.VMEM)] * len(late_in),
        out_specs=[
            pl.BlockSpec((rows, width), fixed),
            pl.BlockSpec((8, width), fixed),
            pl.BlockSpec(small, fixed),
            any_spec,
        ]
        + [any_spec] * (len(extras) + len(late_out)),
        out_shape=[
            jax.ShapeDtypeStruct((rows, width), BF16),
            jax.ShapeDtypeStruct((8, width), F32),
            jax.ShapeDtypeStruct(small, F32),
            jax.ShapeDtypeStruct((rows, width), BF16),
        ]
        + [jax.ShapeDtypeStruct(source.shape, BF16) for source in sources]
        + [jax.ShapeDtypeStruct(shape, BF16) for shape in late_out],
        scratch_shapes=[
            pltpu.VMEM((rows, width), F32),
            pltpu.VMEM((2, count - 1, rows, width), BF16),
            pltpu.VMEM((2, count - 1, rows, width), BF16),
            pltpu.VMEM((count - 1, rows, cols), BF16),
            pltpu.VMEM((rows // chunks, width), F32),
            pltpu.VMEM((members,) + small, F32),
            pltpu.VMEM((count,) + small, F32),
            dma((1,)),
            dma((2, count - 1, chunks)),
            dma((2, count - 1, chunks)),
            dma((chunks,)),
            dma((chunks,)),
            dma((2, members + count - 2)),
        ]
        + [dma((2, extra_moves(*extra))) for extra in extras]
        + late_scratch,
        compiler_params=pltpu.CompilerParams(
            collective_id=1 + index, has_side_effects=True, vmem_limit_bytes=VMEM_LIMIT
        ),
        cost_estimate=pl.CostEstimate(flops=80_000_000_000, bytes_accessed=1, transcendentals=0),
    )(parts, weight, edge_weight, layer_input, hidden_grad, gain, vectors, *sources, *late_in)


def weight_grad_kernel(
    tile,
    second_ref,
    grad_ref,
    hidden_ref,
    pre_ref,
    act_ref,
    att_ref,
    trade_source,
    pair_source,
    keep,
    away,
    down_own,
    down_near,
    trade_target,
    pair_target,
    turned,
    slots,
    sending,
    received,
    slot_sems,
    send_sems,
    recv_sems,
    out_sems,
    pair_sems,
    *trade_sems,
):
    rows, width = second_ref.shape
    units = pre_ref.shape[1]
    me = lax.axis_index("batch")
    place = lax.axis_index("mp")
    parity = me % 2
    mate = me + 1 - 2 * parity
    barrier = pltpu.get_barrier_semaphore()
    pl.semaphore_signal(barrier, inc=1, device_id={"batch": mate}, device_id_type=MESH)
    trade = Trade(trade_source, trade_target, *trade_sems, (pair_source, pair_target, pair_sems))
    trade.start(1)

    depth = slots.shape[0]
    piece = units // 4
    head_piece = width // 4
    side = (me // 2) % 2
    jobs = []
    for half, first_sent, first_kept in (
        (0, (1 - parity) * piece, parity * piece),
        (1, 3 * piece, 2 * piece),
    ):
        for target, start in ((away, (1 - side) * tile), (keep, side * tile)):
            puts = [(0, tile, target.at[half], 0)]
            jobs.append((0, pre_ref, tile, first_sent + start, first_kept + start, puts))
    for target, first_sent, first_kept in (
        (down_near, 3 * piece, 2 * piece),
        (down_own, (1 - parity) * piece, parity * piece),
    ):
        for start in range(0, piece, tile):
            puts = [(0, tile, target, start)]
            jobs.append((1, act_ref, tile, first_sent + start, first_kept + start, puts))
    for half, owner in ((0, place), (1, 1 - place)):
        first = 2 * owner * head_piece
        size = head_piece // 2
        puts = [
            (side * size, size, keep.at[half], tile),
            ((1 - side) * size, size, away.at[half], tile),
        ]
        jobs.append(
            (
                2,
                att_ref,
                head_piece,
                first + (1 - parity) * head_piece,
                first + parity * head_piece,
                puts,
            )
        )
    count = len(jobs)
    order = [(job, 3) for job in range(count)] + [(job, 4) for job in range(count)]

    def fetch(index):
        job, which = order[index]
        _, source, size, *_ = jobs[job]
        start = jobs[job][which]
        return pltpu.make_async_copy(
            source.at[:, pl.ds(pl.multiple_of(start, 128), size)],
            slots.at[index % depth, :, pl.ds(0, size)],
            slot_sems.at[index % depth],
        )

    def exchange(job):
        size = jobs[job][2]
        return pltpu.make_async_remote_copy(
            src_ref=sending.at[job, :, pl.ds(0, size)],
            dst_ref=received.at[job, :, pl.ds(0, size)],
            send_sem=send_sems.at[job],
            recv_sem=recv_sems.at[job],
            device_id={"batch": mate},
            device_id_type=MESH,
        )

    def put(job):
        copies = []
        for which, (first, size, target, start) in enumerate(jobs[job][5]):
            from_here = pl.ds(first if isinstance(first, int) else pl.multiple_of(first, 128), size)
            copies.append(
                pltpu.make_async_copy(
                    received.at[job, :, from_here],
                    target.at[:, pl.ds(start, size)],
                    out_sems.at[which, job],
                )
            )
        return copies

    for index in range(depth - 1):
        fetch(index).start()
    block = min(1024, width)
    for matrix, source in enumerate((second_ref, grad_ref, hidden_ref)):

        def turn(index, _):
            here = pl.ds(pl.multiple_of(index * 128, 128), 128)
            turned[matrix, :, here] = source[here, :].T
            return 0

        lax.fori_loop(0, rows // 128, turn, 0)

    for index, (job, which) in enumerate(order):
        matrix, _, size, *_ = jobs[job]
        fetch(index).wait()
        if index + depth - 1 < len(order):
            fetch(index + depth - 1).start()
        if which == 4:
            exchange(job).wait_recv()

        def multiply(part, _):
            here = pl.ds(pl.multiple_of(part * block, block), block)
            total = dot_nn(turned[matrix, here, :], slots[index % depth, :, 0:size])
            if which == 3:
                sending[job, here, 0:size] = total.astype(BF16)
            else:
                total = total + received[job, here, 0:size].astype(F32)
                received[job, here, 0:size] = total.astype(BF16)
            return 0

        lax.fori_loop(0, width // block, multiply, 0)
        if which == 3:
            exchange(job).start()
        else:
            for copy in put(job):
                copy.start()
    for job in range(count):
        exchange(job).wait_send()
        for copy in put(job):
            copy.wait()
    trade.finish()


def weight_grads(second_low, grad_low, hidden_low, pre_grad, activated, attended, source, pair):
    rows, width = second_low.shape
    units = pre_grad.shape[1]
    piece = units // 4
    tile = piece // 2
    jobs = 10
    any_spec = pl.BlockSpec(memory_space=pl.ANY)
    vmem = pl.BlockSpec(memory_space=pltpu.VMEM)
    dma = pltpu.SemaphoreType.DMA
    shapes = [(2, width, tile + width // 8)] * 2 + [(width, piece)] * 2
    return pl.pallas_call(
        functools.partial(weight_grad_kernel, tile),
        in_specs=[vmem] * 3 + [any_spec] * 5,
        out_specs=[any_spec] * 6,
        out_shape=[
            jax.ShapeDtypeStruct(shape, BF16) for shape in shapes + [source.shape, pair.shape]
        ],
        scratch_shapes=[
            pltpu.VMEM((3, width, rows), BF16),
            pltpu.VMEM((3, rows, tile), BF16),
            pltpu.VMEM((jobs, width, tile), BF16),
            pltpu.VMEM((jobs, width, tile), BF16),
            dma((3,)),
            dma((jobs,)),
            dma((jobs,)),
            dma((2, jobs)),
            dma((2,)),
        ]
        + trade_scratch(source.shape[0]),
        compiler_params=pltpu.CompilerParams(
            collective_id=3, has_side_effects=True, vmem_limit_bytes=VMEM_LIMIT
        ),
        cost_estimate=pl.CostEstimate(
            flops=2 * rows * width * (2 * units + width),
            bytes_accessed=4 * rows * units,
            transcendentals=0,
        ),
    )(second_low, grad_low, hidden_low, pre_grad, activated, attended, source, pair)


def swap(value, axis, distance=1):
    size = lax.axis_size(axis)
    return lax.ppermute(value, axis, [(j, j ^ distance) for j in range(size)])


def after(value, *earlier):
    return lax.optimization_barrier((value,) + earlier)[0]


def all_to_all(value):
    return lax.all_to_all(value, "seq", 0, 0, tiled=True)


def halves(value):
    return jnp.split(value, 2, axis=1)


def trade_pieces(value):
    place, count = lax.axis_index("seq"), lax.axis_size("seq")
    pieces = [pick(value, place, count)]
    for distance in range(1, count):
        pairs = [(j, (j + distance) % count) for j in range(count)]
        pieces.append(
            lax.ppermute(pick(value, (place + distance) % count, count), "seq", pairs)
        )
    return pieces


def place_pieces(pieces):
    place, count = lax.axis_index("seq"), len(pieces)
    whole = jnp.concatenate(pieces, axis=0)
    return jnp.roll(whole[::-1], place + 1, axis=0)


def levels_of(axis):
    return [1 << level for level in range(lax.axis_size(axis).bit_length() - 1)]


def gather_small(value):
    place = lax.axis_index("seq")
    count = lax.axis_size("seq")
    parts = [value] + [swap(value, "seq", distance) for distance in range(1, count)]
    stacked = jnp.stack(parts)
    order = jnp.arange(count, dtype=jnp.int32) ^ place
    return jnp.take(stacked, order, axis=0).reshape((-1,) + value.shape[1:])


def pick(value, index, count, axis=0):
    size = value.shape[axis] // count
    return lax.dynamic_slice_in_dim(value, index * size, size, axis)


def fetch_near(weight, axis):
    return swap(pick(weight, lax.axis_index("batch") % 2, 2, axis), "mp")


def narrow_add(mine, received):
    return (mine.astype(F32) + received.astype(F32)).astype(BF16)


def assemble_kernel(unit_cols, pieces, heads, up_ref, down_ref, out_ref, qkv_ref):
    batch = lax.axis_index("batch")
    batches = pieces.shape[0]
    levels = batches.bit_length() - 1
    for index in range(batches):
        source = jnp.bitwise_xor(batch, index // 2 + 2 * (index % 2))
        slot = 0
        for level in range(levels):
            slot = slot + ((source >> level) % 2) * (batches >> (level + 1))
        start = 0
        for size, target, turn in (
            (unit_cols, up_ref, False),
            (pieces.shape[2] - 2 * unit_cols, out_ref, True),
            (unit_cols, down_ref, True),
        ):
            value = pieces[index, :, start : start + size].astype(F32)
            here = pl.ds(pl.multiple_of(slot * size, 128), size)
            if turn:
                target[here, :] = value.T
            else:
                target[:, here] = value
            start = start + size
    members, parts, rows, cols = heads.shape
    cols = cols // 3
    for member in range(members):
        for matrix in range(3):
            for part in range(parts):
                start = (matrix * parts + part) * cols
                qkv_ref[member * rows : (member + 1) * rows, start : start + cols] = heads[
                    member, part, :, matrix * cols : (matrix + 1) * cols
                ].astype(F32)


def assemble(unit_cols, pieces, heads):
    batches, rows, all_cols = pieces.shape
    out_cols = all_cols - 2 * unit_cols
    shapes = [
        (rows, batches * unit_cols),
        (batches * unit_cols, rows),
        (batches * out_cols, rows),
        (heads.shape[0] * heads.shape[2], heads.shape[1] * heads.shape[3]),
    ]
    vmem = pl.BlockSpec(memory_space=pltpu.VMEM)
    return pl.pallas_call(
        functools.partial(assemble_kernel, unit_cols),
        in_specs=[vmem] * 2,
        out_specs=[vmem] * 4,
        out_shape=[jax.ShapeDtypeStruct(shape, F32) for shape in shapes],
        compiler_params=pltpu.CompilerParams(vmem_limit_bytes=VMEM_LIMIT),
    )(pieces, heads)


def place_kernel(place_ref, own_first, own_second, other_first, other_second, out_ref):
    place = place_ref[0]

    @pl.when(pl.program_id(0) == 0)
    def _():
        out_ref[place] = own_first[...].astype(F32)
        out_ref[1 - place] = other_first[...].astype(F32)

    @pl.when(pl.program_id(0) == 1)
    def _():
        out_ref[place] = own_second[...].astype(F32)
        out_ref[1 - place] = other_second[...].astype(F32)


def both_sequences(own, other):
    rows, width = own[0].shape
    step = min(256, rows)
    steps = rows // step
    first = pl.BlockSpec(
        (step, width), lambda half, index, place_ref: (index * (1 - half) + (steps - 1) * half, 0)
    )
    second = pl.BlockSpec((step, width), lambda half, index, place_ref: (index * half, 0))
    return pl.pallas_call(
        place_kernel,
        grid_spec=pltpu.PrefetchScalarGridSpec(
            num_scalar_prefetch=1,
            grid=(2, steps),
            in_specs=[first, second, first, second],
            out_specs=pl.BlockSpec(
                (2, step, width), lambda half, index, place_ref: (0, half * steps + index, 0)
            ),
        ),
        out_shape=jax.ShapeDtypeStruct((2, 2 * rows, width), F32),
    )(lax.axis_index("mp").astype(jnp.int32)[None], *own, *other)


def local(
    layer_input,
    lengths,
    random_blocks,
    first_gain,
    first_bias,
    qkv_weight,
    out_weight,
    second_gain,
    second_bias,
    up_weight,
    up_bias,
    down_weight,
    down_bias,
    cotangent,
):
    seq_count = lax.axis_size("seq")
    seq_index = lax.axis_index("seq")
    mp_index = lax.axis_index("mp")
    parity = lax.axis_index("batch") % 2
    _, local_rows, width = layer_input.shape
    rows_total = local_rows * seq_count
    blocks = rows_total // BLOCK
    half_cols = qkv_weight.shape[2]
    cols = width // seq_count
    units = up_weight.shape[1]

    doc_ends = jnp.cumsum(lax.dynamic_index_in_dim(lengths, mp_index, 0, keepdims=False))
    randoms = lax.dynamic_index_in_dim(random_blocks, mp_index, 0, keepdims=False)
    randoms = gather_small(randoms)
    lists, admits = block_lists(jnp.arange(blocks, dtype=jnp.int32), randoms, blocks)
    lists, admits = lists.reshape(-1), admits.reshape(-1)

    qkv_near = lax.dynamic_slice_in_dim(qkv_weight, (seq_index * cols) % half_cols, cols, 2)
    qkv_near = qkv_near.reshape(width, 3 * cols)
    up_near = fetch_near(up_weight, 1)
    bias_near = fetch_near(up_bias, 0)
    out_other = swap(out_weight, "mp")

    first_all, qkv, qkv_own = gather_project(
        layer_input, first_gain[None], first_bias[None], qkv_near, half_cols
    )
    first_all = first_all.reshape(rows_total, width)
    qkv, up_near, out_other, bias_near, lists, down_cut = lax.optimization_barrier(
        (qkv.reshape(rows_total, 3 * cols), up_near, out_other, bias_near, lists, down_weight)
    )
    up_far, bias_far = swap(up_near, "batch"), swap(bias_near, "batch")
    down_near = fetch_near(down_cut, 0)
    attended_first, lse_first = attention_forward(0, qkv, doc_ends, lists, admits, seq_count)
    att_pieces = trade_pieces(attended_first)
    attended_second, lse_second = attention_forward(1, qkv, doc_ends, lists, admits, seq_count)
    *att_pieces, attended_second = lax.optimization_barrier((*att_pieces, attended_second))
    att_first = place_pieces(att_pieces)
    att_first, up_far, down_near, bias_far = lax.optimization_barrier(
        (att_first, up_far, down_near, bias_far)
    )
    down_far = swap(down_near, "batch")
    bias_full = jnp.concatenate([up_bias, bias_near, bias_far])[None]
    outs = [part.reshape(seq_count // 2, cols, width) for part in (out_weight, out_other)]
    kept, results = None, []
    att, source, pair = att_first, attended_second, jnp.zeros((8, 128), BF16)
    for index in range(2):
        result = token_part(
            index,
            doc_ends,
            att,
            layer_input,
            cotangent,
            outs,
            (up_weight, up_near, up_far),
            (down_weight, down_near, down_far),
            bias_full,
            second_gain[None],
            second_bias[None],
            down_bias[None],
            source,
            pair,
            kept,
        )
        kept = result[3:9]
        results.append(result[:3] + result[9:])
        att, source, pair = result[11], result[2], result[0]
        other_output = result[12]
    grad_first = att
    activated, pre_grad, second_low, hidden_low, grad_low, attended_low = kept
    sums = results[0][3][:3] + results[1][3][:3]
    unit_sums = results[0][4][0] + results[1][4][0]
    bias_sums = [unit_sums[:units], unit_sums[units : units * 3 // 2], unit_sums[units * 3 // 2 :]]
    keep, away, down_own, down_near, grad_second, other_second = weight_grads(
        second_low, grad_low, hidden_low, pre_grad, activated, attended_low, source, pair
    )
    outputs, other_outputs = [result[0] for result in results], [other_output, other_second]
    bias_other = jnp.where(
        parity == 0,
        jnp.concatenate([bias_sums[1], bias_sums[2]]),
        jnp.concatenate([bias_sums[2], bias_sums[1]]),
    )
    bias_all = jnp.where(
        mp_index == 0,
        jnp.concatenate([bias_sums[0], bias_other]),
        jnp.concatenate([bias_other, bias_sums[0]]),
    )
    qkv_cut, grad_second = lax.optimization_barrier((qkv_own, grad_second))
    qkv_edge = lax.ppermute(qkv_cut, "seq", [(0, 1), (seq_count - 1, seq_count - 2)])

    come, down_come = swap(away, "batch", 2), swap(down_near, "mp")
    qkv_low_grad = attention_backward(
        qkv,
        (attended_first, attended_second),
        (grad_first, grad_second),
        (lse_first, lse_second),
        doc_ends,
        lists,
        admits,
    )
    qkv_sum = dot_tn(first_all, qkv_low_grad).astype(BF16)
    members = lax.axis_size("batch") * 2
    mine = lax.axis_index("batch") * 2 + mp_index
    qkv_sum = qkv_sum.reshape(seq_count, members, -1, 3 * cols).transpose(1, 0, 2, 3)
    qkv_low_grad, qkv_sum, come, down_come = lax.optimization_barrier(
        (qkv_low_grad, qkv_sum, come, down_come)
    )
    parts = qkv_low_grad.reshape(seq_count, local_rows, 3 * cols)
    early = jnp.concatenate([sums, bias_all.reshape(-1, width)], axis=0)
    input_first, first_sums, early, _, qkv_terms, *weight_terms = return_part(
        0,
        parts,
        qkv_own,
        qkv_edge,
        layer_input,
        results[0][1],
        first_gain[None],
        early.reshape(8, -1),
        [("group", qkv_sum)],
        (keep, come, down_own, down_come),
    )
    input_second, _, late, other_second, other_first, weights_back, qkv_back = return_part(
        1,
        parts,
        qkv_own,
        qkv_edge,
        layer_input,
        results[1][1],
        first_gain[None],
        first_sums,
        [("mp", input_first)],
        weight_terms,
        qkv_terms,
    )
    layer_output = both_sequences(outputs, other_outputs)
    input_grad = both_sequences([input_first, input_second], [other_first, other_second])
    up_grad, down_grad, out_grad, qkv_grad = assemble(units // 4, weights_back, qkv_back)
    early, late = early.reshape(-1), late.reshape(-1)
    up_bias_grad = lax.dynamic_slice_in_dim(early, 3 * width + mp_index * units, units)
    return (
        layer_output,
        input_grad,
        late[:width],
        late[width:],
        qkv_grad.reshape(-1, 3, half_cols),
        out_grad,
        early[width : 2 * width],
        early[2 * width : 3 * width],
        up_grad,
        up_bias_grad,
        down_grad,
        early[:width],
    )


MB = 2
NBLK = 64
LEN = 4096
HIGH = lax.Precision.HIGHEST


def segment_of(places, doc_ends):
    return jnp.sum((places[..., None] >= doc_ends).astype(jnp.int32), axis=-1)


def block_lists_by_index(blocks, randoms):
    leading = randoms.shape[:-1]
    globals_part = jnp.broadcast_to(jnp.arange(GLOB, dtype=jnp.int32), leading + (GLOB,))
    window_part = jnp.broadcast_to(
        blocks[:, None] + jnp.arange(WIN, dtype=jnp.int32) - WIN // 2, leading + (WIN,)
    )
    block_list = jnp.concatenate([globals_part, window_part, randoms], axis=-1)
    inside = (block_list >= 0) & (block_list < NBLK)
    same_entry = block_list[..., :, None] == block_list[..., None, :]
    order_ids = jnp.arange(LIST)
    earlier = order_ids[None, :] < order_ids[:, None]
    repeated = jnp.any(same_entry & earlier, axis=-1)
    return (block_list, inside & jnp.logical_not(repeated))


def fetch_rows(key_rows, values, wanted):
    batch_seqs, local_rows, head_cols = key_rows.shape
    total_rows = local_rows * lax.axis_size("seq")
    empty_rows = jnp.zeros((batch_seqs, wanted.shape[1], head_cols), jnp.bfloat16)
    initial = (empty_rows, empty_rows)
    empty_whole = jnp.zeros((batch_seqs, total_rows, head_cols), jnp.bfloat16)
    initial = initial + (empty_whole, empty_whole)
    shards_in = (
        lax.all_gather(key_rows, "seq", axis=1, tiled=True),
        lax.all_gather(values, "seq", axis=1, tiled=True),
    )
    piece_rows = shards_in[0].shape[1]
    inside = ((wanted >= 0) & (wanted < piece_rows))[..., None]
    take_index = jnp.clip(wanted, 0, piece_rows - 1)[..., None]
    picked = tuple(
        (
            jnp.where(inside, jnp.take_along_axis(source, take_index, axis=1), previous)
            for source, previous in zip(shards_in, initial[:2])
        )
    )
    placed = tuple((source for source in shards_in))
    return picked + placed


def scatter_rows(kv_source):
    return lax.psum_scatter(
        kv_source.astype(jnp.bfloat16), "seq", scatter_dimension=0, tiled=True
    ).astype(jnp.float32)


def global_partial(seq_item):
    query_rows, key_rows, value_rows, keep_mask = seq_item
    head_count = query_rows.shape[1] // HD
    query_heads = query_rows.reshape(query_rows.shape[0], head_count, HD)
    key_heads = key_rows.reshape(key_rows.shape[0], head_count, HD)
    value_heads = value_rows.astype(jnp.float32).reshape(value_rows.shape[0], head_count, HD)
    raw_scores = jnp.einsum(
        "qhd,khd->hqk", query_heads, key_heads, preferred_element_type=jnp.float32
    ) * HD ** (-0.5)
    masked = jnp.where(keep_mask[None], raw_scores, NEG)
    row_top = jnp.max(masked, axis=-1)
    weights = jnp.exp(masked - row_top[..., None]) * keep_mask[None].astype(jnp.float32)
    numer = jnp.einsum("hqk,khd->hqd", weights, value_heads, precision=HIGH)
    return (row_top, jnp.sum(weights, axis=-1), numer)


def global_back(seq_item):
    query_rows, key_rows, value_rows, keep_mask, row_top, row_total, glob_out, glob_grad = seq_item
    row_count, head_cols = query_rows.shape
    head_count = head_cols // HD
    query_heads = query_rows.reshape(row_count, head_count, HD)
    key_heads = key_rows.reshape(key_rows.shape[0], head_count, HD)
    value_heads = value_rows.astype(jnp.float32).reshape(value_rows.shape[0], head_count, HD)
    raw_scores = jnp.einsum(
        "qhd,khd->hqk", query_heads, key_heads, preferred_element_type=jnp.float32
    ) * HD ** (-0.5)
    masked = jnp.where(keep_mask[None], raw_scores, NEG)
    probs_glob = (
        jnp.exp(masked - row_top[..., None])
        * keep_mask[None].astype(jnp.float32)
        / row_total[..., None]
    )
    grad_heads = glob_grad.astype(jnp.float32).reshape(row_count, head_count, HD)
    prob_grad = jnp.einsum("qhd,khd->hqk", grad_heads, value_heads, precision=HIGH)
    delta = jnp.einsum("qhd,hqd->hq", grad_heads, glob_out, precision=HIGH)
    score_grad = (probs_glob * (prob_grad - delta[..., None])).astype(jnp.bfloat16)
    query_grad = jnp.einsum(
        "hqk,khd->qhd", score_grad, key_heads, preferred_element_type=jnp.float32
    ) * HD ** (-0.5)
    key_grad = jnp.einsum(
        "hqk,qhd->khd", score_grad, query_heads, preferred_element_type=jnp.float32
    ) * HD ** (-0.5)
    value_grad = jnp.einsum("hqk,qhd->khd", probs_glob, grad_heads, precision=HIGH)
    return (
        query_grad.reshape(row_count, head_cols),
        key_grad.reshape(-1, head_cols),
        value_grad.reshape(-1, head_cols),
    )


def local_by_blocks(
    layer_input,
    lengths,
    random_blocks,
    first_gain,
    first_bias,
    qkv_weight,
    out_weight,
    second_gain,
    second_bias,
    up_weight,
    up_bias,
    down_weight,
    down_bias,
    cotangent,
):
    seq_index = lax.axis_index("seq")
    local_seqs, local_rows, model_width = layer_input.shape
    blocks_dev = local_rows // BLOCK
    head_cols = qkv_weight.shape[2]
    head_count = head_cols // HD
    unit_cols = up_weight.shape[1]
    score_scale = HD ** (-0.5)
    glob_rows = GLOB * BLOCK
    batch_seqs = local_seqs // MB
    picked_rows = blocks_dev * LIST * BLOCK
    qkv_flat = qkv_weight.reshape(model_width, 3 * head_cols)
    doc_ends = jnp.cumsum(lengths, axis=1)
    places = seq_index * local_rows + jnp.arange(local_rows, dtype=jnp.int32)
    seg_local = segment_of(places[None, :], doc_ends[:, None, :])
    valid_rows = (places[None, :] < doc_ends[:, -1:]).astype(jnp.float32)
    glob_flag = (places < glob_rows)[None, :, None]
    query_blocks = seq_index * blocks_dev + jnp.arange(blocks_dev, dtype=jnp.int32)
    block_list, admitted = block_lists_by_index(query_blocks, random_blocks)
    key_places = block_list[..., None] * BLOCK + jnp.arange(BLOCK, dtype=jnp.int32)
    key_segs = segment_of(key_places, doc_ends[:, None, None, None, :]).reshape(
        local_seqs, blocks_dev, LIST * BLOCK
    )
    admit_keys = jnp.broadcast_to(admitted[..., None], key_places.shape).reshape(
        local_seqs, blocks_dev, LIST * BLOCK
    )
    query_segs = seg_local.reshape(local_seqs, blocks_dev, BLOCK)
    list_mask = admit_keys[:, :, None, :] & (query_segs[..., None] == key_segs[:, :, None, :])
    wanted_all = jnp.clip(key_places, 0, LEN - 1).reshape(local_seqs, picked_rows)
    glob_segs = segment_of(jnp.arange(glob_rows, dtype=jnp.int32)[None, :], doc_ends[:, None, :])
    qkv_total = jnp.zeros((model_width, 3 * head_cols), jnp.float32)
    out_total = jnp.zeros(out_weight.shape, jnp.float32)
    up_total = jnp.zeros(up_weight.shape, jnp.float32)
    down_total = jnp.zeros(down_weight.shape, jnp.float32)
    gain_one_total = jnp.zeros((model_width,), jnp.float32)
    bias_one_total = jnp.zeros((model_width,), jnp.float32)
    gain_two_total = jnp.zeros((model_width,), jnp.float32)
    bias_two_total = jnp.zeros((model_width,), jnp.float32)
    up_bias_total = jnp.zeros((unit_cols,), jnp.float32)
    down_bias_total = jnp.zeros((model_width,), jnp.float32)
    outputs_all = []
    input_grads = []
    for micro_index in range(MB):
        first_seq = micro_index * batch_seqs
        last_seq = first_seq + batch_seqs
        rows_in = layer_input[first_seq:last_seq]
        ends_now = doc_ends[first_seq:last_seq]
        valid_now = valid_rows[first_seq:last_seq]
        mask_now = list_mask[first_seq:last_seq]
        wanted = wanted_all[first_seq:last_seq]
        glob_segs_now = glob_segs[first_seq:last_seq]
        normed_one, inverse_one = norm_stats(rows_in)
        first_low = (
            (normed_one * first_gain + first_bias).astype(jnp.bfloat16).reshape(-1, model_width)
        )
        qkv_rows = (
            jnp.dot(first_low, qkv_flat, preferred_element_type=jnp.float32)
            .astype(jnp.bfloat16)
            .reshape(batch_seqs, local_rows, 3, head_cols)
        )
        queries = qkv_rows[:, :, 0]
        key_rows = qkv_rows[:, :, 1]
        values = qkv_rows[:, :, 2]
        glob_queries_own = queries[:, :glob_rows]
        picked_keys, picked_values, whole_keys, whole_values = fetch_rows(key_rows, values, wanted)
        glob_queries = glob_queries_own
        seg_whole = segment_of(jnp.arange(LEN, dtype=jnp.int32)[None, :], ends_now[:, None, :])
        glob_mask = glob_segs_now[:, :, None] == seg_whole[:, None, :]

        def global_here():
            return lax.map(global_partial, (glob_queries, whole_keys, whole_values, glob_mask))

        def global_skip():
            return (
                jnp.zeros((batch_seqs, head_count, glob_rows), jnp.float32),
                jnp.ones((batch_seqs, head_count, glob_rows), jnp.float32),
                jnp.zeros((batch_seqs, head_count, glob_rows, HD), jnp.float32),
            )

        glob_top, glob_total, glob_numer = lax.cond(seq_index == 0, global_here, global_skip)
        glob_out = glob_numer / glob_total[..., None]
        query_split = queries.reshape(batch_seqs, blocks_dev, BLOCK, head_count, HD)
        key_split = picked_keys.reshape(batch_seqs, blocks_dev, LIST * BLOCK, head_count, HD)
        value_split = picked_values.reshape(batch_seqs, blocks_dev, LIST * BLOCK, head_count, HD)
        raw_scores = (
            jnp.einsum(
                "sbqhd,sbkhd->sbhqk", query_split, key_split, preferred_element_type=jnp.float32
            )
            * score_scale
        )
        keep_now = mask_now[:, :, None]
        masked = jnp.where(keep_now, raw_scores, NEG)
        row_top = jnp.max(masked, axis=-1, keepdims=True)
        weights = jnp.exp(masked - row_top) * keep_now.astype(jnp.float32)
        row_total = jnp.sum(weights, axis=-1, keepdims=True)
        probs_list = weights / row_total
        probs_low = probs_list.astype(jnp.bfloat16)
        listed = jnp.einsum(
            "sbhqk,sbkhd->sbqhd", probs_low, value_split, preferred_element_type=jnp.float32
        ).reshape(batch_seqs, local_rows, head_cols)
        glob_rows_out = jnp.transpose(glob_out, (0, 2, 1, 3)).reshape(
            batch_seqs, glob_rows, head_cols
        )
        glob_full = jnp.pad(glob_rows_out, ((0, 0), (0, local_rows - glob_rows), (0, 0)))
        attended = jnp.where(glob_flag, glob_full, listed) * valid_now[..., None]
        attended_low = attended.astype(jnp.bfloat16).reshape(-1, head_cols)
        branch = lax.psum(
            jnp.dot(attended_low, out_weight, preferred_element_type=jnp.float32).astype(
                jnp.bfloat16
            ),
            "mp",
        ).astype(jnp.float32)
        hidden = rows_in + branch.reshape(rows_in.shape)
        normed_two, inverse_two = norm_stats(hidden)
        second_low = (
            (normed_two * second_gain + second_bias).astype(jnp.bfloat16).reshape(-1, model_width)
        )
        pre_act = jnp.dot(second_low, up_weight, preferred_element_type=jnp.float32) + up_bias
        activated = jax.nn.gelu(pre_act, approximate=True).astype(jnp.bfloat16)
        ffn_branch = lax.psum(
            jnp.dot(activated, down_weight, preferred_element_type=jnp.float32).astype(
                jnp.bfloat16
            ),
            "mp",
        ).astype(jnp.float32)
        outputs_all.append(hidden + ffn_branch.reshape(rows_in.shape) + down_bias)
        grad_rows = cotangent[first_seq:last_seq].reshape(-1, model_width)
        down_bias_total = down_bias_total + jnp.sum(grad_rows, axis=0)
        grad_low = grad_rows.astype(jnp.bfloat16)
        down_total = down_total + jnp.einsum(
            "rf,rd->fd", activated, grad_low, preferred_element_type=jnp.float32
        )
        act_grad = jnp.einsum(
            "rd,fd->rf", grad_low, down_weight, preferred_element_type=jnp.float32
        )
        _, gelu_pull = jax.vjp(lambda inner: jax.nn.gelu(inner, approximate=True), pre_act)
        pre_grad = gelu_pull(act_grad)[0].astype(jnp.bfloat16)
        up_bias_total = up_bias_total + jnp.sum(pre_grad.astype(jnp.float32), axis=0)
        up_total = up_total + jnp.einsum(
            "rd,rf->df", second_low, pre_grad, preferred_element_type=jnp.float32
        )
        second_grad = (
            lax.psum(
                jnp.einsum(
                    "rf,df->rd", pre_grad, up_weight, preferred_element_type=jnp.float32
                ).astype(jnp.bfloat16),
                "mp",
            )
            .astype(jnp.float32)
            .reshape(rows_in.shape)
        )
        gain_two_total = gain_two_total + jnp.sum(second_grad * normed_two, axis=(0, 1))
        bias_two_total = bias_two_total + jnp.sum(second_grad, axis=(0, 1))
        hidden_grad = grad_rows.reshape(rows_in.shape) + norm_back(
            second_grad, normed_two, inverse_two, second_gain
        )
        hidden_low = hidden_grad.astype(jnp.bfloat16).reshape(-1, model_width)
        out_total = out_total + jnp.einsum(
            "rc,rd->cd", attended_low, hidden_low, preferred_element_type=jnp.float32
        )
        attended_grad = jnp.einsum(
            "rd,cd->rc", hidden_low, out_weight, preferred_element_type=jnp.float32
        ).astype(jnp.bfloat16).reshape(batch_seqs, local_rows, head_cols) * valid_now[
            ..., None
        ].astype(
            jnp.bfloat16
        )
        list_grad = jnp.where(glob_flag, jnp.zeros_like(attended_grad), attended_grad).reshape(
            batch_seqs, blocks_dev, BLOCK, head_count, HD
        )
        prob_grad = jnp.einsum(
            "sbqhd,sbkhd->sbhqk", list_grad, value_split, preferred_element_type=jnp.float32
        )
        delta = jnp.sum(probs_list * prob_grad, axis=-1, keepdims=True)
        score_grad = (probs_list * (prob_grad - delta)).astype(jnp.bfloat16)
        query_grad = (
            jnp.einsum(
                "sbhqk,sbkhd->sbqhd", score_grad, key_split, preferred_element_type=jnp.float32
            )
            * score_scale
        ).reshape(batch_seqs, local_rows, head_cols)
        key_picked_grad = (
            jnp.einsum(
                "sbhqk,sbqhd->sbkhd", score_grad, query_split, preferred_element_type=jnp.float32
            )
            * score_scale
        )
        value_picked_grad = jnp.einsum(
            "sbhqk,sbqhd->sbkhd", probs_low, list_grad, preferred_element_type=jnp.float32
        )
        picked_grads = jnp.concatenate(
            [
                key_picked_grad.reshape(batch_seqs, picked_rows, head_cols),
                value_picked_grad.reshape(batch_seqs, picked_rows, head_cols),
            ],
            axis=-1,
        )
        seg_ids = wanted * batch_seqs + jnp.arange(batch_seqs, dtype=jnp.int32)[:, None]
        kv_term = jax.ops.segment_sum(
            picked_grads.reshape(batch_seqs * picked_rows, 2 * head_cols),
            seg_ids.reshape(-1),
            num_segments=LEN * batch_seqs,
        ).reshape(LEN, batch_seqs, 2 * head_cols)
        glob_grad_own = attended_grad[:, :glob_rows]

        def back_here():
            return lax.map(
                global_back,
                (
                    glob_queries,
                    whole_keys,
                    whole_values,
                    glob_mask,
                    glob_top,
                    glob_total,
                    glob_out,
                    glob_grad_own,
                ),
            )

        def back_skip():
            return (
                jnp.zeros((batch_seqs, glob_rows, head_cols), jnp.float32),
                jnp.zeros((batch_seqs, LEN, head_cols), jnp.float32),
                jnp.zeros((batch_seqs, LEN, head_cols), jnp.float32),
            )

        glob_query_grad, whole_key_grad, whole_value_grad = lax.cond(
            seq_index == 0, back_here, back_skip
        )
        glob_dense = jnp.transpose(
            jnp.concatenate([whole_key_grad, whole_value_grad], axis=-1), (1, 0, 2)
        )
        kv_source = kv_term + glob_dense
        kv_grad = jnp.transpose(scatter_rows(kv_source), (1, 0, 2))
        glob_query_full = jnp.pad(glob_query_grad, ((0, 0), (0, local_rows - glob_rows), (0, 0)))
        query_total = query_grad + jnp.where(glob_flag, glob_query_full, 0.0)
        qkv_low_grad = (
            jnp.stack([query_total, kv_grad[..., :head_cols], kv_grad[..., head_cols:]], axis=2)
            .astype(jnp.bfloat16)
            .reshape(-1, 3 * head_cols)
        )
        qkv_total = qkv_total + jnp.einsum(
            "rd,rc->dc", first_low, qkv_low_grad, preferred_element_type=jnp.float32
        )
        first_grad = (
            lax.psum(
                jnp.einsum(
                    "rc,dc->rd", qkv_low_grad, qkv_flat, preferred_element_type=jnp.float32
                ).astype(jnp.bfloat16),
                "mp",
            )
            .astype(jnp.float32)
            .reshape(rows_in.shape)
        )
        gain_one_total = gain_one_total + jnp.sum(first_grad * normed_one, axis=(0, 1))
        bias_one_total = bias_one_total + jnp.sum(first_grad, axis=(0, 1))
        input_grads.append(hidden_grad + norm_back(first_grad, normed_one, inverse_one, first_gain))
    matrix_grads = (
        lax.psum_scatter(
            qkv_total.reshape(model_width, 3, head_cols).astype(jnp.bfloat16),
            "seq",
            scatter_dimension=0,
            tiled=True,
        ).astype(jnp.float32),
        lax.psum_scatter(
            out_total.astype(jnp.bfloat16), "seq", scatter_dimension=1, tiled=True
        ).astype(jnp.float32),
        lax.psum_scatter(
            up_total.astype(jnp.bfloat16), "seq", scatter_dimension=0, tiled=True
        ).astype(jnp.float32),
        lax.psum_scatter(
            down_total.astype(jnp.bfloat16), "seq", scatter_dimension=1, tiled=True
        ).astype(jnp.float32),
    )
    matrix_grads = (
        lax.psum(matrix_grads[0].astype(jnp.bfloat16), "batch").astype(jnp.float32),
        lax.psum(matrix_grads[1].astype(jnp.bfloat16), "batch").astype(jnp.float32),
        lax.psum(matrix_grads[2].astype(jnp.bfloat16), "batch").astype(jnp.float32),
        lax.psum(matrix_grads[3].astype(jnp.bfloat16), "batch").astype(jnp.float32),
    )
    vector_grads = lax.psum(
        (
            gain_one_total,
            bias_one_total,
            gain_two_total,
            bias_two_total,
            up_bias_total,
            down_bias_total,
        ),
        ("seq", "batch"),
    )
    return (
        jnp.concatenate(outputs_all, axis=0),
        jnp.concatenate(input_grads, axis=0),
        vector_grads[0],
        vector_grads[1],
        matrix_grads[0],
        matrix_grads[1],
        vector_grads[2],
        vector_grads[3],
        matrix_grads[2],
        vector_grads[4],
        matrix_grads[3],
        vector_grads[5],
    )


def solution(mesh):
    placed = (
        P("batch", "seq", None),
        P("batch", None),
        P("batch", "seq", None),
        P(),
        P(),
        P(None, None, "mp"),
        P("mp", None),
        P(),
        P(),
        P(None, "mp"),
        P("mp"),
        P("mp", None),
        P(),
        P("batch", "seq", None),
    )
    sizes = mesh.shape
    by_heads = sizes["seq"] in (4, 8) and sizes["batch"] == 4 and sizes["mp"] == 2
    return jax.shard_map(
        local if by_heads else local_by_blocks,
        mesh=mesh,
        in_specs=placed,
        out_specs=(
            P("batch", "seq", None),
            P("batch", "seq", None),
            P(),
            P(),
            P("seq", None, "mp"),
            P("mp", "seq"),
            P(),
            P(),
            P("seq", "mp"),
            P("mp"),
            P("mp", "seq"),
            P(),
        ),
        check_vma=False,
    )
```

```python
import functools

import jax
import jax.numpy as jnp
from jax import lax
from jax.experimental import pallas as pl
from jax.experimental.pallas import tpu as pltpu
from jax.sharding import PartitionSpec as P

BLOCK = 64
GLOB = 2
WIN = 3
HD = 64
LIST = 8

NEG = -1e30
EPS = 1e-05
F32 = jnp.float32
BF16 = jnp.bfloat16
VMEM_LIMIT = 60 * 1024 * 1024


def norm_stats(rows):
    centre = rows - jnp.mean(rows, axis=-1, keepdims=True)
    spread = jnp.mean(centre * centre, axis=-1, keepdims=True)
    inverse = lax.rsqrt(spread + EPS)
    return (centre * inverse, inverse)


def norm_back(grad_out, normed, inverse, gain):
    scaled = grad_out * gain
    return inverse * (
        scaled
        - jnp.mean(scaled, axis=-1, keepdims=True)
        - normed * jnp.mean(scaled * normed, axis=-1, keepdims=True)
    )


def block_lists(blocks, randoms, block_count):
    leading = randoms.shape[:-1]
    globals_part = jnp.broadcast_to(jnp.arange(GLOB, dtype=jnp.int32), leading + (GLOB,))
    window_part = jnp.broadcast_to(
        blocks[:, None] + jnp.arange(WIN, dtype=jnp.int32) - WIN // 2, leading + (WIN,)
    )
    block_list = jnp.concatenate([globals_part, window_part, randoms], axis=-1)
    inside = (block_list >= 0) & (block_list < block_count)
    same_entry = block_list[..., :, None] == block_list[..., None, :]
    order_ids = jnp.arange(LIST)
    earlier = order_ids[None, :] < order_ids[:, None]
    repeated = jnp.any(same_entry & earlier, axis=-1)
    admitted = inside & jnp.logical_not(repeated)
    return (jnp.clip(block_list, 0, block_count - 1), admitted.astype(jnp.int32))


MESH = pl.DeviceIdType.MESH


class Trade:
    def __init__(self, source, target, send_sems, recv_sems, own_sem, pair=None):
        self.source, self.target, self.pair = source, target, pair
        self.send_sems, self.recv_sems, self.own_sem = send_sems, recv_sems, own_sem
        self.count = source.shape[0]
        self.me = lax.axis_index("seq")

    def greet(self, others):
        barrier = pltpu.get_barrier_semaphore()
        for distance in range(1, self.count):
            other = lax.rem(self.me + distance, self.count)
            pl.semaphore_signal(barrier, inc=1, device_id={"seq": other}, device_id_type=MESH)
        if self.pair is not None:
            partner = 1 - lax.axis_index("mp")
            pl.semaphore_signal(barrier, inc=1, device_id={"mp": partner}, device_id_type=MESH)
            others = others + 1
        pl.semaphore_wait(barrier, self.count - 1 + others)

    def copy(self, distance):
        other = lax.rem(self.me + distance, self.count)
        return pltpu.make_async_remote_copy(
            src_ref=self.source.at[other],
            dst_ref=self.target.at[self.me],
            send_sem=self.send_sems.at[distance - 1],
            recv_sem=self.recv_sems.at[distance - 1],
            device_id={"seq": other},
            device_id_type=MESH,
        )

    def pair_copy(self):
        source, target, sems = self.pair
        return pltpu.make_async_remote_copy(
            src_ref=source,
            dst_ref=target,
            send_sem=sems.at[0],
            recv_sem=sems.at[1],
            device_id={"mp": 1 - lax.axis_index("mp")},
            device_id_type=MESH,
        )

    def own(self):
        return pltpu.make_async_copy(
            self.source.at[self.me], self.target.at[self.me], self.own_sem.at[0]
        )

    def start(self, others=0):
        self.greet(others)
        for distance in range(1, self.count):
            self.copy(distance).start()
        if self.pair is not None:
            self.pair_copy().start()
        self.own().start()

    def finish(self):
        for distance in range(1, self.count):
            self.copy(distance).wait()
        if self.pair is not None:
            self.pair_copy().wait()
        self.own().wait()


def trade_scratch(count):
    dma = pltpu.SemaphoreType.DMA
    return [dma((count - 1,)), dma((count - 1,)), dma((1,))]


def segment_at(places, ends_ref):
    total = jnp.zeros(places.shape, jnp.int32)
    for doc in range(ends_ref.shape[0]):
        total = total + (places >= ends_ref[doc]).astype(jnp.int32)
    return total


def head_spread(rows, heads):
    lane_head = lax.broadcasted_iota(jnp.int32, (1, rows.shape[1]), 1) // HD
    return jnp.concatenate(
        [rows * (lane_head == head).astype(F32).astype(rows.dtype) for head in range(heads)], axis=0
    )


def head_fold(wide, heads):
    rows = wide.shape[0] // heads
    lane_head = lax.broadcasted_iota(jnp.int32, (rows, wide.shape[1]), 1) // HD
    folded = jnp.zeros((rows, wide.shape[1]), wide.dtype)
    for head in range(heads):
        folded = jnp.where(lane_head == head, wide[head * rows : (head + 1) * rows], folded)
    return folded


def block_at(block):
    return pl.ds(pl.multiple_of(block * BLOCK, BLOCK), BLOCK)


def fill_segments(token_segs, ends_ref):
    def fill(block, _):
        places = block * BLOCK + lax.broadcasted_iota(jnp.int32, (BLOCK, token_segs.shape[1]), 0)
        token_segs[block_at(block), :] = segment_at(places, ends_ref)
        return 0

    lax.fori_loop(0, token_segs.shape[0] // BLOCK, fill, 0)


def query_segments(block, heads, ends_ref):
    lanes = lax.broadcasted_iota(jnp.int32, (8, heads * BLOCK), 1)
    return segment_at(block * BLOCK + lanes % BLOCK, ends_ref)[0:1]


def key_segments(starts, keeps, ends_ref):
    lanes = lax.broadcasted_iota(jnp.int32, (8, 2 * BLOCK), 1)
    first = lanes < BLOCK
    pieces = []
    for entry in range(0, LIST, 2):
        places = lanes + jnp.where(
            first, starts[entry] * BLOCK, (starts[entry + 1] - 1) * BLOCK
        )
        keep = jnp.where(first, keeps[entry], keeps[entry + 1]) > 0
        pieces.append(jnp.where(keep, segment_at(places, ends_ref), -1))
    return jnp.concatenate(pieces, axis=1)[0:1]


def gathered(ref, starts):
    return jnp.concatenate([ref[block_at(start), :] for start in starts], axis=0)


def block_parts(wide):
    return [wide[start : start + BLOCK] for start in range(0, wide.shape[0], BLOCK)]


def dot_nt(left, right):
    return lax.dot_general(left, right, (((1,), (1,)), ((), ())), preferred_element_type=F32)


def dot_tn(left, right):
    return lax.dot_general(left, right, (((0,), (0,)), ((), ())), preferred_element_type=F32)


def dot_nn(left, right):
    return lax.dot_general(left, right, (((1,), (0,)), ((), ())), preferred_element_type=F32)


def as_row(tall):
    count = tall.shape[0]
    row_ids = lax.broadcasted_iota(jnp.int32, (count, count), 0)
    lane_ids = lax.broadcasted_iota(jnp.int32, (count, count), 1)
    return jnp.sum(jnp.where(row_ids == lane_ids, tall, 0.0), axis=0, keepdims=True)


def together(running):
    while running:
        still = []
        for each in running:
            if next(each, 0) is None:
                still.append(each)
        running = still


def unit_block(unit, half, parts, rows_total):
    per = rows_total // parts // BLOCK // 2
    part = unit // per
    inside = unit - part * per
    return part, inside, part * 2 * per + half * per + inside


def forward_kernel(heads, half, ends_ref, lists_ref, admit_ref, q_ref, k_ref, v_ref, *rest):
    o_ref, lse_ref, token_segs, *held = rest
    held = held[0] if held else None
    scale = HD ** (-0.5)
    rows_total = q_ref.shape[0]
    units = o_ref.shape[0] * o_ref.shape[1] // BLOCK
    first_unit = GLOB if half == 0 else 0
    chunk = LIST * BLOCK
    fill_segments(token_segs, ends_ref)

    def store(unit, wide, top, total):
        part, inside, block = unit_block(unit, half, o_ref.shape[0], rows_total)
        out = head_fold(wide, heads)
        places = block * BLOCK + lax.broadcasted_iota(jnp.int32, out.shape, 0)
        out = jnp.where(places < ends_ref[ends_ref.shape[0] - 1], out, 0.0)
        o_ref[part, block_at(inside), :] = out.astype(BF16)
        lse_ref[unit] = jnp.broadcast_to(as_row(top + jnp.log(total)), lse_ref.shape[1:])

    def kept(block, key_segs):
        own = token_segs[block_at(block), :]
        return jnp.concatenate([own] * (chunk // own.shape[1]), axis=1) == key_segs

    def global_blocks():
        query_wide = jnp.concatenate(
            [head_spread(q_ref[block_at(block), :] * scale, heads) for block in range(GLOB)], axis=0
        )
        wide_rows = GLOB * heads * BLOCK

        def score(part, top):
            here = pl.ds(pl.multiple_of(part * chunk, chunk), chunk)
            places = part * chunk + lax.broadcasted_iota(jnp.int32, (8, chunk), 1)
            key_segs = segment_at(places, ends_ref)[0:1]
            keeps = [kept(block, key_segs) for block in range(GLOB)]
            scores = dot_nt(query_wide, k_ref[here, :])
            tops = []
            for place, rows in enumerate(block_parts(scores)):
                rows = jnp.where(keeps[place // heads], rows, NEG)
                held[place * BLOCK : (place + 1) * BLOCK, here] = rows
                tops.append(jnp.max(rows, axis=1, keepdims=True))
            return jnp.maximum(top, jnp.concatenate(tops, axis=0))

        top = lax.fori_loop(0, rows_total // chunk, score, jnp.full((wide_rows, 1), NEG, F32))

        def gather(part, carried):
            total, wide = carried
            here = pl.ds(pl.multiple_of(part * chunk, chunk), chunk)
            totals, weights = [], []
            for place, part_top in enumerate(block_parts(top)):
                weight = jnp.exp(held[place * BLOCK : (place + 1) * BLOCK, here] - part_top)
                totals.append(jnp.sum(weight, axis=1, keepdims=True))
                weights.append(weight.astype(BF16))
            wide = wide + dot_nn(jnp.concatenate(weights, axis=0), v_ref[here, :])
            return total + jnp.concatenate(totals, axis=0), wide

        total, wide = lax.fori_loop(
            0,
            rows_total // chunk,
            gather,
            (jnp.zeros((wide_rows, 1), F32), jnp.zeros((wide_rows, q_ref.shape[1]), F32)),
        )
        wide = wide * (1.0 / total)
        for block in range(GLOB):
            own = slice(block * heads * BLOCK, (block + 1) * heads * BLOCK)
            store(block, wide[own], top[own], total[own])

    if half == 0:
        global_blocks()

    def listed_block(unit):
        _, _, block = unit_block(unit, half, o_ref.shape[0], rows_total)
        query_wide = head_spread(q_ref[block_at(block), :] * scale, heads)
        starts = [lists_ref[block * LIST + entry] for entry in range(LIST)]
        keeps = [admit_ref[block * LIST + entry] for entry in range(LIST)]
        keep = kept(block, key_segments(starts, keeps, ends_ref))
        scores = dot_nt(query_wide, gathered(k_ref, starts))
        yield
        tops, totals, probs = [], [], []
        for rows in block_parts(scores):
            rows = jnp.where(keep, rows, NEG)
            top = jnp.max(rows, axis=1, keepdims=True)
            weights = jnp.exp(rows - top)
            total = jnp.sum(weights, axis=1, keepdims=True)
            probs.append((weights * (1.0 / total)).astype(BF16))
            tops.append(top)
            totals.append(total)
            yield
        wide = dot_nn(jnp.concatenate(probs, axis=0), gathered(v_ref, starts))
        store(unit, wide, jnp.concatenate(tops, axis=0), jnp.concatenate(totals, axis=0))

    def listed_group(group, _):
        together([listed_block(first_unit + 4 * group + place) for place in range(4)])
        return 0

    lax.fori_loop(0, (units - first_unit) // 4, listed_group, 0)
    together([listed_block(units - 1 - place) for place in range((units - first_unit) % 4)])


def backward_kernel(
    heads,
    ends_ref,
    lists_ref,
    admit_ref,
    q_ref,
    k_ref,
    v_ref,
    o_first,
    o_second,
    do_first,
    do_second,
    lse_first,
    lse_second,
    out_ref,
    token_segs,
    dk_ref,
    dv_ref,
    dq_ref,
):
    scale = HD ** (-0.5)
    rows_total, cols = q_ref.shape
    blocks = rows_total // BLOCK
    pair_rows = 2 * BLOCK
    fill_segments(token_segs, ends_ref)

    def prepare(pair, _):
        here = pl.ds(pl.multiple_of(pair * pair_rows, pair_rows), pair_rows)
        dk_ref[here, :] = jnp.zeros((pair_rows, cols), F32)
        dv_ref[here, :] = jnp.zeros((pair_rows, cols), F32)
        return 0

    lax.fori_loop(0, blocks // 2, prepare, 0)

    parts = o_first.shape[0]
    halves_of = ((o_first, do_first, lse_first), (o_second, do_second, lse_second))

    def query_side(unit, half):
        o_ref, do_ref, lse_ref = halves_of[half]
        part, inside, block = unit_block(unit, half, parts, rows_total)
        query_wide = head_spread(q_ref[block_at(block), :] * scale, heads)
        grad_rows = do_ref[part, block_at(inside), :]
        grad_wide = head_spread(grad_rows, heads)
        product = grad_rows.astype(F32) * o_ref[part, block_at(inside), :].astype(F32)
        spread = head_spread(product.astype(BF16), heads)
        delta = dot_nt(jnp.ones((8, cols), BF16), spread)[0:1]
        seg_row = query_segments(block, heads, ends_ref)
        return query_wide, grad_wide, delta, lse_ref[unit, 0:1], seg_row

    def unit(starts, keeps, query_wide, grad_wide, delta, lse, seg_row, finish_query):
        keys = gathered(k_ref, starts)
        scores = block_parts(dot_nt(keys, query_wide))
        prob_grads = block_parts(dot_nt(gathered(v_ref, starts), grad_wide))
        yield
        probs, score_grads = [], []
        for entry in range(LIST):
            wanted = seg_row if keeps is None else jnp.where(keeps[entry] > 0, seg_row, -1)
            own = token_segs[block_at(starts[entry]), :]
            keep = jnp.concatenate([own] * (seg_row.shape[1] // own.shape[1]), axis=1) == wanted
            prob = jnp.exp(jnp.where(keep, scores[entry], NEG) - lse)
            probs.append(prob.astype(BF16))
            score_grads.append((prob * (prob_grads[entry] - delta)).astype(BF16))
            if entry % 2:
                yield
        score_grad = jnp.concatenate(score_grads, axis=0)
        finish_query(dot_tn(score_grad, keys))
        dk = dot_nn(score_grad, query_wide)
        dv = dot_nn(jnp.concatenate(probs, axis=0), grad_wide)
        yield
        for entry in range(LIST):
            here = block_at(starts[entry])
            dk_ref[here, :] += dk[entry * BLOCK : (entry + 1) * BLOCK]
            dv_ref[here, :] += dv[entry * BLOCK : (entry + 1) * BLOCK]
        yield

    def store_query(block, wide):
        out_ref[block_at(block), 0:cols] = (head_fold(wide, heads) * scale).astype(BF16)

    def global_blocks():
        sides = [query_side(block, 0) for block in range(GLOB)]
        side = [jnp.concatenate(both, axis=axis) for both, axis in zip(zip(*sides), (0, 0, 1, 1, 1))]
        dq_ref[...] = jnp.zeros_like(dq_ref)

        def part_of(part, _):
            def add_query(wide):
                dq_ref[...] += wide

            together([unit([part * LIST + entry for entry in range(LIST)], None, *side, add_query)])
            return 0

        lax.fori_loop(0, blocks // LIST, part_of, 0)
        for block in range(GLOB):
            store_query(block, dq_ref[block * heads * BLOCK : (block + 1) * heads * BLOCK])

    global_blocks()

    def listed_block(place, half):
        _, _, block = unit_block(place, half, parts, rows_total)
        starts = [lists_ref[block * LIST + entry] for entry in range(LIST)]
        keeps = [admit_ref[block * LIST + entry] for entry in range(LIST)]
        return unit(
            starts, keeps, *query_side(place, half), functools.partial(store_query, block)
        )

    for half, first_unit in ((0, GLOB), (1, 0)):
        units = blocks // 2

        def listed_group(group, _):
            together([listed_block(first_unit + 4 * group + place, half) for place in range(4)])
            return 0

        lax.fori_loop(0, (units - first_unit) // 4, listed_group, 0)
        together([listed_block(units - 1 - place, half) for place in range((units - first_unit) % 4)])

    def finish(block, _):
        here = block_at(block)
        out_ref[here, cols : 2 * cols] = dk_ref[here, :].astype(BF16)
        out_ref[here, 2 * cols : 3 * cols] = dv_ref[here, :].astype(BF16)
        return 0

    lax.fori_loop(0, blocks, finish, 0)


def smem():
    return pl.BlockSpec(memory_space=pltpu.SMEM)


def column(rows, cols, index):
    return pl.BlockSpec((rows, cols), lambda step: (0, index))


def attention_forward(half, qkv, doc_ends, lists, admits, parts):
    rows = qkv.shape[0]
    cols = qkv.shape[1] // 3
    heads = cols // HD
    blocks = rows // BLOCK
    out = jax.ShapeDtypeStruct((parts, rows // parts // 2, cols), BF16)
    lse = jax.ShapeDtypeStruct((blocks // 2, 8, heads * BLOCK), F32)
    cube = lambda step: (0, 0, 0)
    return pl.pallas_call(
        functools.partial(forward_kernel, heads, half),
        grid=(1,),
        in_specs=[smem(), smem(), smem()] + [column(rows, cols, part) for part in range(3)],
        out_specs=[pl.BlockSpec(out.shape, cube), pl.BlockSpec(lse.shape, cube)],
        out_shape=[out, lse],
        scratch_shapes=[pltpu.VMEM((rows, 2 * BLOCK), jnp.int32)]
        + ([] if half else [pltpu.VMEM((GLOB * heads * BLOCK, rows), F32)]),
        compiler_params=pltpu.CompilerParams(vmem_limit_bytes=VMEM_LIMIT),
        cost_estimate=pl.CostEstimate(
            flops=rows * LIST * BLOCK * cols * heads * 5,
            bytes_accessed=8 * rows * cols,
            transcendentals=0,
        ),
    )(doc_ends, lists, admits, qkv, qkv, qkv)


def attention_backward(qkv, attended, attended_grad, lse, doc_ends, lists, admits):
    rows = qkv.shape[0]
    cols = qkv.shape[1] // 3
    heads = cols // HD
    cube = lambda step: (0, 0, 0)
    return pl.pallas_call(
        functools.partial(backward_kernel, heads),
        grid=(1,),
        in_specs=[smem(), smem(), smem()]
        + [column(rows, cols, part) for part in range(3)]
        + [pl.BlockSpec(part.shape, cube) for part in (*attended, *attended_grad, *lse)],
        out_specs=column(rows, 3 * cols, 0),
        out_shape=jax.ShapeDtypeStruct((rows, 3 * cols), BF16),
        scratch_shapes=[
            pltpu.VMEM((rows, 2 * BLOCK), jnp.int32),
            pltpu.VMEM((rows, cols), F32),
            pltpu.VMEM((rows, cols), F32),
            pltpu.VMEM((GLOB * heads * BLOCK, cols), F32),
        ],
        compiler_params=pltpu.CompilerParams(vmem_limit_bytes=VMEM_LIMIT),
        cost_estimate=pl.CostEstimate(
            flops=rows * LIST * BLOCK * cols * heads * 15,
            bytes_accessed=20 * rows * cols,
            transcendentals=0,
        ),
    )(doc_ends, lists, admits, qkv, qkv, qkv, *attended, *attended_grad, *lse)


def row_stats(rows):
    mean = jnp.mean(rows, axis=-1, keepdims=True)
    centre = rows - mean
    spread = jnp.mean(centre * centre, axis=-1, keepdims=True)
    inverse = lax.rsqrt(spread + EPS)
    return centre * inverse, inverse


def gelu_pair(inner):
    root = 0.7978845608028654
    cube = 0.044715
    square = inner * inner
    bent = jnp.tanh(inner * (root + (root * cube) * square))
    half = 0.5 + 0.5 * bent
    value = inner * half
    return value, half + value * (1.0 - bent) * (root + (3.0 * root * cube) * square)


def token_kernel(
    tile,
    index,
    ends_ref,
    att_ref,
    x_ref,
    cotangent_ref,
    out_own_ref,
    out_other_ref,
    up_own_ref,
    up_near_ref,
    up_far_ref,
    down_own_ref,
    down_near_ref,
    down_far_ref,
    up_bias_ref,
    gain_ref,
    bias_ref,
    down_bias_ref,
    trade_source,
    pair_source,
    act_in,
    pre_in,
    second_in,
    hidden_in,
    grad_in,
    att_in,
    output_ref,
    hidden_grad_ref,
    datt_ref,
    act_ref,
    pre_ref,
    second_ref,
    hidden_low_ref,
    grad_low_ref,
    att_rows_ref,
    sums_ref,
    unit_sums_ref,
    trade_target,
    pair_target,
    hidden,
    normed,
    inverse,
    ffn,
    second_grad,
    grad_rows,
    up_slots,
    down_slots,
    slot_sems,
    row_sems,
    pair_sems,
    *trade_sems,
):
    step = pl.program_id(0)
    steps = pl.num_programs(0)
    rows = hidden.shape[0]
    parts = att_ref.shape[0]
    tiles = [slice(start, start + tile) for start in range(0, rows, tile)]
    chunk = up_slots.shape[2]
    own_steps = up_own_ref.shape[1] // chunk
    near_steps = up_near_ref.shape[1] // chunk

    def copies(up_from, down_from, index, slot):
        here = pl.ds(pl.multiple_of(index * chunk, chunk), chunk)
        return (
            pltpu.make_async_copy(up_from.at[:, here], up_slots.at[slot], slot_sems.at[0, slot]),
            pltpu.make_async_copy(down_from.at[here], down_slots.at[slot], slot_sems.at[1, slot]),
        )

    def fetch(index):
        def begin(up_from, down_from, first):
            for copy in copies(up_from, down_from, index - first, index % 2):
                copy.start()

        @pl.when(index < own_steps)
        def _():
            begin(up_own_ref, down_own_ref, 0)

        @pl.when((index >= own_steps) & (index < own_steps + near_steps))
        def _():
            begin(up_near_ref, down_near_ref, own_steps)

        @pl.when(index >= own_steps + near_steps)
        def _():
            begin(up_far_ref, down_far_ref, own_steps + near_steps)

    half = parts // 2
    me = lax.axis_index("seq")
    place = lax.axis_index("mp")
    own_place = place * half
    other_place = (1 - place) * half
    first_row = index * rows
    row_copies = [
        pltpu.make_async_copy(source.at[place, pl.ds(first_row, rows)], target, row_sems.at[which])
        for which, (source, target) in enumerate(((x_ref, hidden), (cotangent_ref, grad_rows)))
    ]
    pair = (pair_source, pair_target, pair_sems) if index else None
    trade = Trade(trade_source, trade_target, *trade_sems, pair)
    out_parts = [(own_place + part, out_own_ref, part) for part in range(half)]
    out_parts += [(other_place + part, out_other_ref, part) for part in range(half)]

    @pl.when(step == 0)
    def _():
        for copy in row_copies:
            copy.start()
        fetch(step)
        trade.start()

    @pl.when(step + 1 < steps)
    def _():
        fetch(step + 1)

    @pl.when(step == 0)
    def _():
        for copy in row_copies:
            copy.wait()
        for here in tiles:
            total = hidden[here, :]
            for part, weight_ref, index in out_parts:
                total = total + dot_nn(att_ref[part, here, :], weight_ref[index])
            for part in range(parts):
                cols = att_ref.shape[2]
                att_rows_ref[here, part * cols : (part + 1) * cols] = att_ref[part, here, :]
            hidden[here, :] = total
            unit, scale = row_stats(total)
            normed[here, :] = unit
            inverse[here, :] = jnp.broadcast_to(scale, (tile, inverse.shape[1]))
            second_ref[here, :] = (unit * gain_ref[...] + bias_ref[...]).astype(BF16)
            grad_low_ref[here, :] = grad_rows[here, :].astype(BF16)
            ffn[here, :] = jnp.zeros((tile, ffn.shape[1]), F32)
            second_grad[here, :] = jnp.zeros((tile, ffn.shape[1]), F32)

    slot = step % 2
    for copy in copies(up_own_ref, down_own_ref, 0, slot):
        copy.wait()
    up_ref = up_slots.at[slot]
    down_ref = down_slots.at[slot]
    unit_sum = jnp.zeros((1, chunk), F32)
    for here in tiles:
        inner = dot_nn(second_ref[here, :], up_ref[...]) + up_bias_ref[...]
        act_grad = dot_nt(grad_low_ref[here, :], down_ref[...])
        value, slope = gelu_pair(inner)
        value = value.astype(BF16)
        pre_grad = (act_grad * slope).astype(BF16)
        act_ref[here, :] = value
        pre_ref[here, :] = pre_grad
        unit_sum = unit_sum + jnp.sum(pre_grad.astype(F32), axis=0, keepdims=True)
        ffn[here, :] += dot_nn(value, down_ref[...])
        second_grad[here, :] += dot_nt(pre_grad, up_ref[...])
    unit_sums_ref[...] = jnp.broadcast_to(unit_sum, unit_sums_ref.shape)

    @pl.when(step == steps - 1)
    def _():
        width = ffn.shape[1]
        grad_sum = jnp.zeros((1, width), F32)
        gain_sum = jnp.zeros((1, width), F32)
        bias_sum = jnp.zeros((1, width), F32)
        for number, here in enumerate(tiles):
            output_ref[here, :] = (hidden[here, :] + ffn[here, :] + down_bias_ref[...]).astype(BF16)
            grad = grad_rows[here, :]
            back = second_grad[here, :]
            unit = normed[here, :]
            scaled = back * gain_ref[...]
            through = (
                scaled
                - jnp.mean(scaled, axis=-1, keepdims=True)
                - unit * jnp.mean(scaled * unit, axis=-1, keepdims=True)
            )
            total = grad + inverse[here, 0:1] * through
            hidden_grad_ref[here, :] = total
            low = total.astype(BF16)
            hidden_low_ref[here, :] = low
            grad_sum = grad_sum + jnp.sum(grad, axis=0, keepdims=True)
            gain_sum = gain_sum + jnp.sum(back * unit, axis=0, keepdims=True)
            bias_sum = bias_sum + jnp.sum(back, axis=0, keepdims=True)
            for part, weight_ref, piece in out_parts:
                spread = dot_nt(low, weight_ref[piece])
                places = me * 2 * rows + first_row + number * tile
                places = places + lax.broadcasted_iota(jnp.int32, spread.shape, 0)
                inside = places < ends_ref[ends_ref.shape[0] - 1]
                datt_ref[part, here, :] = jnp.where(inside, spread, 0.0).astype(BF16)
        sums_ref[...] = jnp.concatenate(
            [grad_sum, gain_sum, bias_sum, jnp.zeros((5, width), F32)], axis=0
        )
        trade.finish()


def token_part(
    index, doc_ends, att, layer_input, cotangent, outs, ups, downs, up_bias, gain, bias, down_bias, source, pair, kept
):
    parts, rows, cols = att.shape
    width = layer_input.shape[2]
    units = up_bias.shape[1]
    chunk = min(512, units // 4)
    whole = 2 * rows
    shapes = [(whole, units)] * 2 + [(whole, width)] * 4
    if kept is None:
        kept = [jnp.zeros((8, 128), BF16)] * len(shapes)
        aliases = {}
    else:
        aliases = {18 + place: 3 + place for place in range(len(shapes))}
    half = lambda step: (index, 0)
    fixed = lambda step: (0, 0)
    any_spec = pl.BlockSpec(memory_space=pl.ANY)
    cube = lambda step: (0, 0, 0)
    vector = pl.BlockSpec((1, width), fixed)
    return pl.pallas_call(
        functools.partial(token_kernel, min(256, rows), index),
        grid=(units // chunk,),
        in_specs=[
            smem(),
            pl.BlockSpec((parts, rows, cols), cube),
            any_spec,
            any_spec,
            pl.BlockSpec((parts // 2, cols, width), cube),
            pl.BlockSpec((parts // 2, cols, width), cube),
        ]
        + [any_spec] * 6
        + [pl.BlockSpec((1, chunk), lambda step: (0, step)), vector, vector, vector]
        + [any_spec] * (2 + len(shapes)),
        out_specs=[
            pl.BlockSpec((rows, width), fixed),
            pl.BlockSpec((rows, width), fixed),
            pl.BlockSpec((parts, rows, cols), cube),
            pl.BlockSpec((rows, chunk), lambda step: (index, step)),
            pl.BlockSpec((rows, chunk), lambda step: (index, step)),
            pl.BlockSpec((rows, width), half),
            pl.BlockSpec((rows, width), half),
            pl.BlockSpec((rows, width), half),
            pl.BlockSpec((rows, width), half),
            pl.BlockSpec((8, width), fixed),
            pl.BlockSpec((8, chunk), lambda step: (0, step)),
            any_spec,
            any_spec,
        ],
        scratch_shapes=[
            pltpu.VMEM((rows, width), F32),
            pltpu.VMEM((rows, width), F32),
            pltpu.VMEM((rows, 128), F32),
            pltpu.VMEM((rows, width), F32),
            pltpu.VMEM((rows, width), F32),
            pltpu.VMEM((rows, width), F32),
            pltpu.VMEM((2, width, chunk), BF16),
            pltpu.VMEM((2, chunk, width), BF16),
            pltpu.SemaphoreType.DMA((2, 2)),
            pltpu.SemaphoreType.DMA((2,)),
            pltpu.SemaphoreType.DMA((2,)),
        ]
        + trade_scratch(parts),
        out_shape=[
            jax.ShapeDtypeStruct((rows, width), BF16),
            jax.ShapeDtypeStruct((rows, width), F32),
            jax.ShapeDtypeStruct((parts, rows, cols), BF16),
        ]
        + [jax.ShapeDtypeStruct(shape, BF16) for shape in shapes]
        + [
            jax.ShapeDtypeStruct((8, width), F32),
            jax.ShapeDtypeStruct((8, units), F32),
            jax.ShapeDtypeStruct((parts, rows, cols), BF16),
            jax.ShapeDtypeStruct(pair.shape, BF16),
        ],
        input_output_aliases=aliases,
        compiler_params=pltpu.CompilerParams(
            collective_id=5 + index, has_side_effects=True, vmem_limit_bytes=VMEM_LIMIT
        ),
        cost_estimate=pl.CostEstimate(
            flops=rows * width * (8 * units + 4 * width),
            bytes_accessed=8 * units * width,
            transcendentals=0,
        ),
    )(
        doc_ends,
        att,
        layer_input,
        cotangent,
        *outs,
        *ups,
        *downs,
        up_bias,
        gain,
        bias,
        down_bias,
        source,
        pair,
        *kept,
    )


def greet(me, count, partner=None):
    barrier = pltpu.get_barrier_semaphore()

    @pl.when(me > 0)
    def _():
        pl.semaphore_signal(barrier, inc=1, device_id={"seq": me - 1}, device_id_type=MESH)

    @pl.when(me < count - 1)
    def _():
        pl.semaphore_signal(barrier, inc=1, device_id={"seq": me + 1}, device_id_type=MESH)

    peers = jnp.minimum(me, 1) + jnp.minimum(count - 1 - me, 1)
    if partner is not None:
        pl.semaphore_signal(barrier, inc=1, device_id={"mp": partner}, device_id_type=MESH)
        peers = peers + 1
    pl.semaphore_wait(barrier, peers)


def gather_kernel(
    count,
    chunks,
    x_ref,
    gain_ref,
    bias_ref,
    weight_ref,
    out_ref,
    up_ref,
    up_bias_ref,
    all_ref,
    qkv_ref,
    own_ref,
    out_other,
    up_near,
    up_bias_near,
    rows_in,
    shards,
    results,
    weight,
    weight_sems,
    fetch_sems,
    load_sems,
    send_sems,
    recv_sems,
    all_sems,
    qkv_sems,
):
    me = lax.axis_index("seq")
    place = lax.axis_index("mp")
    step = rows_in.shape[0] // chunks
    cols = weight.shape[1] // 3

    def at(chunk):
        return pl.ds(pl.multiple_of(chunk * step, step), step)

    def load(chunk):
        return pltpu.make_async_copy(
            x_ref.at[place, at(chunk)], rows_in.at[at(chunk)], load_sems.at[chunk]
        )

    def send(side, hop, chunk):
        shard = me - hop if side == 0 else me + hop
        target = me + 1 if side == 0 else me - 1
        return pltpu.make_async_remote_copy(
            src_ref=shards.at[shard, at(chunk)],
            dst_ref=shards.at[shard, at(chunk)],
            send_sem=send_sems.at[side, hop, chunk],
            recv_sem=recv_sems.at[side, hop, chunk],
            device_id={"seq": target},
            device_id_type=MESH,
        )

    def keep_all(shard, chunk):
        return pltpu.make_async_copy(
            shards.at[shard, at(chunk)], all_ref.at[shard, at(chunk)], all_sems.at[shard, chunk]
        )

    def keep_qkv(shard, chunk):
        return pltpu.make_async_copy(
            results.at[shard, at(chunk)], qkv_ref.at[shard, at(chunk)], qkv_sems.at[shard, chunk]
        )

    def over_chunks(body):
        def run(chunk, _):
            body(chunk)
            return 0

        lax.fori_loop(0, chunks, run, 0)

    over_chunks(lambda chunk: load(chunk).start())
    greet(me, count, 1 - place)

    half_cols = weight_ref.shape[2]
    here = (me * cols) // half_cols == place
    heads = pl.ds(pl.multiple_of((me * cols) % half_cols, 128), cols)
    fetches, copies = [], []
    for matrix in range(3):
        source = weight_ref.at[matrix, :, heads]
        target = weight.at[:, pl.ds(matrix * cols, cols)]
        fetches.append(
            pltpu.make_async_remote_copy(
                src_ref=source,
                dst_ref=target,
                send_sem=weight_sems.at[0, matrix],
                recv_sem=weight_sems.at[1, matrix],
                device_id={"mp": 1 - place},
                device_id_type=MESH,
            )
        )
        copies.append(pltpu.make_async_copy(source, target, weight_sems.at[2, matrix]))

    @pl.when(here)
    def _():
        for each in fetches + copies:
            each.start()

    parity = lax.axis_index("batch") % 2
    share = up_near.shape[1]
    columns = pl.ds(pl.multiple_of(parity * share, share), share)
    shares = [
        pltpu.make_async_remote_copy(
            src_ref=source,
            dst_ref=target,
            send_sem=fetch_sems.at[0, which],
            recv_sem=fetch_sems.at[1, which],
            device_id={"mp": 1 - place},
            device_id_type=MESH,
        )
        for which, (source, target) in enumerate(
            (
                (out_ref, out_other),
                (up_ref.at[:, columns], up_near),
                (up_bias_ref.at[:, columns], up_bias_near),
            )
        )
    ]
    for each in shares:
        each.start()

    def norm(chunk):
        load(chunk).wait()
        unit, _ = row_stats(rows_in[at(chunk), :])
        shards[me, at(chunk), :] = (unit * gain_ref[...] + bias_ref[...]).astype(BF16)
        keep_all(me, chunk).start()

        @pl.when(me < count - 1)
        def _():
            send(0, 0, chunk).start()

        @pl.when(me > 0)
        def _():
            send(1, 0, chunk).start()

    over_chunks(norm)

    def project(shard, chunk):
        rows = dot_nn(shards[shard, at(chunk), :], weight[...])
        results[shard, at(chunk), :] = rows.astype(BF16)
        keep_qkv(shard, chunk).start()

    def receive(hop, chunk):
        @pl.when(me >= hop + 1)
        def _():
            send(0, hop, chunk).wait_recv()
            if hop + 1 < count - 1:

                @pl.when(me < count - 1)
                def _():
                    send(0, hop + 1, chunk).start()

            keep_all(me - hop - 1, chunk).start()

        @pl.when(me + hop + 1 < count)
        def _():
            send(1, hop, chunk).wait_recv()
            if hop + 1 < count - 1:

                @pl.when(me > 0)
                def _():
                    send(1, hop + 1, chunk).start()

            keep_all(me + hop + 1, chunk).start()

    for hop in range(count - 2):
        over_chunks(functools.partial(receive, hop))

    @pl.when(here)
    def _():
        for each in copies:
            each.wait()

    @pl.when(jnp.logical_not(here))
    def _():
        for each in fetches:
            each.wait_recv()

    keep_weight = pltpu.make_async_copy(weight, own_ref, weight_sems.at[3, 0])
    keep_weight.start()

    def last(chunk):
        project(me, chunk)
        for hop in range(count - 1):
            if hop == count - 2:
                receive(hop, chunk)

            @pl.when(me >= hop + 1)
            def _():
                project(me - hop - 1, chunk)

            @pl.when(me + hop + 1 < count)
            def _():
                project(me + hop + 1, chunk)

    over_chunks(last)

    def finish(chunk):
        for hop in range(count - 1):

            @pl.when((me >= hop) & (me < count - 1))
            def _():
                send(0, hop, chunk).wait_send()

            @pl.when((me + hop < count) & (me > 0))
            def _():
                send(1, hop, chunk).wait_send()

        for shard in range(count):
            keep_all(shard, chunk).wait()
            keep_qkv(shard, chunk).wait()

    over_chunks(finish)
    keep_weight.wait()
    for each in shares:
        each.wait()

    @pl.when(here)
    def _():
        for each in fetches:
            each.wait_send()


def gather_project(layer_input, gain, bias, weight, out_weight, up_weight, up_bias):
    count = lax.axis_size("seq")
    _, rows, width = layer_input.shape
    cols = 3 * width // count
    chunks = max(1, rows // 128)
    any_spec = pl.BlockSpec(memory_space=pl.ANY)
    vmem = pl.BlockSpec(memory_space=pltpu.VMEM)
    dma = pltpu.SemaphoreType.DMA
    return pl.pallas_call(
        functools.partial(gather_kernel, count, chunks),
        in_specs=[any_spec, vmem, vmem] + [any_spec] * 4,
        out_specs=[any_spec] * 6,
        out_shape=[
            jax.ShapeDtypeStruct((count, rows, width), BF16),
            jax.ShapeDtypeStruct((count, rows, cols), BF16),
            jax.ShapeDtypeStruct((width, cols), BF16),
            jax.ShapeDtypeStruct(out_weight.shape, BF16),
            jax.ShapeDtypeStruct((width, up_weight.shape[1] // 2), BF16),
            jax.ShapeDtypeStruct((1, up_weight.shape[1] // 2), F32),
        ],
        scratch_shapes=[
            pltpu.VMEM((rows, width), F32),
            pltpu.VMEM((count, rows, width), BF16),
            pltpu.VMEM((count, rows, cols), BF16),
            pltpu.VMEM((width, cols), BF16),
            dma((4, 3)),
            dma((2, 3)),
            dma((chunks,)),
            dma((2, count - 1, chunks)),
            dma((2, count - 1, chunks)),
            dma((count, chunks)),
            dma((count, chunks)),
        ],
        compiler_params=pltpu.CompilerParams(
            collective_id=0, has_side_effects=True, vmem_limit_bytes=VMEM_LIMIT
        ),
        cost_estimate=pl.CostEstimate(
            flops=150_000_000_000, bytes_accessed=1, transcendentals=0
        ),
    )(layer_input, gain, bias, weight, out_weight, up_weight, up_bias)


class VectorSum:
    def __init__(self, group, line, sems):
        self.group, self.line, self.sems = group, line, sems
        self.me, self.count = lax.axis_index("seq"), lax.axis_size("seq")
        self.pairs = lax.axis_size("mp")
        self.members = lax.axis_size("batch") * self.pairs
        self.mine = lax.axis_index("batch") * self.pairs + lax.axis_index("mp")

    def member(self, distance):
        other = lax.rem(self.mine + distance, self.members)
        return {"batch": other // self.pairs, "mp": lax.rem(other, self.pairs)}

    def along(self, distance):
        return {"seq": lax.rem(self.me + distance, self.count)}

    def greet(self):
        barrier = pltpu.get_barrier_semaphore()
        for distance in range(1, self.members):
            pl.semaphore_signal(
                barrier, inc=1, device_id=self.member(distance), device_id_type=MESH
            )
        for distance in range(1, self.count):
            pl.semaphore_signal(barrier, inc=1, device_id=self.along(distance), device_id_type=MESH)
        pl.semaphore_wait(barrier, self.members + self.count - 2)

    def share(self, distance, along):
        buffer, place = (self.line, self.me) if along else (self.group, self.mine)
        which = distance - 1 + (self.members - 1 if along else 0)
        return pltpu.make_async_remote_copy(
            src_ref=buffer.at[place],
            dst_ref=buffer.at[place],
            send_sem=self.sems.at[0, which],
            recv_sem=self.sems.at[1, which],
            device_id=self.along(distance) if along else self.member(distance),
            device_id_type=MESH,
        )

    def start(self, value):
        self.group[self.mine] = value
        for distance in range(1, self.members):
            self.share(distance, False).start()

    def middle(self):
        for distance in range(1, self.members):
            self.share(distance, False).wait()
        total = self.group[0]
        for place in range(1, self.members):
            total = total + self.group[place]
        self.line[self.me] = total
        for distance in range(1, self.count):
            self.share(distance, True).start()

    def finish(self):
        for distance in range(1, self.count):
            self.share(distance, True).wait()
        total = self.line[0]
        for place in range(1, self.count):
            total = total + self.line[place]
        return total


class Extra:
    def __init__(self, kind, source, target, sems):
        self.source, self.target, self.sems = source, target, sems
        batch, place = lax.axis_index("batch"), lax.axis_index("mp")
        self.local = None
        if kind == "mp":
            self.moves = [(source, target, {"mp": 1 - place})]
        else:
            count = source.shape[0]
            pairs = lax.axis_size("mp")
            mine = batch * pairs + place
            self.moves = []
            for distance in range(1, count):
                other = lax.rem(mine + distance, count)
                device = {"batch": other // pairs, "mp": lax.rem(other, pairs)}
                self.moves.append((source.at[other], target.at[mine], device))
            self.local = (source.at[mine], target.at[mine])

    def copies(self):
        for index, (source, target, device) in enumerate(self.moves):
            yield pltpu.make_async_remote_copy(
                src_ref=source,
                dst_ref=target,
                send_sem=self.sems.at[0, index],
                recv_sem=self.sems.at[1, index],
                device_id=device,
                device_id_type=MESH,
            )
        if self.local is not None:
            yield pltpu.make_async_copy(*self.local, self.sems.at[0, len(self.moves)])

    def start(self):
        for copy in self.copies():
            copy.start()

    def finish(self):
        for copy in self.copies():
            copy.wait()


def extra_moves(kind, source):
    return 1 if kind == "mp" else source.shape[0]


def in_rows(vectors, width):
    pieces = []
    for row in range(vectors.shape[0]):
        for start in range(0, vectors.shape[1], width):
            pieces.append(vectors[row : row + 1, start : start + width])
    return jnp.concatenate(pieces, axis=0)


class ProjectionGrad:
    def __init__(self, first_all, parts, grouped, slots, total, low, slot_sems, out_sems):
        self.first_all, self.parts, self.grouped = first_all, parts, grouped
        self.slots, self.total, self.low = slots, total, low
        self.slot_sems, self.out_sems = slot_sems, out_sems
        self.rows = slots.shape[1]
        self.steps = first_all.shape[0] // self.rows

    def fetch(self, step):
        return pltpu.make_async_copy(
            self.first_all.at[pl.ds(pl.multiple_of(step * self.rows, self.rows), self.rows)],
            self.slots.at[step % 2],
            self.slot_sems.at[step % 2],
        )

    def start(self):
        self.fetch(0).start()
        self.total[...] = jnp.zeros_like(self.total)

    def multiply(self, step):
        self.fetch(step).wait()

        @pl.when(step + 1 < self.steps)
        def _():
            self.fetch(step + 1).start()

        here = pl.ds(pl.multiple_of((step % 2) * self.rows, self.rows), self.rows)
        grads = self.parts[step // 2, here, :]
        width = self.total.shape[0]
        size = width // 4
        for start in range(0, width, size):
            rows = self.slots[step % 2, :, start : start + size]
            self.total[start : start + size, :] += dot_tn(rows, grads)

        @pl.when(step == self.steps - 1)
        def _():
            self.low[...] = self.total[...].astype(BF16)
            for copy in self.copies():
                copy.start()

    def copies(self):
        members, count, rows, _ = self.grouped.shape
        for member in range(members):
            for part in range(count):
                first = (part * members + member) * rows
                yield pltpu.make_async_copy(
                    self.low.at[pl.ds(first, rows)],
                    self.grouped.at[member, part],
                    self.out_sems.at[member, part],
                )

    def finish(self):
        for copy in self.copies():
            copy.wait()


class WeightBegin:
    def __init__(self, terms, targets, near_sum, own_sum, down_sum, sems):
        self.terms, self.targets, self.sems = terms, targets, sems
        self.near_sum, self.own_sum, self.down_sum = near_sum, own_sum, down_sum

    def copies(self):
        own_out, near_target, down_out, down_target = self.targets
        batch, place = lax.axis_index("batch"), lax.axis_index("mp")
        side = (batch // 2) % 2
        size = self.down_sum.shape[1] // 2
        kept = pl.ds(pl.multiple_of(side * size, 128), size)
        there = pl.ds(pl.multiple_of((1 - side) * size, 128), size)
        return [
            pltpu.make_async_remote_copy(
                src_ref=self.near_sum,
                dst_ref=near_target,
                send_sem=self.sems.at[0],
                recv_sem=self.sems.at[1],
                device_id={"mp": 1 - place},
                device_id_type=MESH,
            ),
            pltpu.make_async_remote_copy(
                src_ref=self.down_sum.at[:, there],
                dst_ref=down_target,
                send_sem=self.sems.at[2],
                recv_sem=self.sems.at[3],
                device_id={"batch": batch + 2 - 4 * side},
                device_id_type=MESH,
            ),
            pltpu.make_async_copy(self.own_sum, own_out, self.sems.at[4]),
            pltpu.make_async_copy(self.down_sum.at[:, kept], down_out, self.sems.at[5]),
        ]

    def start(self):
        keep, come, down, down_come = self.terms
        rows = keep.shape[1]
        step = min(128, rows)

        def add(index, _):
            here = pl.ds(pl.multiple_of(index * step, step), step)
            near = keep[1, here, :].astype(F32) + come[1, here, :].astype(F32)
            own = keep[0, here, :].astype(F32) + come[0, here, :].astype(F32)
            low = down[here, :].astype(F32) + down_come[here, :].astype(F32)
            self.near_sum[here, :] = near.astype(BF16)
            self.own_sum[here, :] = own.astype(BF16)
            self.down_sum[here, :] = low.astype(BF16)
            return 0

        lax.fori_loop(0, rows // step, add, 0)
        for copy in self.copies():
            copy.start()

    def finish(self):
        for copy in self.copies():
            copy.wait()


class WeightChain:
    def __init__(self, terms, qkv_terms, gathered, heads_ref, sending, received, result, head_sum, heads_in, sems):
        self.terms = terms
        self.qkv_terms, self.gathered, self.heads_ref = qkv_terms, gathered, heads_ref
        self.sending, self.received, self.result = sending, received, result
        self.head_sum, self.heads_in, self.sems = head_sum, heads_in, sems
        self.me, self.count = lax.axis_index("seq"), lax.axis_size("seq")
        self.batch, self.place = lax.axis_index("batch"), lax.axis_index("mp")
        self.rows = result.shape[1]
        self.chunks = 2
        self.step = self.rows // self.chunks
        self.steps = (self.count - 1) * self.chunks
        self.members = qkv_terms.shape[0]
        self.mine = self.batch * 2 + self.place
        self.used = 2 * self.steps

    def at(self, chunk):
        return pl.ds(pl.multiple_of(chunk * self.step, self.step), self.step)

    def term(self, target, chunk):
        here = pl.ds(pl.multiple_of(target * self.rows + chunk * self.step, self.step), self.step)
        own, own_come, down, down_come = (term[here, :].astype(F32) for term in self.terms)
        return jnp.concatenate([own + own_come, down + down_come], axis=1)

    def send(self, side, message, chunk):
        which = (side * (self.count - 1) + message) * self.chunks + chunk
        return pltpu.make_async_remote_copy(
            src_ref=self.sending.at[side, message, self.at(chunk)],
            dst_ref=self.received.at[side, message, self.at(chunk)],
            send_sem=self.sems.at[0, which],
            recv_sem=self.sems.at[1, which],
            device_id={"seq": self.me + 1 - 2 * side},
            device_id_type=MESH,
        )

    def flow(self, side, index):
        message, chunk = index // self.chunks, index % self.chunks
        target = (1 - side) * (self.count - 1 - message) + side * message

        @pl.when((target - self.me) * (1 - 2 * side) > 0)
        def _():
            total = self.term(target, chunk)
            first = (1 - side) * self.me + side * (self.count - 1 - self.me)

            @pl.when(first == 0)
            def _():
                self.sending[side, message, self.at(chunk), :] = total.astype(BF16)

            @pl.when(first > 0)
            def _():
                self.send(side, message, chunk).wait_recv()
                come = self.received[side, message, self.at(chunk), :].astype(F32)
                self.sending[side, message, self.at(chunk), :] = (total + come).astype(BF16)

            self.send(side, message, chunk).start()

    def heads_line(self, distance):
        other = lax.rem(self.me + distance, self.count)
        which = self.used + distance - 1
        return pltpu.make_async_remote_copy(
            src_ref=self.head_sum.at[other],
            dst_ref=self.heads_in.at[self.me],
            send_sem=self.sems.at[0, which],
            recv_sem=self.sems.at[1, which],
            device_id={"seq": other},
            device_id_type=MESH,
        )

    def heads_member(self, distance):
        other = lax.rem(self.mine + distance, self.members)
        which = self.used + self.count - 1 + distance - 1
        parts = self.count // 2
        return pltpu.make_async_remote_copy(
            src_ref=self.heads_in.at[pl.ds(lax.rem(other, 2) * parts, parts)],
            dst_ref=self.heads_ref.at[self.mine],
            send_sem=self.sems.at[0, which],
            recv_sem=self.sems.at[1, which],
            device_id={"batch": other // 2, "mp": lax.rem(other, 2)},
            device_id_type=MESH,
        )

    def heads_own(self):
        parts = self.count // 2
        return pltpu.make_async_copy(
            self.heads_in.at[pl.ds(self.place * parts, parts)],
            self.heads_ref.at[self.mine],
            self.sems.at[0, self.used + self.count + self.members - 2],
        )

    def piece(self, index):
        which = self.used + self.count + self.members - 1 + index
        side = (self.batch // 2) % 2
        parity = self.batch % 2
        other = self.batch + 1 - 2 * parity if index else self.batch + 2 - 4 * side
        source = max(index - 1, 0)
        return pltpu.make_async_remote_copy(
            src_ref=self.result.at[source],
            dst_ref=self.result.at[source + (2 if index else 1)],
            send_sem=self.sems.at[0, which],
            recv_sem=self.sems.at[1, which],
            device_id={"batch": other},
            device_id_type=MESH,
        )

    def start(self):
        total = self.qkv_terms[0].astype(F32)
        for member in range(1, self.members):
            total = total + self.qkv_terms[member].astype(F32)
        self.head_sum[...] = total.astype(BF16)
        self.heads_in[self.me] = self.head_sum[self.me]
        for distance in range(1, self.count):
            self.heads_line(distance).start()

    def own(self):
        for chunk in range(self.chunks):
            here = self.at(chunk)
            total = self.term(self.me, chunk)

            @pl.when(self.me > 0)
            def _():
                self.send(0, self.count - 1 - self.me, chunk).wait_recv()

            @pl.when(self.me < self.count - 1)
            def _():
                self.send(1, self.me, chunk).wait_recv()

            left = self.received[0, jnp.minimum(self.count - 1 - self.me, self.count - 2), here, :]
            right = self.received[1, jnp.minimum(self.me, self.count - 2), here, :]
            total = total + jnp.where(self.me > 0, left.astype(F32), 0.0)
            total = total + jnp.where(self.me < self.count - 1, right.astype(F32), 0.0)
            self.result[0, here, :] = total.astype(BF16)
        self.piece(0).start()
        for distance in range(1, self.count):
            self.heads_line(distance).wait()
        for distance in range(1, self.members):
            self.heads_member(distance).start()
        self.heads_own().start()

    def spread(self):
        self.piece(0).wait()
        self.piece(1).start()
        self.piece(2).start()

    def finish(self):
        for index in range(self.steps):
            message, chunk = index // self.chunks, index % self.chunks

            @pl.when(self.count - 1 - message > self.me)
            def _():
                self.send(0, message, chunk).wait_send()

            @pl.when(message < self.me)
            def _():
                self.send(1, message, chunk).wait_send()

        self.piece(1).wait()
        self.piece(2).wait()
        self.heads_own().wait()
        for distance in range(1, self.members):
            self.heads_member(distance).wait()
        copy = pltpu.make_async_copy(
            self.result, self.gathered, self.sems.at[0, self.used + self.count + self.members + 2]
        )
        copy.start()
        copy.wait()


def return_kernel(
    count,
    chunks,
    lag,
    index_of,
    kinds,
    parts_ref,
    weight_from,
    edge_weight_from,
    x_ref,
    hidden_grad_from,
    gain_ref,
    vectors_ref,
    *rest,
):
    extras = len(kinds)
    sources, rest = rest[:extras], rest[extras:]
    terms_from, qkv_from, rest = rest[:4], rest[4], rest[5:]
    input_ref, sums_ref, total_ref, other_ref, *rest = rest
    targets, rest = rest[:extras], rest[extras:]
    late_out, rest = (rest[:2], rest[2:]) if index_of else (rest[:5], rest[5:])
    weight_ref, edge_weight_ref, hidden_grad_ref, *rest = rest
    weight_terms, rest = rest[:4], rest[4:]
    rows_in, sending, received, edge_in, summed, group, line, load_sems, *rest = rest
    send_sems, recv_sems, pair_send_sems, pair_recv_sems, vector_sems, *extra_sems = rest
    late = extra_sems[extras:]
    extras = [Extra(*each) for each in zip(kinds, sources, targets, extra_sems)]
    me = lax.axis_index("seq")
    place = lax.axis_index("mp")
    rows, width = rows_in.shape
    step = rows // chunks
    steps = (count - 1) * chunks

    def at(chunk):
        return pl.ds(pl.multiple_of(chunk * step, step), step)

    pairs = [(weight_from, weight_ref), (edge_weight_from, edge_weight_ref)]
    pairs += list(zip(terms_from, weight_terms))
    pairs += [(hidden_grad_from, hidden_grad_ref), (x_ref.at[place, pl.ds(index_of * rows, rows)], rows_in)]
    loads = [
        pltpu.make_async_copy(source, target, load_sems.at[which])
        for which, (source, target) in enumerate(pairs)
    ]
    for load in loads:
        load.start()
    vector_sum = VectorSum(group, line, vector_sems)
    vector_sum.greet()
    if index_of == 0:
        vector_sum.start(vectors_ref[...])
    for extra in extras:
        extra.start()

    def send(side, message, chunk):
        return pltpu.make_async_remote_copy(
            src_ref=sending.at[side, message, at(chunk)],
            dst_ref=received.at[side, message, at(chunk)],
            send_sem=send_sems.at[side, message, chunk],
            recv_sem=recv_sems.at[side, message, chunk],
            device_id={"seq": me + 1 - 2 * side},
            device_id_type=MESH,
        )

    def send_edge(side, message, chunk):
        target = (1 - side) * (count - 1 - message) + side * message
        return pltpu.make_async_remote_copy(
            src_ref=parts_ref.at[target, at(chunk)],
            dst_ref=edge_in.at[message, at(chunk)],
            send_sem=send_sems.at[side, message, chunk],
            recv_sem=recv_sems.at[side, message, chunk],
            device_id={"seq": me + 1 - 2 * side},
            device_id_type=MESH,
        )

    def flow(side, index):
        message = index // chunks
        chunk = index % chunks
        target = (1 - side) * (count - 1 - message) + side * message

        @pl.when((target - me) * (1 - 2 * side) > 0)
        def _():
            first = (1 - side) * me + side * (count - 1 - me)

            @pl.when(first == 0)
            def _():
                send_edge(side, message, chunk).start()

            @pl.when(first == 1)
            def _():
                send_edge(side, message, chunk).wait_recv()
                total = dot_nt(parts_ref[target, at(chunk), :], weight_ref[...])
                total = total + dot_nt(edge_in[message, at(chunk), :], edge_weight_ref[...])
                sending[side, message, at(chunk), :] = total.astype(BF16)
                send(side, message, chunk).start()

            @pl.when(first > 1)
            def _():
                total = dot_nt(parts_ref[target, at(chunk), :], weight_ref[...])
                send(side, message, chunk).wait_recv()
                come = received[side, message, at(chunk), :].astype(F32)
                sending[side, message, at(chunk), :] = (total + come).astype(BF16)
                send(side, message, chunk).start()

    if index_of:
        qkv_terms, qkv_sems, *late = late
        trade = Extra("group", qkv_from, qkv_terms, qkv_sems)
        trade.start()
        chain = WeightChain(weight_terms, qkv_terms, *late_out, *late)
        begin = None
    else:
        chain = None
        begin = WeightBegin(weight_terms, late_out[:4], *late[:4])
        projection = ProjectionGrad(qkv_from, parts_ref, late_out[4], *late[4:])
        projection.start()
    ahead = chain.steps if chain else 0
    near = me // (count // 2)

    def pair(chunk):
        return pltpu.make_async_remote_copy(
            src_ref=input_ref.at[at(chunk)],
            dst_ref=other_ref.at[at(chunk)],
            send_sem=pair_send_sems.at[chunk],
            recv_sem=pair_recv_sems.at[chunk],
            device_id={"mp": 1 - place},
            device_id_type=MESH,
        )

    def own(chunk):
        here = at(chunk)
        summed[...] = dot_nt(parts_ref[me, here, :], weight_ref[...])
        for side in range(2):
            first = me if side == 0 else count - 1 - me
            message = count - 1 - me if side == 0 else me

            @pl.when(first == 1)
            def _():
                send_edge(side, message, chunk).wait_recv()
                summed[...] += dot_nt(edge_in[message, here, :], edge_weight_ref[...])

            @pl.when(first > 1)
            def _():
                send(side, message, chunk).wait_recv()
                summed[...] += received[side, message, here, :].astype(F32)

        total = summed[...]
        unit, inverse = row_stats(rows_in[here, :])
        scaled = total * gain_ref[...]
        through = (
            scaled
            - jnp.mean(scaled, axis=-1, keepdims=True)
            - unit * jnp.mean(scaled * unit, axis=-1, keepdims=True)
        )
        input_ref[here, :] = (hidden_grad_ref[here, :] + inverse * through).astype(BF16)
        if index_of:
            pair(chunk).start()
        sums_ref[0:1, :] += jnp.sum(total * unit, axis=0, keepdims=True)
        sums_ref[1:2, :] += jnp.sum(total, axis=0, keepdims=True)

    sums_ref[...] = jnp.zeros_like(sums_ref)
    for load in loads[:2] + (loads[2:6] if index_of else []):
        load.wait()
    wait_for = ahead + ((count - 2) * chunks + lag + 1 if index_of else steps + lag)
    steps_all = ahead + steps

    def flow_of(side, index):
        if chain is not None:

            @pl.when(index < ahead)
            def _():
                chain.flow(side, index)

        @pl.when(index >= ahead)
        def _():
            flow(side, index - ahead)

    def advance(index, _):
        @pl.when(index < steps_all)
        def _():
            flow_of(near, index)

        @pl.when((index >= lag) & (index < steps_all + lag))
        def _():
            flow_of(1 - near, index - lag)

        if begin is not None:
            @pl.when(index == 2)
            def _():
                for load in loads[2:6]:
                    load.wait()
                begin.start()

            @pl.when((index >= 3) & (index < 3 + projection.steps))
            def _():
                projection.multiply(index - 3)

        if chain is not None:

            @pl.when(index == 6)
            def _():
                trade.finish()
                chain.start()

            @pl.when(index == ahead + lag + 2)
            def _():
                chain.own()

            @pl.when(index == ahead + lag + 6)
            def _():
                chain.spread()

        @pl.when(index == wait_for)
        def _():
            for load in loads[-2:]:
                load.wait()

        @pl.when(index >= wait_for)
        def _():
            own(index - wait_for)

        return 0

    lax.fori_loop(0, wait_for + chunks, advance, 0)
    if index_of:
        vector_sum.start(in_rows(sums_ref[0:2, :] + vectors_ref[0:2, :], group.shape[2]))
    vector_sum.middle()

    def finish(index, _):
        message = index // chunks
        chunk = index % chunks

        @pl.when((count - 1 - message > me) & (me > 0))
        def _():
            send(0, message, chunk).wait_send()

        @pl.when((count - 1 - message > me) & (me == 0))
        def _():
            send_edge(0, message, chunk).wait_send()

        @pl.when((message < me) & (me < count - 1))
        def _():
            send(1, message, chunk).wait_send()

        @pl.when((message < me) & (me == count - 1))
        def _():
            send_edge(1, message, chunk).wait_send()

        return 0

    lax.fori_loop(0, steps, finish, 0)

    def finish_pair(chunk, _):
        pair(chunk).wait()
        return 0

    if index_of:
        lax.fori_loop(0, chunks, finish_pair, 0)
    total_ref[...] = vector_sum.finish()
    if chain is not None:
        chain.finish()
    else:
        begin.finish()
        projection.finish()
    for extra in extras:
        extra.finish()


def return_part(
    index, parts, weight, edge_weight, layer_input, hidden_grad, gain, vectors, extras, weight_terms, qkv_from
):
    count, rows, cols = parts.shape
    rows = rows // 2
    width = weight.shape[0]
    chunks = max(1, rows // 128)
    members = lax.axis_size("batch") * lax.axis_size("mp")
    small = (8, 2 * width // 8) if index else vectors.shape
    kinds, sources = [kind for kind, _ in extras], [source for _, source in extras]
    dma = pltpu.SemaphoreType.DMA
    late_in = [*weight_terms]
    if not index:
        keep, _, down, _ = weight_terms
        half = (width, down.shape[1] // 2)
        grouped = (members, count, width // count // members, cols)
        late_out = [keep.shape[1:], keep.shape[1:], half, half, grouped]
        late_scratch = [
            pltpu.VMEM(keep.shape[1:], BF16),
            pltpu.VMEM(keep.shape[1:], BF16),
            pltpu.VMEM(down.shape, BF16),
            dma((6,)),
            pltpu.VMEM((2, rows, width), BF16),
            pltpu.VMEM((width, cols), F32),
            pltpu.VMEM((width, cols), BF16),
            dma((2,)),
            dma((members, count)),
        ]
    else:
        part = (width // count, weight_terms[0].shape[1] + weight_terms[2].shape[1])
        batches = lax.axis_size("batch")
        head = qkv_from.shape[2:]
        late_out = [(batches,) + part, (members, count // 2) + head]
        messages = (2, count - 1) + part
        late_scratch = [
            pltpu.VMEM(qkv_from.shape, BF16),
            dma((2, members)),
            pltpu.VMEM(messages, BF16),
            pltpu.VMEM(messages, BF16),
            pltpu.VMEM((batches,) + part, BF16),
            pltpu.VMEM((count,) + head, BF16),
            pltpu.VMEM((count,) + head, BF16),
            pltpu.SemaphoreType.DMA((2, 4 * (count - 1) + count + members + 3)),
        ]
    any_spec = pl.BlockSpec(memory_space=pl.ANY)
    fixed = lambda step: (0, 0)
    parts_rows = rows if index else 2 * rows
    return pl.pallas_call(
        functools.partial(return_kernel, count, chunks, 2, index, kinds),
        grid=(1,),
        in_specs=[
            pl.BlockSpec((count, parts_rows, cols), lambda step: (0, index, 0)),
            any_spec,
            any_spec,
            any_spec,
            any_spec,
            pl.BlockSpec((1, width), fixed),
            pl.BlockSpec(vectors.shape, fixed),
        ]
        + [any_spec] * (len(extras) + len(late_in) + 1),
        out_specs=[
            pl.BlockSpec((rows, width), fixed),
            pl.BlockSpec((8, width), fixed),
            pl.BlockSpec(small, fixed),
            any_spec,
        ]
        + [any_spec] * (len(extras) + len(late_out)),
        out_shape=[
            jax.ShapeDtypeStruct((rows, width), BF16),
            jax.ShapeDtypeStruct((8, width), F32),
            jax.ShapeDtypeStruct(small, F32),
            jax.ShapeDtypeStruct((rows, width), BF16),
        ]
        + [jax.ShapeDtypeStruct(source.shape, BF16) for source in sources]
        + [jax.ShapeDtypeStruct(shape, BF16) for shape in late_out],
        scratch_shapes=[
            pltpu.VMEM((width, cols), BF16),
            pltpu.VMEM((width, cols), BF16),
            pltpu.VMEM((rows, width), F32),
        ]
        + [pltpu.VMEM(each.shape, BF16) for each in late_in]
        + [
            pltpu.VMEM((rows, width), F32),
            pltpu.VMEM((2, count - 1, rows, width), BF16),
            pltpu.VMEM((2, count - 1, rows, width), BF16),
            pltpu.VMEM((count - 1, rows, cols), BF16),
            pltpu.VMEM((rows // chunks, width), F32),
            pltpu.VMEM((members,) + small, F32),
            pltpu.VMEM((count,) + small, F32),
            dma((4 + len(late_in),)),
            dma((2, count - 1, chunks)),
            dma((2, count - 1, chunks)),
            dma((chunks,)),
            dma((chunks,)),
            dma((2, members + count - 2)),
        ]
        + [dma((2, extra_moves(*extra))) for extra in extras]
        + late_scratch,
        compiler_params=pltpu.CompilerParams(
            collective_id=1 + index, has_side_effects=True, vmem_limit_bytes=VMEM_LIMIT
        ),
        cost_estimate=pl.CostEstimate(flops=80_000_000_000, bytes_accessed=1, transcendentals=0),
    )(parts, weight, edge_weight, layer_input, hidden_grad, gain, vectors, *sources, *late_in, qkv_from)


def weight_grad_kernel(
    tile,
    second_ref,
    grad_ref,
    hidden_ref,
    pre_ref,
    act_ref,
    att_ref,
    trade_source,
    pair_source,
    keep,
    away,
    down_own,
    down_near,
    trade_target,
    pair_target,
    turned,
    slots,
    sending,
    received,
    slot_sems,
    send_sems,
    recv_sems,
    out_sems,
    pair_sems,
    *trade_sems,
):
    rows, width = second_ref.shape
    units = pre_ref.shape[1]
    me = lax.axis_index("batch")
    place = lax.axis_index("mp")
    parity = me % 2
    mate = me + 1 - 2 * parity
    barrier = pltpu.get_barrier_semaphore()
    pl.semaphore_signal(barrier, inc=1, device_id={"batch": mate}, device_id_type=MESH)
    trade = Trade(trade_source, trade_target, *trade_sems, (pair_source, pair_target, pair_sems))
    trade.start(1)

    depth = slots.shape[0]
    piece = units // 4
    head_piece = width // 4
    side = (me // 2) % 2
    jobs = []
    for half, first_sent, first_kept in (
        (0, (1 - parity) * piece, parity * piece),
        (1, 3 * piece, 2 * piece),
    ):
        for target, start in ((away, (1 - side) * tile), (keep, side * tile)):
            puts = [(0, tile, target.at[half], 0)]
            jobs.append((0, pre_ref, tile, first_sent + start, first_kept + start, puts))
    for target, first_sent, first_kept in (
        (down_near, 3 * piece, 2 * piece),
        (down_own, (1 - parity) * piece, parity * piece),
    ):
        for start in range(0, piece, tile):
            puts = [(0, tile, target, start)]
            jobs.append((1, act_ref, tile, first_sent + start, first_kept + start, puts))
    for half, owner in ((0, place), (1, 1 - place)):
        first = 2 * owner * head_piece
        size = head_piece // 2
        puts = [
            (side * size, size, keep.at[half], tile),
            ((1 - side) * size, size, away.at[half], tile),
        ]
        jobs.append(
            (
                2,
                att_ref,
                head_piece,
                first + (1 - parity) * head_piece,
                first + parity * head_piece,
                puts,
            )
        )
    count = len(jobs)
    order = [(job, 3) for job in range(count)] + [(job, 4) for job in range(count)]

    def fetch(index):
        job, which = order[index]
        _, source, size, *_ = jobs[job]
        start = jobs[job][which]
        return pltpu.make_async_copy(
            source.at[:, pl.ds(pl.multiple_of(start, 128), size)],
            slots.at[index % depth, :, pl.ds(0, size)],
            slot_sems.at[index % depth],
        )

    def exchange(job):
        size = jobs[job][2]
        return pltpu.make_async_remote_copy(
            src_ref=sending.at[job, :, pl.ds(0, size)],
            dst_ref=received.at[job, :, pl.ds(0, size)],
            send_sem=send_sems.at[job],
            recv_sem=recv_sems.at[job],
            device_id={"batch": mate},
            device_id_type=MESH,
        )

    def put(job):
        copies = []
        for which, (first, size, target, start) in enumerate(jobs[job][5]):
            from_here = pl.ds(first if isinstance(first, int) else pl.multiple_of(first, 128), size)
            copies.append(
                pltpu.make_async_copy(
                    received.at[job, :, from_here],
                    target.at[:, pl.ds(start, size)],
                    out_sems.at[which, job],
                )
            )
        return copies

    for index in range(depth - 1):
        fetch(index).start()
    block = min(1024, width)
    for matrix, source in enumerate((second_ref, grad_ref, hidden_ref)):

        def turn(index, _):
            here = pl.ds(pl.multiple_of(index * 128, 128), 128)
            turned[matrix, :, here] = source[here, :].T
            return 0

        lax.fori_loop(0, rows // 128, turn, 0)

    for index, (job, which) in enumerate(order):
        matrix, _, size, *_ = jobs[job]
        fetch(index).wait()
        if index + depth - 1 < len(order):
            fetch(index + depth - 1).start()
        if which == 4:
            exchange(job).wait_recv()

        def multiply(part, _):
            here = pl.ds(pl.multiple_of(part * block, block), block)
            total = dot_nn(turned[matrix, here, :], slots[index % depth, :, 0:size])
            if which == 3:
                sending[job, here, 0:size] = total.astype(BF16)
            else:
                total = total + received[job, here, 0:size].astype(F32)
                received[job, here, 0:size] = total.astype(BF16)
            return 0

        lax.fori_loop(0, width // block, multiply, 0)
        if which == 3:
            exchange(job).start()
        else:
            for copy in put(job):
                copy.start()
    for job in range(count):
        exchange(job).wait_send()
        for copy in put(job):
            copy.wait()
    trade.finish()


def weight_grads(second_low, grad_low, hidden_low, pre_grad, activated, attended, source, pair):
    rows, width = second_low.shape
    units = pre_grad.shape[1]
    piece = units // 4
    tile = piece // 2
    jobs = 10
    any_spec = pl.BlockSpec(memory_space=pl.ANY)
    vmem = pl.BlockSpec(memory_space=pltpu.VMEM)
    dma = pltpu.SemaphoreType.DMA
    shapes = [(2, width, tile + width // 8)] * 2 + [(width, piece)] * 2
    return pl.pallas_call(
        functools.partial(weight_grad_kernel, tile),
        in_specs=[vmem] * 3 + [any_spec] * 5,
        out_specs=[any_spec] * 6,
        out_shape=[
            jax.ShapeDtypeStruct(shape, BF16) for shape in shapes + [source.shape, pair.shape]
        ],
        scratch_shapes=[
            pltpu.VMEM((3, width, rows), BF16),
            pltpu.VMEM((3, rows, tile), BF16),
            pltpu.VMEM((jobs, width, tile), BF16),
            pltpu.VMEM((jobs, width, tile), BF16),
            dma((3,)),
            dma((jobs,)),
            dma((jobs,)),
            dma((2, jobs)),
            dma((2,)),
        ]
        + trade_scratch(source.shape[0]),
        compiler_params=pltpu.CompilerParams(
            collective_id=3, has_side_effects=True, vmem_limit_bytes=VMEM_LIMIT
        ),
        cost_estimate=pl.CostEstimate(
            flops=2 * rows * width * (2 * units + width),
            bytes_accessed=4 * rows * units,
            transcendentals=0,
        ),
    )(second_low, grad_low, hidden_low, pre_grad, activated, attended, source, pair)


def swap(value, axis, distance=1):
    size = lax.axis_size(axis)
    return lax.ppermute(value, axis, [(j, j ^ distance) for j in range(size)])


def after(value, *earlier):
    return lax.optimization_barrier((value,) + earlier)[0]


def all_to_all(value):
    return lax.all_to_all(value, "seq", 0, 0, tiled=True)


def halves(value):
    return jnp.split(value, 2, axis=1)


def trade_pieces(value):
    place, count = lax.axis_index("seq"), lax.axis_size("seq")
    pieces = [pick(value, place, count)]
    for distance in range(1, count):
        pairs = [(j, (j + distance) % count) for j in range(count)]
        pieces.append(
            lax.ppermute(pick(value, (place + distance) % count, count), "seq", pairs)
        )
    return pieces


def place_pieces(pieces):
    place, count = lax.axis_index("seq"), len(pieces)
    whole = jnp.concatenate(pieces, axis=0)
    return jnp.roll(whole[::-1], place + 1, axis=0)


def levels_of(axis):
    return [1 << level for level in range(lax.axis_size(axis).bit_length() - 1)]


def gather_small(value):
    place = lax.axis_index("seq")
    count = lax.axis_size("seq")
    parts = [value] + [swap(value, "seq", distance) for distance in range(1, count)]
    stacked = jnp.stack(parts)
    order = jnp.arange(count, dtype=jnp.int32) ^ place
    return jnp.take(stacked, order, axis=0).reshape((-1,) + value.shape[1:])


def pick(value, index, count, axis=0):
    size = value.shape[axis] // count
    return lax.dynamic_slice_in_dim(value, index * size, size, axis)


def fetch_near(weight, axis):
    return swap(pick(weight, lax.axis_index("batch") % 2, 2, axis), "mp")


def narrow_add(mine, received):
    return (mine.astype(F32) + received.astype(F32)).astype(BF16)


def assemble_kernel(unit_cols, pieces, heads, up_ref, down_ref, out_ref, qkv_ref):
    batch = lax.axis_index("batch")
    batches = pieces.shape[0]
    levels = batches.bit_length() - 1
    for index in range(batches):
        source = jnp.bitwise_xor(batch, index // 2 + 2 * (index % 2))
        slot = 0
        for level in range(levels):
            slot = slot + ((source >> level) % 2) * (batches >> (level + 1))
        start = 0
        for size, target, turn in (
            (unit_cols, up_ref, False),
            (pieces.shape[2] - 2 * unit_cols, out_ref, True),
            (unit_cols, down_ref, True),
        ):
            value = pieces[index, :, start : start + size].astype(F32)
            here = pl.ds(pl.multiple_of(slot * size, 128), size)
            if turn:
                target[here, :] = value.T
            else:
                target[:, here] = value
            start = start + size
    members, parts, rows, cols = heads.shape
    cols = cols // 3
    for member in range(members):
        here = slice(member * rows, (member + 1) * rows)
        for matrix in range(3):
            for part in range(parts):
                qkv_ref[matrix, here, part * cols : (part + 1) * cols] = heads[
                    member, part, :, matrix * cols : (matrix + 1) * cols
                ].astype(F32)


def assemble(unit_cols, pieces, heads):
    batches, rows, all_cols = pieces.shape
    out_cols = all_cols - 2 * unit_cols
    shapes = [
        (rows, batches * unit_cols),
        (batches * unit_cols, rows),
        (batches * out_cols, rows),
        (3, heads.shape[0] * heads.shape[2], heads.shape[1] * heads.shape[3] // 3),
    ]
    vmem = pl.BlockSpec(memory_space=pltpu.VMEM)
    return pl.pallas_call(
        functools.partial(assemble_kernel, unit_cols),
        in_specs=[vmem] * 2,
        out_specs=[vmem] * 4,
        out_shape=[jax.ShapeDtypeStruct(shape, F32) for shape in shapes],
        compiler_params=pltpu.CompilerParams(vmem_limit_bytes=VMEM_LIMIT),
    )(pieces, heads)


def place_kernel(own_first, own_second, other_first, other_second, out_ref, low, high, in_sems, out_sems):
    place = lax.axis_index("mp")
    pieces, step = low.shape[0], low.shape[1]
    per = pieces // 4

    def fetch(index):
        source = (own_first, own_second, other_first, other_second)[index // per]
        return pltpu.make_async_copy(
            source.at[pl.ds(index % per * step, step)], low.at[index], in_sems.at[index]
        )

    def put(index):
        which = index // per
        sequence = place if which < 2 else 1 - place
        row = ((which % 2) * per + index % per) * step
        return pltpu.make_async_copy(
            high.at[index], out_ref.at[sequence, pl.ds(row, step)], out_sems.at[index]
        )

    for index in range(pieces):
        fetch(index).start()
    for index in range(pieces):
        fetch(index).wait()
        high[index] = low[index].astype(F32)
        put(index).start()
    for index in range(pieces):
        put(index).wait()


def both_sequences(own, other):
    rows, width = own[0].shape
    step = min(128, rows)
    pieces = 4 * rows // step
    any_spec = pl.BlockSpec(memory_space=pl.ANY)
    return pl.pallas_call(
        place_kernel,
        in_specs=[any_spec] * 4,
        out_specs=any_spec,
        out_shape=jax.ShapeDtypeStruct((2, 2 * rows, width), F32),
        scratch_shapes=[
            pltpu.VMEM((pieces, step, width), BF16),
            pltpu.VMEM((pieces, step, width), F32),
            pltpu.SemaphoreType.DMA((pieces,)),
            pltpu.SemaphoreType.DMA((pieces,)),
        ],
        compiler_params=pltpu.CompilerParams(vmem_limit_bytes=VMEM_LIMIT),
    )(*own, *other)


def local(
    layer_input,
    lengths,
    random_blocks,
    first_gain,
    first_bias,
    qkv_weight,
    out_weight,
    second_gain,
    second_bias,
    up_weight,
    up_bias,
    down_weight,
    down_bias,
    cotangent,
):
    seq_count = lax.axis_size("seq")
    seq_index = lax.axis_index("seq")
    mp_index = lax.axis_index("mp")
    parity = lax.axis_index("batch") % 2
    _, local_rows, width = layer_input.shape
    rows_total = local_rows * seq_count
    blocks = rows_total // BLOCK
    half_cols = qkv_weight.shape[2]
    cols = width // seq_count
    units = up_weight.shape[1]

    doc_ends = jnp.cumsum(lax.dynamic_index_in_dim(lengths, mp_index, 0, keepdims=False))
    randoms = lax.dynamic_index_in_dim(random_blocks, mp_index, 0, keepdims=False)
    randoms = gather_small(randoms)
    lists, admits = block_lists(jnp.arange(blocks, dtype=jnp.int32), randoms, blocks)
    lists, admits = lists.reshape(-1), admits.reshape(-1)

    first_all, qkv, qkv_own, out_other, up_near, bias_near = gather_project(
        layer_input,
        first_gain[None],
        first_bias[None],
        qkv_weight.transpose(1, 0, 2),
        out_weight,
        up_weight,
        up_bias[None],
    )
    bias_near = bias_near[0]
    first_all = first_all.reshape(rows_total, width)
    qkv, lists, down_cut = lax.optimization_barrier(
        (qkv.reshape(rows_total, 3 * cols), lists, down_weight)
    )
    up_far, bias_far = swap(up_near, "batch"), swap(bias_near, "batch")
    down_near = fetch_near(down_cut, 0)
    attended_first, lse_first = attention_forward(0, qkv, doc_ends, lists, admits, seq_count)
    att_pieces = trade_pieces(attended_first)
    attended_second, lse_second = attention_forward(1, qkv, doc_ends, lists, admits, seq_count)
    *att_pieces, attended_second = lax.optimization_barrier((*att_pieces, attended_second))
    att_first = place_pieces(att_pieces)
    att_first, up_far, down_near, bias_far = lax.optimization_barrier(
        (att_first, up_far, down_near, bias_far)
    )
    down_far = swap(down_near, "batch")
    bias_full = jnp.concatenate([up_bias, bias_near, bias_far])[None]
    outs = [part.reshape(seq_count // 2, cols, width) for part in (out_weight, out_other)]
    kept, results = None, []
    att, source, pair = att_first, attended_second, jnp.zeros((8, 128), BF16)
    for index in range(2):
        result = token_part(
            index,
            doc_ends,
            att,
            layer_input,
            cotangent,
            outs,
            (up_weight, up_near, up_far),
            (down_weight, down_near, down_far),
            bias_full,
            second_gain[None],
            second_bias[None],
            down_bias[None],
            source,
            pair,
            kept,
        )
        kept = result[3:9]
        results.append(result[:3] + result[9:])
        att, source, pair = result[11], result[2], result[0]
        other_output = result[12]
    grad_first = att
    activated, pre_grad, second_low, hidden_low, grad_low, attended_low = kept
    sums = results[0][3][:3] + results[1][3][:3]
    unit_sums = results[0][4][0] + results[1][4][0]
    bias_sums = [unit_sums[:units], unit_sums[units : units * 3 // 2], unit_sums[units * 3 // 2 :]]
    keep, away, down_own, down_near, grad_second, other_second = weight_grads(
        second_low, grad_low, hidden_low, pre_grad, activated, attended_low, source, pair
    )
    outputs, other_outputs = [result[0] for result in results], [other_output, other_second]
    bias_other = jnp.where(
        parity == 0,
        jnp.concatenate([bias_sums[1], bias_sums[2]]),
        jnp.concatenate([bias_sums[2], bias_sums[1]]),
    )
    bias_all = jnp.where(
        mp_index == 0,
        jnp.concatenate([bias_sums[0], bias_other]),
        jnp.concatenate([bias_other, bias_sums[0]]),
    )
    qkv_cut, grad_second = lax.optimization_barrier((qkv_own, grad_second))
    qkv_edge = lax.ppermute(qkv_cut, "seq", [(0, 1), (seq_count - 1, seq_count - 2)])

    come, down_come = swap(away, "batch", 2), swap(down_near, "mp")
    qkv_low_grad = attention_backward(
        qkv,
        (attended_first, attended_second),
        (grad_first, grad_second),
        (lse_first, lse_second),
        doc_ends,
        lists,
        admits,
    )
    qkv_low_grad, come, down_come = lax.optimization_barrier((qkv_low_grad, come, down_come))
    parts = qkv_low_grad.reshape(seq_count, local_rows, 3 * cols)
    early = jnp.concatenate([sums, bias_all.reshape(-1, width)], axis=0)
    input_first, first_sums, early, _, *weight_terms, qkv_grouped = return_part(
        0,
        parts,
        qkv_own,
        qkv_edge,
        layer_input,
        results[0][1],
        first_gain[None],
        early.reshape(8, -1),
        [],
        (keep, come, down_own, down_come),
        first_all,
    )
    input_second, _, late, other_second, other_first, weights_back, qkv_back = return_part(
        1,
        parts,
        qkv_own,
        qkv_edge,
        layer_input,
        results[1][1],
        first_gain[None],
        first_sums,
        [("mp", input_first)],
        weight_terms,
        qkv_grouped,
    )
    layer_output = both_sequences(outputs, other_outputs)
    input_grad = both_sequences([input_first, input_second], [other_first, other_second])
    up_grad, down_grad, out_grad, qkv_grad = assemble(units // 4, weights_back, qkv_back)
    early, late = early.reshape(-1), late.reshape(-1)
    up_bias_grad = lax.dynamic_slice_in_dim(early, 3 * width + mp_index * units, units)
    return (
        layer_output,
        input_grad,
        late[:width],
        late[width:],
        qkv_grad.transpose(1, 0, 2),
        out_grad,
        early[width : 2 * width],
        early[2 * width : 3 * width],
        up_grad,
        up_bias_grad,
        down_grad,
        early[:width],
    )


MB = 2
NBLK = 64
LEN = 4096
HIGH = lax.Precision.HIGHEST


def segment_of(places, doc_ends):
    return jnp.sum((places[..., None] >= doc_ends).astype(jnp.int32), axis=-1)


def block_lists_by_index(blocks, randoms):
    leading = randoms.shape[:-1]
    globals_part = jnp.broadcast_to(jnp.arange(GLOB, dtype=jnp.int32), leading + (GLOB,))
    window_part = jnp.broadcast_to(
        blocks[:, None] + jnp.arange(WIN, dtype=jnp.int32) - WIN // 2, leading + (WIN,)
    )
    block_list = jnp.concatenate([globals_part, window_part, randoms], axis=-1)
    inside = (block_list >= 0) & (block_list < NBLK)
    same_entry = block_list[..., :, None] == block_list[..., None, :]
    order_ids = jnp.arange(LIST)
    earlier = order_ids[None, :] < order_ids[:, None]
    repeated = jnp.any(same_entry & earlier, axis=-1)
    return (block_list, inside & jnp.logical_not(repeated))


def fetch_rows(key_rows, values, wanted):
    batch_seqs, local_rows, head_cols = key_rows.shape
    total_rows = local_rows * lax.axis_size("seq")
    empty_rows = jnp.zeros((batch_seqs, wanted.shape[1], head_cols), jnp.bfloat16)
    initial = (empty_rows, empty_rows)
    empty_whole = jnp.zeros((batch_seqs, total_rows, head_cols), jnp.bfloat16)
    initial = initial + (empty_whole, empty_whole)
    shards_in = (
        lax.all_gather(key_rows, "seq", axis=1, tiled=True),
        lax.all_gather(values, "seq", axis=1, tiled=True),
    )
    piece_rows = shards_in[0].shape[1]
    inside = ((wanted >= 0) & (wanted < piece_rows))[..., None]
    take_index = jnp.clip(wanted, 0, piece_rows - 1)[..., None]
    picked = tuple(
        (
            jnp.where(inside, jnp.take_along_axis(source, take_index, axis=1), previous)
            for source, previous in zip(shards_in, initial[:2])
        )
    )
    placed = tuple((source for source in shards_in))
    return picked + placed


def scatter_rows(kv_source):
    return lax.psum_scatter(
        kv_source.astype(jnp.bfloat16), "seq", scatter_dimension=0, tiled=True
    ).astype(jnp.float32)


def global_partial(seq_item):
    query_rows, key_rows, value_rows, keep_mask = seq_item
    head_count = query_rows.shape[1] // HD
    query_heads = query_rows.reshape(query_rows.shape[0], head_count, HD)
    key_heads = key_rows.reshape(key_rows.shape[0], head_count, HD)
    value_heads = value_rows.astype(jnp.float32).reshape(value_rows.shape[0], head_count, HD)
    raw_scores = jnp.einsum(
        "qhd,khd->hqk", query_heads, key_heads, preferred_element_type=jnp.float32
    ) * HD ** (-0.5)
    masked = jnp.where(keep_mask[None], raw_scores, NEG)
    row_top = jnp.max(masked, axis=-1)
    weights = jnp.exp(masked - row_top[..., None]) * keep_mask[None].astype(jnp.float32)
    numer = jnp.einsum("hqk,khd->hqd", weights, value_heads, precision=HIGH)
    return (row_top, jnp.sum(weights, axis=-1), numer)


def global_back(seq_item):
    query_rows, key_rows, value_rows, keep_mask, row_top, row_total, glob_out, glob_grad = seq_item
    row_count, head_cols = query_rows.shape
    head_count = head_cols // HD
    query_heads = query_rows.reshape(row_count, head_count, HD)
    key_heads = key_rows.reshape(key_rows.shape[0], head_count, HD)
    value_heads = value_rows.astype(jnp.float32).reshape(value_rows.shape[0], head_count, HD)
    raw_scores = jnp.einsum(
        "qhd,khd->hqk", query_heads, key_heads, preferred_element_type=jnp.float32
    ) * HD ** (-0.5)
    masked = jnp.where(keep_mask[None], raw_scores, NEG)
    probs_glob = (
        jnp.exp(masked - row_top[..., None])
        * keep_mask[None].astype(jnp.float32)
        / row_total[..., None]
    )
    grad_heads = glob_grad.astype(jnp.float32).reshape(row_count, head_count, HD)
    prob_grad = jnp.einsum("qhd,khd->hqk", grad_heads, value_heads, precision=HIGH)
    delta = jnp.einsum("qhd,hqd->hq", grad_heads, glob_out, precision=HIGH)
    score_grad = (probs_glob * (prob_grad - delta[..., None])).astype(jnp.bfloat16)
    query_grad = jnp.einsum(
        "hqk,khd->qhd", score_grad, key_heads, preferred_element_type=jnp.float32
    ) * HD ** (-0.5)
    key_grad = jnp.einsum(
        "hqk,qhd->khd", score_grad, query_heads, preferred_element_type=jnp.float32
    ) * HD ** (-0.5)
    value_grad = jnp.einsum("hqk,qhd->khd", probs_glob, grad_heads, precision=HIGH)
    return (
        query_grad.reshape(row_count, head_cols),
        key_grad.reshape(-1, head_cols),
        value_grad.reshape(-1, head_cols),
    )


def local_by_blocks(
    layer_input,
    lengths,
    random_blocks,
    first_gain,
    first_bias,
    qkv_weight,
    out_weight,
    second_gain,
    second_bias,
    up_weight,
    up_bias,
    down_weight,
    down_bias,
    cotangent,
):
    seq_index = lax.axis_index("seq")
    local_seqs, local_rows, model_width = layer_input.shape
    blocks_dev = local_rows // BLOCK
    head_cols = qkv_weight.shape[2]
    head_count = head_cols // HD
    unit_cols = up_weight.shape[1]
    score_scale = HD ** (-0.5)
    glob_rows = GLOB * BLOCK
    batch_seqs = local_seqs // MB
    picked_rows = blocks_dev * LIST * BLOCK
    qkv_flat = qkv_weight.reshape(model_width, 3 * head_cols)
    doc_ends = jnp.cumsum(lengths, axis=1)
    places = seq_index * local_rows + jnp.arange(local_rows, dtype=jnp.int32)
    seg_local = segment_of(places[None, :], doc_ends[:, None, :])
    valid_rows = (places[None, :] < doc_ends[:, -1:]).astype(jnp.float32)
    glob_flag = (places < glob_rows)[None, :, None]
    query_blocks = seq_index * blocks_dev + jnp.arange(blocks_dev, dtype=jnp.int32)
    block_list, admitted = block_lists_by_index(query_blocks, random_blocks)
    key_places = block_list[..., None] * BLOCK + jnp.arange(BLOCK, dtype=jnp.int32)
    key_segs = segment_of(key_places, doc_ends[:, None, None, None, :]).reshape(
        local_seqs, blocks_dev, LIST * BLOCK
    )
    admit_keys = jnp.broadcast_to(admitted[..., None], key_places.shape).reshape(
        local_seqs, blocks_dev, LIST * BLOCK
    )
    query_segs = seg_local.reshape(local_seqs, blocks_dev, BLOCK)
    list_mask = admit_keys[:, :, None, :] & (query_segs[..., None] == key_segs[:, :, None, :])
    wanted_all = jnp.clip(key_places, 0, LEN - 1).reshape(local_seqs, picked_rows)
    glob_segs = segment_of(jnp.arange(glob_rows, dtype=jnp.int32)[None, :], doc_ends[:, None, :])
    qkv_total = jnp.zeros((model_width, 3 * head_cols), jnp.float32)
    out_total = jnp.zeros(out_weight.shape, jnp.float32)
    up_total = jnp.zeros(up_weight.shape, jnp.float32)
    down_total = jnp.zeros(down_weight.shape, jnp.float32)
    gain_one_total = jnp.zeros((model_width,), jnp.float32)
    bias_one_total = jnp.zeros((model_width,), jnp.float32)
    gain_two_total = jnp.zeros((model_width,), jnp.float32)
    bias_two_total = jnp.zeros((model_width,), jnp.float32)
    up_bias_total = jnp.zeros((unit_cols,), jnp.float32)
    down_bias_total = jnp.zeros((model_width,), jnp.float32)
    outputs_all = []
    input_grads = []
    for micro_index in range(MB):
        first_seq = micro_index * batch_seqs
        last_seq = first_seq + batch_seqs
        rows_in = layer_input[first_seq:last_seq]
        ends_now = doc_ends[first_seq:last_seq]
        valid_now = valid_rows[first_seq:last_seq]
        mask_now = list_mask[first_seq:last_seq]
        wanted = wanted_all[first_seq:last_seq]
        glob_segs_now = glob_segs[first_seq:last_seq]
        normed_one, inverse_one = norm_stats(rows_in)
        first_low = (
            (normed_one * first_gain + first_bias).astype(jnp.bfloat16).reshape(-1, model_width)
        )
        qkv_rows = (
            jnp.dot(first_low, qkv_flat, preferred_element_type=jnp.float32)
            .astype(jnp.bfloat16)
            .reshape(batch_seqs, local_rows, 3, head_cols)
        )
        queries = qkv_rows[:, :, 0]
        key_rows = qkv_rows[:, :, 1]
        values = qkv_rows[:, :, 2]
        glob_queries_own = queries[:, :glob_rows]
        picked_keys, picked_values, whole_keys, whole_values = fetch_rows(key_rows, values, wanted)
        glob_queries = glob_queries_own
        seg_whole = segment_of(jnp.arange(LEN, dtype=jnp.int32)[None, :], ends_now[:, None, :])
        glob_mask = glob_segs_now[:, :, None] == seg_whole[:, None, :]

        def global_here():
            return lax.map(global_partial, (glob_queries, whole_keys, whole_values, glob_mask))

        def global_skip():
            return (
                jnp.zeros((batch_seqs, head_count, glob_rows), jnp.float32),
                jnp.ones((batch_seqs, head_count, glob_rows), jnp.float32),
                jnp.zeros((batch_seqs, head_count, glob_rows, HD), jnp.float32),
            )

        glob_top, glob_total, glob_numer = lax.cond(seq_index == 0, global_here, global_skip)
        glob_out = glob_numer / glob_total[..., None]
        query_split = queries.reshape(batch_seqs, blocks_dev, BLOCK, head_count, HD)
        key_split = picked_keys.reshape(batch_seqs, blocks_dev, LIST * BLOCK, head_count, HD)
        value_split = picked_values.reshape(batch_seqs, blocks_dev, LIST * BLOCK, head_count, HD)
        raw_scores = (
            jnp.einsum(
                "sbqhd,sbkhd->sbhqk", query_split, key_split, preferred_element_type=jnp.float32
            )
            * score_scale
        )
        keep_now = mask_now[:, :, None]
        masked = jnp.where(keep_now, raw_scores, NEG)
        row_top = jnp.max(masked, axis=-1, keepdims=True)
        weights = jnp.exp(masked - row_top) * keep_now.astype(jnp.float32)
        row_total = jnp.sum(weights, axis=-1, keepdims=True)
        probs_list = weights / row_total
        probs_low = probs_list.astype(jnp.bfloat16)
        listed = jnp.einsum(
            "sbhqk,sbkhd->sbqhd", probs_low, value_split, preferred_element_type=jnp.float32
        ).reshape(batch_seqs, local_rows, head_cols)
        glob_rows_out = jnp.transpose(glob_out, (0, 2, 1, 3)).reshape(
            batch_seqs, glob_rows, head_cols
        )
        glob_full = jnp.pad(glob_rows_out, ((0, 0), (0, local_rows - glob_rows), (0, 0)))
        attended = jnp.where(glob_flag, glob_full, listed) * valid_now[..., None]
        attended_low = attended.astype(jnp.bfloat16).reshape(-1, head_cols)
        branch = lax.psum(
            jnp.dot(attended_low, out_weight, preferred_element_type=jnp.float32).astype(
                jnp.bfloat16
            ),
            "mp",
        ).astype(jnp.float32)
        hidden = rows_in + branch.reshape(rows_in.shape)
        normed_two, inverse_two = norm_stats(hidden)
        second_low = (
            (normed_two * second_gain + second_bias).astype(jnp.bfloat16).reshape(-1, model_width)
        )
        pre_act = jnp.dot(second_low, up_weight, preferred_element_type=jnp.float32) + up_bias
        activated = jax.nn.gelu(pre_act, approximate=True).astype(jnp.bfloat16)
        ffn_branch = lax.psum(
            jnp.dot(activated, down_weight, preferred_element_type=jnp.float32).astype(
                jnp.bfloat16
            ),
            "mp",
        ).astype(jnp.float32)
        outputs_all.append(hidden + ffn_branch.reshape(rows_in.shape) + down_bias)
        grad_rows = cotangent[first_seq:last_seq].reshape(-1, model_width)
        down_bias_total = down_bias_total + jnp.sum(grad_rows, axis=0)
        grad_low = grad_rows.astype(jnp.bfloat16)
        down_total = down_total + jnp.einsum(
            "rf,rd->fd", activated, grad_low, preferred_element_type=jnp.float32
        )
        act_grad = jnp.einsum(
            "rd,fd->rf", grad_low, down_weight, preferred_element_type=jnp.float32
        )
        _, gelu_pull = jax.vjp(lambda inner: jax.nn.gelu(inner, approximate=True), pre_act)
        pre_grad = gelu_pull(act_grad)[0].astype(jnp.bfloat16)
        up_bias_total = up_bias_total + jnp.sum(pre_grad.astype(jnp.float32), axis=0)
        up_total = up_total + jnp.einsum(
            "rd,rf->df", second_low, pre_grad, preferred_element_type=jnp.float32
        )
        second_grad = (
            lax.psum(
                jnp.einsum(
                    "rf,df->rd", pre_grad, up_weight, preferred_element_type=jnp.float32
                ).astype(jnp.bfloat16),
                "mp",
            )
            .astype(jnp.float32)
            .reshape(rows_in.shape)
        )
        gain_two_total = gain_two_total + jnp.sum(second_grad * normed_two, axis=(0, 1))
        bias_two_total = bias_two_total + jnp.sum(second_grad, axis=(0, 1))
        hidden_grad = grad_rows.reshape(rows_in.shape) + norm_back(
            second_grad, normed_two, inverse_two, second_gain
        )
        hidden_low = hidden_grad.astype(jnp.bfloat16).reshape(-1, model_width)
        out_total = out_total + jnp.einsum(
            "rc,rd->cd", attended_low, hidden_low, preferred_element_type=jnp.float32
        )
        attended_grad = jnp.einsum(
            "rd,cd->rc", hidden_low, out_weight, preferred_element_type=jnp.float32
        ).astype(jnp.bfloat16).reshape(batch_seqs, local_rows, head_cols) * valid_now[
            ..., None
        ].astype(
            jnp.bfloat16
        )
        list_grad = jnp.where(glob_flag, jnp.zeros_like(attended_grad), attended_grad).reshape(
            batch_seqs, blocks_dev, BLOCK, head_count, HD
        )
        prob_grad = jnp.einsum(
            "sbqhd,sbkhd->sbhqk", list_grad, value_split, preferred_element_type=jnp.float32
        )
        delta = jnp.sum(probs_list * prob_grad, axis=-1, keepdims=True)
        score_grad = (probs_list * (prob_grad - delta)).astype(jnp.bfloat16)
        query_grad = (
            jnp.einsum(
                "sbhqk,sbkhd->sbqhd", score_grad, key_split, preferred_element_type=jnp.float32
            )
            * score_scale
        ).reshape(batch_seqs, local_rows, head_cols)
        key_picked_grad = (
            jnp.einsum(
                "sbhqk,sbqhd->sbkhd", score_grad, query_split, preferred_element_type=jnp.float32
            )
            * score_scale
        )
        value_picked_grad = jnp.einsum(
            "sbhqk,sbqhd->sbkhd", probs_low, list_grad, preferred_element_type=jnp.float32
        )
        picked_grads = jnp.concatenate(
            [
                key_picked_grad.reshape(batch_seqs, picked_rows, head_cols),
                value_picked_grad.reshape(batch_seqs, picked_rows, head_cols),
            ],
            axis=-1,
        )
        seg_ids = wanted * batch_seqs + jnp.arange(batch_seqs, dtype=jnp.int32)[:, None]
        kv_term = jax.ops.segment_sum(
            picked_grads.reshape(batch_seqs * picked_rows, 2 * head_cols),
            seg_ids.reshape(-1),
            num_segments=LEN * batch_seqs,
        ).reshape(LEN, batch_seqs, 2 * head_cols)
        glob_grad_own = attended_grad[:, :glob_rows]

        def back_here():
            return lax.map(
                global_back,
                (
                    glob_queries,
                    whole_keys,
                    whole_values,
                    glob_mask,
                    glob_top,
                    glob_total,
                    glob_out,
                    glob_grad_own,
                ),
            )

        def back_skip():
            return (
                jnp.zeros((batch_seqs, glob_rows, head_cols), jnp.float32),
                jnp.zeros((batch_seqs, LEN, head_cols), jnp.float32),
                jnp.zeros((batch_seqs, LEN, head_cols), jnp.float32),
            )

        glob_query_grad, whole_key_grad, whole_value_grad = lax.cond(
            seq_index == 0, back_here, back_skip
        )
        glob_dense = jnp.transpose(
            jnp.concatenate([whole_key_grad, whole_value_grad], axis=-1), (1, 0, 2)
        )
        kv_source = kv_term + glob_dense
        kv_grad = jnp.transpose(scatter_rows(kv_source), (1, 0, 2))
        glob_query_full = jnp.pad(glob_query_grad, ((0, 0), (0, local_rows - glob_rows), (0, 0)))
        query_total = query_grad + jnp.where(glob_flag, glob_query_full, 0.0)
        qkv_low_grad = (
            jnp.stack([query_total, kv_grad[..., :head_cols], kv_grad[..., head_cols:]], axis=2)
            .astype(jnp.bfloat16)
            .reshape(-1, 3 * head_cols)
        )
        qkv_total = qkv_total + jnp.einsum(
            "rd,rc->dc", first_low, qkv_low_grad, preferred_element_type=jnp.float32
        )
        first_grad = (
            lax.psum(
                jnp.einsum(
                    "rc,dc->rd", qkv_low_grad, qkv_flat, preferred_element_type=jnp.float32
                ).astype(jnp.bfloat16),
                "mp",
            )
            .astype(jnp.float32)
            .reshape(rows_in.shape)
        )
        gain_one_total = gain_one_total + jnp.sum(first_grad * normed_one, axis=(0, 1))
        bias_one_total = bias_one_total + jnp.sum(first_grad, axis=(0, 1))
        input_grads.append(hidden_grad + norm_back(first_grad, normed_one, inverse_one, first_gain))
    matrix_grads = (
        lax.psum_scatter(
            qkv_total.reshape(model_width, 3, head_cols).astype(jnp.bfloat16),
            "seq",
            scatter_dimension=0,
            tiled=True,
        ).astype(jnp.float32),
        lax.psum_scatter(
            out_total.astype(jnp.bfloat16), "seq", scatter_dimension=1, tiled=True
        ).astype(jnp.float32),
        lax.psum_scatter(
            up_total.astype(jnp.bfloat16), "seq", scatter_dimension=0, tiled=True
        ).astype(jnp.float32),
        lax.psum_scatter(
            down_total.astype(jnp.bfloat16), "seq", scatter_dimension=1, tiled=True
        ).astype(jnp.float32),
    )
    matrix_grads = (
        lax.psum(matrix_grads[0].astype(jnp.bfloat16), "batch").astype(jnp.float32),
        lax.psum(matrix_grads[1].astype(jnp.bfloat16), "batch").astype(jnp.float32),
        lax.psum(matrix_grads[2].astype(jnp.bfloat16), "batch").astype(jnp.float32),
        lax.psum(matrix_grads[3].astype(jnp.bfloat16), "batch").astype(jnp.float32),
    )
    vector_grads = lax.psum(
        (
            gain_one_total,
            bias_one_total,
            gain_two_total,
            bias_two_total,
            up_bias_total,
            down_bias_total,
        ),
        ("seq", "batch"),
    )
    return (
        jnp.concatenate(outputs_all, axis=0),
        jnp.concatenate(input_grads, axis=0),
        vector_grads[0],
        vector_grads[1],
        matrix_grads[0],
        matrix_grads[1],
        vector_grads[2],
        vector_grads[3],
        matrix_grads[2],
        vector_grads[4],
        matrix_grads[3],
        vector_grads[5],
    )


def solution(mesh):
    placed = (
        P("batch", "seq", None),
        P("batch", None),
        P("batch", "seq", None),
        P(),
        P(),
        P(None, None, "mp"),
        P("mp", None),
        P(),
        P(),
        P(None, "mp"),
        P("mp"),
        P("mp", None),
        P(),
        P("batch", "seq", None),
    )
    sizes = mesh.shape
    by_heads = sizes["seq"] in (4, 8) and sizes["batch"] == 4 and sizes["mp"] == 2
    return jax.shard_map(
        local if by_heads else local_by_blocks,
        mesh=mesh,
        in_specs=placed,
        out_specs=(
            P("batch", "seq", None),
            P("batch", "seq", None),
            P(),
            P(),
            P("seq", None, "mp"),
            P("mp", "seq"),
            P(),
            P(),
            P("seq", "mp"),
            P("mp"),
            P("mp", "seq"),
            P(),
        ),
        check_vma=False,
    )
```

```python
import functools

import jax
import jax.numpy as jnp
from jax import lax
from jax.experimental import pallas as pl
from jax.experimental.pallas import tpu as pltpu
from jax.sharding import PartitionSpec as P

BLOCK = 64
GLOB = 2
WIN = 3
HD = 64
LIST = 8

NEG = -1e30
EPS = 1e-05
F32 = jnp.float32
BF16 = jnp.bfloat16
VMEM_LIMIT = 60 * 1024 * 1024


def norm_stats(rows):
    centre = rows - jnp.mean(rows, axis=-1, keepdims=True)
    spread = jnp.mean(centre * centre, axis=-1, keepdims=True)
    inverse = lax.rsqrt(spread + EPS)
    return (centre * inverse, inverse)


def norm_back(grad_out, normed, inverse, gain):
    scaled = grad_out * gain
    return inverse * (
        scaled
        - jnp.mean(scaled, axis=-1, keepdims=True)
        - normed * jnp.mean(scaled * normed, axis=-1, keepdims=True)
    )


def block_lists(blocks, randoms, block_count):
    leading = randoms.shape[:-1]
    globals_part = jnp.broadcast_to(jnp.arange(GLOB, dtype=jnp.int32), leading + (GLOB,))
    window_part = jnp.broadcast_to(
        blocks[:, None] + jnp.arange(WIN, dtype=jnp.int32) - WIN // 2, leading + (WIN,)
    )
    block_list = jnp.concatenate([globals_part, window_part, randoms], axis=-1)
    inside = (block_list >= 0) & (block_list < block_count)
    same_entry = block_list[..., :, None] == block_list[..., None, :]
    order_ids = jnp.arange(LIST)
    earlier = order_ids[None, :] < order_ids[:, None]
    repeated = jnp.any(same_entry & earlier, axis=-1)
    admitted = inside & jnp.logical_not(repeated)
    return (jnp.clip(block_list, 0, block_count - 1), admitted.astype(jnp.int32))


MESH = pl.DeviceIdType.MESH


class Trade:
    def __init__(self, source, target, send_sems, recv_sems, own_sem, pair=None):
        self.source, self.target, self.pair = source, target, pair
        self.send_sems, self.recv_sems, self.own_sem = send_sems, recv_sems, own_sem
        self.count = source.shape[0]
        self.me = lax.axis_index("seq")

    def greet(self):
        barrier = pltpu.get_barrier_semaphore()
        for distance in range(1, self.count):
            other = lax.rem(self.me + distance, self.count)
            pl.semaphore_signal(barrier, inc=1, device_id={"seq": other}, device_id_type=MESH)
        if self.pair is not None:
            partner = 1 - lax.axis_index("mp")
            pl.semaphore_signal(barrier, inc=1, device_id={"mp": partner}, device_id_type=MESH)

    def copy(self, distance):
        other = lax.rem(self.me + distance, self.count)
        return pltpu.make_async_remote_copy(
            src_ref=self.source.at[other],
            dst_ref=self.target.at[self.me],
            send_sem=self.send_sems.at[distance - 1],
            recv_sem=self.recv_sems.at[distance - 1],
            device_id={"seq": other},
            device_id_type=MESH,
        )

    def pair_copy(self):
        source, target, sems = self.pair
        return pltpu.make_async_remote_copy(
            src_ref=source,
            dst_ref=target,
            send_sem=sems.at[0],
            recv_sem=sems.at[1],
            device_id={"mp": 1 - lax.axis_index("mp")},
            device_id_type=MESH,
        )

    def own(self):
        return pltpu.make_async_copy(
            self.source.at[self.me], self.target.at[self.me], self.own_sem.at[0]
        )

    def start(self, others=0):
        others = others + (self.pair is not None)
        pl.semaphore_wait(pltpu.get_barrier_semaphore(), self.count - 1 + others)
        for distance in range(1, self.count):
            self.copy(distance).start()
        if self.pair is not None:
            self.pair_copy().start()
        self.own().start()

    def finish(self):
        for distance in range(1, self.count):
            self.copy(distance).wait()
        if self.pair is not None:
            self.pair_copy().wait()
        self.own().wait()


def trade_scratch(count):
    dma = pltpu.SemaphoreType.DMA
    return [dma((count - 1,)), dma((count - 1,)), dma((1,))]


def segment_at(places, ends_ref):
    total = jnp.zeros(places.shape, jnp.int32)
    for doc in range(ends_ref.shape[0]):
        total = total + (places >= ends_ref[doc]).astype(jnp.int32)
    return total


def head_spread(rows, heads):
    lane_head = lax.broadcasted_iota(jnp.int32, (1, rows.shape[1]), 1) // HD
    return jnp.concatenate(
        [rows * (lane_head == head).astype(F32).astype(rows.dtype) for head in range(heads)], axis=0
    )


def head_fold(wide, heads):
    rows = wide.shape[0] // heads
    lane_head = lax.broadcasted_iota(jnp.int32, (rows, wide.shape[1]), 1) // HD
    folded = jnp.zeros((rows, wide.shape[1]), wide.dtype)
    for head in range(heads):
        folded = jnp.where(lane_head == head, wide[head * rows : (head + 1) * rows], folded)
    return folded


def block_at(block):
    return pl.ds(pl.multiple_of(block * BLOCK, BLOCK), BLOCK)


def fill_segments(token_segs, ends_ref):
    def fill(block, _):
        places = block * BLOCK + lax.broadcasted_iota(jnp.int32, (BLOCK, token_segs.shape[1]), 0)
        token_segs[block_at(block), :] = segment_at(places, ends_ref)
        return 0

    lax.fori_loop(0, token_segs.shape[0] // BLOCK, fill, 0)


def query_segments(block, heads, ends_ref):
    lanes = lax.broadcasted_iota(jnp.int32, (8, heads * BLOCK), 1)
    return segment_at(block * BLOCK + lanes % BLOCK, ends_ref)[0:1]


def key_segments(starts, keeps, ends_ref):
    lanes = lax.broadcasted_iota(jnp.int32, (8, 2 * BLOCK), 1)
    first = lanes < BLOCK
    pieces = []
    for entry in range(0, LIST, 2):
        places = lanes + jnp.where(
            first, starts[entry] * BLOCK, (starts[entry + 1] - 1) * BLOCK
        )
        keep = jnp.where(first, keeps[entry], keeps[entry + 1]) > 0
        pieces.append(jnp.where(keep, segment_at(places, ends_ref), -1))
    return jnp.concatenate(pieces, axis=1)[0:1]


def gathered(ref, starts):
    return jnp.concatenate([ref[block_at(start), :] for start in starts], axis=0)


def block_parts(wide):
    return [wide[start : start + BLOCK] for start in range(0, wide.shape[0], BLOCK)]


def dot_nt(left, right):
    return lax.dot_general(left, right, (((1,), (1,)), ((), ())), preferred_element_type=F32)


def dot_tn(left, right):
    return lax.dot_general(left, right, (((0,), (0,)), ((), ())), preferred_element_type=F32)


def dot_nn(left, right):
    return lax.dot_general(left, right, (((1,), (0,)), ((), ())), preferred_element_type=F32)


def as_row(tall):
    count = tall.shape[0]
    row_ids = lax.broadcasted_iota(jnp.int32, (count, count), 0)
    lane_ids = lax.broadcasted_iota(jnp.int32, (count, count), 1)
    return jnp.sum(jnp.where(row_ids == lane_ids, tall, 0.0), axis=0, keepdims=True)


def together(running):
    while running:
        still = []
        for each in running:
            if next(each, 0) is None:
                still.append(each)
        running = still


def unit_block(unit, half, parts, rows_total):
    per = rows_total // parts // BLOCK // 2
    part = unit // per
    inside = unit - part * per
    return part, inside, part * 2 * per + half * per + inside


def forward_kernel(heads, half, ends_ref, lists_ref, admit_ref, q_ref, k_ref, v_ref, *rest):
    o_ref, lse_ref, token_segs, *held = rest
    held = held[0] if held else None
    scale = HD ** (-0.5)
    rows_total = q_ref.shape[0]
    units = o_ref.shape[0] * o_ref.shape[1] // BLOCK
    first_unit = GLOB if half == 0 else 0
    chunk = LIST * BLOCK
    fill_segments(token_segs, ends_ref)

    def store(unit, wide, top, total):
        part, inside, block = unit_block(unit, half, o_ref.shape[0], rows_total)
        out = head_fold(wide, heads)
        places = block * BLOCK + lax.broadcasted_iota(jnp.int32, out.shape, 0)
        out = jnp.where(places < ends_ref[ends_ref.shape[0] - 1], out, 0.0)
        o_ref[part, block_at(inside), :] = out.astype(BF16)
        lse_ref[unit] = jnp.broadcast_to(as_row(top + jnp.log(total)), lse_ref.shape[1:])

    def kept(block, key_segs):
        own = token_segs[block_at(block), :]
        return jnp.concatenate([own] * (chunk // own.shape[1]), axis=1) == key_segs

    def global_blocks():
        query_wide = jnp.concatenate(
            [head_spread(q_ref[block_at(block), :] * scale, heads) for block in range(GLOB)], axis=0
        )
        wide_rows = GLOB * heads * BLOCK

        def score(part, top):
            here = pl.ds(pl.multiple_of(part * chunk, chunk), chunk)
            places = part * chunk + lax.broadcasted_iota(jnp.int32, (8, chunk), 1)
            key_segs = segment_at(places, ends_ref)[0:1]
            keeps = [kept(block, key_segs) for block in range(GLOB)]
            scores = dot_nt(query_wide, k_ref[here, :])
            tops = []
            for place, rows in enumerate(block_parts(scores)):
                rows = jnp.where(keeps[place // heads], rows, NEG)
                held[place * BLOCK : (place + 1) * BLOCK, here] = rows
                tops.append(jnp.max(rows, axis=1, keepdims=True))
            return jnp.maximum(top, jnp.concatenate(tops, axis=0))

        top = lax.fori_loop(0, rows_total // chunk, score, jnp.full((wide_rows, 1), NEG, F32))

        def gather(part, carried):
            total, wide = carried
            here = pl.ds(pl.multiple_of(part * chunk, chunk), chunk)
            totals, weights = [], []
            for place, part_top in enumerate(block_parts(top)):
                weight = jnp.exp(held[place * BLOCK : (place + 1) * BLOCK, here] - part_top)
                totals.append(jnp.sum(weight, axis=1, keepdims=True))
                weights.append(weight.astype(BF16))
            wide = wide + dot_nn(jnp.concatenate(weights, axis=0), v_ref[here, :])
            return total + jnp.concatenate(totals, axis=0), wide

        total, wide = lax.fori_loop(
            0,
            rows_total // chunk,
            gather,
            (jnp.zeros((wide_rows, 1), F32), jnp.zeros((wide_rows, q_ref.shape[1]), F32)),
        )
        wide = wide * (1.0 / total)
        for block in range(GLOB):
            own = slice(block * heads * BLOCK, (block + 1) * heads * BLOCK)
            store(block, wide[own], top[own], total[own])

    if half == 0:
        global_blocks()

    def listed_block(unit):
        _, _, block = unit_block(unit, half, o_ref.shape[0], rows_total)
        query_wide = head_spread(q_ref[block_at(block), :] * scale, heads)
        starts = [lists_ref[block * LIST + entry] for entry in range(LIST)]
        keeps = [admit_ref[block * LIST + entry] for entry in range(LIST)]
        keep = kept(block, key_segments(starts, keeps, ends_ref))
        scores = dot_nt(query_wide, gathered(k_ref, starts))
        yield
        tops, totals, probs = [], [], []
        for rows in block_parts(scores):
            rows = jnp.where(keep, rows, NEG)
            top = jnp.max(rows, axis=1, keepdims=True)
            weights = jnp.exp(rows - top)
            total = jnp.sum(weights, axis=1, keepdims=True)
            probs.append((weights * (1.0 / total)).astype(BF16))
            tops.append(top)
            totals.append(total)
            yield
        wide = dot_nn(jnp.concatenate(probs, axis=0), gathered(v_ref, starts))
        store(unit, wide, jnp.concatenate(tops, axis=0), jnp.concatenate(totals, axis=0))

    def listed_group(group, _):
        together([listed_block(first_unit + 4 * group + place) for place in range(4)])
        return 0

    lax.fori_loop(0, (units - first_unit) // 4, listed_group, 0)
    together([listed_block(units - 1 - place) for place in range((units - first_unit) % 4)])


def backward_kernel(
    heads,
    ends_ref,
    lists_ref,
    admit_ref,
    q_ref,
    k_ref,
    v_ref,
    o_first,
    o_second,
    do_first,
    do_second,
    lse_first,
    lse_second,
    out_ref,
    token_segs,
    dk_ref,
    dv_ref,
    dq_ref,
):
    scale = HD ** (-0.5)
    rows_total, cols = q_ref.shape
    blocks = rows_total // BLOCK
    pair_rows = 2 * BLOCK
    fill_segments(token_segs, ends_ref)

    def prepare(pair, _):
        here = pl.ds(pl.multiple_of(pair * pair_rows, pair_rows), pair_rows)
        dk_ref[here, :] = jnp.zeros((pair_rows, cols), F32)
        dv_ref[here, :] = jnp.zeros((pair_rows, cols), F32)
        return 0

    lax.fori_loop(0, blocks // 2, prepare, 0)

    parts = o_first.shape[0]
    halves_of = ((o_first, do_first, lse_first), (o_second, do_second, lse_second))

    def query_side(unit, half):
        o_ref, do_ref, lse_ref = halves_of[half]
        part, inside, block = unit_block(unit, half, parts, rows_total)
        query_wide = head_spread(q_ref[block_at(block), :] * scale, heads)
        grad_rows = do_ref[part, block_at(inside), :]
        grad_wide = head_spread(grad_rows, heads)
        product = grad_rows.astype(F32) * o_ref[part, block_at(inside), :].astype(F32)
        spread = head_spread(product.astype(BF16), heads)
        delta = dot_nt(jnp.ones((8, cols), BF16), spread)[0:1]
        seg_row = query_segments(block, heads, ends_ref)
        return query_wide, grad_wide, delta, lse_ref[unit, 0:1], seg_row

    def unit(starts, keeps, query_wide, grad_wide, delta, lse, seg_row, finish_query):
        keys = gathered(k_ref, starts)
        scores = block_parts(dot_nt(keys, query_wide))
        prob_grads = block_parts(dot_nt(gathered(v_ref, starts), grad_wide))
        yield
        probs, score_grads = [], []
        for entry in range(LIST):
            wanted = seg_row if keeps is None else jnp.where(keeps[entry] > 0, seg_row, -1)
            own = token_segs[block_at(starts[entry]), :]
            keep = jnp.concatenate([own] * (seg_row.shape[1] // own.shape[1]), axis=1) == wanted
            prob = jnp.exp(jnp.where(keep, scores[entry], NEG) - lse)
            probs.append(prob.astype(BF16))
            score_grads.append((prob * (prob_grads[entry] - delta)).astype(BF16))
            if entry % 2:
                yield
        score_grad = jnp.concatenate(score_grads, axis=0)
        finish_query(dot_tn(score_grad, keys))
        dk = dot_nn(score_grad, query_wide)
        dv = dot_nn(jnp.concatenate(probs, axis=0), grad_wide)
        yield
        for entry in range(LIST):
            here = block_at(starts[entry])
            dk_ref[here, :] += dk[entry * BLOCK : (entry + 1) * BLOCK]
            dv_ref[here, :] += dv[entry * BLOCK : (entry + 1) * BLOCK]
        yield

    def store_query(block, wide):
        out_ref[block_at(block), 0:cols] = (head_fold(wide, heads) * scale).astype(BF16)

    def global_blocks():
        sides = [query_side(block, 0) for block in range(GLOB)]
        side = [jnp.concatenate(both, axis=axis) for both, axis in zip(zip(*sides), (0, 0, 1, 1, 1))]
        dq_ref[...] = jnp.zeros_like(dq_ref)

        def part_of(part, _):
            def add_query(wide):
                dq_ref[...] += wide

            together([unit([part * LIST + entry for entry in range(LIST)], None, *side, add_query)])
            return 0

        lax.fori_loop(0, blocks // LIST, part_of, 0)
        for block in range(GLOB):
            store_query(block, dq_ref[block * heads * BLOCK : (block + 1) * heads * BLOCK])

    global_blocks()

    def listed_block(place, half):
        _, _, block = unit_block(place, half, parts, rows_total)
        starts = [lists_ref[block * LIST + entry] for entry in range(LIST)]
        keeps = [admit_ref[block * LIST + entry] for entry in range(LIST)]
        return unit(
            starts, keeps, *query_side(place, half), functools.partial(store_query, block)
        )

    for half, first_unit in ((0, GLOB), (1, 0)):
        units = blocks // 2

        def listed_group(group, _):
            together([listed_block(first_unit + 4 * group + place, half) for place in range(4)])
            return 0

        lax.fori_loop(0, (units - first_unit) // 4, listed_group, 0)
        together([listed_block(units - 1 - place, half) for place in range((units - first_unit) % 4)])

    def finish(block, _):
        here = block_at(block)
        out_ref[here, cols : 2 * cols] = dk_ref[here, :].astype(BF16)
        out_ref[here, 2 * cols : 3 * cols] = dv_ref[here, :].astype(BF16)
        return 0

    lax.fori_loop(0, blocks, finish, 0)


def smem():
    return pl.BlockSpec(memory_space=pltpu.SMEM)


def column(rows, cols, index):
    return pl.BlockSpec((rows, cols), lambda step: (0, index))


def attention_forward(half, qkv, doc_ends, lists, admits, parts):
    rows = qkv.shape[0]
    cols = qkv.shape[1] // 3
    heads = cols // HD
    blocks = rows // BLOCK
    out = jax.ShapeDtypeStruct((parts, rows // parts // 2, cols), BF16)
    lse = jax.ShapeDtypeStruct((blocks // 2, 8, heads * BLOCK), F32)
    cube = lambda step: (0, 0, 0)
    return pl.pallas_call(
        functools.partial(forward_kernel, heads, half),
        grid=(1,),
        in_specs=[smem(), smem(), smem()] + [column(rows, cols, part) for part in range(3)],
        out_specs=[pl.BlockSpec(out.shape, cube), pl.BlockSpec(lse.shape, cube)],
        out_shape=[out, lse],
        scratch_shapes=[pltpu.VMEM((rows, 2 * BLOCK), jnp.int32)]
        + ([] if half else [pltpu.VMEM((GLOB * heads * BLOCK, rows), F32)]),
        compiler_params=pltpu.CompilerParams(vmem_limit_bytes=VMEM_LIMIT),
        cost_estimate=pl.CostEstimate(
            flops=rows * LIST * BLOCK * cols * heads * 5,
            bytes_accessed=8 * rows * cols,
            transcendentals=0,
        ),
    )(doc_ends, lists, admits, qkv, qkv, qkv)


def attention_backward(qkv, attended, attended_grad, lse, doc_ends, lists, admits):
    rows = qkv.shape[0]
    cols = qkv.shape[1] // 3
    heads = cols // HD
    cube = lambda step: (0, 0, 0)
    return pl.pallas_call(
        functools.partial(backward_kernel, heads),
        grid=(1,),
        in_specs=[smem(), smem(), smem()]
        + [column(rows, cols, part) for part in range(3)]
        + [pl.BlockSpec(part.shape, cube) for part in (*attended, *attended_grad, *lse)],
        out_specs=column(rows, 3 * cols, 0),
        out_shape=jax.ShapeDtypeStruct((rows, 3 * cols), BF16),
        scratch_shapes=[
            pltpu.VMEM((rows, 2 * BLOCK), jnp.int32),
            pltpu.VMEM((rows, cols), F32),
            pltpu.VMEM((rows, cols), F32),
            pltpu.VMEM((GLOB * heads * BLOCK, cols), F32),
        ],
        compiler_params=pltpu.CompilerParams(vmem_limit_bytes=VMEM_LIMIT),
        cost_estimate=pl.CostEstimate(
            flops=rows * LIST * BLOCK * cols * heads * 15,
            bytes_accessed=20 * rows * cols,
            transcendentals=0,
        ),
    )(doc_ends, lists, admits, qkv, qkv, qkv, *attended, *attended_grad, *lse)


def row_stats(rows):
    mean = jnp.mean(rows, axis=-1, keepdims=True)
    centre = rows - mean
    spread = jnp.mean(centre * centre, axis=-1, keepdims=True)
    inverse = lax.rsqrt(spread + EPS)
    return centre * inverse, inverse


def gelu_pair(inner):
    root = 0.7978845608028654
    cube = 0.044715
    square = inner * inner
    bent = jnp.tanh(inner * (root + (root * cube) * square))
    half = 0.5 + 0.5 * bent
    value = inner * half
    return value, half + value * (1.0 - bent) * (root + (3.0 * root * cube) * square)


def token_kernel(
    tile,
    index,
    ends_ref,
    att_ref,
    x_ref,
    cotangent_ref,
    out_own_ref,
    out_other_ref,
    up_own_ref,
    up_near_ref,
    up_far_ref,
    down_own_ref,
    down_near_ref,
    down_far_ref,
    up_bias_ref,
    gain_ref,
    bias_ref,
    down_bias_ref,
    trade_source,
    pair_source,
    act_in,
    pre_in,
    second_in,
    hidden_in,
    grad_in,
    att_in,
    output_ref,
    hidden_grad_ref,
    datt_ref,
    act_ref,
    pre_ref,
    second_ref,
    hidden_low_ref,
    grad_low_ref,
    att_rows_ref,
    sums_ref,
    unit_sums_ref,
    trade_target,
    pair_target,
    hidden,
    normed,
    inverse,
    ffn,
    second_grad,
    grad_rows,
    up_slots,
    down_slots,
    slot_sems,
    row_sems,
    pair_sems,
    *trade_sems,
):
    step = pl.program_id(0)
    steps = pl.num_programs(0)
    rows = hidden.shape[0]
    parts = att_ref.shape[0]
    tiles = [slice(start, start + tile) for start in range(0, rows, tile)]
    chunk = up_slots.shape[2]
    own_steps = up_own_ref.shape[1] // chunk
    near_steps = up_near_ref.shape[1] // chunk

    def copies(up_from, down_from, index, slot):
        here = pl.ds(pl.multiple_of(index * chunk, chunk), chunk)
        return (
            pltpu.make_async_copy(up_from.at[:, here], up_slots.at[slot], slot_sems.at[0, slot]),
            pltpu.make_async_copy(down_from.at[here], down_slots.at[slot], slot_sems.at[1, slot]),
        )

    def fetch(index):
        def begin(up_from, down_from, first):
            for copy in copies(up_from, down_from, index - first, index % 2):
                copy.start()

        @pl.when(index < own_steps)
        def _():
            begin(up_own_ref, down_own_ref, 0)

        @pl.when((index >= own_steps) & (index < own_steps + near_steps))
        def _():
            begin(up_near_ref, down_near_ref, own_steps)

        @pl.when(index >= own_steps + near_steps)
        def _():
            begin(up_far_ref, down_far_ref, own_steps + near_steps)

    half = parts // 2
    me = lax.axis_index("seq")
    place = lax.axis_index("mp")
    own_place = place * half
    other_place = (1 - place) * half
    first_row = index * rows
    row_copies = [
        pltpu.make_async_copy(source.at[place, pl.ds(first_row, rows)], target, row_sems.at[which])
        for which, (source, target) in enumerate(((x_ref, hidden), (cotangent_ref, grad_rows)))
    ]
    pair = (pair_source, pair_target, pair_sems) if index else None
    trade = Trade(trade_source, trade_target, *trade_sems, pair)
    out_parts = [(own_place + part, out_own_ref, part) for part in range(half)]
    out_parts += [(other_place + part, out_other_ref, part) for part in range(half)]

    @pl.when(step == 0)
    def _():
        for copy in row_copies:
            copy.start()
        fetch(step)
        trade.greet()
        trade.start()

    @pl.when(step + 1 < steps)
    def _():
        fetch(step + 1)

    @pl.when(step == 0)
    def _():
        for copy in row_copies:
            copy.wait()
        for here in tiles:
            total = hidden[here, :]
            for part, weight_ref, index in out_parts:
                total = total + dot_nn(att_ref[part, here, :], weight_ref[index])
            for part in range(parts):
                cols = att_ref.shape[2]
                att_rows_ref[here, part * cols : (part + 1) * cols] = att_ref[part, here, :]
            hidden[here, :] = total
            unit, scale = row_stats(total)
            normed[here, :] = unit
            inverse[here, :] = jnp.broadcast_to(scale, (tile, inverse.shape[1]))
            second_ref[here, :] = (unit * gain_ref[...] + bias_ref[...]).astype(BF16)
            grad_low_ref[here, :] = grad_rows[here, :].astype(BF16)
            ffn[here, :] = jnp.zeros((tile, ffn.shape[1]), F32)
            second_grad[here, :] = jnp.zeros((tile, ffn.shape[1]), F32)

    slot = step % 2
    for copy in copies(up_own_ref, down_own_ref, 0, slot):
        copy.wait()
    up_ref = up_slots.at[slot]
    down_ref = down_slots.at[slot]
    unit_sum = jnp.zeros((1, chunk), F32)
    for here in tiles:
        inner = dot_nn(second_ref[here, :], up_ref[...]) + up_bias_ref[...]
        act_grad = dot_nt(grad_low_ref[here, :], down_ref[...])
        value, slope = gelu_pair(inner)
        value = value.astype(BF16)
        pre_grad = (act_grad * slope).astype(BF16)
        act_ref[here, :] = value
        pre_ref[here, :] = pre_grad
        unit_sum = unit_sum + jnp.sum(pre_grad.astype(F32), axis=0, keepdims=True)
        ffn[here, :] += dot_nn(value, down_ref[...])
        second_grad[here, :] += dot_nt(pre_grad, up_ref[...])
    unit_sums_ref[...] = jnp.broadcast_to(unit_sum, unit_sums_ref.shape)

    @pl.when(step == steps - 1)
    def _():
        width = ffn.shape[1]
        grad_sum = jnp.zeros((1, width), F32)
        gain_sum = jnp.zeros((1, width), F32)
        bias_sum = jnp.zeros((1, width), F32)
        for number, here in enumerate(tiles):
            output_ref[here, :] = (hidden[here, :] + ffn[here, :] + down_bias_ref[...]).astype(BF16)
            grad = grad_rows[here, :]
            back = second_grad[here, :]
            unit = normed[here, :]
            scaled = back * gain_ref[...]
            through = (
                scaled
                - jnp.mean(scaled, axis=-1, keepdims=True)
                - unit * jnp.mean(scaled * unit, axis=-1, keepdims=True)
            )
            total = grad + inverse[here, 0:1] * through
            hidden_grad_ref[here, :] = total
            low = total.astype(BF16)
            hidden_low_ref[here, :] = low
            grad_sum = grad_sum + jnp.sum(grad, axis=0, keepdims=True)
            gain_sum = gain_sum + jnp.sum(back * unit, axis=0, keepdims=True)
            bias_sum = bias_sum + jnp.sum(back, axis=0, keepdims=True)
            for part, weight_ref, piece in out_parts:
                spread = dot_nt(low, weight_ref[piece])
                places = me * 2 * rows + first_row + number * tile
                places = places + lax.broadcasted_iota(jnp.int32, spread.shape, 0)
                inside = places < ends_ref[ends_ref.shape[0] - 1]
                datt_ref[part, here, :] = jnp.where(inside, spread, 0.0).astype(BF16)
        sums_ref[...] = jnp.concatenate(
            [grad_sum, gain_sum, bias_sum, jnp.zeros((5, width), F32)], axis=0
        )
        trade.finish()


def token_part(
    index, doc_ends, att, layer_input, cotangent, outs, ups, downs, up_bias, gain, bias, down_bias, source, pair, kept
):
    parts, rows, cols = att.shape
    width = layer_input.shape[2]
    units = up_bias.shape[1]
    chunk = min(512, units // 4)
    whole = 2 * rows
    shapes = [(whole, units)] * 2 + [(whole, width)] * 4
    if kept is None:
        kept = [jnp.zeros((8, 128), BF16)] * len(shapes)
        aliases = {}
    else:
        aliases = {18 + place: 3 + place for place in range(len(shapes))}
    half = lambda step: (index, 0)
    fixed = lambda step: (0, 0)
    any_spec = pl.BlockSpec(memory_space=pl.ANY)
    cube = lambda step: (0, 0, 0)
    vector = pl.BlockSpec((1, width), fixed)
    return pl.pallas_call(
        functools.partial(token_kernel, min(256, rows), index),
        grid=(units // chunk,),
        in_specs=[
            smem(),
            pl.BlockSpec((parts, rows, cols), cube),
            any_spec,
            any_spec,
            pl.BlockSpec((parts // 2, cols, width), cube),
            pl.BlockSpec((parts // 2, cols, width), cube),
        ]
        + [any_spec] * 6
        + [pl.BlockSpec((1, chunk), lambda step: (0, step)), vector, vector, vector]
        + [any_spec] * (2 + len(shapes)),
        out_specs=[
            pl.BlockSpec((rows, width), fixed),
            pl.BlockSpec((rows, width), fixed),
            pl.BlockSpec((parts, rows, cols), cube),
            pl.BlockSpec((rows, chunk), lambda step: (index, step)),
            pl.BlockSpec((rows, chunk), lambda step: (index, step)),
            pl.BlockSpec((rows, width), half),
            pl.BlockSpec((rows, width), half),
            pl.BlockSpec((rows, width), half),
            pl.BlockSpec((rows, width), half),
            pl.BlockSpec((8, width), fixed),
            pl.BlockSpec((8, chunk), lambda step: (0, step)),
            any_spec,
            any_spec,
        ],
        scratch_shapes=[
            pltpu.VMEM((rows, width), F32),
            pltpu.VMEM((rows, width), F32),
            pltpu.VMEM((rows, 128), F32),
            pltpu.VMEM((rows, width), F32),
            pltpu.VMEM((rows, width), F32),
            pltpu.VMEM((rows, width), F32),
            pltpu.VMEM((2, width, chunk), BF16),
            pltpu.VMEM((2, chunk, width), BF16),
            pltpu.SemaphoreType.DMA((2, 2)),
            pltpu.SemaphoreType.DMA((2,)),
            pltpu.SemaphoreType.DMA((2,)),
        ]
        + trade_scratch(parts),
        out_shape=[
            jax.ShapeDtypeStruct((rows, width), BF16),
            jax.ShapeDtypeStruct((rows, width), F32),
            jax.ShapeDtypeStruct((parts, rows, cols), BF16),
        ]
        + [jax.ShapeDtypeStruct(shape, BF16) for shape in shapes]
        + [
            jax.ShapeDtypeStruct((8, width), F32),
            jax.ShapeDtypeStruct((8, units), F32),
            jax.ShapeDtypeStruct((parts, rows, cols), BF16),
            jax.ShapeDtypeStruct(pair.shape, BF16),
        ],
        input_output_aliases=aliases,
        compiler_params=pltpu.CompilerParams(
            collective_id=5 + index, has_side_effects=True, vmem_limit_bytes=VMEM_LIMIT
        ),
        cost_estimate=pl.CostEstimate(
            flops=rows * width * (8 * units + 4 * width),
            bytes_accessed=8 * units * width,
            transcendentals=0,
        ),
    )(
        doc_ends,
        att,
        layer_input,
        cotangent,
        *outs,
        *ups,
        *downs,
        up_bias,
        gain,
        bias,
        down_bias,
        source,
        pair,
        *kept,
    )


def batch_mate(distance):
    batch = lax.axis_index("batch")
    return batch + distance - 2 * distance * ((batch // distance) % 2)


def greet(me, count, partner, mate):
    barrier = pltpu.get_barrier_semaphore()

    @pl.when(me > 0)
    def _():
        pl.semaphore_signal(barrier, inc=1, device_id={"seq": me - 1}, device_id_type=MESH)

    @pl.when(me < count - 1)
    def _():
        pl.semaphore_signal(barrier, inc=1, device_id={"seq": me + 1}, device_id_type=MESH)

    pl.semaphore_signal(barrier, inc=1, device_id={"mp": partner}, device_id_type=MESH)
    pl.semaphore_signal(barrier, inc=1, device_id={"batch": mate}, device_id_type=MESH)
    pl.semaphore_wait(barrier, jnp.minimum(me, 1) + jnp.minimum(count - 1 - me, 1) + 2)


def gather_kernel(
    count,
    chunks,
    x_ref,
    gain_ref,
    bias_ref,
    weight_ref,
    out_ref,
    up_ref,
    down_ref,
    up_bias_ref,
    all_ref,
    qkv_ref,
    own_ref,
    edge_ref,
    out_other,
    up_near,
    down_near,
    up_bias_near,
    rows_in,
    shards,
    results,
    weight,
    weight_sems,
    fetch_sems,
    load_sems,
    send_sems,
    recv_sems,
    all_sems,
    qkv_sems,
):
    me = lax.axis_index("seq")
    place = lax.axis_index("mp")
    step = rows_in.shape[0] // chunks
    cols = weight.shape[1] // 3

    def at(chunk):
        return pl.ds(pl.multiple_of(chunk * step, step), step)

    def load(chunk):
        return pltpu.make_async_copy(
            x_ref.at[place, at(chunk)], rows_in.at[at(chunk)], load_sems.at[chunk]
        )

    def send(side, hop, chunk):
        shard = me - hop if side == 0 else me + hop
        target = me + 1 if side == 0 else me - 1
        return pltpu.make_async_remote_copy(
            src_ref=shards.at[shard, at(chunk)],
            dst_ref=shards.at[shard, at(chunk)],
            send_sem=send_sems.at[side, hop, chunk],
            recv_sem=recv_sems.at[side, hop, chunk],
            device_id={"seq": target},
            device_id_type=MESH,
        )

    def keep_all(shard, chunk):
        return pltpu.make_async_copy(
            shards.at[shard, at(chunk)], all_ref.at[shard, at(chunk)], all_sems.at[shard, chunk]
        )

    def keep_qkv(shard, chunk):
        return pltpu.make_async_copy(
            results.at[shard, at(chunk)], qkv_ref.at[shard, at(chunk)], qkv_sems.at[shard, chunk]
        )

    def over_chunks(body):
        def run(chunk, _):
            body(chunk)
            return 0

        lax.fori_loop(0, chunks, run, 0)

    over_chunks(lambda chunk: load(chunk).start())
    greet(me, count, 1 - place, batch_mate(2))

    half_cols = weight_ref.shape[2]
    here = (me * cols) // half_cols == place
    heads = pl.ds(pl.multiple_of((me * cols) % half_cols, 128), cols)
    fetches, copies = [], []
    for matrix in range(3):
        source = weight_ref.at[matrix, :, heads]
        target = weight.at[:, pl.ds(matrix * cols, cols)]
        fetches.append(
            pltpu.make_async_remote_copy(
                src_ref=source,
                dst_ref=target,
                send_sem=weight_sems.at[0, matrix],
                recv_sem=weight_sems.at[1, matrix],
                device_id={"mp": 1 - place},
                device_id_type=MESH,
            )
        )
        copies.append(pltpu.make_async_copy(source, target, weight_sems.at[2, matrix]))

    @pl.when(here)
    def _():
        for each in fetches + copies:
            each.start()

    batch = lax.axis_index("batch")
    parity, side = batch % 2, batch // 2
    share = up_near.shape[1] // 2
    quarter = pl.ds(pl.multiple_of((2 * parity + side) * share, share), share)
    there = pl.ds(pl.multiple_of(side * share, share), share)
    half = up_bias_near.shape[1]
    bias_half = pl.ds(pl.multiple_of(parity * half, half), half)

    def give(which, source, target, device):
        return pltpu.make_async_remote_copy(
            src_ref=source,
            dst_ref=target,
            send_sem=fetch_sems.at[0, which],
            recv_sem=fetch_sems.at[1, which],
            device_id=device,
            device_id_type=MESH,
        )

    partner, chip = {"mp": 1 - place}, {"batch": batch + 2 - 4 * side}
    shares = [
        give(0, out_ref, out_other, partner),
        give(1, up_ref.at[:, quarter], up_near.at[:, there], partner),
        give(2, down_ref.at[quarter], down_near.at[there], partner),
        give(3, up_bias_ref.at[:, bias_half], up_bias_near, partner),
    ]
    passed = [
        give(4, up_near.at[:, there], up_near.at[:, there], chip),
        give(5, down_near.at[there], down_near.at[there], chip),
    ]
    for each in (shares[1], shares[2], shares[3], shares[0]):
        each.start()

    def pass_on(which):
        shares[1 + which].wait()
        passed[which].start()

    def norm(chunk):
        load(chunk).wait()
        unit, _ = row_stats(rows_in[at(chunk), :])
        shards[me, at(chunk), :] = (unit * gain_ref[...] + bias_ref[...]).astype(BF16)
        keep_all(me, chunk).start()

        @pl.when(me < count - 1)
        def _():
            send(0, 0, chunk).start()

        @pl.when(me > 0)
        def _():
            send(1, 0, chunk).start()

    over_chunks(norm)

    def project(shard, chunk):
        rows = dot_nn(shards[shard, at(chunk), :], weight[...])
        results[shard, at(chunk), :] = rows.astype(BF16)
        keep_qkv(shard, chunk).start()

    def receive(hop, chunk):
        @pl.when(me >= hop + 1)
        def _():
            send(0, hop, chunk).wait_recv()
            if hop + 1 < count - 1:

                @pl.when(me < count - 1)
                def _():
                    send(0, hop + 1, chunk).start()

            keep_all(me - hop - 1, chunk).start()

        @pl.when(me + hop + 1 < count)
        def _():
            send(1, hop, chunk).wait_recv()
            if hop + 1 < count - 1:

                @pl.when(me > 0)
                def _():
                    send(1, hop + 1, chunk).start()

            keep_all(me + hop + 1, chunk).start()

    for hop in range(count - 2):
        over_chunks(functools.partial(receive, hop))
        if hop == (count - 2) // 2 - 1:
            pass_on(0)

    @pl.when(here)
    def _():
        for each in copies:
            each.wait()

    @pl.when(jnp.logical_not(here))
    def _():
        for each in fetches:
            each.wait_recv()

    keep_weight = pltpu.make_async_copy(weight, own_ref, weight_sems.at[3, 0])
    keep_weight.start()

    last_place = count - 1
    at_end, by_end = (me == 0) | (me == last_place), (me == 1) | (me == last_place - 1)
    low_half = me // (count // 2)
    edge = pltpu.make_async_remote_copy(
        src_ref=weight,
        dst_ref=edge_ref,
        send_sem=weight_sems.at[3, 1],
        recv_sem=weight_sems.at[3, 2],
        device_id={"seq": me + 1 - 2 * low_half},
        device_id_type=MESH,
    )

    @pl.when(at_end)
    def _():
        edge.start()

    def last(chunk):
        project(me, chunk)
        for hop in range(count - 1):
            if hop == count - 2:
                receive(hop, chunk)

            @pl.when(me >= hop + 1)
            def _():
                project(me - hop - 1, chunk)

            @pl.when(me + hop + 1 < count)
            def _():
                project(me + hop + 1, chunk)

        @pl.when(chunk == 1)
        def _():
            pass_on(1)

    over_chunks(last)

    def finish(chunk):
        for hop in range(count - 1):

            @pl.when((me >= hop) & (me < count - 1))
            def _():
                send(0, hop, chunk).wait_send()

            @pl.when((me + hop < count) & (me > 0))
            def _():
                send(1, hop, chunk).wait_send()

        for shard in range(count):
            keep_all(shard, chunk).wait()
            keep_qkv(shard, chunk).wait()

    over_chunks(finish)
    keep_weight.wait()

    @pl.when(at_end)
    def _():
        edge.wait_send()

    @pl.when(by_end)
    def _():
        edge.wait_recv()

    for each in (shares[0], shares[3], *passed):
        each.wait()

    @pl.when(here)
    def _():
        for each in fetches:
            each.wait_send()


def gather_project(layer_input, gain, bias, weight, out_weight, up_weight, down_weight, up_bias):
    count = lax.axis_size("seq")
    _, rows, width = layer_input.shape
    cols = 3 * width // count
    chunks = max(1, rows // 128)
    any_spec = pl.BlockSpec(memory_space=pl.ANY)
    vmem = pl.BlockSpec(memory_space=pltpu.VMEM)
    dma = pltpu.SemaphoreType.DMA
    return pl.pallas_call(
        functools.partial(gather_kernel, count, chunks),
        in_specs=[any_spec, vmem, vmem] + [any_spec] * 5,
        out_specs=[any_spec] * 8,
        out_shape=[
            jax.ShapeDtypeStruct((count, rows, width), BF16),
            jax.ShapeDtypeStruct((count, rows, cols), BF16),
            jax.ShapeDtypeStruct((width, cols), BF16),
            jax.ShapeDtypeStruct((width, cols), BF16),
            jax.ShapeDtypeStruct(out_weight.shape, BF16),
            jax.ShapeDtypeStruct((width, up_weight.shape[1] // 2), BF16),
            jax.ShapeDtypeStruct((down_weight.shape[0] // 2, width), BF16),
            jax.ShapeDtypeStruct((1, up_weight.shape[1] // 2), F32),
        ],
        scratch_shapes=[
            pltpu.VMEM((rows, width), F32),
            pltpu.VMEM((count, rows, width), BF16),
            pltpu.VMEM((count, rows, cols), BF16),
            pltpu.VMEM((width, cols), BF16),
            dma((4, 3)),
            dma((2, 6)),
            dma((chunks,)),
            dma((2, count - 1, chunks)),
            dma((2, count - 1, chunks)),
            dma((count, chunks)),
            dma((count, chunks)),
        ],
        compiler_params=pltpu.CompilerParams(
            collective_id=0, has_side_effects=True, vmem_limit_bytes=VMEM_LIMIT
        ),
        cost_estimate=pl.CostEstimate(
            flops=150_000_000_000, bytes_accessed=1, transcendentals=0
        ),
    )(layer_input, gain, bias, weight, out_weight, up_weight, down_weight, up_bias)


class VectorSum:
    def __init__(self, group, line, sems):
        self.group, self.line, self.sems = group, line, sems
        self.me, self.count = lax.axis_index("seq"), lax.axis_size("seq")
        self.pairs = lax.axis_size("mp")
        self.members = lax.axis_size("batch") * self.pairs
        self.mine = lax.axis_index("batch") * self.pairs + lax.axis_index("mp")

    def member(self, distance):
        other = lax.rem(self.mine + distance, self.members)
        return {"batch": other // self.pairs, "mp": lax.rem(other, self.pairs)}

    def along(self, distance):
        return {"seq": lax.rem(self.me + distance, self.count)}

    def greet(self):
        barrier = pltpu.get_barrier_semaphore()
        for distance in range(1, self.members):
            pl.semaphore_signal(
                barrier, inc=1, device_id=self.member(distance), device_id_type=MESH
            )
        for distance in range(1, self.count):
            pl.semaphore_signal(barrier, inc=1, device_id=self.along(distance), device_id_type=MESH)
        pl.semaphore_wait(barrier, self.members + self.count - 2)

    def share(self, distance, along):
        buffer, place = (self.line, self.me) if along else (self.group, self.mine)
        which = distance - 1 + (self.members - 1 if along else 0)
        return pltpu.make_async_remote_copy(
            src_ref=buffer.at[place],
            dst_ref=buffer.at[place],
            send_sem=self.sems.at[0, which],
            recv_sem=self.sems.at[1, which],
            device_id=self.along(distance) if along else self.member(distance),
            device_id_type=MESH,
        )

    def start(self, value):
        self.group[self.mine] = value
        for distance in range(1, self.members):
            self.share(distance, False).start()

    def middle(self):
        for distance in range(1, self.members):
            self.share(distance, False).wait()
        total = self.group[0]
        for place in range(1, self.members):
            total = total + self.group[place]
        self.line[self.me] = total
        for distance in range(1, self.count):
            self.share(distance, True).start()

    def finish(self):
        for distance in range(1, self.count):
            self.share(distance, True).wait()
        total = self.line[0]
        for place in range(1, self.count):
            total = total + self.line[place]
        return total


class Extra:
    def __init__(self, kind, source, target, sems):
        self.source, self.target, self.sems = source, target, sems
        batch, place = lax.axis_index("batch"), lax.axis_index("mp")
        self.local = None
        if kind == "mp":
            self.moves = [(source, target, {"mp": 1 - place})]
        else:
            count = source.shape[0]
            pairs = lax.axis_size("mp")
            mine = batch * pairs + place
            self.moves = []
            for distance in range(1, count):
                other = lax.rem(mine + distance, count)
                device = {"batch": other // pairs, "mp": lax.rem(other, pairs)}
                self.moves.append((source.at[other], target.at[mine], device))
            self.local = (source.at[mine], target.at[mine])

    def copies(self):
        for index, (source, target, device) in enumerate(self.moves):
            yield pltpu.make_async_remote_copy(
                src_ref=source,
                dst_ref=target,
                send_sem=self.sems.at[0, index],
                recv_sem=self.sems.at[1, index],
                device_id=device,
                device_id_type=MESH,
            )
        if self.local is not None:
            yield pltpu.make_async_copy(*self.local, self.sems.at[0, len(self.moves)])

    def start(self):
        for copy in self.copies():
            copy.start()

    def finish(self):
        for copy in self.copies():
            copy.wait()


def extra_moves(kind, source):
    return 1 if kind == "mp" else source.shape[0]


def in_rows(vectors, width):
    pieces = []
    for row in range(vectors.shape[0]):
        for start in range(0, vectors.shape[1], width):
            pieces.append(vectors[row : row + 1, start : start + width])
    return jnp.concatenate(pieces, axis=0)


class ProjectionGrad:
    def __init__(self, first_all, parts, grouped, slots, total, low, slot_sems, out_sems):
        self.first_all, self.parts, self.grouped = first_all, parts, grouped
        self.slots, self.total, self.low = slots, total, low
        self.slot_sems, self.out_sems = slot_sems, out_sems
        self.rows = slots.shape[1]
        self.steps = first_all.shape[0] // self.rows

    def fetch(self, step):
        return pltpu.make_async_copy(
            self.first_all.at[pl.ds(pl.multiple_of(step * self.rows, self.rows), self.rows)],
            self.slots.at[step % 2],
            self.slot_sems.at[step % 2],
        )

    def start(self):
        self.fetch(0).start()
        self.total[...] = jnp.zeros_like(self.total)

    def multiply(self, step):
        self.fetch(step).wait()

        @pl.when(step + 1 < self.steps)
        def _():
            self.fetch(step + 1).start()

        here = pl.ds(pl.multiple_of((step % 2) * self.rows, self.rows), self.rows)
        grads = self.parts[step // 2, here, :]
        width = self.total.shape[0]
        size = width // 4
        for start in range(0, width, size):
            rows = self.slots[step % 2, :, start : start + size]
            self.total[start : start + size, :] += dot_tn(rows, grads)

        @pl.when(step == self.steps - 1)
        def _():
            self.low[...] = self.total[...].astype(BF16)
            for copy in self.copies():
                copy.start()

    def copies(self):
        members, count, rows, _ = self.grouped.shape
        for member in range(members):
            for part in range(count):
                first = (part * members + member) * rows
                yield pltpu.make_async_copy(
                    self.low.at[pl.ds(first, rows)],
                    self.grouped.at[member, part],
                    self.out_sems.at[member, part],
                )

    def finish(self):
        for copy in self.copies():
            copy.wait()


class WeightBegin:
    def __init__(self, terms, targets, near_sum, own_sum, down_sum, sems):
        self.terms, self.targets, self.sems = terms, targets, sems
        self.near_sum, self.own_sum, self.down_sum = near_sum, own_sum, down_sum

    def copies(self):
        own_out, near_target, down_out, down_target = self.targets
        batch, place = lax.axis_index("batch"), lax.axis_index("mp")
        side = (batch // 2) % 2
        size = self.down_sum.shape[1] // 2
        kept = pl.ds(pl.multiple_of(side * size, 128), size)
        there = pl.ds(pl.multiple_of((1 - side) * size, 128), size)
        return [
            pltpu.make_async_remote_copy(
                src_ref=self.near_sum,
                dst_ref=near_target,
                send_sem=self.sems.at[0],
                recv_sem=self.sems.at[1],
                device_id={"mp": 1 - place},
                device_id_type=MESH,
            ),
            pltpu.make_async_remote_copy(
                src_ref=self.down_sum.at[:, there],
                dst_ref=down_target,
                send_sem=self.sems.at[2],
                recv_sem=self.sems.at[3],
                device_id={"batch": batch + 2 - 4 * side},
                device_id_type=MESH,
            ),
            pltpu.make_async_copy(self.own_sum, own_out, self.sems.at[4]),
            pltpu.make_async_copy(self.down_sum.at[:, kept], down_out, self.sems.at[5]),
        ]

    def start(self):
        keep, come, down, down_come = self.terms
        rows = keep.shape[1]
        step = min(128, rows)

        def add(index, _):
            here = pl.ds(pl.multiple_of(index * step, step), step)
            near = keep[1, here, :].astype(F32) + come[1, here, :].astype(F32)
            own = keep[0, here, :].astype(F32) + come[0, here, :].astype(F32)
            low = down[here, :].astype(F32) + down_come[here, :].astype(F32)
            self.near_sum[here, :] = near.astype(BF16)
            self.own_sum[here, :] = own.astype(BF16)
            self.down_sum[here, :] = low.astype(BF16)
            return 0

        lax.fori_loop(0, rows // step, add, 0)
        for copy in self.copies():
            copy.start()

    def finish(self):
        for copy in self.copies():
            copy.wait()


class WeightChain:
    def __init__(self, terms, qkv_terms, gathered, heads_ref, sending, received, result, head_sum, heads_in, sems):
        self.terms = terms
        self.qkv_terms, self.gathered, self.heads_ref = qkv_terms, gathered, heads_ref
        self.sending, self.received, self.result = sending, received, result
        self.head_sum, self.heads_in, self.sems = head_sum, heads_in, sems
        self.me, self.count = lax.axis_index("seq"), lax.axis_size("seq")
        self.batch, self.place = lax.axis_index("batch"), lax.axis_index("mp")
        self.rows = result.shape[1]
        self.chunks = 2
        self.step = self.rows // self.chunks
        self.steps = (self.count - 1) * self.chunks
        self.members = qkv_terms.shape[0]
        self.mine = self.batch * 2 + self.place
        self.used = 2 * self.steps

    def at(self, chunk):
        return pl.ds(pl.multiple_of(chunk * self.step, self.step), self.step)

    def term(self, target, chunk):
        here = pl.ds(pl.multiple_of(target * self.rows + chunk * self.step, self.step), self.step)
        own, own_come, down, down_come = (term[here, :].astype(F32) for term in self.terms)
        return jnp.concatenate([own + own_come, down + down_come], axis=1)

    def send(self, side, message, chunk):
        which = (side * (self.count - 1) + message) * self.chunks + chunk
        return pltpu.make_async_remote_copy(
            src_ref=self.sending.at[side, message, self.at(chunk)],
            dst_ref=self.received.at[side, message, self.at(chunk)],
            send_sem=self.sems.at[0, which],
            recv_sem=self.sems.at[1, which],
            device_id={"seq": self.me + 1 - 2 * side},
            device_id_type=MESH,
        )

    def flow(self, side, index):
        message, chunk = index // self.chunks, index % self.chunks
        target = (1 - side) * (self.count - 1 - message) + side * message

        @pl.when((target - self.me) * (1 - 2 * side) > 0)
        def _():
            total = self.term(target, chunk)
            first = (1 - side) * self.me + side * (self.count - 1 - self.me)

            @pl.when(first == 0)
            def _():
                self.sending[side, message, self.at(chunk), :] = total.astype(BF16)

            @pl.when(first > 0)
            def _():
                self.send(side, message, chunk).wait_recv()
                come = self.received[side, message, self.at(chunk), :].astype(F32)
                self.sending[side, message, self.at(chunk), :] = (total + come).astype(BF16)

            self.send(side, message, chunk).start()

    def heads_line(self, distance):
        other = lax.rem(self.me + distance, self.count)
        which = self.used + distance - 1
        return pltpu.make_async_remote_copy(
            src_ref=self.head_sum.at[other],
            dst_ref=self.heads_in.at[self.me],
            send_sem=self.sems.at[0, which],
            recv_sem=self.sems.at[1, which],
            device_id={"seq": other},
            device_id_type=MESH,
        )

    def heads_member(self, distance):
        other = lax.rem(self.mine + distance, self.members)
        which = self.used + self.count - 1 + distance - 1
        parts = self.count // 2
        return pltpu.make_async_remote_copy(
            src_ref=self.heads_in.at[pl.ds(lax.rem(other, 2) * parts, parts)],
            dst_ref=self.heads_ref.at[self.mine],
            send_sem=self.sems.at[0, which],
            recv_sem=self.sems.at[1, which],
            device_id={"batch": other // 2, "mp": lax.rem(other, 2)},
            device_id_type=MESH,
        )

    def heads_own(self):
        parts = self.count // 2
        return pltpu.make_async_copy(
            self.heads_in.at[pl.ds(self.place * parts, parts)],
            self.heads_ref.at[self.mine],
            self.sems.at[0, self.used + self.count + self.members - 2],
        )

    def piece(self, index):
        which = self.used + self.count + self.members - 1 + index
        side = (self.batch // 2) % 2
        parity = self.batch % 2
        other = self.batch + 1 - 2 * parity if index else self.batch + 2 - 4 * side
        source = max(index - 1, 0)
        return pltpu.make_async_remote_copy(
            src_ref=self.result.at[source],
            dst_ref=self.result.at[source + (2 if index else 1)],
            send_sem=self.sems.at[0, which],
            recv_sem=self.sems.at[1, which],
            device_id={"batch": other},
            device_id_type=MESH,
        )

    def start(self):
        total = self.qkv_terms[0].astype(F32)
        for member in range(1, self.members):
            total = total + self.qkv_terms[member].astype(F32)
        self.head_sum[...] = total.astype(BF16)
        self.heads_in[self.me] = self.head_sum[self.me]
        for distance in range(1, self.count):
            self.heads_line(distance).start()

    def own(self):
        for chunk in range(self.chunks):
            here = self.at(chunk)
            total = self.term(self.me, chunk)

            @pl.when(self.me > 0)
            def _():
                self.send(0, self.count - 1 - self.me, chunk).wait_recv()

            @pl.when(self.me < self.count - 1)
            def _():
                self.send(1, self.me, chunk).wait_recv()

            left = self.received[0, jnp.minimum(self.count - 1 - self.me, self.count - 2), here, :]
            right = self.received[1, jnp.minimum(self.me, self.count - 2), here, :]
            total = total + jnp.where(self.me > 0, left.astype(F32), 0.0)
            total = total + jnp.where(self.me < self.count - 1, right.astype(F32), 0.0)
            self.result[0, here, :] = total.astype(BF16)
        self.piece(0).start()
        for distance in range(1, self.count):
            self.heads_line(distance).wait()
        for distance in range(1, self.members):
            self.heads_member(distance).start()
        self.heads_own().start()

    def spread(self):
        self.piece(0).wait()
        self.piece(1).start()
        self.piece(2).start()

    def finish(self):
        for index in range(self.steps):
            message, chunk = index // self.chunks, index % self.chunks

            @pl.when(self.count - 1 - message > self.me)
            def _():
                self.send(0, message, chunk).wait_send()

            @pl.when(message < self.me)
            def _():
                self.send(1, message, chunk).wait_send()

        self.piece(1).wait()
        self.piece(2).wait()
        self.heads_own().wait()
        for distance in range(1, self.members):
            self.heads_member(distance).wait()
        copy = pltpu.make_async_copy(
            self.result, self.gathered, self.sems.at[0, self.used + self.count + self.members + 2]
        )
        copy.start()
        copy.wait()


def return_kernel(
    count,
    chunks,
    lag,
    index_of,
    kinds,
    parts_ref,
    weight_from,
    edge_weight_from,
    x_ref,
    hidden_grad_from,
    gain_ref,
    vectors_ref,
    *rest,
):
    extras = len(kinds)
    sources, rest = rest[:extras], rest[extras:]
    terms_from, qkv_from, rest = rest[:4], rest[4], rest[5:]
    input_ref, sums_ref, total_ref, other_ref, *rest = rest
    targets, rest = rest[:extras], rest[extras:]
    late_out, rest = (rest[:2], rest[2:]) if index_of else (rest[:5], rest[5:])
    weight_ref, edge_weight_ref, hidden_grad_ref, *rest = rest
    weight_terms, rest = rest[:4], rest[4:]
    rows_in, sending, received, edge_in, summed, group, line, load_sems, *rest = rest
    send_sems, recv_sems, pair_send_sems, pair_recv_sems, vector_sems, *extra_sems = rest
    late = extra_sems[extras:]
    extras = [Extra(*each) for each in zip(kinds, sources, targets, extra_sems)]
    me = lax.axis_index("seq")
    place = lax.axis_index("mp")
    rows, width = rows_in.shape
    step = rows // chunks
    steps = (count - 1) * chunks

    def at(chunk):
        return pl.ds(pl.multiple_of(chunk * step, step), step)

    pairs = [(weight_from, weight_ref), (edge_weight_from, edge_weight_ref)]
    pairs += list(zip(terms_from, weight_terms))
    pairs += [(hidden_grad_from, hidden_grad_ref), (x_ref.at[place, pl.ds(index_of * rows, rows)], rows_in)]
    loads = [
        pltpu.make_async_copy(source, target, load_sems.at[which])
        for which, (source, target) in enumerate(pairs)
    ]
    for load in loads:
        load.start()
    vector_sum = VectorSum(group, line, vector_sems)
    vector_sum.greet()
    if index_of == 0:
        vector_sum.start(vectors_ref[...])

    def send(side, message, chunk):
        return pltpu.make_async_remote_copy(
            src_ref=sending.at[side, message, at(chunk)],
            dst_ref=received.at[side, message, at(chunk)],
            send_sem=send_sems.at[side, message, chunk],
            recv_sem=recv_sems.at[side, message, chunk],
            device_id={"seq": me + 1 - 2 * side},
            device_id_type=MESH,
        )

    def send_edge(side, message, chunk):
        target = (1 - side) * (count - 1 - message) + side * message
        return pltpu.make_async_remote_copy(
            src_ref=parts_ref.at[target, at(chunk)],
            dst_ref=edge_in.at[message, at(chunk)],
            send_sem=send_sems.at[side, message, chunk],
            recv_sem=recv_sems.at[side, message, chunk],
            device_id={"seq": me + 1 - 2 * side},
            device_id_type=MESH,
        )

    def flow(side, index):
        message = index // chunks
        chunk = index % chunks
        target = (1 - side) * (count - 1 - message) + side * message

        @pl.when((target - me) * (1 - 2 * side) > 0)
        def _():
            first = (1 - side) * me + side * (count - 1 - me)

            @pl.when(first == 0)
            def _():
                send_edge(side, message, chunk).start()

            @pl.when(first == 1)
            def _():
                send_edge(side, message, chunk).wait_recv()
                total = dot_nt(parts_ref[target, at(chunk), :], weight_ref[...])
                total = total + dot_nt(edge_in[message, at(chunk), :], edge_weight_ref[...])
                sending[side, message, at(chunk), :] = total.astype(BF16)
                send(side, message, chunk).start()

            @pl.when(first > 1)
            def _():
                total = dot_nt(parts_ref[target, at(chunk), :], weight_ref[...])
                send(side, message, chunk).wait_recv()
                come = received[side, message, at(chunk), :].astype(F32)
                sending[side, message, at(chunk), :] = (total + come).astype(BF16)
                send(side, message, chunk).start()

    if index_of:
        qkv_terms, qkv_sems, *late = late
        trade = Extra("group", qkv_from, qkv_terms, qkv_sems)
        trade.start()
        for extra in extras:
            extra.start()
        chain = WeightChain(weight_terms, qkv_terms, *late_out, *late)
        begin = None
    else:
        chain = None
        begin = WeightBegin(weight_terms, late_out[:4], *late[:4])
        projection = ProjectionGrad(qkv_from, parts_ref, late_out[4], *late[4:])
        projection.start()
    ahead = chain.steps if chain else 0
    near = me // (count // 2)

    def pair(chunk):
        return pltpu.make_async_remote_copy(
            src_ref=input_ref.at[at(chunk)],
            dst_ref=other_ref.at[at(chunk)],
            send_sem=pair_send_sems.at[chunk],
            recv_sem=pair_recv_sems.at[chunk],
            device_id={"mp": 1 - place},
            device_id_type=MESH,
        )

    def own(chunk):
        here = at(chunk)
        summed[...] = dot_nt(parts_ref[me, here, :], weight_ref[...])
        for side in range(2):
            first = me if side == 0 else count - 1 - me
            message = count - 1 - me if side == 0 else me

            @pl.when(first == 1)
            def _():
                send_edge(side, message, chunk).wait_recv()
                summed[...] += dot_nt(edge_in[message, here, :], edge_weight_ref[...])

            @pl.when(first > 1)
            def _():
                send(side, message, chunk).wait_recv()
                summed[...] += received[side, message, here, :].astype(F32)

        total = summed[...]
        unit, inverse = row_stats(rows_in[here, :])
        scaled = total * gain_ref[...]
        through = (
            scaled
            - jnp.mean(scaled, axis=-1, keepdims=True)
            - unit * jnp.mean(scaled * unit, axis=-1, keepdims=True)
        )
        input_ref[here, :] = (hidden_grad_ref[here, :] + inverse * through).astype(BF16)
        if index_of:
            pair(chunk).start()
        sums_ref[0:1, :] += jnp.sum(total * unit, axis=0, keepdims=True)
        sums_ref[1:2, :] += jnp.sum(total, axis=0, keepdims=True)

    sums_ref[...] = jnp.zeros_like(sums_ref)
    for load in loads[:2] + (loads[2:6] if index_of else []):
        load.wait()
    wait_for = ahead + ((count - 2) * chunks + lag + 1 if index_of else steps + lag)
    steps_all = ahead + steps

    def flow_of(side, index):
        if chain is not None:

            @pl.when(index < ahead)
            def _():
                chain.flow(side, index)

        @pl.when(index >= ahead)
        def _():
            flow(side, index - ahead)

    def advance(index, _):
        @pl.when(index < steps_all)
        def _():
            flow_of(near, index)

        @pl.when((index >= lag) & (index < steps_all + lag))
        def _():
            flow_of(1 - near, index - lag)

        if begin is not None:
            @pl.when(index == 2)
            def _():
                for load in loads[2:6]:
                    load.wait()
                begin.start()

            @pl.when((index >= 3) & (index < 3 + projection.steps))
            def _():
                projection.multiply(index - 3)

        if chain is not None:

            @pl.when(index == 6)
            def _():
                trade.finish()
                chain.start()

            @pl.when(index == ahead + lag)
            def _():
                chain.own()

            @pl.when(index == ahead + lag + 3)
            def _():
                chain.spread()

        @pl.when(index == wait_for)
        def _():
            for load in loads[-2:]:
                load.wait()

        @pl.when(index >= wait_for)
        def _():
            own(index - wait_for)

        return 0

    lax.fori_loop(0, wait_for + chunks, advance, 0)
    if index_of:
        vector_sum.start(in_rows(sums_ref[0:2, :] + vectors_ref[0:2, :], group.shape[2]))
    vector_sum.middle()

    def finish(index, _):
        message = index // chunks
        chunk = index % chunks

        @pl.when((count - 1 - message > me) & (me > 0))
        def _():
            send(0, message, chunk).wait_send()

        @pl.when((count - 1 - message > me) & (me == 0))
        def _():
            send_edge(0, message, chunk).wait_send()

        @pl.when((message < me) & (me < count - 1))
        def _():
            send(1, message, chunk).wait_send()

        @pl.when((message < me) & (me == count - 1))
        def _():
            send_edge(1, message, chunk).wait_send()

        return 0

    lax.fori_loop(0, steps, finish, 0)

    def finish_pair(chunk, _):
        pair(chunk).wait()
        return 0

    if index_of:
        lax.fori_loop(0, chunks, finish_pair, 0)
    total_ref[...] = vector_sum.finish()
    if chain is not None:
        chain.finish()
    else:
        begin.finish()
        projection.finish()
    for extra in extras:
        extra.finish()


def return_part(
    index, parts, weight, edge_weight, layer_input, hidden_grad, gain, vectors, extras, weight_terms, qkv_from
):
    count, rows, cols = parts.shape
    rows = rows // 2
    width = weight.shape[0]
    chunks = max(1, rows // 128)
    members = lax.axis_size("batch") * lax.axis_size("mp")
    small = (8, 2 * width // 8) if index else vectors.shape
    kinds, sources = [kind for kind, _ in extras], [source for _, source in extras]
    dma = pltpu.SemaphoreType.DMA
    late_in = [*weight_terms]
    if not index:
        keep, _, down, _ = weight_terms
        half = (width, down.shape[1] // 2)
        grouped = (members, count, width // count // members, cols)
        late_out = [keep.shape[1:], keep.shape[1:], half, half, grouped]
        late_scratch = [
            pltpu.VMEM(keep.shape[1:], BF16),
            pltpu.VMEM(keep.shape[1:], BF16),
            pltpu.VMEM(down.shape, BF16),
            dma((6,)),
            pltpu.VMEM((2, rows, width), BF16),
            pltpu.VMEM((width, cols), F32),
            pltpu.VMEM((width, cols), BF16),
            dma((2,)),
            dma((members, count)),
        ]
    else:
        part = (width // count, weight_terms[0].shape[1] + weight_terms[2].shape[1])
        batches = lax.axis_size("batch")
        head = qkv_from.shape[2:]
        late_out = [(batches,) + part, (members, count // 2) + head]
        messages = (2, count - 1) + part
        late_scratch = [
            pltpu.VMEM(qkv_from.shape, BF16),
            dma((2, members)),
            pltpu.VMEM(messages, BF16),
            pltpu.VMEM(messages, BF16),
            pltpu.VMEM((batches,) + part, BF16),
            pltpu.VMEM((count,) + head, BF16),
            pltpu.VMEM((count,) + head, BF16),
            pltpu.SemaphoreType.DMA((2, 4 * (count - 1) + count + members + 3)),
        ]
    any_spec = pl.BlockSpec(memory_space=pl.ANY)
    fixed = lambda step: (0, 0)
    parts_rows = rows if index else 2 * rows
    return pl.pallas_call(
        functools.partial(return_kernel, count, chunks, 2, index, kinds),
        grid=(1,),
        in_specs=[
            pl.BlockSpec((count, parts_rows, cols), lambda step: (0, index, 0)),
            any_spec,
            any_spec,
            any_spec,
            any_spec,
            pl.BlockSpec((1, width), fixed),
            pl.BlockSpec(vectors.shape, fixed),
        ]
        + [any_spec] * (len(extras) + len(late_in) + 1),
        out_specs=[
            pl.BlockSpec((rows, width), fixed),
            pl.BlockSpec((8, width), fixed),
            pl.BlockSpec(small, fixed),
            any_spec,
        ]
        + [any_spec] * (len(extras) + len(late_out)),
        out_shape=[
            jax.ShapeDtypeStruct((rows, width), BF16),
            jax.ShapeDtypeStruct((8, width), F32),
            jax.ShapeDtypeStruct(small, F32),
            jax.ShapeDtypeStruct((rows, width), BF16),
        ]
        + [jax.ShapeDtypeStruct(source.shape, BF16) for source in sources]
        + [jax.ShapeDtypeStruct(shape, BF16) for shape in late_out],
        scratch_shapes=[
            pltpu.VMEM((width, cols), BF16),
            pltpu.VMEM((width, cols), BF16),
            pltpu.VMEM((rows, width), F32),
        ]
        + [pltpu.VMEM(each.shape, BF16) for each in late_in]
        + [
            pltpu.VMEM((rows, width), F32),
            pltpu.VMEM((2, count - 1, rows, width), BF16),
            pltpu.VMEM((2, count - 1, rows, width), BF16),
            pltpu.VMEM((count - 1, rows, cols), BF16),
            pltpu.VMEM((rows // chunks, width), F32),
            pltpu.VMEM((members,) + small, F32),
            pltpu.VMEM((count,) + small, F32),
            dma((4 + len(late_in),)),
            dma((2, count - 1, chunks)),
            dma((2, count - 1, chunks)),
            dma((chunks,)),
            dma((chunks,)),
            dma((2, members + count - 2)),
        ]
        + [dma((2, extra_moves(*extra))) for extra in extras]
        + late_scratch,
        compiler_params=pltpu.CompilerParams(
            collective_id=1 + index, has_side_effects=True, vmem_limit_bytes=VMEM_LIMIT
        ),
        cost_estimate=pl.CostEstimate(flops=80_000_000_000, bytes_accessed=1, transcendentals=0),
    )(parts, weight, edge_weight, layer_input, hidden_grad, gain, vectors, *sources, *late_in, qkv_from)


def weight_grad_kernel(
    tile,
    second_ref,
    grad_ref,
    hidden_ref,
    pre_ref,
    act_ref,
    att_ref,
    trade_source,
    pair_source,
    keep,
    away,
    down_own,
    down_near,
    trade_target,
    pair_target,
    turned,
    slots,
    sending,
    received,
    slot_sems,
    send_sems,
    recv_sems,
    out_sems,
    pair_sems,
    *trade_sems,
):
    rows, width = second_ref.shape
    units = pre_ref.shape[1]
    me = lax.axis_index("batch")
    place = lax.axis_index("mp")
    parity = me % 2
    mate = me + 1 - 2 * parity
    barrier = pltpu.get_barrier_semaphore()
    pl.semaphore_signal(barrier, inc=1, device_id={"batch": mate}, device_id_type=MESH)
    trade = Trade(trade_source, trade_target, *trade_sems, (pair_source, pair_target, pair_sems))
    trade.greet()

    depth = slots.shape[0]
    piece = units // 4
    head_piece = width // 4
    side = (me // 2) % 2
    jobs = []
    for half, first_sent, first_kept in (
        (0, (1 - parity) * piece, parity * piece),
        (1, 3 * piece, 2 * piece),
    ):
        for target, start in ((away, (1 - side) * tile), (keep, side * tile)):
            puts = [(0, tile, target.at[half], 0)]
            jobs.append((0, pre_ref, tile, first_sent + start, first_kept + start, puts))
    for target, first_sent, first_kept in (
        (down_near, 3 * piece, 2 * piece),
        (down_own, (1 - parity) * piece, parity * piece),
    ):
        for start in range(0, piece, tile):
            puts = [(0, tile, target, start)]
            jobs.append((1, act_ref, tile, first_sent + start, first_kept + start, puts))
    for half, owner in ((0, place), (1, 1 - place)):
        first = 2 * owner * head_piece
        size = head_piece // 2
        puts = [
            (side * size, size, keep.at[half], tile),
            ((1 - side) * size, size, away.at[half], tile),
        ]
        jobs.append(
            (
                2,
                att_ref,
                head_piece,
                first + (1 - parity) * head_piece,
                first + parity * head_piece,
                puts,
            )
        )
    count = len(jobs)
    order = [(job, 3) for job in range(count)] + [(job, 4) for job in range(count)]

    def fetch(index):
        job, which = order[index]
        _, source, size, *_ = jobs[job]
        start = jobs[job][which]
        return pltpu.make_async_copy(
            source.at[:, pl.ds(pl.multiple_of(start, 128), size)],
            slots.at[index % depth, :, pl.ds(0, size)],
            slot_sems.at[index % depth],
        )

    def exchange(job):
        size = jobs[job][2]
        return pltpu.make_async_remote_copy(
            src_ref=sending.at[job, :, pl.ds(0, size)],
            dst_ref=received.at[job, :, pl.ds(0, size)],
            send_sem=send_sems.at[job],
            recv_sem=recv_sems.at[job],
            device_id={"batch": mate},
            device_id_type=MESH,
        )

    def put(job):
        copies = []
        for which, (first, size, target, start) in enumerate(jobs[job][5]):
            from_here = pl.ds(first if isinstance(first, int) else pl.multiple_of(first, 128), size)
            copies.append(
                pltpu.make_async_copy(
                    received.at[job, :, from_here],
                    target.at[:, pl.ds(start, size)],
                    out_sems.at[which, job],
                )
            )
        return copies

    for index in range(depth - 1):
        fetch(index).start()
    block = min(1024, width)
    for matrix, source in enumerate((second_ref, grad_ref, hidden_ref)):

        def turn(index, _):
            here = pl.ds(pl.multiple_of(index * 128, 128), 128)
            turned[matrix, :, here] = source[here, :].T
            return 0

        lax.fori_loop(0, rows // 128, turn, 0)
    trade.start(1)

    for index, (job, which) in enumerate(order):
        matrix, _, size, *_ = jobs[job]
        fetch(index).wait()
        if index + depth - 1 < len(order):
            fetch(index + depth - 1).start()
        if which == 4:
            exchange(job).wait_recv()

        def multiply(part, _):
            here = pl.ds(pl.multiple_of(part * block, block), block)
            total = dot_nn(turned[matrix, here, :], slots[index % depth, :, 0:size])
            if which == 3:
                sending[job, here, 0:size] = total.astype(BF16)
            else:
                total = total + received[job, here, 0:size].astype(F32)
                received[job, here, 0:size] = total.astype(BF16)
            return 0

        lax.fori_loop(0, width // block, multiply, 0)
        if which == 3:
            exchange(job).start()
        else:
            for copy in put(job):
                copy.start()
    for job in range(count):
        exchange(job).wait_send()
        for copy in put(job):
            copy.wait()
    trade.finish()


def weight_grads(second_low, grad_low, hidden_low, pre_grad, activated, attended, source, pair):
    rows, width = second_low.shape
    units = pre_grad.shape[1]
    piece = units // 4
    tile = piece // 2
    jobs = 10
    any_spec = pl.BlockSpec(memory_space=pl.ANY)
    vmem = pl.BlockSpec(memory_space=pltpu.VMEM)
    dma = pltpu.SemaphoreType.DMA
    shapes = [(2, width, tile + width // 8)] * 2 + [(width, piece)] * 2
    return pl.pallas_call(
        functools.partial(weight_grad_kernel, tile),
        in_specs=[vmem] * 3 + [any_spec] * 5,
        out_specs=[any_spec] * 6,
        out_shape=[
            jax.ShapeDtypeStruct(shape, BF16) for shape in shapes + [source.shape, pair.shape]
        ],
        scratch_shapes=[
            pltpu.VMEM((3, width, rows), BF16),
            pltpu.VMEM((3, rows, tile), BF16),
            pltpu.VMEM((jobs, width, tile), BF16),
            pltpu.VMEM((jobs, width, tile), BF16),
            dma((3,)),
            dma((jobs,)),
            dma((jobs,)),
            dma((2, jobs)),
            dma((2,)),
        ]
        + trade_scratch(source.shape[0]),
        compiler_params=pltpu.CompilerParams(
            collective_id=3, has_side_effects=True, vmem_limit_bytes=VMEM_LIMIT
        ),
        cost_estimate=pl.CostEstimate(
            flops=2 * rows * width * (2 * units + width),
            bytes_accessed=4 * rows * units,
            transcendentals=0,
        ),
    )(second_low, grad_low, hidden_low, pre_grad, activated, attended, source, pair)


def swap(value, axis, distance=1):
    size = lax.axis_size(axis)
    return lax.ppermute(value, axis, [(j, j ^ distance) for j in range(size)])


def after(value, *earlier):
    return lax.optimization_barrier((value,) + earlier)[0]


def all_to_all(value):
    return lax.all_to_all(value, "seq", 0, 0, tiled=True)


def halves(value):
    return jnp.split(value, 2, axis=1)


def trade_pieces(value):
    place, count = lax.axis_index("seq"), lax.axis_size("seq")
    pieces = [pick(value, place, count)]
    for distance in range(1, count):
        pairs = [(j, (j + distance) % count) for j in range(count)]
        pieces.append(
            lax.ppermute(pick(value, (place + distance) % count, count), "seq", pairs)
        )
    return pieces


def place_pieces(pieces):
    place, count = lax.axis_index("seq"), len(pieces)
    whole = jnp.concatenate(pieces, axis=0)
    return jnp.roll(whole[::-1], place + 1, axis=0)


def levels_of(axis):
    return [1 << level for level in range(lax.axis_size(axis).bit_length() - 1)]


def gather_small(value):
    place = lax.axis_index("seq")
    count = lax.axis_size("seq")
    parts = [value] + [swap(value, "seq", distance) for distance in range(1, count)]
    stacked = jnp.stack(parts)
    order = jnp.arange(count, dtype=jnp.int32) ^ place
    return jnp.take(stacked, order, axis=0).reshape((-1,) + value.shape[1:])


def pick(value, index, count, axis=0):
    size = value.shape[axis] // count
    return lax.dynamic_slice_in_dim(value, index * size, size, axis)


def assemble_kernel(unit_cols, pieces, heads, up_ref, down_ref, out_ref, qkv_ref):
    batch = lax.axis_index("batch")
    batches = pieces.shape[0]
    levels = batches.bit_length() - 1
    for index in range(batches):
        source = jnp.bitwise_xor(batch, index // 2 + 2 * (index % 2))
        slot = 0
        for level in range(levels):
            slot = slot + ((source >> level) % 2) * (batches >> (level + 1))
        start = 0
        for size, target, turn in (
            (unit_cols, up_ref, False),
            (pieces.shape[2] - 2 * unit_cols, out_ref, True),
            (unit_cols, down_ref, True),
        ):
            value = pieces[index, :, start : start + size].astype(F32)
            here = pl.ds(pl.multiple_of(slot * size, 128), size)
            if turn:
                target[here, :] = value.T
            else:
                target[:, here] = value
            start = start + size
    members, parts, rows, cols = heads.shape
    cols = cols // 3
    for member in range(members):
        here = slice(member * rows, (member + 1) * rows)
        for matrix in range(3):
            for part in range(parts):
                qkv_ref[matrix, here, part * cols : (part + 1) * cols] = heads[
                    member, part, :, matrix * cols : (matrix + 1) * cols
                ].astype(F32)


def assemble(unit_cols, pieces, heads):
    batches, rows, all_cols = pieces.shape
    out_cols = all_cols - 2 * unit_cols
    shapes = [
        (rows, batches * unit_cols),
        (batches * unit_cols, rows),
        (batches * out_cols, rows),
        (3, heads.shape[0] * heads.shape[2], heads.shape[1] * heads.shape[3] // 3),
    ]
    vmem = pl.BlockSpec(memory_space=pltpu.VMEM)
    return pl.pallas_call(
        functools.partial(assemble_kernel, unit_cols),
        in_specs=[vmem] * 2,
        out_specs=[vmem] * 4,
        out_shape=[jax.ShapeDtypeStruct(shape, F32) for shape in shapes],
        compiler_params=pltpu.CompilerParams(vmem_limit_bytes=VMEM_LIMIT),
    )(pieces, heads)


def place_kernel(own_first, own_second, other_first, other_second, out_ref, low, high, in_sems, out_sems):
    place = lax.axis_index("mp")
    pieces, step = low.shape[0], low.shape[1]
    per = pieces // 4

    def fetch(index):
        source = (own_first, own_second, other_first, other_second)[index // per]
        return pltpu.make_async_copy(
            source.at[pl.ds(index % per * step, step)], low.at[index], in_sems.at[index]
        )

    def put(index):
        which = index // per
        sequence = place if which < 2 else 1 - place
        row = ((which % 2) * per + index % per) * step
        return pltpu.make_async_copy(
            high.at[index], out_ref.at[sequence, pl.ds(row, step)], out_sems.at[index]
        )

    for index in range(pieces):
        fetch(index).start()
    for index in range(pieces):
        fetch(index).wait()
        high[index] = low[index].astype(F32)
        put(index).start()
    for index in range(pieces):
        put(index).wait()


def both_sequences(own, other):
    rows, width = own[0].shape
    step = min(128, rows)
    pieces = 4 * rows // step
    any_spec = pl.BlockSpec(memory_space=pl.ANY)
    return pl.pallas_call(
        place_kernel,
        in_specs=[any_spec] * 4,
        out_specs=any_spec,
        out_shape=jax.ShapeDtypeStruct((2, 2 * rows, width), F32),
        scratch_shapes=[
            pltpu.VMEM((pieces, step, width), BF16),
            pltpu.VMEM((pieces, step, width), F32),
            pltpu.SemaphoreType.DMA((pieces,)),
            pltpu.SemaphoreType.DMA((pieces,)),
        ],
        compiler_params=pltpu.CompilerParams(vmem_limit_bytes=VMEM_LIMIT),
    )(*own, *other)


def local(
    layer_input,
    lengths,
    random_blocks,
    first_gain,
    first_bias,
    qkv_weight,
    out_weight,
    second_gain,
    second_bias,
    up_weight,
    up_bias,
    down_weight,
    down_bias,
    cotangent,
):
    seq_count = lax.axis_size("seq")
    seq_index = lax.axis_index("seq")
    mp_index = lax.axis_index("mp")
    parity = lax.axis_index("batch") % 2
    _, local_rows, width = layer_input.shape
    rows_total = local_rows * seq_count
    blocks = rows_total // BLOCK
    half_cols = qkv_weight.shape[2]
    cols = width // seq_count
    units = up_weight.shape[1]

    doc_ends = jnp.cumsum(lax.dynamic_index_in_dim(lengths, mp_index, 0, keepdims=False))
    randoms = lax.dynamic_index_in_dim(random_blocks, mp_index, 0, keepdims=False)
    randoms = gather_small(randoms)
    lists, admits = block_lists(jnp.arange(blocks, dtype=jnp.int32), randoms, blocks)
    lists, admits = lists.reshape(-1), admits.reshape(-1)

    first_all, qkv, qkv_own, qkv_edge, out_other, up_near, down_near, bias_near = gather_project(
        layer_input,
        first_gain[None],
        first_bias[None],
        qkv_weight.transpose(1, 0, 2),
        out_weight,
        up_weight,
        down_weight,
        up_bias[None],
    )
    bias_near = bias_near[0]
    first_all = first_all.reshape(rows_total, width)
    qkv = qkv.reshape(rows_total, 3 * cols)
    up_far, down_far, bias_far = (swap(near, "batch") for near in (up_near, down_near, bias_near))
    attended_first, lse_first = attention_forward(0, qkv, doc_ends, lists, admits, seq_count)
    att_pieces = trade_pieces(attended_first)
    attended_second, lse_second = attention_forward(1, qkv, doc_ends, lists, admits, seq_count)
    *att_pieces, attended_second = lax.optimization_barrier((*att_pieces, attended_second))
    att_first = place_pieces(att_pieces)
    att_first, up_far, down_far, bias_far = lax.optimization_barrier(
        (att_first, up_far, down_far, bias_far)
    )
    bias_full = jnp.concatenate([up_bias, bias_near, bias_far])[None]
    outs = [part.reshape(seq_count // 2, cols, width) for part in (out_weight, out_other)]
    kept, results = None, []
    att, source, pair = att_first, attended_second, jnp.zeros((8, 128), BF16)
    for index in range(2):
        result = token_part(
            index,
            doc_ends,
            att,
            layer_input,
            cotangent,
            outs,
            (up_weight, up_near, up_far),
            (down_weight, down_near, down_far),
            bias_full,
            second_gain[None],
            second_bias[None],
            down_bias[None],
            source,
            pair,
            kept,
        )
        kept = result[3:9]
        results.append(result[:3] + result[9:])
        att, source, pair = result[11], result[2], result[0]
        other_output = result[12]
    grad_first = att
    activated, pre_grad, second_low, hidden_low, grad_low, attended_low = kept
    sums = results[0][3][:3] + results[1][3][:3]
    unit_sums = results[0][4][0] + results[1][4][0]
    bias_sums = [unit_sums[:units], unit_sums[units : units * 3 // 2], unit_sums[units * 3 // 2 :]]
    keep, away, down_own, down_near, grad_second, other_second = weight_grads(
        second_low, grad_low, hidden_low, pre_grad, activated, attended_low, source, pair
    )
    outputs, other_outputs = [result[0] for result in results], [other_output, other_second]
    bias_other = jnp.where(
        parity == 0,
        jnp.concatenate([bias_sums[1], bias_sums[2]]),
        jnp.concatenate([bias_sums[2], bias_sums[1]]),
    )
    bias_all = jnp.where(
        mp_index == 0,
        jnp.concatenate([bias_sums[0], bias_other]),
        jnp.concatenate([bias_other, bias_sums[0]]),
    )
    come, down_come = swap(away, "batch", 2), swap(down_near, "mp")
    qkv_low_grad = attention_backward(
        qkv,
        (attended_first, attended_second),
        (grad_first, grad_second),
        (lse_first, lse_second),
        doc_ends,
        lists,
        admits,
    )
    qkv_low_grad, come, down_come = lax.optimization_barrier((qkv_low_grad, come, down_come))
    parts = qkv_low_grad.reshape(seq_count, local_rows, 3 * cols)
    early = jnp.concatenate([sums, bias_all.reshape(-1, width)], axis=0)
    input_first, first_sums, early, _, *weight_terms, qkv_grouped = return_part(
        0,
        parts,
        qkv_own,
        qkv_edge,
        layer_input,
        results[0][1],
        first_gain[None],
        early.reshape(8, -1),
        [],
        (keep, come, down_own, down_come),
        first_all,
    )
    input_second, _, late, other_second, other_first, weights_back, qkv_back = return_part(
        1,
        parts,
        qkv_own,
        qkv_edge,
        layer_input,
        results[1][1],
        first_gain[None],
        first_sums,
        [("mp", input_first)],
        weight_terms,
        qkv_grouped,
    )
    layer_output = both_sequences(outputs, other_outputs)
    input_grad = both_sequences([input_first, input_second], [other_first, other_second])
    up_grad, down_grad, out_grad, qkv_grad = assemble(units // 4, weights_back, qkv_back)
    early, late = early.reshape(-1), late.reshape(-1)
    up_bias_grad = lax.dynamic_slice_in_dim(early, 3 * width + mp_index * units, units)
    return (
        layer_output,
        input_grad,
        late[:width],
        late[width:],
        qkv_grad.transpose(1, 0, 2),
        out_grad,
        early[width : 2 * width],
        early[2 * width : 3 * width],
        up_grad,
        up_bias_grad,
        down_grad,
        early[:width],
    )


MB = 2
NBLK = 64
LEN = 4096
HIGH = lax.Precision.HIGHEST


def segment_of(places, doc_ends):
    return jnp.sum((places[..., None] >= doc_ends).astype(jnp.int32), axis=-1)


def block_lists_by_index(blocks, randoms):
    leading = randoms.shape[:-1]
    globals_part = jnp.broadcast_to(jnp.arange(GLOB, dtype=jnp.int32), leading + (GLOB,))
    window_part = jnp.broadcast_to(
        blocks[:, None] + jnp.arange(WIN, dtype=jnp.int32) - WIN // 2, leading + (WIN,)
    )
    block_list = jnp.concatenate([globals_part, window_part, randoms], axis=-1)
    inside = (block_list >= 0) & (block_list < NBLK)
    same_entry = block_list[..., :, None] == block_list[..., None, :]
    order_ids = jnp.arange(LIST)
    earlier = order_ids[None, :] < order_ids[:, None]
    repeated = jnp.any(same_entry & earlier, axis=-1)
    return (block_list, inside & jnp.logical_not(repeated))


def fetch_rows(key_rows, values, wanted):
    batch_seqs, local_rows, head_cols = key_rows.shape
    total_rows = local_rows * lax.axis_size("seq")
    empty_rows = jnp.zeros((batch_seqs, wanted.shape[1], head_cols), jnp.bfloat16)
    initial = (empty_rows, empty_rows)
    empty_whole = jnp.zeros((batch_seqs, total_rows, head_cols), jnp.bfloat16)
    initial = initial + (empty_whole, empty_whole)
    shards_in = (
        lax.all_gather(key_rows, "seq", axis=1, tiled=True),
        lax.all_gather(values, "seq", axis=1, tiled=True),
    )
    piece_rows = shards_in[0].shape[1]
    inside = ((wanted >= 0) & (wanted < piece_rows))[..., None]
    take_index = jnp.clip(wanted, 0, piece_rows - 1)[..., None]
    picked = tuple(
        (
            jnp.where(inside, jnp.take_along_axis(source, take_index, axis=1), previous)
            for source, previous in zip(shards_in, initial[:2])
        )
    )
    placed = tuple((source for source in shards_in))
    return picked + placed


def scatter_rows(kv_source):
    return lax.psum_scatter(
        kv_source.astype(jnp.bfloat16), "seq", scatter_dimension=0, tiled=True
    ).astype(jnp.float32)


def global_partial(seq_item):
    query_rows, key_rows, value_rows, keep_mask = seq_item
    head_count = query_rows.shape[1] // HD
    query_heads = query_rows.reshape(query_rows.shape[0], head_count, HD)
    key_heads = key_rows.reshape(key_rows.shape[0], head_count, HD)
    value_heads = value_rows.astype(jnp.float32).reshape(value_rows.shape[0], head_count, HD)
    raw_scores = jnp.einsum(
        "qhd,khd->hqk", query_heads, key_heads, preferred_element_type=jnp.float32
    ) * HD ** (-0.5)
    masked = jnp.where(keep_mask[None], raw_scores, NEG)
    row_top = jnp.max(masked, axis=-1)
    weights = jnp.exp(masked - row_top[..., None]) * keep_mask[None].astype(jnp.float32)
    numer = jnp.einsum("hqk,khd->hqd", weights, value_heads, precision=HIGH)
    return (row_top, jnp.sum(weights, axis=-1), numer)


def global_back(seq_item):
    query_rows, key_rows, value_rows, keep_mask, row_top, row_total, glob_out, glob_grad = seq_item
    row_count, head_cols = query_rows.shape
    head_count = head_cols // HD
    query_heads = query_rows.reshape(row_count, head_count, HD)
    key_heads = key_rows.reshape(key_rows.shape[0], head_count, HD)
    value_heads = value_rows.astype(jnp.float32).reshape(value_rows.shape[0], head_count, HD)
    raw_scores = jnp.einsum(
        "qhd,khd->hqk", query_heads, key_heads, preferred_element_type=jnp.float32
    ) * HD ** (-0.5)
    masked = jnp.where(keep_mask[None], raw_scores, NEG)
    probs_glob = (
        jnp.exp(masked - row_top[..., None])
        * keep_mask[None].astype(jnp.float32)
        / row_total[..., None]
    )
    grad_heads = glob_grad.astype(jnp.float32).reshape(row_count, head_count, HD)
    prob_grad = jnp.einsum("qhd,khd->hqk", grad_heads, value_heads, precision=HIGH)
    delta = jnp.einsum("qhd,hqd->hq", grad_heads, glob_out, precision=HIGH)
    score_grad = (probs_glob * (prob_grad - delta[..., None])).astype(jnp.bfloat16)
    query_grad = jnp.einsum(
        "hqk,khd->qhd", score_grad, key_heads, preferred_element_type=jnp.float32
    ) * HD ** (-0.5)
    key_grad = jnp.einsum(
        "hqk,qhd->khd", score_grad, query_heads, preferred_element_type=jnp.float32
    ) * HD ** (-0.5)
    value_grad = jnp.einsum("hqk,qhd->khd", probs_glob, grad_heads, precision=HIGH)
    return (
        query_grad.reshape(row_count, head_cols),
        key_grad.reshape(-1, head_cols),
        value_grad.reshape(-1, head_cols),
    )


def local_by_blocks(
    layer_input,
    lengths,
    random_blocks,
    first_gain,
    first_bias,
    qkv_weight,
    out_weight,
    second_gain,
    second_bias,
    up_weight,
    up_bias,
    down_weight,
    down_bias,
    cotangent,
):
    seq_index = lax.axis_index("seq")
    local_seqs, local_rows, model_width = layer_input.shape
    blocks_dev = local_rows // BLOCK
    head_cols = qkv_weight.shape[2]
    head_count = head_cols // HD
    unit_cols = up_weight.shape[1]
    score_scale = HD ** (-0.5)
    glob_rows = GLOB * BLOCK
    batch_seqs = local_seqs // MB
    picked_rows = blocks_dev * LIST * BLOCK
    qkv_flat = qkv_weight.reshape(model_width, 3 * head_cols)
    doc_ends = jnp.cumsum(lengths, axis=1)
    places = seq_index * local_rows + jnp.arange(local_rows, dtype=jnp.int32)
    seg_local = segment_of(places[None, :], doc_ends[:, None, :])
    valid_rows = (places[None, :] < doc_ends[:, -1:]).astype(jnp.float32)
    glob_flag = (places < glob_rows)[None, :, None]
    query_blocks = seq_index * blocks_dev + jnp.arange(blocks_dev, dtype=jnp.int32)
    block_list, admitted = block_lists_by_index(query_blocks, random_blocks)
    key_places = block_list[..., None] * BLOCK + jnp.arange(BLOCK, dtype=jnp.int32)
    key_segs = segment_of(key_places, doc_ends[:, None, None, None, :]).reshape(
        local_seqs, blocks_dev, LIST * BLOCK
    )
    admit_keys = jnp.broadcast_to(admitted[..., None], key_places.shape).reshape(
        local_seqs, blocks_dev, LIST * BLOCK
    )
    query_segs = seg_local.reshape(local_seqs, blocks_dev, BLOCK)
    list_mask = admit_keys[:, :, None, :] & (query_segs[..., None] == key_segs[:, :, None, :])
    wanted_all = jnp.clip(key_places, 0, LEN - 1).reshape(local_seqs, picked_rows)
    glob_segs = segment_of(jnp.arange(glob_rows, dtype=jnp.int32)[None, :], doc_ends[:, None, :])
    qkv_total = jnp.zeros((model_width, 3 * head_cols), jnp.float32)
    out_total = jnp.zeros(out_weight.shape, jnp.float32)
    up_total = jnp.zeros(up_weight.shape, jnp.float32)
    down_total = jnp.zeros(down_weight.shape, jnp.float32)
    gain_one_total = jnp.zeros((model_width,), jnp.float32)
    bias_one_total = jnp.zeros((model_width,), jnp.float32)
    gain_two_total = jnp.zeros((model_width,), jnp.float32)
    bias_two_total = jnp.zeros((model_width,), jnp.float32)
    up_bias_total = jnp.zeros((unit_cols,), jnp.float32)
    down_bias_total = jnp.zeros((model_width,), jnp.float32)
    outputs_all = []
    input_grads = []
    for micro_index in range(MB):
        first_seq = micro_index * batch_seqs
        last_seq = first_seq + batch_seqs
        rows_in = layer_input[first_seq:last_seq]
        ends_now = doc_ends[first_seq:last_seq]
        valid_now = valid_rows[first_seq:last_seq]
        mask_now = list_mask[first_seq:last_seq]
        wanted = wanted_all[first_seq:last_seq]
        glob_segs_now = glob_segs[first_seq:last_seq]
        normed_one, inverse_one = norm_stats(rows_in)
        first_low = (
            (normed_one * first_gain + first_bias).astype(jnp.bfloat16).reshape(-1, model_width)
        )
        qkv_rows = (
            jnp.dot(first_low, qkv_flat, preferred_element_type=jnp.float32)
            .astype(jnp.bfloat16)
            .reshape(batch_seqs, local_rows, 3, head_cols)
        )
        queries = qkv_rows[:, :, 0]
        key_rows = qkv_rows[:, :, 1]
        values = qkv_rows[:, :, 2]
        glob_queries_own = queries[:, :glob_rows]
        picked_keys, picked_values, whole_keys, whole_values = fetch_rows(key_rows, values, wanted)
        glob_queries = glob_queries_own
        seg_whole = segment_of(jnp.arange(LEN, dtype=jnp.int32)[None, :], ends_now[:, None, :])
        glob_mask = glob_segs_now[:, :, None] == seg_whole[:, None, :]

        def global_here():
            return lax.map(global_partial, (glob_queries, whole_keys, whole_values, glob_mask))

        def global_skip():
            return (
                jnp.zeros((batch_seqs, head_count, glob_rows), jnp.float32),
                jnp.ones((batch_seqs, head_count, glob_rows), jnp.float32),
                jnp.zeros((batch_seqs, head_count, glob_rows, HD), jnp.float32),
            )

        glob_top, glob_total, glob_numer = lax.cond(seq_index == 0, global_here, global_skip)
        glob_out = glob_numer / glob_total[..., None]
        query_split = queries.reshape(batch_seqs, blocks_dev, BLOCK, head_count, HD)
        key_split = picked_keys.reshape(batch_seqs, blocks_dev, LIST * BLOCK, head_count, HD)
        value_split = picked_values.reshape(batch_seqs, blocks_dev, LIST * BLOCK, head_count, HD)
        raw_scores = (
            jnp.einsum(
                "sbqhd,sbkhd->sbhqk", query_split, key_split, preferred_element_type=jnp.float32
            )
            * score_scale
        )
        keep_now = mask_now[:, :, None]
        masked = jnp.where(keep_now, raw_scores, NEG)
        row_top = jnp.max(masked, axis=-1, keepdims=True)
        weights = jnp.exp(masked - row_top) * keep_now.astype(jnp.float32)
        row_total = jnp.sum(weights, axis=-1, keepdims=True)
        probs_list = weights / row_total
        probs_low = probs_list.astype(jnp.bfloat16)
        listed = jnp.einsum(
            "sbhqk,sbkhd->sbqhd", probs_low, value_split, preferred_element_type=jnp.float32
        ).reshape(batch_seqs, local_rows, head_cols)
        glob_rows_out = jnp.transpose(glob_out, (0, 2, 1, 3)).reshape(
            batch_seqs, glob_rows, head_cols
        )
        glob_full = jnp.pad(glob_rows_out, ((0, 0), (0, local_rows - glob_rows), (0, 0)))
        attended = jnp.where(glob_flag, glob_full, listed) * valid_now[..., None]
        attended_low = attended.astype(jnp.bfloat16).reshape(-1, head_cols)
        branch = lax.psum(
            jnp.dot(attended_low, out_weight, preferred_element_type=jnp.float32).astype(
                jnp.bfloat16
            ),
            "mp",
        ).astype(jnp.float32)
        hidden = rows_in + branch.reshape(rows_in.shape)
        normed_two, inverse_two = norm_stats(hidden)
        second_low = (
            (normed_two * second_gain + second_bias).astype(jnp.bfloat16).reshape(-1, model_width)
        )
        pre_act = jnp.dot(second_low, up_weight, preferred_element_type=jnp.float32) + up_bias
        activated = jax.nn.gelu(pre_act, approximate=True).astype(jnp.bfloat16)
        ffn_branch = lax.psum(
            jnp.dot(activated, down_weight, preferred_element_type=jnp.float32).astype(
                jnp.bfloat16
            ),
            "mp",
        ).astype(jnp.float32)
        outputs_all.append(hidden + ffn_branch.reshape(rows_in.shape) + down_bias)
        grad_rows = cotangent[first_seq:last_seq].reshape(-1, model_width)
        down_bias_total = down_bias_total + jnp.sum(grad_rows, axis=0)
        grad_low = grad_rows.astype(jnp.bfloat16)
        down_total = down_total + jnp.einsum(
            "rf,rd->fd", activated, grad_low, preferred_element_type=jnp.float32
        )
        act_grad = jnp.einsum(
            "rd,fd->rf", grad_low, down_weight, preferred_element_type=jnp.float32
        )
        _, gelu_pull = jax.vjp(lambda inner: jax.nn.gelu(inner, approximate=True), pre_act)
        pre_grad = gelu_pull(act_grad)[0].astype(jnp.bfloat16)
        up_bias_total = up_bias_total + jnp.sum(pre_grad.astype(jnp.float32), axis=0)
        up_total = up_total + jnp.einsum(
            "rd,rf->df", second_low, pre_grad, preferred_element_type=jnp.float32
        )
        second_grad = (
            lax.psum(
                jnp.einsum(
                    "rf,df->rd", pre_grad, up_weight, preferred_element_type=jnp.float32
                ).astype(jnp.bfloat16),
                "mp",
            )
            .astype(jnp.float32)
            .reshape(rows_in.shape)
        )
        gain_two_total = gain_two_total + jnp.sum(second_grad * normed_two, axis=(0, 1))
        bias_two_total = bias_two_total + jnp.sum(second_grad, axis=(0, 1))
        hidden_grad = grad_rows.reshape(rows_in.shape) + norm_back(
            second_grad, normed_two, inverse_two, second_gain
        )
        hidden_low = hidden_grad.astype(jnp.bfloat16).reshape(-1, model_width)
        out_total = out_total + jnp.einsum(
            "rc,rd->cd", attended_low, hidden_low, preferred_element_type=jnp.float32
        )
        attended_grad = jnp.einsum(
            "rd,cd->rc", hidden_low, out_weight, preferred_element_type=jnp.float32
        ).astype(jnp.bfloat16).reshape(batch_seqs, local_rows, head_cols) * valid_now[
            ..., None
        ].astype(
            jnp.bfloat16
        )
        list_grad = jnp.where(glob_flag, jnp.zeros_like(attended_grad), attended_grad).reshape(
            batch_seqs, blocks_dev, BLOCK, head_count, HD
        )
        prob_grad = jnp.einsum(
            "sbqhd,sbkhd->sbhqk", list_grad, value_split, preferred_element_type=jnp.float32
        )
        delta = jnp.sum(probs_list * prob_grad, axis=-1, keepdims=True)
        score_grad = (probs_list * (prob_grad - delta)).astype(jnp.bfloat16)
        query_grad = (
            jnp.einsum(
                "sbhqk,sbkhd->sbqhd", score_grad, key_split, preferred_element_type=jnp.float32
            )
            * score_scale
        ).reshape(batch_seqs, local_rows, head_cols)
        key_picked_grad = (
            jnp.einsum(
                "sbhqk,sbqhd->sbkhd", score_grad, query_split, preferred_element_type=jnp.float32
            )
            * score_scale
        )
        value_picked_grad = jnp.einsum(
            "sbhqk,sbqhd->sbkhd", probs_low, list_grad, preferred_element_type=jnp.float32
        )
        picked_grads = jnp.concatenate(
            [
                key_picked_grad.reshape(batch_seqs, picked_rows, head_cols),
                value_picked_grad.reshape(batch_seqs, picked_rows, head_cols),
            ],
            axis=-1,
        )
        seg_ids = wanted * batch_seqs + jnp.arange(batch_seqs, dtype=jnp.int32)[:, None]
        kv_term = jax.ops.segment_sum(
            picked_grads.reshape(batch_seqs * picked_rows, 2 * head_cols),
            seg_ids.reshape(-1),
            num_segments=LEN * batch_seqs,
        ).reshape(LEN, batch_seqs, 2 * head_cols)
        glob_grad_own = attended_grad[:, :glob_rows]

        def back_here():
            return lax.map(
                global_back,
                (
                    glob_queries,
                    whole_keys,
                    whole_values,
                    glob_mask,
                    glob_top,
                    glob_total,
                    glob_out,
                    glob_grad_own,
                ),
            )

        def back_skip():
            return (
                jnp.zeros((batch_seqs, glob_rows, head_cols), jnp.float32),
                jnp.zeros((batch_seqs, LEN, head_cols), jnp.float32),
                jnp.zeros((batch_seqs, LEN, head_cols), jnp.float32),
            )

        glob_query_grad, whole_key_grad, whole_value_grad = lax.cond(
            seq_index == 0, back_here, back_skip
        )
        glob_dense = jnp.transpose(
            jnp.concatenate([whole_key_grad, whole_value_grad], axis=-1), (1, 0, 2)
        )
        kv_source = kv_term + glob_dense
        kv_grad = jnp.transpose(scatter_rows(kv_source), (1, 0, 2))
        glob_query_full = jnp.pad(glob_query_grad, ((0, 0), (0, local_rows - glob_rows), (0, 0)))
        query_total = query_grad + jnp.where(glob_flag, glob_query_full, 0.0)
        qkv_low_grad = (
            jnp.stack([query_total, kv_grad[..., :head_cols], kv_grad[..., head_cols:]], axis=2)
            .astype(jnp.bfloat16)
            .reshape(-1, 3 * head_cols)
        )
        qkv_total = qkv_total + jnp.einsum(
            "rd,rc->dc", first_low, qkv_low_grad, preferred_element_type=jnp.float32
        )
        first_grad = (
            lax.psum(
                jnp.einsum(
                    "rc,dc->rd", qkv_low_grad, qkv_flat, preferred_element_type=jnp.float32
                ).astype(jnp.bfloat16),
                "mp",
            )
            .astype(jnp.float32)
            .reshape(rows_in.shape)
        )
        gain_one_total = gain_one_total + jnp.sum(first_grad * normed_one, axis=(0, 1))
        bias_one_total = bias_one_total + jnp.sum(first_grad, axis=(0, 1))
        input_grads.append(hidden_grad + norm_back(first_grad, normed_one, inverse_one, first_gain))
    matrix_grads = (
        lax.psum_scatter(
            qkv_total.reshape(model_width, 3, head_cols).astype(jnp.bfloat16),
            "seq",
            scatter_dimension=0,
            tiled=True,
        ).astype(jnp.float32),
        lax.psum_scatter(
            out_total.astype(jnp.bfloat16), "seq", scatter_dimension=1, tiled=True
        ).astype(jnp.float32),
        lax.psum_scatter(
            up_total.astype(jnp.bfloat16), "seq", scatter_dimension=0, tiled=True
        ).astype(jnp.float32),
        lax.psum_scatter(
            down_total.astype(jnp.bfloat16), "seq", scatter_dimension=1, tiled=True
        ).astype(jnp.float32),
    )
    matrix_grads = (
        lax.psum(matrix_grads[0].astype(jnp.bfloat16), "batch").astype(jnp.float32),
        lax.psum(matrix_grads[1].astype(jnp.bfloat16), "batch").astype(jnp.float32),
        lax.psum(matrix_grads[2].astype(jnp.bfloat16), "batch").astype(jnp.float32),
        lax.psum(matrix_grads[3].astype(jnp.bfloat16), "batch").astype(jnp.float32),
    )
    vector_grads = lax.psum(
        (
            gain_one_total,
            bias_one_total,
            gain_two_total,
            bias_two_total,
            up_bias_total,
            down_bias_total,
        ),
        ("seq", "batch"),
    )
    return (
        jnp.concatenate(outputs_all, axis=0),
        jnp.concatenate(input_grads, axis=0),
        vector_grads[0],
        vector_grads[1],
        matrix_grads[0],
        matrix_grads[1],
        vector_grads[2],
        vector_grads[3],
        matrix_grads[2],
        vector_grads[4],
        matrix_grads[3],
        vector_grads[5],
    )


def solution(mesh):
    placed = (
        P("batch", "seq", None),
        P("batch", None),
        P("batch", "seq", None),
        P(),
        P(),
        P(None, None, "mp"),
        P("mp", None),
        P(),
        P(),
        P(None, "mp"),
        P("mp"),
        P("mp", None),
        P(),
        P("batch", "seq", None),
    )
    sizes = mesh.shape
    by_heads = sizes["seq"] in (4, 8) and sizes["batch"] == 4 and sizes["mp"] == 2
    return jax.shard_map(
        local if by_heads else local_by_blocks,
        mesh=mesh,
        in_specs=placed,
        out_specs=(
            P("batch", "seq", None),
            P("batch", "seq", None),
            P(),
            P(),
            P("seq", None, "mp"),
            P("mp", "seq"),
            P(),
            P(),
            P("seq", "mp"),
            P("mp"),
            P("mp", "seq"),
            P(),
        ),
        check_vma=False,
    )
```

```python
import functools

import jax
import jax.numpy as jnp
from jax import lax
from jax.experimental import pallas as pl
from jax.experimental.pallas import tpu as pltpu
from jax.sharding import PartitionSpec as P

BLOCK = 64
GLOB = 2
WIN = 3
HD = 64
LIST = 8

NEG = -1e30
EPS = 1e-05
F32 = jnp.float32
BF16 = jnp.bfloat16
VMEM_LIMIT = 60 * 1024 * 1024


def norm_stats(rows):
    centre = rows - jnp.mean(rows, axis=-1, keepdims=True)
    spread = jnp.mean(centre * centre, axis=-1, keepdims=True)
    inverse = lax.rsqrt(spread + EPS)
    return (centre * inverse, inverse)


def norm_back(grad_out, normed, inverse, gain):
    scaled = grad_out * gain
    return inverse * (
        scaled
        - jnp.mean(scaled, axis=-1, keepdims=True)
        - normed * jnp.mean(scaled * normed, axis=-1, keepdims=True)
    )


def block_lists(blocks, randoms, block_count):
    leading = randoms.shape[:-1]
    globals_part = jnp.broadcast_to(jnp.arange(GLOB, dtype=jnp.int32), leading + (GLOB,))
    window_part = jnp.broadcast_to(
        blocks[:, None] + jnp.arange(WIN, dtype=jnp.int32) - WIN // 2, leading + (WIN,)
    )
    block_list = jnp.concatenate([globals_part, window_part, randoms], axis=-1)
    inside = (block_list >= 0) & (block_list < block_count)
    same_entry = block_list[..., :, None] == block_list[..., None, :]
    order_ids = jnp.arange(LIST)
    earlier = order_ids[None, :] < order_ids[:, None]
    repeated = jnp.any(same_entry & earlier, axis=-1)
    admitted = inside & jnp.logical_not(repeated)
    return (jnp.clip(block_list, 0, block_count - 1), admitted.astype(jnp.int32))


MESH = pl.DeviceIdType.MESH


class Trade:
    def __init__(self, source, target, send_sems, recv_sems, own_sem, pair=None):
        self.source, self.target, self.pair = source, target, pair
        self.send_sems, self.recv_sems, self.own_sem = send_sems, recv_sems, own_sem
        self.count = source.shape[0]
        self.me = lax.axis_index("seq")

    def greet(self):
        barrier = pltpu.get_barrier_semaphore()
        for distance in range(1, self.count):
            other = lax.rem(self.me + distance, self.count)
            pl.semaphore_signal(barrier, inc=1, device_id={"seq": other}, device_id_type=MESH)
        if self.pair is not None:
            partner = 1 - lax.axis_index("mp")
            pl.semaphore_signal(barrier, inc=1, device_id={"mp": partner}, device_id_type=MESH)

    def copy(self, distance):
        other = lax.rem(self.me + distance, self.count)
        return pltpu.make_async_remote_copy(
            src_ref=self.source.at[other],
            dst_ref=self.target.at[self.me],
            send_sem=self.send_sems.at[distance - 1],
            recv_sem=self.recv_sems.at[distance - 1],
            device_id={"seq": other},
            device_id_type=MESH,
        )

    def pair_copy(self):
        source, target, sems = self.pair
        return pltpu.make_async_remote_copy(
            src_ref=source,
            dst_ref=target,
            send_sem=sems.at[0],
            recv_sem=sems.at[1],
            device_id={"mp": 1 - lax.axis_index("mp")},
            device_id_type=MESH,
        )

    def own(self):
        return pltpu.make_async_copy(
            self.source.at[self.me], self.target.at[self.me], self.own_sem.at[0]
        )

    def start(self, others=0):
        others = others + (self.pair is not None)
        pl.semaphore_wait(pltpu.get_barrier_semaphore(), self.count - 1 + others)
        for distance in range(1, self.count):
            self.copy(distance).start()
        if self.pair is not None:
            self.pair_copy().start()
        self.own().start()

    def finish(self):
        for distance in range(1, self.count):
            self.copy(distance).wait()
        if self.pair is not None:
            self.pair_copy().wait()
        self.own().wait()


def trade_scratch(count):
    dma = pltpu.SemaphoreType.DMA
    return [dma((count - 1,)), dma((count - 1,)), dma((1,))]


def segment_at(places, ends_ref):
    total = jnp.zeros(places.shape, jnp.int32)
    for doc in range(ends_ref.shape[0]):
        total = total + (places >= ends_ref[doc]).astype(jnp.int32)
    return total


def head_spread(rows, heads):
    lane_head = lax.broadcasted_iota(jnp.int32, (1, rows.shape[1]), 1) // HD
    return jnp.concatenate(
        [rows * (lane_head == head).astype(F32).astype(rows.dtype) for head in range(heads)], axis=0
    )


def head_fold(wide, heads):
    rows = wide.shape[0] // heads
    lane_head = lax.broadcasted_iota(jnp.int32, (rows, wide.shape[1]), 1) // HD
    folded = jnp.zeros((rows, wide.shape[1]), wide.dtype)
    for head in range(heads):
        folded = jnp.where(lane_head == head, wide[head * rows : (head + 1) * rows], folded)
    return folded


def block_at(block):
    return pl.ds(pl.multiple_of(block * BLOCK, BLOCK), BLOCK)


def fill_segments(token_segs, ends_ref):
    def fill(block, _):
        places = block * BLOCK + lax.broadcasted_iota(jnp.int32, (BLOCK, token_segs.shape[1]), 0)
        token_segs[block_at(block), :] = segment_at(places, ends_ref)
        return 0

    lax.fori_loop(0, token_segs.shape[0] // BLOCK, fill, 0)


def query_segments(block, heads, ends_ref):
    lanes = lax.broadcasted_iota(jnp.int32, (8, heads * BLOCK), 1)
    return segment_at(block * BLOCK + lanes % BLOCK, ends_ref)[0:1]


def key_segments(starts, keeps, ends_ref):
    lanes = lax.broadcasted_iota(jnp.int32, (8, 2 * BLOCK), 1)
    first = lanes < BLOCK
    pieces = []
    for entry in range(0, LIST, 2):
        places = lanes + jnp.where(
            first, starts[entry] * BLOCK, (starts[entry + 1] - 1) * BLOCK
        )
        keep = jnp.where(first, keeps[entry], keeps[entry + 1]) > 0
        pieces.append(jnp.where(keep, segment_at(places, ends_ref), -1))
    return jnp.concatenate(pieces, axis=1)[0:1]


def gathered(ref, starts):
    return jnp.concatenate([ref[block_at(start), :] for start in starts], axis=0)


def block_parts(wide):
    return [wide[start : start + BLOCK] for start in range(0, wide.shape[0], BLOCK)]


def dot_nt(left, right):
    return lax.dot_general(left, right, (((1,), (1,)), ((), ())), preferred_element_type=F32)


def dot_tn(left, right):
    return lax.dot_general(left, right, (((0,), (0,)), ((), ())), preferred_element_type=F32)


def dot_nn(left, right):
    return lax.dot_general(left, right, (((1,), (0,)), ((), ())), preferred_element_type=F32)


def as_row(tall):
    count = tall.shape[0]
    row_ids = lax.broadcasted_iota(jnp.int32, (count, count), 0)
    lane_ids = lax.broadcasted_iota(jnp.int32, (count, count), 1)
    return jnp.sum(jnp.where(row_ids == lane_ids, tall, 0.0), axis=0, keepdims=True)


def together(running):
    while running:
        still = []
        for each in running:
            if next(each, 0) is None:
                still.append(each)
        running = still


def unit_block(unit, half, parts, rows_total):
    per = rows_total // parts // BLOCK // 2
    part = unit // per
    inside = unit - part * per
    return part, inside, part * 2 * per + half * per + inside


def forward_kernel(heads, half, ends_ref, lists_ref, admit_ref, q_ref, k_ref, v_ref, *rest):
    o_ref, lse_ref, token_segs, *held = rest
    held = held[0] if held else None
    scale = HD ** (-0.5)
    rows_total = q_ref.shape[0]
    units = o_ref.shape[0] * o_ref.shape[1] // BLOCK
    first_unit = GLOB if half == 0 else 0
    chunk = LIST * BLOCK
    fill_segments(token_segs, ends_ref)

    def store(unit, wide, top, total):
        part, inside, block = unit_block(unit, half, o_ref.shape[0], rows_total)
        out = head_fold(wide, heads)
        places = block * BLOCK + lax.broadcasted_iota(jnp.int32, out.shape, 0)
        out = jnp.where(places < ends_ref[ends_ref.shape[0] - 1], out, 0.0)
        o_ref[part, block_at(inside), :] = out.astype(BF16)
        lse_ref[unit] = jnp.broadcast_to(as_row(top + jnp.log(total)), lse_ref.shape[1:])

    def kept(block, key_segs):
        own = token_segs[block_at(block), :]
        return jnp.concatenate([own] * (chunk // own.shape[1]), axis=1) == key_segs

    def global_blocks():
        query_wide = jnp.concatenate(
            [head_spread(q_ref[block_at(block), :] * scale, heads) for block in range(GLOB)], axis=0
        )
        wide_rows = GLOB * heads * BLOCK

        def score(part, top):
            here = pl.ds(pl.multiple_of(part * chunk, chunk), chunk)
            places = part * chunk + lax.broadcasted_iota(jnp.int32, (8, chunk), 1)
            key_segs = segment_at(places, ends_ref)[0:1]
            keeps = [kept(block, key_segs) for block in range(GLOB)]
            scores = dot_nt(query_wide, k_ref[here, :])
            tops = []
            for place, rows in enumerate(block_parts(scores)):
                rows = jnp.where(keeps[place // heads], rows, NEG)
                held[place * BLOCK : (place + 1) * BLOCK, here] = rows
                tops.append(jnp.max(rows, axis=1, keepdims=True))
            return jnp.maximum(top, jnp.concatenate(tops, axis=0))

        top = lax.fori_loop(0, rows_total // chunk, score, jnp.full((wide_rows, 1), NEG, F32))

        def gather(part, carried):
            total, wide = carried
            here = pl.ds(pl.multiple_of(part * chunk, chunk), chunk)
            totals, weights = [], []
            for place, part_top in enumerate(block_parts(top)):
                weight = jnp.exp(held[place * BLOCK : (place + 1) * BLOCK, here] - part_top)
                totals.append(jnp.sum(weight, axis=1, keepdims=True))
                weights.append(weight.astype(BF16))
            wide = wide + dot_nn(jnp.concatenate(weights, axis=0), v_ref[here, :])
            return total + jnp.concatenate(totals, axis=0), wide

        total, wide = lax.fori_loop(
            0,
            rows_total // chunk,
            gather,
            (jnp.zeros((wide_rows, 1), F32), jnp.zeros((wide_rows, q_ref.shape[1]), F32)),
        )
        wide = wide * (1.0 / total)
        for block in range(GLOB):
            own = slice(block * heads * BLOCK, (block + 1) * heads * BLOCK)
            store(block, wide[own], top[own], total[own])

    if half == 0:
        global_blocks()

    def listed_block(unit):
        _, _, block = unit_block(unit, half, o_ref.shape[0], rows_total)
        query_wide = head_spread(q_ref[block_at(block), :] * scale, heads)
        starts = [lists_ref[block * LIST + entry] for entry in range(LIST)]
        keeps = [admit_ref[block * LIST + entry] for entry in range(LIST)]
        keep = kept(block, key_segments(starts, keeps, ends_ref))
        scores = dot_nt(query_wide, gathered(k_ref, starts))
        yield
        tops, totals, probs = [], [], []
        for rows in block_parts(scores):
            rows = jnp.where(keep, rows, NEG)
            top = jnp.max(rows, axis=1, keepdims=True)
            weights = jnp.exp(rows - top)
            total = jnp.sum(weights, axis=1, keepdims=True)
            probs.append((weights * (1.0 / total)).astype(BF16))
            tops.append(top)
            totals.append(total)
            yield
        wide = dot_nn(jnp.concatenate(probs, axis=0), gathered(v_ref, starts))
        store(unit, wide, jnp.concatenate(tops, axis=0), jnp.concatenate(totals, axis=0))

    def listed_group(group, _):
        together([listed_block(first_unit + 6 * group + place) for place in range(6)])
        return 0

    lax.fori_loop(0, (units - first_unit) // 6, listed_group, 0)
    together([listed_block(units - 1 - place) for place in range((units - first_unit) % 6)])


def backward_kernel(
    heads,
    ends_ref,
    lists_ref,
    admit_ref,
    q_ref,
    k_ref,
    v_ref,
    o_first,
    o_second,
    do_first,
    do_second,
    lse_first,
    lse_second,
    out_ref,
    token_segs,
    dk_ref,
    dv_ref,
    dq_ref,
):
    scale = HD ** (-0.5)
    rows_total, cols = q_ref.shape
    blocks = rows_total // BLOCK
    pair_rows = 2 * BLOCK
    fill_segments(token_segs, ends_ref)

    def prepare(pair, _):
        here = pl.ds(pl.multiple_of(pair * pair_rows, pair_rows), pair_rows)
        dk_ref[here, :] = jnp.zeros((pair_rows, cols), F32)
        dv_ref[here, :] = jnp.zeros((pair_rows, cols), F32)
        return 0

    lax.fori_loop(0, blocks // 2, prepare, 0)

    parts = o_first.shape[0]
    halves_of = ((o_first, do_first, lse_first), (o_second, do_second, lse_second))

    def query_side(unit, half):
        o_ref, do_ref, lse_ref = halves_of[half]
        part, inside, block = unit_block(unit, half, parts, rows_total)
        query_wide = head_spread(q_ref[block_at(block), :] * scale, heads)
        grad_rows = do_ref[part, block_at(inside), :]
        grad_wide = head_spread(grad_rows, heads)
        product = grad_rows.astype(F32) * o_ref[part, block_at(inside), :].astype(F32)
        spread = head_spread(product.astype(BF16), heads)
        delta = dot_nt(jnp.ones((8, cols), BF16), spread)[0:1]
        seg_row = query_segments(block, heads, ends_ref)
        return query_wide, grad_wide, delta, lse_ref[unit, 0:1], seg_row

    def unit(starts, keeps, query_wide, grad_wide, delta, lse, seg_row, finish_query):
        keys = gathered(k_ref, starts)
        scores = block_parts(dot_nt(keys, query_wide))
        prob_grads = block_parts(dot_nt(gathered(v_ref, starts), grad_wide))
        yield
        probs, score_grads = [], []
        for entry in range(LIST):
            wanted = seg_row if keeps is None else jnp.where(keeps[entry] > 0, seg_row, -1)
            own = token_segs[block_at(starts[entry]), :]
            keep = jnp.concatenate([own] * (seg_row.shape[1] // own.shape[1]), axis=1) == wanted
            prob = jnp.exp(jnp.where(keep, scores[entry], NEG) - lse)
            probs.append(prob.astype(BF16))
            score_grads.append((prob * (prob_grads[entry] - delta)).astype(BF16))
            if entry % 2:
                yield
        score_grad = jnp.concatenate(score_grads, axis=0)
        finish_query(dot_tn(score_grad, keys))
        dk = dot_nn(score_grad, query_wide)
        dv = dot_nn(jnp.concatenate(probs, axis=0), grad_wide)
        yield
        for entry in range(LIST):
            here = block_at(starts[entry])
            dk_ref[here, :] += dk[entry * BLOCK : (entry + 1) * BLOCK]
            dv_ref[here, :] += dv[entry * BLOCK : (entry + 1) * BLOCK]
        yield

    def store_query(block, wide):
        out_ref[block_at(block), 0:cols] = (head_fold(wide, heads) * scale).astype(BF16)

    def global_blocks():
        sides = [query_side(block, 0) for block in range(GLOB)]
        side = [jnp.concatenate(both, axis=axis) for both, axis in zip(zip(*sides), (0, 0, 1, 1, 1))]
        dq_ref[...] = jnp.zeros_like(dq_ref)

        def part_of(part, _):
            def add_query(wide):
                dq_ref[...] += wide

            together([unit([part * LIST + entry for entry in range(LIST)], None, *side, add_query)])
            return 0

        lax.fori_loop(0, blocks // LIST, part_of, 0)
        for block in range(GLOB):
            store_query(block, dq_ref[block * heads * BLOCK : (block + 1) * heads * BLOCK])

    global_blocks()

    def listed_block(place, half):
        _, _, block = unit_block(place, half, parts, rows_total)
        starts = [lists_ref[block * LIST + entry] for entry in range(LIST)]
        keeps = [admit_ref[block * LIST + entry] for entry in range(LIST)]
        return unit(
            starts, keeps, *query_side(place, half), functools.partial(store_query, block)
        )

    for half, first_unit in ((0, GLOB), (1, 0)):
        units = blocks // 2

        def listed_group(group, _):
            together([listed_block(first_unit + 6 * group + place, half) for place in range(6)])
            return 0

        lax.fori_loop(0, (units - first_unit) // 6, listed_group, 0)
        together([listed_block(units - 1 - place, half) for place in range((units - first_unit) % 6)])

    def finish(block, _):
        here = block_at(block)
        out_ref[here, cols : 2 * cols] = dk_ref[here, :].astype(BF16)
        out_ref[here, 2 * cols : 3 * cols] = dv_ref[here, :].astype(BF16)
        return 0

    lax.fori_loop(0, blocks, finish, 0)


def smem():
    return pl.BlockSpec(memory_space=pltpu.SMEM)


def column(rows, cols, index):
    return pl.BlockSpec((rows, cols), lambda step: (0, index))


def attention_forward(half, qkv, doc_ends, lists, admits, parts):
    rows = qkv.shape[0]
    cols = qkv.shape[1] // 3
    heads = cols // HD
    blocks = rows // BLOCK
    out = jax.ShapeDtypeStruct((parts, rows // parts // 2, cols), BF16)
    lse = jax.ShapeDtypeStruct((blocks // 2, 8, heads * BLOCK), F32)
    cube = lambda step: (0, 0, 0)
    return pl.pallas_call(
        functools.partial(forward_kernel, heads, half),
        grid=(1,),
        in_specs=[smem(), smem(), smem()] + [column(rows, cols, part) for part in range(3)],
        out_specs=[pl.BlockSpec(out.shape, cube), pl.BlockSpec(lse.shape, cube)],
        out_shape=[out, lse],
        scratch_shapes=[pltpu.VMEM((rows, 2 * BLOCK), jnp.int32)]
        + ([] if half else [pltpu.VMEM((GLOB * heads * BLOCK, rows), F32)]),
        compiler_params=pltpu.CompilerParams(vmem_limit_bytes=VMEM_LIMIT),
        cost_estimate=pl.CostEstimate(
            flops=rows * LIST * BLOCK * cols * heads * 5,
            bytes_accessed=8 * rows * cols,
            transcendentals=0,
        ),
    )(doc_ends, lists, admits, qkv, qkv, qkv)


def attention_backward(qkv, attended, attended_grad, lse, doc_ends, lists, admits):
    rows = qkv.shape[0]
    cols = qkv.shape[1] // 3
    heads = cols // HD
    cube = lambda step: (0, 0, 0)
    return pl.pallas_call(
        functools.partial(backward_kernel, heads),
        grid=(1,),
        in_specs=[smem(), smem(), smem()]
        + [column(rows, cols, part) for part in range(3)]
        + [pl.BlockSpec(part.shape, cube) for part in (*attended, *attended_grad, *lse)],
        out_specs=column(rows, 3 * cols, 0),
        out_shape=jax.ShapeDtypeStruct((rows, 3 * cols), BF16),
        scratch_shapes=[
            pltpu.VMEM((rows, 2 * BLOCK), jnp.int32),
            pltpu.VMEM((rows, cols), F32),
            pltpu.VMEM((rows, cols), F32),
            pltpu.VMEM((GLOB * heads * BLOCK, cols), F32),
        ],
        compiler_params=pltpu.CompilerParams(vmem_limit_bytes=VMEM_LIMIT),
        cost_estimate=pl.CostEstimate(
            flops=rows * LIST * BLOCK * cols * heads * 15,
            bytes_accessed=20 * rows * cols,
            transcendentals=0,
        ),
    )(doc_ends, lists, admits, qkv, qkv, qkv, *attended, *attended_grad, *lse)


def row_stats(rows):
    mean = jnp.mean(rows, axis=-1, keepdims=True)
    centre = rows - mean
    spread = jnp.mean(centre * centre, axis=-1, keepdims=True)
    inverse = lax.rsqrt(spread + EPS)
    return centre * inverse, inverse


def gelu_pair(inner):
    root = 0.7978845608028654
    cube = 0.044715
    square = inner * inner
    bent = jnp.tanh(inner * (root + (root * cube) * square))
    half = 0.5 + 0.5 * bent
    value = inner * half
    return value, half + value * (1.0 - bent) * (root + (3.0 * root * cube) * square)


def token_kernel(
    tile,
    index,
    ends_ref,
    att_ref,
    x_ref,
    cotangent_ref,
    out_own_ref,
    out_other_ref,
    up_own_ref,
    up_near_ref,
    up_far_ref,
    down_own_ref,
    down_near_ref,
    down_far_ref,
    up_bias_ref,
    gain_ref,
    bias_ref,
    down_bias_ref,
    trade_source,
    pair_source,
    act_in,
    pre_in,
    second_in,
    hidden_in,
    grad_in,
    att_in,
    output_ref,
    hidden_grad_ref,
    datt_ref,
    act_ref,
    pre_ref,
    second_ref,
    hidden_low_ref,
    grad_low_ref,
    att_rows_ref,
    sums_ref,
    unit_sums_ref,
    trade_target,
    pair_target,
    hidden,
    normed,
    inverse,
    ffn,
    second_grad,
    grad_rows,
    up_slots,
    down_slots,
    slot_sems,
    row_sems,
    pair_sems,
    *trade_sems,
):
    step = pl.program_id(0)
    steps = pl.num_programs(0)
    rows = hidden.shape[0]
    parts = att_ref.shape[0]
    tiles = [slice(start, start + tile) for start in range(0, rows, tile)]
    chunk = up_slots.shape[2]
    own_steps = up_own_ref.shape[1] // chunk
    near_steps = up_near_ref.shape[1] // chunk

    def copies(up_from, down_from, index, slot):
        here = pl.ds(pl.multiple_of(index * chunk, chunk), chunk)
        return (
            pltpu.make_async_copy(up_from.at[:, here], up_slots.at[slot], slot_sems.at[0, slot]),
            pltpu.make_async_copy(down_from.at[here], down_slots.at[slot], slot_sems.at[1, slot]),
        )

    def fetch(index):
        def begin(up_from, down_from, first):
            for copy in copies(up_from, down_from, index - first, index % 2):
                copy.start()

        @pl.when(index < own_steps)
        def _():
            begin(up_own_ref, down_own_ref, 0)

        @pl.when((index >= own_steps) & (index < own_steps + near_steps))
        def _():
            begin(up_near_ref, down_near_ref, own_steps)

        @pl.when(index >= own_steps + near_steps)
        def _():
            begin(up_far_ref, down_far_ref, own_steps + near_steps)

    half = parts // 2
    me = lax.axis_index("seq")
    place = lax.axis_index("mp")
    own_place = place * half
    other_place = (1 - place) * half
    first_row = index * rows
    row_copies = [
        pltpu.make_async_copy(source.at[place, pl.ds(first_row, rows)], target, row_sems.at[which])
        for which, (source, target) in enumerate(((x_ref, hidden), (cotangent_ref, grad_rows)))
    ]
    pair = (pair_source, pair_target, pair_sems) if index else None
    trade = Trade(trade_source, trade_target, *trade_sems, pair)
    out_parts = [(own_place + part, out_own_ref, part) for part in range(half)]
    out_parts += [(other_place + part, out_other_ref, part) for part in range(half)]

    @pl.when(step == 0)
    def _():
        for copy in row_copies:
            copy.start()
        fetch(step)
        trade.greet()
        trade.start()

    @pl.when(step + 1 < steps)
    def _():
        fetch(step + 1)

    @pl.when(step == 0)
    def _():
        for copy in row_copies:
            copy.wait()
        for here in tiles:
            total = hidden[here, :]
            for part, weight_ref, index in out_parts:
                total = total + dot_nn(att_ref[part, here, :], weight_ref[index])
            for part in range(parts):
                cols = att_ref.shape[2]
                att_rows_ref[here, part * cols : (part + 1) * cols] = att_ref[part, here, :]
            hidden[here, :] = total
            unit, scale = row_stats(total)
            normed[here, :] = unit
            inverse[here, :] = jnp.broadcast_to(scale, (tile, inverse.shape[1]))
            second_ref[here, :] = (unit * gain_ref[...] + bias_ref[...]).astype(BF16)
            grad_low_ref[here, :] = grad_rows[here, :].astype(BF16)
            ffn[here, :] = jnp.zeros((tile, ffn.shape[1]), F32)
            second_grad[here, :] = jnp.zeros((tile, ffn.shape[1]), F32)

    slot = step % 2
    for copy in copies(up_own_ref, down_own_ref, 0, slot):
        copy.wait()
    up_ref = up_slots.at[slot]
    down_ref = down_slots.at[slot]
    unit_sum = jnp.zeros((1, chunk), F32)
    for here in tiles:
        inner = dot_nn(second_ref[here, :], up_ref[...]) + up_bias_ref[...]
        act_grad = dot_nt(grad_low_ref[here, :], down_ref[...])
        value, slope = gelu_pair(inner)
        value = value.astype(BF16)
        pre_grad = (act_grad * slope).astype(BF16)
        act_ref[here, :] = value
        pre_ref[here, :] = pre_grad
        unit_sum = unit_sum + jnp.sum(pre_grad.astype(F32), axis=0, keepdims=True)
        ffn[here, :] += dot_nn(value, down_ref[...])
        second_grad[here, :] += dot_nt(pre_grad, up_ref[...])
    unit_sums_ref[...] = jnp.broadcast_to(unit_sum, unit_sums_ref.shape)

    @pl.when(step == steps - 1)
    def _():
        width = ffn.shape[1]
        grad_sum = jnp.zeros((1, width), F32)
        gain_sum = jnp.zeros((1, width), F32)
        bias_sum = jnp.zeros((1, width), F32)
        for number, here in enumerate(tiles):
            output_ref[here, :] = (hidden[here, :] + ffn[here, :] + down_bias_ref[...]).astype(BF16)
            grad = grad_rows[here, :]
            back = second_grad[here, :]
            unit = normed[here, :]
            scaled = back * gain_ref[...]
            through = (
                scaled
                - jnp.mean(scaled, axis=-1, keepdims=True)
                - unit * jnp.mean(scaled * unit, axis=-1, keepdims=True)
            )
            total = grad + inverse[here, 0:1] * through
            hidden_grad_ref[here, :] = total
            low = total.astype(BF16)
            hidden_low_ref[here, :] = low
            grad_sum = grad_sum + jnp.sum(grad, axis=0, keepdims=True)
            gain_sum = gain_sum + jnp.sum(back * unit, axis=0, keepdims=True)
            bias_sum = bias_sum + jnp.sum(back, axis=0, keepdims=True)
            for part, weight_ref, piece in out_parts:
                spread = dot_nt(low, weight_ref[piece])
                places = me * 2 * rows + first_row + number * tile
                places = places + lax.broadcasted_iota(jnp.int32, spread.shape, 0)
                inside = places < ends_ref[ends_ref.shape[0] - 1]
                datt_ref[part, here, :] = jnp.where(inside, spread, 0.0).astype(BF16)
        sums_ref[...] = jnp.concatenate(
            [grad_sum, gain_sum, bias_sum, jnp.zeros((5, width), F32)], axis=0
        )
        trade.finish()


def token_part(
    index, doc_ends, att, layer_input, cotangent, outs, ups, downs, up_bias, gain, bias, down_bias, source, pair, kept
):
    parts, rows, cols = att.shape
    width = layer_input.shape[2]
    units = up_bias.shape[1]
    chunk = min(512, units // 4)
    whole = 2 * rows
    shapes = [(whole, units)] * 2 + [(whole, width)] * 4
    if kept is None:
        kept = [jnp.zeros((8, 128), BF16)] * len(shapes)
        aliases = {}
    else:
        aliases = {18 + place: 3 + place for place in range(len(shapes))}
    half = lambda step: (index, 0)
    fixed = lambda step: (0, 0)
    any_spec = pl.BlockSpec(memory_space=pl.ANY)
    cube = lambda step: (0, 0, 0)
    vector = pl.BlockSpec((1, width), fixed)
    return pl.pallas_call(
        functools.partial(token_kernel, min(256, rows), index),
        grid=(units // chunk,),
        in_specs=[
            smem(),
            pl.BlockSpec((parts, rows, cols), cube),
            any_spec,
            any_spec,
            pl.BlockSpec((parts // 2, cols, width), cube),
            pl.BlockSpec((parts // 2, cols, width), cube),
        ]
        + [any_spec] * 6
        + [pl.BlockSpec((1, chunk), lambda step: (0, step)), vector, vector, vector]
        + [any_spec] * (2 + len(shapes)),
        out_specs=[
            pl.BlockSpec((rows, width), fixed),
            pl.BlockSpec((rows, width), fixed),
            pl.BlockSpec((parts, rows, cols), cube),
            pl.BlockSpec((rows, chunk), lambda step: (index, step)),
            pl.BlockSpec((rows, chunk), lambda step: (index, step)),
            pl.BlockSpec((rows, width), half),
            pl.BlockSpec((rows, width), half),
            pl.BlockSpec((rows, width), half),
            pl.BlockSpec((rows, width), half),
            pl.BlockSpec((8, width), fixed),
            pl.BlockSpec((8, chunk), lambda step: (0, step)),
            any_spec,
            any_spec,
        ],
        scratch_shapes=[
            pltpu.VMEM((rows, width), F32),
            pltpu.VMEM((rows, width), F32),
            pltpu.VMEM((rows, 128), F32),
            pltpu.VMEM((rows, width), F32),
            pltpu.VMEM((rows, width), F32),
            pltpu.VMEM((rows, width), F32),
            pltpu.VMEM((2, width, chunk), BF16),
            pltpu.VMEM((2, chunk, width), BF16),
            pltpu.SemaphoreType.DMA((2, 2)),
            pltpu.SemaphoreType.DMA((2,)),
            pltpu.SemaphoreType.DMA((2,)),
        ]
        + trade_scratch(parts),
        out_shape=[
            jax.ShapeDtypeStruct((rows, width), BF16),
            jax.ShapeDtypeStruct((rows, width), F32),
            jax.ShapeDtypeStruct((parts, rows, cols), BF16),
        ]
        + [jax.ShapeDtypeStruct(shape, BF16) for shape in shapes]
        + [
            jax.ShapeDtypeStruct((8, width), F32),
            jax.ShapeDtypeStruct((8, units), F32),
            jax.ShapeDtypeStruct((parts, rows, cols), BF16),
            jax.ShapeDtypeStruct(pair.shape, BF16),
        ],
        input_output_aliases=aliases,
        compiler_params=pltpu.CompilerParams(
            collective_id=5 + index, has_side_effects=True, vmem_limit_bytes=VMEM_LIMIT
        ),
        cost_estimate=pl.CostEstimate(
            flops=rows * width * (8 * units + 4 * width),
            bytes_accessed=8 * units * width,
            transcendentals=0,
        ),
    )(
        doc_ends,
        att,
        layer_input,
        cotangent,
        *outs,
        *ups,
        *downs,
        up_bias,
        gain,
        bias,
        down_bias,
        source,
        pair,
        *kept,
    )


def batch_mate(distance):
    batch = lax.axis_index("batch")
    return batch + distance - 2 * distance * ((batch // distance) % 2)


def greet(me, count, partner, mate):
    barrier = pltpu.get_barrier_semaphore()

    @pl.when(me > 0)
    def _():
        pl.semaphore_signal(barrier, inc=1, device_id={"seq": me - 1}, device_id_type=MESH)

    @pl.when(me < count - 1)
    def _():
        pl.semaphore_signal(barrier, inc=1, device_id={"seq": me + 1}, device_id_type=MESH)

    pl.semaphore_signal(barrier, inc=1, device_id={"mp": partner}, device_id_type=MESH)
    pl.semaphore_signal(barrier, inc=1, device_id={"batch": mate}, device_id_type=MESH)
    pl.semaphore_wait(barrier, jnp.minimum(me, 1) + jnp.minimum(count - 1 - me, 1) + 2)


def gather_kernel(
    count,
    chunks,
    x_ref,
    gain_ref,
    bias_ref,
    weight_ref,
    out_ref,
    up_ref,
    down_ref,
    up_bias_ref,
    all_ref,
    qkv_ref,
    own_ref,
    edge_ref,
    out_other,
    up_near,
    down_near,
    up_bias_near,
    rows_in,
    shards,
    results,
    weight,
    weight_sems,
    fetch_sems,
    load_sems,
    send_sems,
    recv_sems,
    all_sems,
    qkv_sems,
):
    me = lax.axis_index("seq")
    place = lax.axis_index("mp")
    step = rows_in.shape[0] // chunks
    cols = weight.shape[1] // 3

    def at(chunk):
        return pl.ds(pl.multiple_of(chunk * step, step), step)

    def load(chunk):
        return pltpu.make_async_copy(
            x_ref.at[place, at(chunk)], rows_in.at[at(chunk)], load_sems.at[chunk]
        )

    def send(side, hop, chunk):
        shard = me - hop if side == 0 else me + hop
        target = me + 1 if side == 0 else me - 1
        return pltpu.make_async_remote_copy(
            src_ref=shards.at[shard, at(chunk)],
            dst_ref=shards.at[shard, at(chunk)],
            send_sem=send_sems.at[side, hop, chunk],
            recv_sem=recv_sems.at[side, hop, chunk],
            device_id={"seq": target},
            device_id_type=MESH,
        )

    def keep_all(shard, chunk):
        return pltpu.make_async_copy(
            shards.at[shard, at(chunk)], all_ref.at[shard, at(chunk)], all_sems.at[shard, chunk]
        )

    def keep_qkv(shard, chunk):
        return pltpu.make_async_copy(
            results.at[shard, at(chunk)], qkv_ref.at[shard, at(chunk)], qkv_sems.at[shard, chunk]
        )

    def over_chunks(body):
        def run(chunk, _):
            body(chunk)
            return 0

        lax.fori_loop(0, chunks, run, 0)

    over_chunks(lambda chunk: load(chunk).start())
    greet(me, count, 1 - place, batch_mate(2))

    half_cols = weight_ref.shape[2]
    here = (me * cols) // half_cols == place
    heads = pl.ds(pl.multiple_of((me * cols) % half_cols, 128), cols)
    fetches, copies = [], []
    for matrix in range(3):
        source = weight_ref.at[matrix, :, heads]
        target = weight.at[:, pl.ds(matrix * cols, cols)]
        fetches.append(
            pltpu.make_async_remote_copy(
                src_ref=source,
                dst_ref=target,
                send_sem=weight_sems.at[0, matrix],
                recv_sem=weight_sems.at[1, matrix],
                device_id={"mp": 1 - place},
                device_id_type=MESH,
            )
        )
        copies.append(pltpu.make_async_copy(source, target, weight_sems.at[2, matrix]))

    @pl.when(here)
    def _():
        for each in fetches + copies:
            each.start()

    batch = lax.axis_index("batch")
    parity, side = batch % 2, batch // 2
    share = up_near.shape[1] // 2
    quarter = pl.ds(pl.multiple_of((2 * parity + side) * share, share), share)
    there = pl.ds(pl.multiple_of(side * share, share), share)
    half = up_bias_near.shape[1]
    bias_half = pl.ds(pl.multiple_of(parity * half, half), half)

    def give(which, source, target, device):
        return pltpu.make_async_remote_copy(
            src_ref=source,
            dst_ref=target,
            send_sem=fetch_sems.at[0, which],
            recv_sem=fetch_sems.at[1, which],
            device_id=device,
            device_id_type=MESH,
        )

    partner, chip = {"mp": 1 - place}, {"batch": batch + 2 - 4 * side}
    shares = [
        give(0, out_ref, out_other, partner),
        give(1, up_ref.at[:, quarter], up_near.at[:, there], partner),
        give(2, down_ref.at[quarter], down_near.at[there], partner),
        give(3, up_bias_ref.at[:, bias_half], up_bias_near, partner),
    ]
    passed = [
        give(4, up_near.at[:, there], up_near.at[:, there], chip),
        give(5, down_near.at[there], down_near.at[there], chip),
    ]
    for each in (shares[1], shares[2], shares[3], shares[0]):
        each.start()

    def pass_on(which):
        shares[1 + which].wait()
        passed[which].start()

    def norm(chunk):
        load(chunk).wait()
        unit, _ = row_stats(rows_in[at(chunk), :])
        shards[me, at(chunk), :] = (unit * gain_ref[...] + bias_ref[...]).astype(BF16)
        keep_all(me, chunk).start()

        @pl.when(me < count - 1)
        def _():
            send(0, 0, chunk).start()

        @pl.when(me > 0)
        def _():
            send(1, 0, chunk).start()

    over_chunks(norm)

    def project(shard, chunk):
        rows = dot_nn(shards[shard, at(chunk), :], weight[...])
        results[shard, at(chunk), :] = rows.astype(BF16)
        keep_qkv(shard, chunk).start()

    def receive(hop, chunk):
        @pl.when(me >= hop + 1)
        def _():
            send(0, hop, chunk).wait_recv()
            if hop + 1 < count - 1:

                @pl.when(me < count - 1)
                def _():
                    send(0, hop + 1, chunk).start()

            keep_all(me - hop - 1, chunk).start()

        @pl.when(me + hop + 1 < count)
        def _():
            send(1, hop, chunk).wait_recv()
            if hop + 1 < count - 1:

                @pl.when(me > 0)
                def _():
                    send(1, hop + 1, chunk).start()

            keep_all(me + hop + 1, chunk).start()

    for hop in range(count - 2):
        over_chunks(functools.partial(receive, hop))
        if hop == (count - 2) // 2 - 1:
            pass_on(0)

    @pl.when(here)
    def _():
        for each in copies:
            each.wait()

    @pl.when(jnp.logical_not(here))
    def _():
        for each in fetches:
            each.wait_recv()

    keep_weight = pltpu.make_async_copy(weight, own_ref, weight_sems.at[3, 0])
    keep_weight.start()

    last_place = count - 1
    at_end, by_end = (me == 0) | (me == last_place), (me == 1) | (me == last_place - 1)
    low_half = me // (count // 2)
    edge = pltpu.make_async_remote_copy(
        src_ref=weight,
        dst_ref=edge_ref,
        send_sem=weight_sems.at[3, 1],
        recv_sem=weight_sems.at[3, 2],
        device_id={"seq": me + 1 - 2 * low_half},
        device_id_type=MESH,
    )

    @pl.when(at_end)
    def _():
        edge.start()

    def last(chunk):
        project(me, chunk)
        for hop in range(count - 1):
            if hop == count - 2:
                receive(hop, chunk)

            @pl.when(me >= hop + 1)
            def _():
                project(me - hop - 1, chunk)

            @pl.when(me + hop + 1 < count)
            def _():
                project(me + hop + 1, chunk)

        @pl.when(chunk == 1)
        def _():
            pass_on(1)

    over_chunks(last)

    def finish(chunk):
        for hop in range(count - 1):

            @pl.when((me >= hop) & (me < count - 1))
            def _():
                send(0, hop, chunk).wait_send()

            @pl.when((me + hop < count) & (me > 0))
            def _():
                send(1, hop, chunk).wait_send()

        for shard in range(count):
            keep_all(shard, chunk).wait()
            keep_qkv(shard, chunk).wait()

    over_chunks(finish)
    keep_weight.wait()

    @pl.when(at_end)
    def _():
        edge.wait_send()

    @pl.when(by_end)
    def _():
        edge.wait_recv()

    for each in (shares[0], shares[3], *passed):
        each.wait()

    @pl.when(here)
    def _():
        for each in fetches:
            each.wait_send()


def gather_project(layer_input, gain, bias, weight, out_weight, up_weight, down_weight, up_bias):
    count = lax.axis_size("seq")
    _, rows, width = layer_input.shape
    cols = 3 * width // count
    chunks = max(1, rows // 128)
    any_spec = pl.BlockSpec(memory_space=pl.ANY)
    vmem = pl.BlockSpec(memory_space=pltpu.VMEM)
    dma = pltpu.SemaphoreType.DMA
    return pl.pallas_call(
        functools.partial(gather_kernel, count, chunks),
        in_specs=[any_spec, vmem, vmem] + [any_spec] * 5,
        out_specs=[any_spec] * 8,
        out_shape=[
            jax.ShapeDtypeStruct((count, rows, width), BF16),
            jax.ShapeDtypeStruct((count, rows, cols), BF16),
            jax.ShapeDtypeStruct((width, cols), BF16),
            jax.ShapeDtypeStruct((width, cols), BF16),
            jax.ShapeDtypeStruct(out_weight.shape, BF16),
            jax.ShapeDtypeStruct((width, up_weight.shape[1] // 2), BF16),
            jax.ShapeDtypeStruct((down_weight.shape[0] // 2, width), BF16),
            jax.ShapeDtypeStruct((1, up_weight.shape[1] // 2), F32),
        ],
        scratch_shapes=[
            pltpu.VMEM((rows, width), F32),
            pltpu.VMEM((count, rows, width), BF16),
            pltpu.VMEM((count, rows, cols), BF16),
            pltpu.VMEM((width, cols), BF16),
            dma((4, 3)),
            dma((2, 6)),
            dma((chunks,)),
            dma((2, count - 1, chunks)),
            dma((2, count - 1, chunks)),
            dma((count, chunks)),
            dma((count, chunks)),
        ],
        compiler_params=pltpu.CompilerParams(
            collective_id=0, has_side_effects=True, vmem_limit_bytes=VMEM_LIMIT
        ),
        cost_estimate=pl.CostEstimate(
            flops=150_000_000_000, bytes_accessed=1, transcendentals=0
        ),
    )(layer_input, gain, bias, weight, out_weight, up_weight, down_weight, up_bias)


class VectorSum:
    def __init__(self, group, line, sems):
        self.group, self.line, self.sems = group, line, sems
        self.me, self.count = lax.axis_index("seq"), lax.axis_size("seq")
        self.pairs = lax.axis_size("mp")
        self.members = lax.axis_size("batch") * self.pairs
        self.mine = lax.axis_index("batch") * self.pairs + lax.axis_index("mp")

    def member(self, distance):
        other = lax.rem(self.mine + distance, self.members)
        return {"batch": other // self.pairs, "mp": lax.rem(other, self.pairs)}

    def along(self, distance):
        return {"seq": lax.rem(self.me + distance, self.count)}

    def greet(self):
        barrier = pltpu.get_barrier_semaphore()
        for distance in range(1, self.members):
            pl.semaphore_signal(
                barrier, inc=1, device_id=self.member(distance), device_id_type=MESH
            )
        for distance in range(1, self.count):
            pl.semaphore_signal(barrier, inc=1, device_id=self.along(distance), device_id_type=MESH)
        pl.semaphore_wait(barrier, self.members + self.count - 2)

    def share(self, distance, along):
        buffer, place = (self.line, self.me) if along else (self.group, self.mine)
        which = distance - 1 + (self.members - 1 if along else 0)
        return pltpu.make_async_remote_copy(
            src_ref=buffer.at[place],
            dst_ref=buffer.at[place],
            send_sem=self.sems.at[0, which],
            recv_sem=self.sems.at[1, which],
            device_id=self.along(distance) if along else self.member(distance),
            device_id_type=MESH,
        )

    def start(self, value):
        self.group[self.mine] = value
        for distance in range(1, self.members):
            self.share(distance, False).start()

    def middle(self):
        for distance in range(1, self.members):
            self.share(distance, False).wait()
        total = self.group[0]
        for place in range(1, self.members):
            total = total + self.group[place]
        self.line[self.me] = total
        for distance in range(1, self.count):
            self.share(distance, True).start()

    def finish(self):
        for distance in range(1, self.count):
            self.share(distance, True).wait()
        total = self.line[0]
        for place in range(1, self.count):
            total = total + self.line[place]
        return total


class Extra:
    def __init__(self, kind, source, target, sems):
        self.source, self.target, self.sems = source, target, sems
        batch, place = lax.axis_index("batch"), lax.axis_index("mp")
        self.local = None
        if kind == "mp":
            self.moves = [(source, target, {"mp": 1 - place})]
        else:
            count = source.shape[0]
            pairs = lax.axis_size("mp")
            mine = batch * pairs + place
            self.moves = []
            for distance in range(1, count):
                other = lax.rem(mine + distance, count)
                device = {"batch": other // pairs, "mp": lax.rem(other, pairs)}
                self.moves.append((source.at[other], target.at[mine], device))
            self.local = (source.at[mine], target.at[mine])

    def copies(self):
        for index, (source, target, device) in enumerate(self.moves):
            yield pltpu.make_async_remote_copy(
                src_ref=source,
                dst_ref=target,
                send_sem=self.sems.at[0, index],
                recv_sem=self.sems.at[1, index],
                device_id=device,
                device_id_type=MESH,
            )
        if self.local is not None:
            yield pltpu.make_async_copy(*self.local, self.sems.at[0, len(self.moves)])

    def start(self):
        for copy in self.copies():
            copy.start()

    def finish(self):
        for copy in self.copies():
            copy.wait()


def extra_moves(kind, source):
    return 1 if kind == "mp" else source.shape[0]


def in_rows(vectors, width):
    pieces = []
    for row in range(vectors.shape[0]):
        for start in range(0, vectors.shape[1], width):
            pieces.append(vectors[row : row + 1, start : start + width])
    return jnp.concatenate(pieces, axis=0)


class ProjectionGrad:
    def __init__(self, first_all, parts, grouped, slots, total, low, slot_sems, out_sems):
        self.first_all, self.parts, self.grouped = first_all, parts, grouped
        self.slots, self.total, self.low = slots, total, low
        self.slot_sems, self.out_sems = slot_sems, out_sems
        self.rows = slots.shape[1]
        self.steps = first_all.shape[0] // self.rows

    def fetch(self, step):
        return pltpu.make_async_copy(
            self.first_all.at[pl.ds(pl.multiple_of(step * self.rows, self.rows), self.rows)],
            self.slots.at[step % 2],
            self.slot_sems.at[step % 2],
        )

    def start(self):
        self.fetch(0).start()
        self.total[...] = jnp.zeros_like(self.total)

    def multiply(self, step):
        self.fetch(step).wait()

        @pl.when(step + 1 < self.steps)
        def _():
            self.fetch(step + 1).start()

        here = pl.ds(pl.multiple_of((step % 2) * self.rows, self.rows), self.rows)
        grads = self.parts[step // 2, here, :]
        width = self.total.shape[0]
        size = width // 4
        for start in range(0, width, size):
            rows = self.slots[step % 2, :, start : start + size]
            self.total[start : start + size, :] += dot_tn(rows, grads)

        @pl.when(step == self.steps - 1)
        def _():
            self.low[...] = self.total[...].astype(BF16)
            for copy in self.copies():
                copy.start()

    def copies(self):
        members, count, rows, _ = self.grouped.shape
        for member in range(members):
            for part in range(count):
                first = (part * members + member) * rows
                yield pltpu.make_async_copy(
                    self.low.at[pl.ds(first, rows)],
                    self.grouped.at[member, part],
                    self.out_sems.at[member, part],
                )

    def finish(self):
        for copy in self.copies():
            copy.wait()


class WeightBegin:
    def __init__(self, terms, targets, near_sum, own_sum, down_sum, sems):
        self.terms, self.targets, self.sems = terms, targets, sems
        self.near_sum, self.own_sum, self.down_sum = near_sum, own_sum, down_sum

    def copies(self):
        own_out, near_target, down_out, down_target = self.targets
        batch, place = lax.axis_index("batch"), lax.axis_index("mp")
        side = (batch // 2) % 2
        size = self.down_sum.shape[1] // 2
        kept = pl.ds(pl.multiple_of(side * size, 128), size)
        there = pl.ds(pl.multiple_of((1 - side) * size, 128), size)
        return [
            pltpu.make_async_remote_copy(
                src_ref=self.near_sum,
                dst_ref=near_target,
                send_sem=self.sems.at[0],
                recv_sem=self.sems.at[1],
                device_id={"mp": 1 - place},
                device_id_type=MESH,
            ),
            pltpu.make_async_remote_copy(
                src_ref=self.down_sum.at[:, there],
                dst_ref=down_target,
                send_sem=self.sems.at[2],
                recv_sem=self.sems.at[3],
                device_id={"batch": batch + 2 - 4 * side},
                device_id_type=MESH,
            ),
            pltpu.make_async_copy(self.own_sum, own_out, self.sems.at[4]),
            pltpu.make_async_copy(self.down_sum.at[:, kept], down_out, self.sems.at[5]),
        ]

    def start(self):
        keep, come, down, down_come = self.terms
        rows = keep.shape[1]
        step = min(128, rows)

        def add(index, _):
            here = pl.ds(pl.multiple_of(index * step, step), step)
            near = keep[1, here, :].astype(F32) + come[1, here, :].astype(F32)
            own = keep[0, here, :].astype(F32) + come[0, here, :].astype(F32)
            low = down[here, :].astype(F32) + down_come[here, :].astype(F32)
            self.near_sum[here, :] = near.astype(BF16)
            self.own_sum[here, :] = own.astype(BF16)
            self.down_sum[here, :] = low.astype(BF16)
            return 0

        lax.fori_loop(0, rows // step, add, 0)
        for copy in self.copies():
            copy.start()

    def finish(self):
        for copy in self.copies():
            copy.wait()


class WeightChain:
    def __init__(self, terms, qkv_terms, gathered, heads_ref, sending, received, result, head_sum, heads_in, sems):
        self.terms = terms
        self.qkv_terms, self.gathered, self.heads_ref = qkv_terms, gathered, heads_ref
        self.sending, self.received, self.result = sending, received, result
        self.head_sum, self.heads_in, self.sems = head_sum, heads_in, sems
        self.me, self.count = lax.axis_index("seq"), lax.axis_size("seq")
        self.batch, self.place = lax.axis_index("batch"), lax.axis_index("mp")
        self.rows = result.shape[1]
        self.chunks = 2
        self.step = self.rows // self.chunks
        self.steps = (self.count - 1) * self.chunks
        self.members = qkv_terms.shape[0]
        self.mine = self.batch * 2 + self.place
        self.used = 2 * self.steps

    def at(self, chunk):
        return pl.ds(pl.multiple_of(chunk * self.step, self.step), self.step)

    def term(self, target, chunk):
        here = pl.ds(pl.multiple_of(target * self.rows + chunk * self.step, self.step), self.step)
        own, own_come, down, down_come = (term[here, :].astype(F32) for term in self.terms)
        return jnp.concatenate([own + own_come, down + down_come], axis=1)

    def send(self, side, message, chunk):
        which = (side * (self.count - 1) + message) * self.chunks + chunk
        return pltpu.make_async_remote_copy(
            src_ref=self.sending.at[side, message, self.at(chunk)],
            dst_ref=self.received.at[side, message, self.at(chunk)],
            send_sem=self.sems.at[0, which],
            recv_sem=self.sems.at[1, which],
            device_id={"seq": self.me + 1 - 2 * side},
            device_id_type=MESH,
        )

    def flow(self, side, index):
        message, chunk = index // self.chunks, index % self.chunks
        target = (1 - side) * (self.count - 1 - message) + side * message

        @pl.when((target - self.me) * (1 - 2 * side) > 0)
        def _():
            total = self.term(target, chunk)
            first = (1 - side) * self.me + side * (self.count - 1 - self.me)

            @pl.when(first == 0)
            def _():
                self.sending[side, message, self.at(chunk), :] = total.astype(BF16)

            @pl.when(first > 0)
            def _():
                self.send(side, message, chunk).wait_recv()
                come = self.received[side, message, self.at(chunk), :].astype(F32)
                self.sending[side, message, self.at(chunk), :] = (total + come).astype(BF16)

            self.send(side, message, chunk).start()

    def heads_line(self, distance):
        other = lax.rem(self.me + distance, self.count)
        which = self.used + distance - 1
        return pltpu.make_async_remote_copy(
            src_ref=self.head_sum.at[other],
            dst_ref=self.heads_in.at[self.me],
            send_sem=self.sems.at[0, which],
            recv_sem=self.sems.at[1, which],
            device_id={"seq": other},
            device_id_type=MESH,
        )

    def heads_member(self, distance):
        other = lax.rem(self.mine + distance, self.members)
        which = self.used + self.count - 1 + distance - 1
        parts = self.count // 2
        return pltpu.make_async_remote_copy(
            src_ref=self.heads_in.at[pl.ds(lax.rem(other, 2) * parts, parts)],
            dst_ref=self.heads_ref.at[self.mine],
            send_sem=self.sems.at[0, which],
            recv_sem=self.sems.at[1, which],
            device_id={"batch": other // 2, "mp": lax.rem(other, 2)},
            device_id_type=MESH,
        )

    def heads_own(self):
        parts = self.count // 2
        return pltpu.make_async_copy(
            self.heads_in.at[pl.ds(self.place * parts, parts)],
            self.heads_ref.at[self.mine],
            self.sems.at[0, self.used + self.count + self.members - 2],
        )

    def piece(self, index):
        which = self.used + self.count + self.members - 1 + index
        side = (self.batch // 2) % 2
        parity = self.batch % 2
        other = self.batch + 1 - 2 * parity if index else self.batch + 2 - 4 * side
        source = max(index - 1, 0)
        return pltpu.make_async_remote_copy(
            src_ref=self.result.at[source],
            dst_ref=self.result.at[source + (2 if index else 1)],
            send_sem=self.sems.at[0, which],
            recv_sem=self.sems.at[1, which],
            device_id={"batch": other},
            device_id_type=MESH,
        )

    def start(self):
        total = self.qkv_terms[0].astype(F32)
        for member in range(1, self.members):
            total = total + self.qkv_terms[member].astype(F32)
        self.head_sum[...] = total.astype(BF16)
        self.heads_in[self.me] = self.head_sum[self.me]
        for distance in range(1, self.count):
            self.heads_line(distance).start()

    def own(self):
        for chunk in range(self.chunks):
            here = self.at(chunk)
            total = self.term(self.me, chunk)

            @pl.when(self.me > 0)
            def _():
                self.send(0, self.count - 1 - self.me, chunk).wait_recv()

            @pl.when(self.me < self.count - 1)
            def _():
                self.send(1, self.me, chunk).wait_recv()

            left = self.received[0, jnp.minimum(self.count - 1 - self.me, self.count - 2), here, :]
            right = self.received[1, jnp.minimum(self.me, self.count - 2), here, :]
            total = total + jnp.where(self.me > 0, left.astype(F32), 0.0)
            total = total + jnp.where(self.me < self.count - 1, right.astype(F32), 0.0)
            self.result[0, here, :] = total.astype(BF16)
        self.piece(0).start()
        for distance in range(1, self.count):
            self.heads_line(distance).wait()
        for distance in range(1, self.members):
            self.heads_member(distance).start()
        self.heads_own().start()

    def spread(self):
        self.piece(0).wait()
        self.piece(1).start()
        self.piece(2).start()

    def finish(self):
        for index in range(self.steps):
            message, chunk = index // self.chunks, index % self.chunks

            @pl.when(self.count - 1 - message > self.me)
            def _():
                self.send(0, message, chunk).wait_send()

            @pl.when(message < self.me)
            def _():
                self.send(1, message, chunk).wait_send()

        self.piece(1).wait()
        self.piece(2).wait()
        self.heads_own().wait()
        for distance in range(1, self.members):
            self.heads_member(distance).wait()
        copy = pltpu.make_async_copy(
            self.result, self.gathered, self.sems.at[0, self.used + self.count + self.members + 2]
        )
        copy.start()
        copy.wait()


def return_kernel(
    count,
    chunks,
    lag,
    index_of,
    kinds,
    parts_ref,
    weight_from,
    edge_weight_from,
    x_ref,
    hidden_grad_from,
    gain_ref,
    vectors_ref,
    *rest,
):
    extras = len(kinds)
    sources, rest = rest[:extras], rest[extras:]
    terms_from, qkv_from, rest = rest[:4], rest[4], rest[5:]
    input_ref, sums_ref, total_ref, other_ref, *rest = rest
    targets, rest = rest[:extras], rest[extras:]
    late_out, rest = (rest[:2], rest[2:]) if index_of else (rest[:5], rest[5:])
    weight_ref, edge_weight_ref, hidden_grad_ref, *rest = rest
    weight_terms, rest = rest[:4], rest[4:]
    rows_in, sending, received, edge_in, summed, group, line, load_sems, *rest = rest
    send_sems, recv_sems, pair_send_sems, pair_recv_sems, vector_sems, *extra_sems = rest
    late = extra_sems[extras:]
    extras = [Extra(*each) for each in zip(kinds, sources, targets, extra_sems)]
    me = lax.axis_index("seq")
    place = lax.axis_index("mp")
    rows, width = rows_in.shape
    step = rows // chunks
    steps = (count - 1) * chunks

    def at(chunk):
        return pl.ds(pl.multiple_of(chunk * step, step), step)

    pairs = [(weight_from, weight_ref), (edge_weight_from, edge_weight_ref)]
    pairs += list(zip(terms_from, weight_terms))
    pairs += [(hidden_grad_from, hidden_grad_ref), (x_ref.at[place, pl.ds(index_of * rows, rows)], rows_in)]
    loads = [
        pltpu.make_async_copy(source, target, load_sems.at[which])
        for which, (source, target) in enumerate(pairs)
    ]
    for load in loads:
        load.start()
    vector_sum = VectorSum(group, line, vector_sems)
    vector_sum.greet()
    if index_of == 0:
        vector_sum.start(vectors_ref[...])

    def send(side, message, chunk):
        return pltpu.make_async_remote_copy(
            src_ref=sending.at[side, message, at(chunk)],
            dst_ref=received.at[side, message, at(chunk)],
            send_sem=send_sems.at[side, message, chunk],
            recv_sem=recv_sems.at[side, message, chunk],
            device_id={"seq": me + 1 - 2 * side},
            device_id_type=MESH,
        )

    def send_edge(side, message, chunk):
        target = (1 - side) * (count - 1 - message) + side * message
        return pltpu.make_async_remote_copy(
            src_ref=parts_ref.at[target, at(chunk)],
            dst_ref=edge_in.at[message, at(chunk)],
            send_sem=send_sems.at[side, message, chunk],
            recv_sem=recv_sems.at[side, message, chunk],
            device_id={"seq": me + 1 - 2 * side},
            device_id_type=MESH,
        )

    def flow(side, index):
        message = index // chunks
        chunk = index % chunks
        target = (1 - side) * (count - 1 - message) + side * message

        @pl.when((target - me) * (1 - 2 * side) > 0)
        def _():
            first = (1 - side) * me + side * (count - 1 - me)

            @pl.when(first == 0)
            def _():
                send_edge(side, message, chunk).start()

            @pl.when(first == 1)
            def _():
                send_edge(side, message, chunk).wait_recv()
                total = dot_nt(parts_ref[target, at(chunk), :], weight_ref[...])
                total = total + dot_nt(edge_in[message, at(chunk), :], edge_weight_ref[...])
                sending[side, message, at(chunk), :] = total.astype(BF16)
                send(side, message, chunk).start()

            @pl.when(first > 1)
            def _():
                total = dot_nt(parts_ref[target, at(chunk), :], weight_ref[...])
                send(side, message, chunk).wait_recv()
                come = received[side, message, at(chunk), :].astype(F32)
                sending[side, message, at(chunk), :] = (total + come).astype(BF16)
                send(side, message, chunk).start()

    if index_of:
        qkv_terms, qkv_sems, *late = late
        trade = Extra("group", qkv_from, qkv_terms, qkv_sems)
        trade.start()
        for extra in extras:
            extra.start()
        chain = WeightChain(weight_terms, qkv_terms, *late_out, *late)
        begin = None
    else:
        chain = None
        begin = WeightBegin(weight_terms, late_out[:4], *late[:4])
        projection = ProjectionGrad(qkv_from, parts_ref, late_out[4], *late[4:])
        projection.start()
    ahead = chain.steps if chain else 0
    near = me // (count // 2)

    def pair(chunk):
        return pltpu.make_async_remote_copy(
            src_ref=input_ref.at[at(chunk)],
            dst_ref=other_ref.at[at(chunk)],
            send_sem=pair_send_sems.at[chunk],
            recv_sem=pair_recv_sems.at[chunk],
            device_id={"mp": 1 - place},
            device_id_type=MESH,
        )

    def own(chunk):
        here = at(chunk)
        summed[...] = dot_nt(parts_ref[me, here, :], weight_ref[...])
        for side in range(2):
            first = me if side == 0 else count - 1 - me
            message = count - 1 - me if side == 0 else me

            @pl.when(first == 1)
            def _():
                send_edge(side, message, chunk).wait_recv()
                summed[...] += dot_nt(edge_in[message, here, :], edge_weight_ref[...])

            @pl.when(first > 1)
            def _():
                send(side, message, chunk).wait_recv()
                summed[...] += received[side, message, here, :].astype(F32)

        total = summed[...]
        unit, inverse = row_stats(rows_in[here, :])
        scaled = total * gain_ref[...]
        through = (
            scaled
            - jnp.mean(scaled, axis=-1, keepdims=True)
            - unit * jnp.mean(scaled * unit, axis=-1, keepdims=True)
        )
        input_ref[here, :] = (hidden_grad_ref[here, :] + inverse * through).astype(BF16)
        if index_of:
            @pl.when(chunk < chunks - 1)
            def _():
                pair(chunk).start()

        sums_ref[0:1, :] += jnp.sum(total * unit, axis=0, keepdims=True)
        sums_ref[1:2, :] += jnp.sum(total, axis=0, keepdims=True)

    sums_ref[...] = jnp.zeros_like(sums_ref)
    for load in loads[:2] + (loads[2:6] if index_of else []):
        load.wait()
    wait_for = ahead + ((count - 2) * chunks + lag + 1 if index_of else steps + lag)
    steps_all = ahead + steps

    def flow_of(side, index):
        if chain is not None:

            @pl.when(index < ahead)
            def _():
                chain.flow(side, index)

        @pl.when(index >= ahead)
        def _():
            flow(side, index - ahead)

    def advance(index, _):
        @pl.when(index < steps_all)
        def _():
            flow_of(near, index)

        @pl.when((index >= lag) & (index < steps_all + lag))
        def _():
            flow_of(1 - near, index - lag)

        if begin is not None:
            @pl.when(index == 2)
            def _():
                for load in loads[2:6]:
                    load.wait()
                begin.start()

            @pl.when((index >= 3) & (index < 3 + projection.steps))
            def _():
                projection.multiply(index - 3)

        if chain is not None:

            @pl.when(index == 6)
            def _():
                trade.finish()
                chain.start()

            @pl.when(index == ahead + lag)
            def _():
                chain.own()

            @pl.when(index == ahead + lag + 3)
            def _():
                chain.spread()

        @pl.when(index == wait_for)
        def _():
            for load in loads[-2:]:
                load.wait()

        @pl.when(index >= wait_for)
        def _():
            own(index - wait_for)

        return 0

    lax.fori_loop(0, wait_for + chunks, advance, 0)
    if index_of:
        vector_sum.start(in_rows(sums_ref[0:2, :] + vectors_ref[0:2, :], group.shape[2]))
        pair(chunks - 1).start()
    vector_sum.middle()

    def finish(index, _):
        message = index // chunks
        chunk = index % chunks

        @pl.when((count - 1 - message > me) & (me > 0))
        def _():
            send(0, message, chunk).wait_send()

        @pl.when((count - 1 - message > me) & (me == 0))
        def _():
            send_edge(0, message, chunk).wait_send()

        @pl.when((message < me) & (me < count - 1))
        def _():
            send(1, message, chunk).wait_send()

        @pl.when((message < me) & (me == count - 1))
        def _():
            send_edge(1, message, chunk).wait_send()

        return 0

    lax.fori_loop(0, steps, finish, 0)

    def finish_pair(chunk, _):
        pair(chunk).wait()
        return 0

    if index_of:
        lax.fori_loop(0, chunks, finish_pair, 0)
    total_ref[...] = vector_sum.finish()
    if chain is not None:
        chain.finish()
    else:
        begin.finish()
        projection.finish()
    for extra in extras:
        extra.finish()


def return_part(
    index, parts, weight, edge_weight, layer_input, hidden_grad, gain, vectors, extras, weight_terms, qkv_from
):
    count, rows, cols = parts.shape
    rows = rows // 2
    width = weight.shape[0]
    chunks = max(1, rows // 128)
    members = lax.axis_size("batch") * lax.axis_size("mp")
    small = (8, 2 * width // 8) if index else vectors.shape
    kinds, sources = [kind for kind, _ in extras], [source for _, source in extras]
    dma = pltpu.SemaphoreType.DMA
    late_in = [*weight_terms]
    if not index:
        keep, _, down, _ = weight_terms
        half = (width, down.shape[1] // 2)
        grouped = (members, count, width // count // members, cols)
        late_out = [keep.shape[1:], keep.shape[1:], half, half, grouped]
        late_scratch = [
            pltpu.VMEM(keep.shape[1:], BF16),
            pltpu.VMEM(keep.shape[1:], BF16),
            pltpu.VMEM(down.shape, BF16),
            dma((6,)),
            pltpu.VMEM((2, rows, width), BF16),
            pltpu.VMEM((width, cols), F32),
            pltpu.VMEM((width, cols), BF16),
            dma((2,)),
            dma((members, count)),
        ]
    else:
        part = (width // count, weight_terms[0].shape[1] + weight_terms[2].shape[1])
        batches = lax.axis_size("batch")
        head = qkv_from.shape[2:]
        late_out = [(batches,) + part, (members, count // 2) + head]
        messages = (2, count - 1) + part
        late_scratch = [
            pltpu.VMEM(qkv_from.shape, BF16),
            dma((2, members)),
            pltpu.VMEM(messages, BF16),
            pltpu.VMEM(messages, BF16),
            pltpu.VMEM((batches,) + part, BF16),
            pltpu.VMEM((count,) + head, BF16),
            pltpu.VMEM((count,) + head, BF16),
            pltpu.SemaphoreType.DMA((2, 4 * (count - 1) + count + members + 3)),
        ]
    any_spec = pl.BlockSpec(memory_space=pl.ANY)
    fixed = lambda step: (0, 0)
    parts_rows = rows if index else 2 * rows
    return pl.pallas_call(
        functools.partial(return_kernel, count, chunks, 2, index, kinds),
        grid=(1,),
        in_specs=[
            pl.BlockSpec((count, parts_rows, cols), lambda step: (0, index, 0)),
            any_spec,
            any_spec,
            any_spec,
            any_spec,
            pl.BlockSpec((1, width), fixed),
            pl.BlockSpec(vectors.shape, fixed),
        ]
        + [any_spec] * (len(extras) + len(late_in) + 1),
        out_specs=[
            pl.BlockSpec((rows, width), fixed),
            pl.BlockSpec((8, width), fixed),
            pl.BlockSpec(small, fixed),
            any_spec,
        ]
        + [any_spec] * (len(extras) + len(late_out)),
        out_shape=[
            jax.ShapeDtypeStruct((rows, width), BF16),
            jax.ShapeDtypeStruct((8, width), F32),
            jax.ShapeDtypeStruct(small, F32),
            jax.ShapeDtypeStruct((rows, width), BF16),
        ]
        + [jax.ShapeDtypeStruct(source.shape, BF16) for source in sources]
        + [jax.ShapeDtypeStruct(shape, BF16) for shape in late_out],
        scratch_shapes=[
            pltpu.VMEM((width, cols), BF16),
            pltpu.VMEM((width, cols), BF16),
            pltpu.VMEM((rows, width), F32),
        ]
        + [pltpu.VMEM(each.shape, BF16) for each in late_in]
        + [
            pltpu.VMEM((rows, width), F32),
            pltpu.VMEM((2, count - 1, rows, width), BF16),
            pltpu.VMEM((2, count - 1, rows, width), BF16),
            pltpu.VMEM((count - 1, rows, cols), BF16),
            pltpu.VMEM((rows // chunks, width), F32),
            pltpu.VMEM((members,) + small, F32),
            pltpu.VMEM((count,) + small, F32),
            dma((4 + len(late_in),)),
            dma((2, count - 1, chunks)),
            dma((2, count - 1, chunks)),
            dma((chunks,)),
            dma((chunks,)),
            dma((2, members + count - 2)),
        ]
        + [dma((2, extra_moves(*extra))) for extra in extras]
        + late_scratch,
        compiler_params=pltpu.CompilerParams(
            collective_id=1 + index, has_side_effects=True, vmem_limit_bytes=VMEM_LIMIT
        ),
        cost_estimate=pl.CostEstimate(flops=80_000_000_000, bytes_accessed=1, transcendentals=0),
    )(parts, weight, edge_weight, layer_input, hidden_grad, gain, vectors, *sources, *late_in, qkv_from)


def weight_grad_kernel(
    tile,
    second_ref,
    grad_ref,
    hidden_ref,
    pre_ref,
    act_ref,
    att_ref,
    trade_source,
    pair_source,
    keep,
    away,
    down_own,
    down_near,
    trade_target,
    pair_target,
    turned,
    slots,
    sending,
    received,
    slot_sems,
    send_sems,
    recv_sems,
    out_sems,
    pair_sems,
    *trade_sems,
):
    rows, width = second_ref.shape
    units = pre_ref.shape[1]
    me = lax.axis_index("batch")
    place = lax.axis_index("mp")
    parity = me % 2
    mate = me + 1 - 2 * parity
    barrier = pltpu.get_barrier_semaphore()
    pl.semaphore_signal(barrier, inc=1, device_id={"batch": mate}, device_id_type=MESH)
    trade = Trade(trade_source, trade_target, *trade_sems, (pair_source, pair_target, pair_sems))
    trade.greet()

    depth = slots.shape[0]
    piece = units // 4
    head_piece = width // 4
    side = (me // 2) % 2
    jobs = []
    for half, first_sent, first_kept in (
        (0, (1 - parity) * piece, parity * piece),
        (1, 3 * piece, 2 * piece),
    ):
        for target, start in ((away, (1 - side) * tile), (keep, side * tile)):
            puts = [(0, tile, target.at[half], 0)]
            jobs.append((0, pre_ref, tile, first_sent + start, first_kept + start, puts))
    for target, first_sent, first_kept in (
        (down_near, 3 * piece, 2 * piece),
        (down_own, (1 - parity) * piece, parity * piece),
    ):
        for start in range(0, piece, tile):
            puts = [(0, tile, target, start)]
            jobs.append((1, act_ref, tile, first_sent + start, first_kept + start, puts))
    for half, owner in ((0, place), (1, 1 - place)):
        first = 2 * owner * head_piece
        size = head_piece // 2
        puts = [
            (side * size, size, keep.at[half], tile),
            ((1 - side) * size, size, away.at[half], tile),
        ]
        jobs.append(
            (
                2,
                att_ref,
                head_piece,
                first + (1 - parity) * head_piece,
                first + parity * head_piece,
                puts,
            )
        )
    count = len(jobs)
    order = [(job, 3) for job in range(count)] + [(job, 4) for job in range(count)]

    def fetch(index):
        job, which = order[index]
        _, source, size, *_ = jobs[job]
        start = jobs[job][which]
        return pltpu.make_async_copy(
            source.at[:, pl.ds(pl.multiple_of(start, 128), size)],
            slots.at[index % depth, :, pl.ds(0, size)],
            slot_sems.at[index % depth],
        )

    def exchange(job):
        size = jobs[job][2]
        return pltpu.make_async_remote_copy(
            src_ref=sending.at[job, :, pl.ds(0, size)],
            dst_ref=received.at[job, :, pl.ds(0, size)],
            send_sem=send_sems.at[job],
            recv_sem=recv_sems.at[job],
            device_id={"batch": mate},
            device_id_type=MESH,
        )

    def put(job):
        copies = []
        for which, (first, size, target, start) in enumerate(jobs[job][5]):
            from_here = pl.ds(first if isinstance(first, int) else pl.multiple_of(first, 128), size)
            copies.append(
                pltpu.make_async_copy(
                    received.at[job, :, from_here],
                    target.at[:, pl.ds(start, size)],
                    out_sems.at[which, job],
                )
            )
        return copies

    for index in range(depth - 1):
        fetch(index).start()
    block = min(1024, width)
    for matrix, source in enumerate((second_ref, grad_ref, hidden_ref)):

        def turn(index, _):
            here = pl.ds(pl.multiple_of(index * 128, 128), 128)
            turned[matrix, :, here] = source[here, :].T
            return 0

        lax.fori_loop(0, rows // 128, turn, 0)
    trade.start(1)

    for index, (job, which) in enumerate(order):
        matrix, _, size, *_ = jobs[job]
        fetch(index).wait()
        if index + depth - 1 < len(order):
            fetch(index + depth - 1).start()
        if which == 4:
            exchange(job).wait_recv()

        def multiply(part, _):
            here = pl.ds(pl.multiple_of(part * block, block), block)
            total = dot_nn(turned[matrix, here, :], slots[index % depth, :, 0:size])
            if which == 3:
                sending[job, here, 0:size] = total.astype(BF16)
            else:
                total = total + received[job, here, 0:size].astype(F32)
                received[job, here, 0:size] = total.astype(BF16)
            return 0

        lax.fori_loop(0, width // block, multiply, 0)
        if which == 3:
            exchange(job).start()
        else:
            for copy in put(job):
                copy.start()
    for job in range(count):
        exchange(job).wait_send()
        for copy in put(job):
            copy.wait()
    trade.finish()


def weight_grads(second_low, grad_low, hidden_low, pre_grad, activated, attended, source, pair):
    rows, width = second_low.shape
    units = pre_grad.shape[1]
    piece = units // 4
    tile = piece // 2
    jobs = 10
    any_spec = pl.BlockSpec(memory_space=pl.ANY)
    vmem = pl.BlockSpec(memory_space=pltpu.VMEM)
    dma = pltpu.SemaphoreType.DMA
    shapes = [(2, width, tile + width // 8)] * 2 + [(width, piece)] * 2
    return pl.pallas_call(
        functools.partial(weight_grad_kernel, tile),
        in_specs=[vmem] * 3 + [any_spec] * 5,
        out_specs=[any_spec] * 6,
        out_shape=[
            jax.ShapeDtypeStruct(shape, BF16) for shape in shapes + [source.shape, pair.shape]
        ],
        scratch_shapes=[
            pltpu.VMEM((3, width, rows), BF16),
            pltpu.VMEM((3, rows, tile), BF16),
            pltpu.VMEM((jobs, width, tile), BF16),
            pltpu.VMEM((jobs, width, tile), BF16),
            dma((3,)),
            dma((jobs,)),
            dma((jobs,)),
            dma((2, jobs)),
            dma((2,)),
        ]
        + trade_scratch(source.shape[0]),
        compiler_params=pltpu.CompilerParams(
            collective_id=3, has_side_effects=True, vmem_limit_bytes=VMEM_LIMIT
        ),
        cost_estimate=pl.CostEstimate(
            flops=2 * rows * width * (2 * units + width),
            bytes_accessed=4 * rows * units,
            transcendentals=0,
        ),
    )(second_low, grad_low, hidden_low, pre_grad, activated, attended, source, pair)


def swap(value, axis, distance=1):
    size = lax.axis_size(axis)
    return lax.ppermute(value, axis, [(j, j ^ distance) for j in range(size)])


def after(value, *earlier):
    return lax.optimization_barrier((value,) + earlier)[0]


def all_to_all(value):
    return lax.all_to_all(value, "seq", 0, 0, tiled=True)


def halves(value):
    return jnp.split(value, 2, axis=1)


def trade_pieces(value):
    place, count = lax.axis_index("seq"), lax.axis_size("seq")
    pieces = [pick(value, place, count)]
    for distance in range(1, count):
        pairs = [(j, (j + distance) % count) for j in range(count)]
        pieces.append(
            lax.ppermute(pick(value, (place + distance) % count, count), "seq", pairs)
        )
    return pieces


def place_pieces(pieces):
    place, count = lax.axis_index("seq"), len(pieces)
    whole = jnp.concatenate(pieces, axis=0)
    return jnp.roll(whole[::-1], place + 1, axis=0)


def levels_of(axis):
    return [1 << level for level in range(lax.axis_size(axis).bit_length() - 1)]


def gather_small(value):
    place = lax.axis_index("seq")
    count = lax.axis_size("seq")
    parts = [value] + [swap(value, "seq", distance) for distance in range(1, count)]
    stacked = jnp.stack(parts)
    order = jnp.arange(count, dtype=jnp.int32) ^ place
    return jnp.take(stacked, order, axis=0).reshape((-1,) + value.shape[1:])


def pick(value, index, count, axis=0):
    size = value.shape[axis] // count
    return lax.dynamic_slice_in_dim(value, index * size, size, axis)


def assemble_kernel(unit_cols, pieces, heads, up_ref, down_ref, out_ref, qkv_ref):
    batch = lax.axis_index("batch")
    batches = pieces.shape[0]
    levels = batches.bit_length() - 1
    for index in range(batches):
        source = jnp.bitwise_xor(batch, index // 2 + 2 * (index % 2))
        slot = 0
        for level in range(levels):
            slot = slot + ((source >> level) % 2) * (batches >> (level + 1))
        start = 0
        for size, target, turn in (
            (unit_cols, up_ref, False),
            (pieces.shape[2] - 2 * unit_cols, out_ref, True),
            (unit_cols, down_ref, True),
        ):
            value = pieces[index, :, start : start + size].astype(F32)
            here = pl.ds(pl.multiple_of(slot * size, 128), size)
            if turn:
                target[here, :] = value.T
            else:
                target[:, here] = value
            start = start + size
    members, parts, rows, cols = heads.shape
    cols = cols // 3
    for member in range(members):
        here = slice(member * rows, (member + 1) * rows)
        for matrix in range(3):
            for part in range(parts):
                qkv_ref[matrix, here, part * cols : (part + 1) * cols] = heads[
                    member, part, :, matrix * cols : (matrix + 1) * cols
                ].astype(F32)


def assemble(unit_cols, pieces, heads):
    batches, rows, all_cols = pieces.shape
    out_cols = all_cols - 2 * unit_cols
    shapes = [
        (rows, batches * unit_cols),
        (batches * unit_cols, rows),
        (batches * out_cols, rows),
        (3, heads.shape[0] * heads.shape[2], heads.shape[1] * heads.shape[3] // 3),
    ]
    vmem = pl.BlockSpec(memory_space=pltpu.VMEM)
    return pl.pallas_call(
        functools.partial(assemble_kernel, unit_cols),
        in_specs=[vmem] * 2,
        out_specs=[vmem] * 4,
        out_shape=[jax.ShapeDtypeStruct(shape, F32) for shape in shapes],
        compiler_params=pltpu.CompilerParams(vmem_limit_bytes=VMEM_LIMIT),
    )(pieces, heads)


def place_kernel(own_first, own_second, other_first, other_second, out_ref, low, high, in_sems, out_sems):
    place = lax.axis_index("mp")
    pieces, step = low.shape[0], low.shape[1]
    per = pieces // 4

    def fetch(index):
        source = (own_first, own_second, other_first, other_second)[index // per]
        return pltpu.make_async_copy(
            source.at[pl.ds(index % per * step, step)], low.at[index], in_sems.at[index]
        )

    def put(index):
        which = index // per
        sequence = place if which < 2 else 1 - place
        row = ((which % 2) * per + index % per) * step
        return pltpu.make_async_copy(
            high.at[index], out_ref.at[sequence, pl.ds(row, step)], out_sems.at[index]
        )

    for index in range(pieces):
        fetch(index).start()
    for index in range(pieces):
        fetch(index).wait()
        high[index] = low[index].astype(F32)
        put(index).start()
    for index in range(pieces):
        put(index).wait()


def both_sequences(own, other):
    rows, width = own[0].shape
    step = min(128, rows)
    pieces = 4 * rows // step
    any_spec = pl.BlockSpec(memory_space=pl.ANY)
    return pl.pallas_call(
        place_kernel,
        in_specs=[any_spec] * 4,
        out_specs=any_spec,
        out_shape=jax.ShapeDtypeStruct((2, 2 * rows, width), F32),
        scratch_shapes=[
            pltpu.VMEM((pieces, step, width), BF16),
            pltpu.VMEM((pieces, step, width), F32),
            pltpu.SemaphoreType.DMA((pieces,)),
            pltpu.SemaphoreType.DMA((pieces,)),
        ],
        compiler_params=pltpu.CompilerParams(vmem_limit_bytes=VMEM_LIMIT),
    )(*own, *other)


def local(
    layer_input,
    lengths,
    random_blocks,
    first_gain,
    first_bias,
    qkv_weight,
    out_weight,
    second_gain,
    second_bias,
    up_weight,
    up_bias,
    down_weight,
    down_bias,
    cotangent,
):
    seq_count = lax.axis_size("seq")
    seq_index = lax.axis_index("seq")
    mp_index = lax.axis_index("mp")
    parity = lax.axis_index("batch") % 2
    _, local_rows, width = layer_input.shape
    rows_total = local_rows * seq_count
    blocks = rows_total // BLOCK
    half_cols = qkv_weight.shape[2]
    cols = width // seq_count
    units = up_weight.shape[1]

    doc_ends = jnp.cumsum(lax.dynamic_index_in_dim(lengths, mp_index, 0, keepdims=False))
    randoms = lax.dynamic_index_in_dim(random_blocks, mp_index, 0, keepdims=False)
    randoms = gather_small(randoms)
    lists, admits = block_lists(jnp.arange(blocks, dtype=jnp.int32), randoms, blocks)
    lists, admits = lists.reshape(-1), admits.reshape(-1)

    first_all, qkv, qkv_own, qkv_edge, out_other, up_near, down_near, bias_near = gather_project(
        layer_input,
        first_gain[None],
        first_bias[None],
        qkv_weight.transpose(1, 0, 2),
        out_weight,
        up_weight,
        down_weight,
        up_bias[None],
    )
    bias_near = bias_near[0]
    first_all = first_all.reshape(rows_total, width)
    qkv = qkv.reshape(rows_total, 3 * cols)
    up_far, down_far, bias_far = (swap(near, "batch") for near in (up_near, down_near, bias_near))
    attended_first, lse_first = attention_forward(0, qkv, doc_ends, lists, admits, seq_count)
    att_pieces = trade_pieces(attended_first)
    attended_second, lse_second = attention_forward(1, qkv, doc_ends, lists, admits, seq_count)
    *att_pieces, attended_second = lax.optimization_barrier((*att_pieces, attended_second))
    att_first = place_pieces(att_pieces)
    att_first, up_far, down_far, bias_far = lax.optimization_barrier(
        (att_first, up_far, down_far, bias_far)
    )
    bias_full = jnp.concatenate([up_bias, bias_near, bias_far])[None]
    outs = [part.reshape(seq_count // 2, cols, width) for part in (out_weight, out_other)]
    kept, results = None, []
    att, source, pair = att_first, attended_second, jnp.zeros((8, 128), BF16)
    for index in range(2):
        result = token_part(
            index,
            doc_ends,
            att,
            layer_input,
            cotangent,
            outs,
            (up_weight, up_near, up_far),
            (down_weight, down_near, down_far),
            bias_full,
            second_gain[None],
            second_bias[None],
            down_bias[None],
            source,
            pair,
            kept,
        )
        kept = result[3:9]
        results.append(result[:3] + result[9:])
        att, source, pair = result[11], result[2], result[0]
        other_output = result[12]
    grad_first = att
    activated, pre_grad, second_low, hidden_low, grad_low, attended_low = kept
    sums = results[0][3][:3] + results[1][3][:3]
    unit_sums = results[0][4][0] + results[1][4][0]
    bias_sums = [unit_sums[:units], unit_sums[units : units * 3 // 2], unit_sums[units * 3 // 2 :]]
    keep, away, down_own, down_near, grad_second, other_second = weight_grads(
        second_low, grad_low, hidden_low, pre_grad, activated, attended_low, source, pair
    )
    outputs, other_outputs = [result[0] for result in results], [other_output, other_second]
    bias_other = jnp.where(
        parity == 0,
        jnp.concatenate([bias_sums[1], bias_sums[2]]),
        jnp.concatenate([bias_sums[2], bias_sums[1]]),
    )
    bias_all = jnp.where(
        mp_index == 0,
        jnp.concatenate([bias_sums[0], bias_other]),
        jnp.concatenate([bias_other, bias_sums[0]]),
    )
    come, down_come = swap(away, "batch", 2), swap(down_near, "mp")
    qkv_low_grad = attention_backward(
        qkv,
        (attended_first, attended_second),
        (grad_first, grad_second),
        (lse_first, lse_second),
        doc_ends,
        lists,
        admits,
    )
    qkv_low_grad, come, down_come = lax.optimization_barrier((qkv_low_grad, come, down_come))
    parts = qkv_low_grad.reshape(seq_count, local_rows, 3 * cols)
    early = jnp.concatenate([sums, bias_all.reshape(-1, width)], axis=0)
    input_first, first_sums, early, _, *weight_terms, qkv_grouped = return_part(
        0,
        parts,
        qkv_own,
        qkv_edge,
        layer_input,
        results[0][1],
        first_gain[None],
        early.reshape(8, -1),
        [],
        (keep, come, down_own, down_come),
        first_all,
    )
    input_second, _, late, other_second, other_first, weights_back, qkv_back = return_part(
        1,
        parts,
        qkv_own,
        qkv_edge,
        layer_input,
        results[1][1],
        first_gain[None],
        first_sums,
        [("mp", input_first)],
        weight_terms,
        qkv_grouped,
    )
    layer_output = both_sequences(outputs, other_outputs)
    input_grad = both_sequences([input_first, input_second], [other_first, other_second])
    up_grad, down_grad, out_grad, qkv_grad = assemble(units // 4, weights_back, qkv_back)
    early, late = early.reshape(-1), late.reshape(-1)
    up_bias_grad = lax.dynamic_slice_in_dim(early, 3 * width + mp_index * units, units)
    return (
        layer_output,
        input_grad,
        late[:width],
        late[width:],
        qkv_grad.transpose(1, 0, 2),
        out_grad,
        early[width : 2 * width],
        early[2 * width : 3 * width],
        up_grad,
        up_bias_grad,
        down_grad,
        early[:width],
    )


MB = 2
NBLK = 64
LEN = 4096
HIGH = lax.Precision.HIGHEST


def segment_of(places, doc_ends):
    return jnp.sum((places[..., None] >= doc_ends).astype(jnp.int32), axis=-1)


def block_lists_by_index(blocks, randoms):
    leading = randoms.shape[:-1]
    globals_part = jnp.broadcast_to(jnp.arange(GLOB, dtype=jnp.int32), leading + (GLOB,))
    window_part = jnp.broadcast_to(
        blocks[:, None] + jnp.arange(WIN, dtype=jnp.int32) - WIN // 2, leading + (WIN,)
    )
    block_list = jnp.concatenate([globals_part, window_part, randoms], axis=-1)
    inside = (block_list >= 0) & (block_list < NBLK)
    same_entry = block_list[..., :, None] == block_list[..., None, :]
    order_ids = jnp.arange(LIST)
    earlier = order_ids[None, :] < order_ids[:, None]
    repeated = jnp.any(same_entry & earlier, axis=-1)
    return (block_list, inside & jnp.logical_not(repeated))


def fetch_rows(key_rows, values, wanted):
    batch_seqs, local_rows, head_cols = key_rows.shape
    total_rows = local_rows * lax.axis_size("seq")
    empty_rows = jnp.zeros((batch_seqs, wanted.shape[1], head_cols), jnp.bfloat16)
    initial = (empty_rows, empty_rows)
    empty_whole = jnp.zeros((batch_seqs, total_rows, head_cols), jnp.bfloat16)
    initial = initial + (empty_whole, empty_whole)
    shards_in = (
        lax.all_gather(key_rows, "seq", axis=1, tiled=True),
        lax.all_gather(values, "seq", axis=1, tiled=True),
    )
    piece_rows = shards_in[0].shape[1]
    inside = ((wanted >= 0) & (wanted < piece_rows))[..., None]
    take_index = jnp.clip(wanted, 0, piece_rows - 1)[..., None]
    picked = tuple(
        (
            jnp.where(inside, jnp.take_along_axis(source, take_index, axis=1), previous)
            for source, previous in zip(shards_in, initial[:2])
        )
    )
    placed = tuple((source for source in shards_in))
    return picked + placed


def scatter_rows(kv_source):
    return lax.psum_scatter(
        kv_source.astype(jnp.bfloat16), "seq", scatter_dimension=0, tiled=True
    ).astype(jnp.float32)


def global_partial(seq_item):
    query_rows, key_rows, value_rows, keep_mask = seq_item
    head_count = query_rows.shape[1] // HD
    query_heads = query_rows.reshape(query_rows.shape[0], head_count, HD)
    key_heads = key_rows.reshape(key_rows.shape[0], head_count, HD)
    value_heads = value_rows.astype(jnp.float32).reshape(value_rows.shape[0], head_count, HD)
    raw_scores = jnp.einsum(
        "qhd,khd->hqk", query_heads, key_heads, preferred_element_type=jnp.float32
    ) * HD ** (-0.5)
    masked = jnp.where(keep_mask[None], raw_scores, NEG)
    row_top = jnp.max(masked, axis=-1)
    weights = jnp.exp(masked - row_top[..., None]) * keep_mask[None].astype(jnp.float32)
    numer = jnp.einsum("hqk,khd->hqd", weights, value_heads, precision=HIGH)
    return (row_top, jnp.sum(weights, axis=-1), numer)


def global_back(seq_item):
    query_rows, key_rows, value_rows, keep_mask, row_top, row_total, glob_out, glob_grad = seq_item
    row_count, head_cols = query_rows.shape
    head_count = head_cols // HD
    query_heads = query_rows.reshape(row_count, head_count, HD)
    key_heads = key_rows.reshape(key_rows.shape[0], head_count, HD)
    value_heads = value_rows.astype(jnp.float32).reshape(value_rows.shape[0], head_count, HD)
    raw_scores = jnp.einsum(
        "qhd,khd->hqk", query_heads, key_heads, preferred_element_type=jnp.float32
    ) * HD ** (-0.5)
    masked = jnp.where(keep_mask[None], raw_scores, NEG)
    probs_glob = (
        jnp.exp(masked - row_top[..., None])
        * keep_mask[None].astype(jnp.float32)
        / row_total[..., None]
    )
    grad_heads = glob_grad.astype(jnp.float32).reshape(row_count, head_count, HD)
    prob_grad = jnp.einsum("qhd,khd->hqk", grad_heads, value_heads, precision=HIGH)
    delta = jnp.einsum("qhd,hqd->hq", grad_heads, glob_out, precision=HIGH)
    score_grad = (probs_glob * (prob_grad - delta[..., None])).astype(jnp.bfloat16)
    query_grad = jnp.einsum(
        "hqk,khd->qhd", score_grad, key_heads, preferred_element_type=jnp.float32
    ) * HD ** (-0.5)
    key_grad = jnp.einsum(
        "hqk,qhd->khd", score_grad, query_heads, preferred_element_type=jnp.float32
    ) * HD ** (-0.5)
    value_grad = jnp.einsum("hqk,qhd->khd", probs_glob, grad_heads, precision=HIGH)
    return (
        query_grad.reshape(row_count, head_cols),
        key_grad.reshape(-1, head_cols),
        value_grad.reshape(-1, head_cols),
    )


def local_by_blocks(
    layer_input,
    lengths,
    random_blocks,
    first_gain,
    first_bias,
    qkv_weight,
    out_weight,
    second_gain,
    second_bias,
    up_weight,
    up_bias,
    down_weight,
    down_bias,
    cotangent,
):
    seq_index = lax.axis_index("seq")
    local_seqs, local_rows, model_width = layer_input.shape
    blocks_dev = local_rows // BLOCK
    head_cols = qkv_weight.shape[2]
    head_count = head_cols // HD
    unit_cols = up_weight.shape[1]
    score_scale = HD ** (-0.5)
    glob_rows = GLOB * BLOCK
    batch_seqs = local_seqs // MB
    picked_rows = blocks_dev * LIST * BLOCK
    qkv_flat = qkv_weight.reshape(model_width, 3 * head_cols)
    doc_ends = jnp.cumsum(lengths, axis=1)
    places = seq_index * local_rows + jnp.arange(local_rows, dtype=jnp.int32)
    seg_local = segment_of(places[None, :], doc_ends[:, None, :])
    valid_rows = (places[None, :] < doc_ends[:, -1:]).astype(jnp.float32)
    glob_flag = (places < glob_rows)[None, :, None]
    query_blocks = seq_index * blocks_dev + jnp.arange(blocks_dev, dtype=jnp.int32)
    block_list, admitted = block_lists_by_index(query_blocks, random_blocks)
    key_places = block_list[..., None] * BLOCK + jnp.arange(BLOCK, dtype=jnp.int32)
    key_segs = segment_of(key_places, doc_ends[:, None, None, None, :]).reshape(
        local_seqs, blocks_dev, LIST * BLOCK
    )
    admit_keys = jnp.broadcast_to(admitted[..., None], key_places.shape).reshape(
        local_seqs, blocks_dev, LIST * BLOCK
    )
    query_segs = seg_local.reshape(local_seqs, blocks_dev, BLOCK)
    list_mask = admit_keys[:, :, None, :] & (query_segs[..., None] == key_segs[:, :, None, :])
    wanted_all = jnp.clip(key_places, 0, LEN - 1).reshape(local_seqs, picked_rows)
    glob_segs = segment_of(jnp.arange(glob_rows, dtype=jnp.int32)[None, :], doc_ends[:, None, :])
    qkv_total = jnp.zeros((model_width, 3 * head_cols), jnp.float32)
    out_total = jnp.zeros(out_weight.shape, jnp.float32)
    up_total = jnp.zeros(up_weight.shape, jnp.float32)
    down_total = jnp.zeros(down_weight.shape, jnp.float32)
    gain_one_total = jnp.zeros((model_width,), jnp.float32)
    bias_one_total = jnp.zeros((model_width,), jnp.float32)
    gain_two_total = jnp.zeros((model_width,), jnp.float32)
    bias_two_total = jnp.zeros((model_width,), jnp.float32)
    up_bias_total = jnp.zeros((unit_cols,), jnp.float32)
    down_bias_total = jnp.zeros((model_width,), jnp.float32)
    outputs_all = []
    input_grads = []
    for micro_index in range(MB):
        first_seq = micro_index * batch_seqs
        last_seq = first_seq + batch_seqs
        rows_in = layer_input[first_seq:last_seq]
        ends_now = doc_ends[first_seq:last_seq]
        valid_now = valid_rows[first_seq:last_seq]
        mask_now = list_mask[first_seq:last_seq]
        wanted = wanted_all[first_seq:last_seq]
        glob_segs_now = glob_segs[first_seq:last_seq]
        normed_one, inverse_one = norm_stats(rows_in)
        first_low = (
            (normed_one * first_gain + first_bias).astype(jnp.bfloat16).reshape(-1, model_width)
        )
        qkv_rows = (
            jnp.dot(first_low, qkv_flat, preferred_element_type=jnp.float32)
            .astype(jnp.bfloat16)
            .reshape(batch_seqs, local_rows, 3, head_cols)
        )
        queries = qkv_rows[:, :, 0]
        key_rows = qkv_rows[:, :, 1]
        values = qkv_rows[:, :, 2]
        glob_queries_own = queries[:, :glob_rows]
        picked_keys, picked_values, whole_keys, whole_values = fetch_rows(key_rows, values, wanted)
        glob_queries = glob_queries_own
        seg_whole = segment_of(jnp.arange(LEN, dtype=jnp.int32)[None, :], ends_now[:, None, :])
        glob_mask = glob_segs_now[:, :, None] == seg_whole[:, None, :]

        def global_here():
            return lax.map(global_partial, (glob_queries, whole_keys, whole_values, glob_mask))

        def global_skip():
            return (
                jnp.zeros((batch_seqs, head_count, glob_rows), jnp.float32),
                jnp.ones((batch_seqs, head_count, glob_rows), jnp.float32),
                jnp.zeros((batch_seqs, head_count, glob_rows, HD), jnp.float32),
            )

        glob_top, glob_total, glob_numer = lax.cond(seq_index == 0, global_here, global_skip)
        glob_out = glob_numer / glob_total[..., None]
        query_split = queries.reshape(batch_seqs, blocks_dev, BLOCK, head_count, HD)
        key_split = picked_keys.reshape(batch_seqs, blocks_dev, LIST * BLOCK, head_count, HD)
        value_split = picked_values.reshape(batch_seqs, blocks_dev, LIST * BLOCK, head_count, HD)
        raw_scores = (
            jnp.einsum(
                "sbqhd,sbkhd->sbhqk", query_split, key_split, preferred_element_type=jnp.float32
            )
            * score_scale
        )
        keep_now = mask_now[:, :, None]
        masked = jnp.where(keep_now, raw_scores, NEG)
        row_top = jnp.max(masked, axis=-1, keepdims=True)
        weights = jnp.exp(masked - row_top) * keep_now.astype(jnp.float32)
        row_total = jnp.sum(weights, axis=-1, keepdims=True)
        probs_list = weights / row_total
        probs_low = probs_list.astype(jnp.bfloat16)
        listed = jnp.einsum(
            "sbhqk,sbkhd->sbqhd", probs_low, value_split, preferred_element_type=jnp.float32
        ).reshape(batch_seqs, local_rows, head_cols)
        glob_rows_out = jnp.transpose(glob_out, (0, 2, 1, 3)).reshape(
            batch_seqs, glob_rows, head_cols
        )
        glob_full = jnp.pad(glob_rows_out, ((0, 0), (0, local_rows - glob_rows), (0, 0)))
        attended = jnp.where(glob_flag, glob_full, listed) * valid_now[..., None]
        attended_low = attended.astype(jnp.bfloat16).reshape(-1, head_cols)
        branch = lax.psum(
            jnp.dot(attended_low, out_weight, preferred_element_type=jnp.float32).astype(
                jnp.bfloat16
            ),
            "mp",
        ).astype(jnp.float32)
        hidden = rows_in + branch.reshape(rows_in.shape)
        normed_two, inverse_two = norm_stats(hidden)
        second_low = (
            (normed_two * second_gain + second_bias).astype(jnp.bfloat16).reshape(-1, model_width)
        )
        pre_act = jnp.dot(second_low, up_weight, preferred_element_type=jnp.float32) + up_bias
        activated = jax.nn.gelu(pre_act, approximate=True).astype(jnp.bfloat16)
        ffn_branch = lax.psum(
            jnp.dot(activated, down_weight, preferred_element_type=jnp.float32).astype(
                jnp.bfloat16
            ),
            "mp",
        ).astype(jnp.float32)
        outputs_all.append(hidden + ffn_branch.reshape(rows_in.shape) + down_bias)
        grad_rows = cotangent[first_seq:last_seq].reshape(-1, model_width)
        down_bias_total = down_bias_total + jnp.sum(grad_rows, axis=0)
        grad_low = grad_rows.astype(jnp.bfloat16)
        down_total = down_total + jnp.einsum(
            "rf,rd->fd", activated, grad_low, preferred_element_type=jnp.float32
        )
        act_grad = jnp.einsum(
            "rd,fd->rf", grad_low, down_weight, preferred_element_type=jnp.float32
        )
        _, gelu_pull = jax.vjp(lambda inner: jax.nn.gelu(inner, approximate=True), pre_act)
        pre_grad = gelu_pull(act_grad)[0].astype(jnp.bfloat16)
        up_bias_total = up_bias_total + jnp.sum(pre_grad.astype(jnp.float32), axis=0)
        up_total = up_total + jnp.einsum(
            "rd,rf->df", second_low, pre_grad, preferred_element_type=jnp.float32
        )
        second_grad = (
            lax.psum(
                jnp.einsum(
                    "rf,df->rd", pre_grad, up_weight, preferred_element_type=jnp.float32
                ).astype(jnp.bfloat16),
                "mp",
            )
            .astype(jnp.float32)
            .reshape(rows_in.shape)
        )
        gain_two_total = gain_two_total + jnp.sum(second_grad * normed_two, axis=(0, 1))
        bias_two_total = bias_two_total + jnp.sum(second_grad, axis=(0, 1))
        hidden_grad = grad_rows.reshape(rows_in.shape) + norm_back(
            second_grad, normed_two, inverse_two, second_gain
        )
        hidden_low = hidden_grad.astype(jnp.bfloat16).reshape(-1, model_width)
        out_total = out_total + jnp.einsum(
            "rc,rd->cd", attended_low, hidden_low, preferred_element_type=jnp.float32
        )
        attended_grad = jnp.einsum(
            "rd,cd->rc", hidden_low, out_weight, preferred_element_type=jnp.float32
        ).astype(jnp.bfloat16).reshape(batch_seqs, local_rows, head_cols) * valid_now[
            ..., None
        ].astype(
            jnp.bfloat16
        )
        list_grad = jnp.where(glob_flag, jnp.zeros_like(attended_grad), attended_grad).reshape(
            batch_seqs, blocks_dev, BLOCK, head_count, HD
        )
        prob_grad = jnp.einsum(
            "sbqhd,sbkhd->sbhqk", list_grad, value_split, preferred_element_type=jnp.float32
        )
        delta = jnp.sum(probs_list * prob_grad, axis=-1, keepdims=True)
        score_grad = (probs_list * (prob_grad - delta)).astype(jnp.bfloat16)
        query_grad = (
            jnp.einsum(
                "sbhqk,sbkhd->sbqhd", score_grad, key_split, preferred_element_type=jnp.float32
            )
            * score_scale
        ).reshape(batch_seqs, local_rows, head_cols)
        key_picked_grad = (
            jnp.einsum(
                "sbhqk,sbqhd->sbkhd", score_grad, query_split, preferred_element_type=jnp.float32
            )
            * score_scale
        )
        value_picked_grad = jnp.einsum(
            "sbhqk,sbqhd->sbkhd", probs_low, list_grad, preferred_element_type=jnp.float32
        )
        picked_grads = jnp.concatenate(
            [
                key_picked_grad.reshape(batch_seqs, picked_rows, head_cols),
                value_picked_grad.reshape(batch_seqs, picked_rows, head_cols),
            ],
            axis=-1,
        )
        seg_ids = wanted * batch_seqs + jnp.arange(batch_seqs, dtype=jnp.int32)[:, None]
        kv_term = jax.ops.segment_sum(
            picked_grads.reshape(batch_seqs * picked_rows, 2 * head_cols),
            seg_ids.reshape(-1),
            num_segments=LEN * batch_seqs,
        ).reshape(LEN, batch_seqs, 2 * head_cols)
        glob_grad_own = attended_grad[:, :glob_rows]

        def back_here():
            return lax.map(
                global_back,
                (
                    glob_queries,
                    whole_keys,
                    whole_values,
                    glob_mask,
                    glob_top,
                    glob_total,
                    glob_out,
                    glob_grad_own,
                ),
            )

        def back_skip():
            return (
                jnp.zeros((batch_seqs, glob_rows, head_cols), jnp.float32),
                jnp.zeros((batch_seqs, LEN, head_cols), jnp.float32),
                jnp.zeros((batch_seqs, LEN, head_cols), jnp.float32),
            )

        glob_query_grad, whole_key_grad, whole_value_grad = lax.cond(
            seq_index == 0, back_here, back_skip
        )
        glob_dense = jnp.transpose(
            jnp.concatenate([whole_key_grad, whole_value_grad], axis=-1), (1, 0, 2)
        )
        kv_source = kv_term + glob_dense
        kv_grad = jnp.transpose(scatter_rows(kv_source), (1, 0, 2))
        glob_query_full = jnp.pad(glob_query_grad, ((0, 0), (0, local_rows - glob_rows), (0, 0)))
        query_total = query_grad + jnp.where(glob_flag, glob_query_full, 0.0)
        qkv_low_grad = (
            jnp.stack([query_total, kv_grad[..., :head_cols], kv_grad[..., head_cols:]], axis=2)
            .astype(jnp.bfloat16)
            .reshape(-1, 3 * head_cols)
        )
        qkv_total = qkv_total + jnp.einsum(
            "rd,rc->dc", first_low, qkv_low_grad, preferred_element_type=jnp.float32
        )
        first_grad = (
            lax.psum(
                jnp.einsum(
                    "rc,dc->rd", qkv_low_grad, qkv_flat, preferred_element_type=jnp.float32
                ).astype(jnp.bfloat16),
                "mp",
            )
            .astype(jnp.float32)
            .reshape(rows_in.shape)
        )
        gain_one_total = gain_one_total + jnp.sum(first_grad * normed_one, axis=(0, 1))
        bias_one_total = bias_one_total + jnp.sum(first_grad, axis=(0, 1))
        input_grads.append(hidden_grad + norm_back(first_grad, normed_one, inverse_one, first_gain))
    matrix_grads = (
        lax.psum_scatter(
            qkv_total.reshape(model_width, 3, head_cols).astype(jnp.bfloat16),
            "seq",
            scatter_dimension=0,
            tiled=True,
        ).astype(jnp.float32),
        lax.psum_scatter(
            out_total.astype(jnp.bfloat16), "seq", scatter_dimension=1, tiled=True
        ).astype(jnp.float32),
        lax.psum_scatter(
            up_total.astype(jnp.bfloat16), "seq", scatter_dimension=0, tiled=True
        ).astype(jnp.float32),
        lax.psum_scatter(
            down_total.astype(jnp.bfloat16), "seq", scatter_dimension=1, tiled=True
        ).astype(jnp.float32),
    )
    matrix_grads = (
        lax.psum(matrix_grads[0].astype(jnp.bfloat16), "batch").astype(jnp.float32),
        lax.psum(matrix_grads[1].astype(jnp.bfloat16), "batch").astype(jnp.float32),
        lax.psum(matrix_grads[2].astype(jnp.bfloat16), "batch").astype(jnp.float32),
        lax.psum(matrix_grads[3].astype(jnp.bfloat16), "batch").astype(jnp.float32),
    )
    vector_grads = lax.psum(
        (
            gain_one_total,
            bias_one_total,
            gain_two_total,
            bias_two_total,
            up_bias_total,
            down_bias_total,
        ),
        ("seq", "batch"),
    )
    return (
        jnp.concatenate(outputs_all, axis=0),
        jnp.concatenate(input_grads, axis=0),
        vector_grads[0],
        vector_grads[1],
        matrix_grads[0],
        matrix_grads[1],
        vector_grads[2],
        vector_grads[3],
        matrix_grads[2],
        vector_grads[4],
        matrix_grads[3],
        vector_grads[5],
    )


def solution(mesh):
    placed = (
        P("batch", "seq", None),
        P("batch", None),
        P("batch", "seq", None),
        P(),
        P(),
        P(None, None, "mp"),
        P("mp", None),
        P(),
        P(),
        P(None, "mp"),
        P("mp"),
        P("mp", None),
        P(),
        P("batch", "seq", None),
    )
    sizes = mesh.shape
    by_heads = sizes["seq"] in (4, 8) and sizes["batch"] == 4 and sizes["mp"] == 2
    return jax.shard_map(
        local if by_heads else local_by_blocks,
        mesh=mesh,
        in_specs=placed,
        out_specs=(
            P("batch", "seq", None),
            P("batch", "seq", None),
            P(),
            P(),
            P("seq", None, "mp"),
            P("mp", "seq"),
            P(),
            P(),
            P("seq", "mp"),
            P("mp"),
            P("mp", "seq"),
            P(),
        ),
        check_vma=False,
    )
```
